256 devices in a mesh: dp: 2 (over y_hi), context: 16 (over y_lo, z), tensor: 8 (over x, core).
Axes of the slice: x: 4, y: 4 (y_hi: 2, y_lo: 2; y = y_hi * 2 + y_lo), z: 8, core: 2. Of those that a mesh axis runs over, the one named last changes fastest.
Arguments:
- queries: bfloat16 [8192, 8192], P(('dp', 'context'), 'tensor'), parts along dimension 0, may hold values from -6 to 6
- keys: bfloat16 [8192, 1024], P(('dp', 'context'), 'tensor'), parts along dimension 0, may hold values from -12 to 12
- values: bfloat16 [8192, 1024], P(('dp', 'context'), 'tensor'), parts along dimension 0, may hold values from -6 to 6
- span_order: int32 [64], P('dp'), parts along dimension 0, may hold values from 0 to 31, each once
- out_weight: bfloat16 [8192, 4096], P('tensor'), may hold values from -0.25 to 0.25
Outputs:
- projected: bfloat16 [8192, 4096], P(('dp', 'context', 'tensor')), parts along dimension 0
The draws below stay inside these ranges and needn't reach their ends.
There are 2 independent parts, one for each index of `dp`. The reference program is written for one: setup_inputs(seed, part) draws one part's arguments, and reference() takes and returns one part's arrays. A program takes and returns all parts, laid end to end along the dimension named above; an argument that names none is the same for every part. Nothing has to cross between parts.
All inputs are finite; a program needn't handle non-finite values.
Results may differ from the reference program's by a relative error of at most 0.02.
Values may be sent and summed in bfloat16 or wider, within the bound.
A program may use at most 64 MiB of HBM per device.

```python
import math
import jax
import jax.numpy as jnp
from jax import lax

HEADS = 64
KV_HEADS = 8
HEAD_DIM = 128
D_OUT = 4096
SPAN = 128
SEQ = 4096
N_CONTEXT = 16
N_TENSOR = 8


def draw_queries(key, part):
    key = jax.random.fold_in(key, 3)
    first_key = jax.random.fold_in(key, 0)
    full_shape = (SEQ, HEADS * HEAD_DIM)
    result = jnp.clip(jax.random.normal(first_key, full_shape, jnp.float32), -6.0, 6.0)
    return result.astype(jnp.bfloat16)


def draw_keys(key, part):
    key = jax.random.fold_in(key, 5)
    first_key, second_key = jax.random.split(key, 2)
    log_scale = jax.random.uniform(second_key, (SEQ, KV_HEADS, 1), jnp.float32, jnp.log(1.2), jnp.log(1.8))
    row_scale = jnp.exp(log_scale)
    result = jax.random.normal(first_key, (SEQ, KV_HEADS, HEAD_DIM), jnp.float32) * row_scale
    result = jnp.clip(result, -12.0, 12.0)
    return result.reshape(SEQ, KV_HEADS * HEAD_DIM).astype(jnp.bfloat16)


def steps_of(rng, shape, cuts, smallest, top_value):
    loudness, own = 1.0, jax.random.fold_in(rng, 6)
    for position, shards_of in cuts:
        draws = jnp.exp(jax.random.uniform(jax.random.fold_in(own, position), (shards_of,), jnp.float32, smallest / len(cuts), top_value / len(cuts)))
        loudness = loudness * jnp.repeat(draws, shape[position] // shards_of).reshape([-1 if axis == position else 1 for axis in range(len(shape))])
    return loudness


def gaussian(own_key, shape, deviation, reach, shards=(), held_as=jnp.bfloat16):
    gain = steps_of(own_key, shape, shards, -0.22, 0.18) if shards else 1.0
    drawn = jax.random.normal(own_key, shape, jnp.float32) * deviation * gain
    return jnp.minimum(jnp.maximum(drawn, -reach), reach).astype(held_as)


def setup_inputs(seed: int = 0, part: int = 0) -> dict:
    seeds = jax.random.split(jax.random.key(seed), 6)
    part_splits = jax.random.split(jax.random.fold_in(seeds[5], part), 6)
    return {
        "queries": draw_queries(jax.random.fold_in(jax.random.fold_in(seeds[5], part), 71), part),
        "keys": draw_keys(jax.random.fold_in(jax.random.fold_in(seeds[5], part), 71), part),
        "values": gaussian(part_splits[2], (SEQ, KV_HEADS * HEAD_DIM), 1.0, 6.0, ((0, 16), (1, 8))),
        "span_order": jax.random.permutation(part_splits[3], 2 * N_CONTEXT).astype(jnp.int32),
        "out_weight": gaussian(seeds[4], (HEADS * HEAD_DIM, D_OUT), 512 ** -0.5, 0.25, ((0, 8),)),
    }


def reference(queries, keys, values, span_order, out_weight):
    seq_len = queries.shape[0]
    group_size = HEADS // KV_HEADS
    row_ids = jnp.arange(seq_len, dtype=jnp.int32)
    positions = span_order[row_ids // SPAN].astype(jnp.int32) * SPAN + row_ids % SPAN
    key_heads = keys.astype(jnp.float32).reshape(seq_len, KV_HEADS, HEAD_DIM)
    value_heads = values.astype(jnp.float32).reshape(seq_len, KV_HEADS, HEAD_DIM)
    block_len = math.gcd(seq_len, 128)
    query_blocks = queries.reshape(seq_len // block_len, block_len, KV_HEADS, group_size, HEAD_DIM)
    pos_blocks = positions.reshape(seq_len // block_len, block_len)
    score_scale = 1.0 / math.sqrt(HEAD_DIM)

    def attend_block(inputs):
        q_block, q_pos = inputs
        scores = jnp.einsum('qkgd,skd->kgqs', q_block.astype(jnp.float32), key_heads) * score_scale
        allowed = positions[None, :] <= q_pos[:, None]
        scores = jnp.where(allowed, scores, jnp.float32(-1e+30))
        row_max = lax.optimization_barrier(jnp.max(scores, axis=-1, keepdims=True))
        weights = jnp.where(allowed, jnp.exp(scores - row_max), jnp.float32(0.0))
        totals = lax.optimization_barrier(jnp.sum(weights, axis=-1))
        rounded = lax.optimization_barrier(weights.astype(jnp.bfloat16))
        mixed = jnp.einsum('kgqs,skd->kgqd', rounded.astype(jnp.float32), value_heads)
        mixed = mixed / totals[..., None]
        mixed = jnp.transpose(mixed, (2, 0, 1, 3))
        return mixed.astype(jnp.bfloat16).reshape(block_len, HEADS * HEAD_DIM)
    attended = lax.map(attend_block, (query_blocks, pos_blocks)).reshape(seq_len, HEADS * HEAD_DIM)
    width = HEADS * HEAD_DIM // N_TENSOR
    result = jnp.zeros((seq_len, out_weight.shape[1]), jnp.float32)
    for member in range(N_TENSOR):
        partial_sum = jnp.dot(attended[:, member * width:(member + 1) * width], out_weight[member * width:(member + 1) * width], preferred_element_type=jnp.float32)
        rounded_sum = lax.optimization_barrier(partial_sum.astype(jnp.bfloat16))
        result = result + rounded_sum.astype(jnp.float32)
    return result.astype(jnp.bfloat16)
```

```python
import math

import jax
import jax.numpy as jnp
from jax import lax
from jax.experimental import pallas as pl
from jax.experimental.pallas import tpu as pltpu
from jax.sharding import PartitionSpec as P

HEAD_DIM = 128
SPAN = 128
RING = 8
COLUMNS = 2
CHIPS = 4
ROUNDS = 10
TILE = 1024
LOWEST = -1e30
MESH = pl.DeviceIdType.MESH

UP = [(0, 1, 0), (0, 1, 1), (0, 2, 0), (0, 2, 1), (0, 3, 0), (0, 3, 1),
      (1, 3, 0), (0, 4, 0), (1, 4, 0), (1, 3, 1)]
DOWN = [(0, -1, 1), (0, -1, 0), (0, -2, 1), (0, -2, 0), (0, -3, 1), (0, -3, 0),
        (0, -4, 1), (1, -3, 1), (1, -3, 0), (1, -4, 1)]
ACROSS = [(1, 0, 0), (1, 0, 1), (1, 1, 0), (1, -1, 1), (1, 2, 0), (1, -2, 1),
          (1, -2, 0), (1, 2, 1), (1, 1, 1), (1, -1, 0)]


def plan():
    slot_of = {(0, 0, 0): 0, (0, 0, 1): 1}
    contents = [(0, 0, 0), (0, 0, 1)]
    up_slot, down_slot, across_slot = {}, {}, {}
    for pair in range(ROUNDS // 2):
        for part in range(2):
            r = 2 * pair + part
            base = 2 * (3 * pair + part + 1)
            up_slot[r], down_slot[r] = base, base + 1
            across_slot[r] = 2 * (3 * pair + 3) + part
    slots = {}
    for r in range(ROUNDS):
        for table, names in ((up_slot, UP), (down_slot, DOWN), (across_slot, ACROSS)):
            slots[table[r]] = names[r]
    for slot in range(2, 2 + 3 * ROUNDS):
        column, offset, half = slots[slot]
        key = (column, offset % RING, half)
        slot_of[key] = slot
        contents.append(key)
    assert len(slot_of) == 2 + 3 * ROUNDS
    copies = []
    for r in range(ROUNDS):
        (uc, uo, uh), (dc, do, dh), (ac, ao, ah) = UP[r], DOWN[r], ACROSS[r]
        copies.append((
            ("minus", slot_of[(uc, (uo - 1) % RING, uh)], up_slot[r]),
            ("plus", slot_of[(dc, (do + 1) % RING, dh)], down_slot[r]),
            ("other", slot_of[(0, ao % RING, ah)], across_slot[r]),
        ))
    return contents, copies


CONTENTS, COPIES = plan()
SPANS = len(CONTENTS)
STEPS = SPANS // 2
NAMES = ("far", "next", "back", "home")
ORDER = (0, 2, 1, 3)


def kernel(order, q_hbm, k_hbm, v_hbm, w_hbm, out,
           q_in, kv_in, kv, w, qt, acc, top, att, own, sib_out, sib_in,
           far_out, far_in, near_out, near_in, span_of,
           load_sem, kv_send, kv_recv, sib_send, sib_recv,
           far_send, far_recv, near_send, near_recv):
    heads = q_in.shape[1] // HEAD_DIM
    rows = q_in.shape[0]
    context = lax.axis_index("context")
    tensor = lax.axis_index("tensor")
    y, z = context // RING, lax.rem(context, RING)
    x, core = tensor // 2, lax.rem(tensor, 2)
    targets = {
        "minus": {"context": y * RING + lax.rem(z + RING - 1, RING)},
        "plus": {"context": y * RING + lax.rem(z + 1, RING)},
        "other": {"context": (1 - y) * RING + z},
    }
    sibling = {"tensor": x * 2 + 1 - core}
    chip_next, chip_back = lax.rem(x + 1, CHIPS), lax.rem(x + CHIPS - 1, CHIPS)
    chip_far = lax.rem(x + 2, CHIPS)
    to_next, to_back = {"tensor": chip_next * 2 + core}, {"tensor": chip_back * 2 + core}

    barrier = pltpu.get_barrier_semaphore()
    for target in (*targets.values(), sibling, to_next, to_back):
        pl.semaphore_signal(barrier, inc=1, device_id=target, device_id_type=MESH)

    loads = [pltpu.make_async_copy(k_hbm, kv_in.at[0], load_sem.at[0]),
             pltpu.make_async_copy(v_hbm, kv_in.at[1], load_sem.at[1])]
    chips = (chip_far, chip_next, chip_back, x)
    for group, chip in enumerate(chips):
        for part, owner in enumerate((core, 1 - core)):
            number = 2 * group + part
            first = pl.multiple_of(chip * 64 + owner * 32, 32)
            loads.append(pltpu.make_async_copy(
                q_hbm.at[pl.ds(first, 32)], q_in.at[pl.ds(32 * number, 32)],
                load_sem.at[2 + number]))
    loads.append(pltpu.make_async_copy(w_hbm, w, load_sem.at[10]))
    for load in loads:
        load.start()

    for slot, (column, offset, half) in enumerate(CONTENTS):
        where = (y if column == 0 else 1 - y) * RING + lax.rem(z + offset, RING)
        span_of[slot] = order[2 * where + half]

    loads[0].wait()
    for half in range(2):
        kv[half, 0] = kv_in[0, half * SPAN:(half + 1) * SPAN]
    loads[1].wait()
    for half in range(2):
        kv[half, 1] = kv_in[1, half * SPAN:(half + 1) * SPAN].T

    pl.semaphore_wait(barrier, 6)

    def copy_of(name, src, dst):
        return pltpu.make_async_remote_copy(
            src_ref=kv.at[src], dst_ref=kv.at[dst],
            send_sem=kv_send.at[dst - 2], recv_sem=kv_recv.at[dst - 2],
            device_id=targets[name], device_id_type=MESH)

    for r in range(2):
        for copy in COPIES[r]:
            copy_of(*copy).start()

    scale = math.log2(math.e) / math.sqrt(HEAD_DIM)
    for load in loads[2:10]:
        load.wait()
    for head in range(heads):
        scaled = q_in[:, head * HEAD_DIM:(head + 1) * HEAD_DIM].astype(jnp.float32).T * scale
        high = scaled.astype(jnp.bfloat16)
        low = (scaled - high.astype(jnp.float32)).astype(jnp.bfloat16)
        qt[head, :HEAD_DIM] = high
        qt[head, HEAD_DIM:] = low

    lane = lax.broadcasted_iota(jnp.int32, (1, rows), 1)
    group_of = lane // 64
    chip_of = jnp.where(group_of == 0, chip_far, jnp.where(
        group_of == 1, chip_next, jnp.where(group_of == 2, chip_back, x)))
    owner_of = jnp.where(lax.rem(lane // 32, 2) == 0, core, 1 - core)
    row_of = chip_of * 64 + owner_of * 32 + lax.rem(lane, 32)
    q_span = jnp.where(row_of < SPAN, span_of[0], span_of[1])
    q_pos = q_span * SPAN + lax.rem(row_of, SPAN)

    def operands(step):
        pair = kv[pl.ds(2 * step, 2)]
        keys = pair[:, 0].reshape(2 * SPAN, HEAD_DIM)
        keys = jnp.concatenate([keys, keys], axis=1)
        values = jnp.concatenate([pair[0, 1], pair[1, 1]], axis=1)
        values = jnp.concatenate([values, jnp.ones((16, 2 * SPAN), jnp.bfloat16)], axis=0)
        return keys, values

    def scores_of(keys, head):
        return jnp.dot(keys, qt[head], preferred_element_type=jnp.float32)

    keys, values = operands(0)
    k_row = lax.broadcasted_iota(jnp.int32, (2 * SPAN, 1), 0)
    k_pos = jnp.where(k_row < SPAN, span_of[0], span_of[1]) * SPAN + lax.rem(k_row, SPAN)
    allowed = k_pos <= q_pos

    @pl.loop(0, heads)
    def _(head):
        scores = jnp.where(allowed, scores_of(keys, head), LOWEST)
        new_top = jnp.max(scores, axis=0, keepdims=True)
        weights = jnp.exp2(scores - new_top).astype(jnp.bfloat16)
        top[head] = new_top
        acc[head] = jnp.dot(values, weights, preferred_element_type=jnp.float32)

    @pl.loop(1, STEPS)
    def _(step):
        for r in range(ROUNDS):
            @pl.when(step == 3 * (r // 2) + r % 2 + 1)
            def _():
                for copy in COPIES[r]:
                    copy_of(*copy).wait_recv()
                if r + 2 < ROUNDS:
                    for copy in COPIES[r + 2]:
                        copy_of(*copy).start()

        keys, values = operands(step)
        hide_a = jnp.where(span_of[2 * step] < q_span, 0.0, LOWEST)
        hide_b = jnp.where(span_of[2 * step + 1] < q_span, 0.0, LOWEST)
        following = scores_of(keys, 0)
        for head in range(heads):
            scores = following
            if head + 1 < heads:
                following = scores_of(keys, head + 1)
            first, second = scores[:SPAN], scores[SPAN:]
            old_top = top[head]
            new_top = jnp.maximum(old_top, jnp.maximum(
                jnp.max(first, axis=0, keepdims=True) + hide_a,
                jnp.max(second, axis=0, keepdims=True) + hide_b))
            factor = jnp.exp2(old_top - new_top)
            weights = jnp.concatenate([
                jnp.exp2(first - (new_top - hide_a)).astype(jnp.bfloat16),
                jnp.exp2(second - (new_top - hide_b)).astype(jnp.bfloat16)], axis=0)
            top[head] = new_top
            acc[head] = acc[head] * factor + jnp.dot(
                values, weights, preferred_element_type=jnp.float32)

    for head in range(heads):
        mixed = acc[head, :HEAD_DIM] / acc[head, HEAD_DIM:HEAD_DIM + 1]
        att[:, head * HEAD_DIM:(head + 1) * HEAD_DIM] = mixed.T.astype(jnp.bfloat16)
    loads[10].wait()

    def sib_copy(group, tile):
        return pltpu.make_async_remote_copy(
            src_ref=sib_out.at[group, tile], dst_ref=sib_in.at[group, tile],
            send_sem=sib_send.at[group, tile], recv_sem=sib_recv.at[group, tile],
            device_id=sibling, device_id_type=MESH)

    def project(groups, tile):
        lo, hi = 64 * groups[0], 64 * (groups[-1] + 1)

        @pl.loop(0, 2)
        def _(half):
            at = pl.multiple_of(half * 512, 512)
            part = jnp.dot(att[lo:hi], w[:, pl.ds(tile * TILE + at, 512)],
                           preferred_element_type=jnp.float32).astype(jnp.bfloat16)
            for number, group in enumerate(groups):
                own[group, tile, :, pl.ds(at, 512)] = part[64 * number:64 * number + 32]
                sib_out[group, tile, :, pl.ds(at, 512)] = part[64 * number + 32:64 * number + 64]
        for group in groups:
            sib_copy(group, tile).start()

    def wide(ref, *at):
        return ref[at].astype(jnp.float32)

    def far_copy(tile):
        return pltpu.make_async_remote_copy(
            src_ref=far_out.at[tile], dst_ref=far_in.at[tile],
            send_sem=far_send.at[tile], recv_sem=far_recv.at[tile],
            device_id=to_next if tile < 2 else to_back, device_id_type=MESH)

    def near_copy(side, tile):
        return pltpu.make_async_remote_copy(
            src_ref=near_out.at[side, tile], dst_ref=near_in.at[side, tile],
            send_sem=near_send.at[side, tile], recv_sem=near_recv.at[side, tile],
            device_id=to_next if side == 0 else to_back, device_id_type=MESH)

    def send_far(tile):
        sib_copy(0, tile).wait_recv()
        far_out[tile] = (wide(own, 0, tile) + wide(sib_in, 0, tile)).astype(jnp.bfloat16)
        far_copy(tile).start()

    def send_near(side, tile):
        sib_copy(1 + side, tile).wait_recv()
        total = wide(own, 1 + side, tile) + wide(sib_in, 1 + side, tile)
        if (tile < 2) == (side == 0):
            far_copy(tile).wait_recv()
            total = total + wide(far_in, tile)
        near_out[side, tile] = total.astype(jnp.bfloat16)
        near_copy(side, tile).start()

    project((0,), 0)
    project((0,), 2)
    send_far(0)
    project((0,), 1)
    send_far(2)
    project((0,), 3)
    send_far(1)
    project((1, 2), 2)
    send_far(3)
    project((1, 2), 0)
    send_near(0, 2)
    project((1, 2), 3)
    send_near(1, 0)
    project((1, 2), 1)
    send_near(0, 3)
    send_near(1, 1)
    for tile in ORDER:
        project((3,), tile)
    for side, tile in ((0, 0), (1, 2), (0, 1), (1, 3)):
        send_near(side, tile)
    for tile in (2, 0, 3, 1):
        sib_copy(3, tile).wait_recv()
        near_copy(0, tile).wait_recv()
        near_copy(1, tile).wait_recv()
        total = (wide(own, 3, tile) + wide(sib_in, 3, tile)) + (
            wide(near_in, 0, tile) + wide(near_in, 1, tile))
        out[:, tile * TILE:(tile + 1) * TILE] = total.astype(out.dtype)

    for copies in COPIES:
        for copy in copies:
            copy_of(*copy).wait_send()
    for tile in range(4):
        for group in range(4):
            sib_copy(group, tile).wait_send()
        far_copy(tile).wait_send()
        for side in range(2):
            near_copy(side, tile).wait_send()


def on_device(queries, keys, values, span_order, out_weight):
    rows, width = queries.shape
    heads = width // HEAD_DIM
    d_out = out_weight.shape[1]
    bf16, f32 = jnp.bfloat16, jnp.float32
    sem = pltpu.SemaphoreType.DMA
    return pl.pallas_call(
        kernel,
        out_shape=jax.ShapeDtypeStruct((rows // 8, d_out), bf16),
        in_specs=[pl.BlockSpec(memory_space=pltpu.SMEM)]
        + [pl.BlockSpec(memory_space=pl.ANY)] * 4,
        out_specs=pl.BlockSpec(memory_space=pltpu.VMEM),
        scratch_shapes=[
            pltpu.VMEM((rows, width), bf16),
            pltpu.VMEM((2, rows, HEAD_DIM), bf16),
            pltpu.VMEM((SPANS, 2, SPAN, HEAD_DIM), bf16),
            pltpu.VMEM((width, d_out), bf16),
            pltpu.VMEM((heads, 2 * HEAD_DIM, rows), bf16),
            pltpu.VMEM((heads, HEAD_DIM + 16, rows), f32),
            pltpu.VMEM((heads, 1, rows), f32),
            pltpu.VMEM((rows, width), bf16),
            pltpu.VMEM((4, 4, 32, TILE), bf16),
            pltpu.VMEM((4, 4, 32, TILE), bf16),
            pltpu.VMEM((4, 4, 32, TILE), bf16),
            pltpu.VMEM((4, 32, TILE), bf16),
            pltpu.VMEM((4, 32, TILE), bf16),
            pltpu.VMEM((2, 4, 32, TILE), bf16),
            pltpu.VMEM((2, 4, 32, TILE), bf16),
            pltpu.SMEM((SPANS,), jnp.int32),
            sem((11,)), sem((SPANS - 2,)), sem((SPANS - 2,)),
            sem((4, 4)), sem((4, 4)), sem((4,)), sem((4,)), sem((2, 4)), sem((2, 4)),
        ],
        compiler_params=pltpu.CompilerParams(
            collective_id=0, has_side_effects=True, vmem_limit_bytes=56 * 1024 * 1024),
        cost_estimate=pl.CostEstimate(
            flops=3 * 2 * rows * width * 4096, bytes_accessed=10 * 2**20,
            transcendentals=heads * rows * 4096),
    )(span_order, queries, keys, values, out_weight)


def solution(mesh):
    return jax.shard_map(
        on_device,
        mesh=mesh,
        in_specs=(
            P(("dp", "context"), "tensor"),
            P(("dp", "context"), "tensor"),
            P(("dp", "context"), "tensor"),
            P("dp"),
            P("tensor", None),
        ),
        out_specs=P(("dp", "context", "tensor"), None),
        check_vma=False,
    )
```

```python
import math

import jax
import jax.numpy as jnp
from jax import lax
from jax.experimental import pallas as pl
from jax.experimental.pallas import tpu as pltpu
from jax.sharding import PartitionSpec as P

HEAD_DIM = 128
SPAN = 128
RING = 8
COLUMNS = 2
CHIPS = 4
ROUNDS = 10
TILE = 512
TILES = 8
HALF = TILES // 2
LOWEST = -1e30
MESH = pl.DeviceIdType.MESH

UP = [(0, 1, 0), (0, 1, 1), (0, 2, 0), (0, 2, 1), (0, 3, 0), (0, 3, 1),
      (1, 3, 0), (0, 4, 0), (1, 4, 0), (1, 3, 1)]
DOWN = [(0, -1, 1), (0, -1, 0), (0, -2, 1), (0, -2, 0), (0, -3, 1), (0, -3, 0),
        (0, -4, 1), (1, -3, 1), (1, -3, 0), (1, -4, 1)]
ACROSS = [(1, 0, 0), (1, 0, 1), (1, 1, 0), (1, -1, 1), (1, 2, 0), (1, -2, 1),
          (1, -2, 0), (1, 2, 1), (1, 1, 1), (1, -1, 0)]


def plan():
    slot_of = {(0, 0, 0): 0, (0, 0, 1): 1}
    contents = [(0, 0, 0), (0, 0, 1)]
    up_slot, down_slot, across_slot = {}, {}, {}
    for pair in range(ROUNDS // 2):
        for part in range(2):
            r = 2 * pair + part
            base = 2 * (3 * pair + part + 1)
            up_slot[r], down_slot[r] = base, base + 1
            across_slot[r] = 2 * (3 * pair + 3) + part
    slots = {}
    for r in range(ROUNDS):
        for table, names in ((up_slot, UP), (down_slot, DOWN), (across_slot, ACROSS)):
            slots[table[r]] = names[r]
    for slot in range(2, 2 + 3 * ROUNDS):
        column, offset, half = slots[slot]
        key = (column, offset % RING, half)
        slot_of[key] = slot
        contents.append(key)
    assert len(slot_of) == 2 + 3 * ROUNDS
    copies = []
    for r in range(ROUNDS):
        (uc, uo, uh), (dc, do, dh), (ac, ao, ah) = UP[r], DOWN[r], ACROSS[r]
        copies.append((
            ("minus", slot_of[(uc, (uo - 1) % RING, uh)], up_slot[r]),
            ("plus", slot_of[(dc, (do + 1) % RING, dh)], down_slot[r]),
            ("other", slot_of[(0, ao % RING, ah)], across_slot[r]),
        ))
    return contents, copies


CONTENTS, COPIES = plan()
SPANS = len(CONTENTS)
STEPS = SPANS // 2
ORDER = tuple(part * HALF + tile for tile in range(HALF) for part in range(2))


def kernel(order, q_hbm, k_hbm, v_hbm, w_hbm, out,
           q_in, kv_in, kv, w, qt, acc, top, att, own, sib_out, sib_in,
           far_out, far_in, near_out, near_in, result, span_of,
           load_sem, kv_send, kv_recv, sib_send, sib_recv,
           far_send, far_recv, near_send, near_recv, out_sem):
    heads = q_in.shape[1] // HEAD_DIM
    rows = q_in.shape[0]
    context = lax.axis_index("context")
    tensor = lax.axis_index("tensor")
    y, z = context // RING, lax.rem(context, RING)
    x, core = tensor // 2, lax.rem(tensor, 2)
    targets = {
        "minus": {"context": y * RING + lax.rem(z + RING - 1, RING)},
        "plus": {"context": y * RING + lax.rem(z + 1, RING)},
        "other": {"context": (1 - y) * RING + z},
    }
    sibling = {"tensor": x * 2 + 1 - core}
    chip_next, chip_back = lax.rem(x + 1, CHIPS), lax.rem(x + CHIPS - 1, CHIPS)
    chip_far = lax.rem(x + 2, CHIPS)
    to_next, to_back = {"tensor": chip_next * 2 + core}, {"tensor": chip_back * 2 + core}

    barrier = pltpu.get_barrier_semaphore()
    for target in (*targets.values(), sibling, to_next, to_back):
        pl.semaphore_signal(barrier, inc=1, device_id=target, device_id_type=MESH)

    loads = [pltpu.make_async_copy(k_hbm, kv_in.at[0], load_sem.at[0]),
             pltpu.make_async_copy(v_hbm, kv_in.at[1], load_sem.at[1])]
    chips = (chip_far, chip_next, chip_back, x)
    for group, chip in enumerate(chips):
        for part, owner in enumerate((core, 1 - core)):
            number = 2 * group + part
            first = pl.multiple_of(chip * 64 + owner * 32, 32)
            loads.append(pltpu.make_async_copy(
                q_hbm.at[pl.ds(first, 32)], q_in.at[pl.ds(32 * number, 32)],
                load_sem.at[2 + number]))
    loads.append(pltpu.make_async_copy(w_hbm, w, load_sem.at[10]))
    for load in loads:
        load.start()

    for slot, (column, offset, half) in enumerate(CONTENTS):
        where = (y if column == 0 else 1 - y) * RING + lax.rem(z + offset, RING)
        span_of[slot] = order[2 * where + half]

    loads[0].wait()
    for half in range(2):
        kv[half, 0] = kv_in[0, half * SPAN:(half + 1) * SPAN]
    loads[1].wait()
    for half in range(2):
        kv[half, 1] = kv_in[1, half * SPAN:(half + 1) * SPAN].T

    pl.semaphore_wait(barrier, 6)

    def copy_of(name, src, dst):
        return pltpu.make_async_remote_copy(
            src_ref=kv.at[src], dst_ref=kv.at[dst],
            send_sem=kv_send.at[dst - 2], recv_sem=kv_recv.at[dst - 2],
            device_id=targets[name], device_id_type=MESH)

    for r in range(2):
        for copy in COPIES[r]:
            copy_of(*copy).start()

    scale = math.log2(math.e) / math.sqrt(HEAD_DIM)
    for load in loads[2:10]:
        load.wait()
    for head in range(heads):
        scaled = q_in[:, head * HEAD_DIM:(head + 1) * HEAD_DIM].astype(jnp.float32).T * scale
        high = scaled.astype(jnp.bfloat16)
        low = (scaled - high.astype(jnp.float32)).astype(jnp.bfloat16)
        qt[head, :HEAD_DIM] = high
        qt[head, HEAD_DIM:] = low

    lane = lax.broadcasted_iota(jnp.int32, (1, rows), 1)
    group_of = lane // 64
    chip_of = jnp.where(group_of == 0, chip_far, jnp.where(
        group_of == 1, chip_next, jnp.where(group_of == 2, chip_back, x)))
    owner_of = jnp.where(lax.rem(lane // 32, 2) == 0, core, 1 - core)
    row_of = chip_of * 64 + owner_of * 32 + lax.rem(lane, 32)
    q_span = jnp.where(row_of < SPAN, span_of[0], span_of[1])
    q_pos = q_span * SPAN + lax.rem(row_of, SPAN)

    def operands(step):
        pair = kv[pl.ds(2 * step, 2)]
        keys = pair[:, 0].reshape(2 * SPAN, HEAD_DIM)
        keys = jnp.concatenate([keys, keys], axis=1)
        values = jnp.concatenate([pair[0, 1], pair[1, 1]], axis=1)
        values = jnp.concatenate([values, jnp.ones((16, 2 * SPAN), jnp.bfloat16)], axis=0)
        return keys, values

    def scores_of(keys, head):
        return jnp.dot(keys, qt[head], preferred_element_type=jnp.float32)

    keys, values = operands(0)
    k_row = lax.broadcasted_iota(jnp.int32, (2 * SPAN, 1), 0)
    k_pos = jnp.where(k_row < SPAN, span_of[0], span_of[1]) * SPAN + lax.rem(k_row, SPAN)
    hide = jnp.where(k_pos <= q_pos, 0.0, LOWEST)
    following = scores_of(keys, 0)
    for head in range(heads):
        scores = following + hide
        if head + 1 < heads:
            following = scores_of(keys, head + 1)
        new_top = jnp.max(scores, axis=0, keepdims=True)
        weights = jnp.exp2(scores - new_top).astype(jnp.bfloat16)
        top[head] = new_top
        acc[head] = jnp.dot(values, weights, preferred_element_type=jnp.float32)

    @pl.loop(1, STEPS)
    def _(step):
        for r in range(ROUNDS):
            @pl.when(step == 3 * (r // 2) + r % 2 + 1)
            def _():
                for copy in COPIES[r]:
                    copy_of(*copy).wait_recv()
                if r + 2 < ROUNDS:
                    for copy in COPIES[r + 2]:
                        copy_of(*copy).start()

        keys, values = operands(step)
        hide_a = jnp.where(span_of[2 * step] < q_span, 0.0, LOWEST)
        hide_b = jnp.where(span_of[2 * step + 1] < q_span, 0.0, LOWEST)
        following = scores_of(keys, 0)
        for head in range(heads):
            scores = following
            if head + 1 < heads:
                following = scores_of(keys, head + 1)
            first, second = scores[:SPAN], scores[SPAN:]
            old_top = top[head]
            new_top = jnp.maximum(old_top, jnp.maximum(
                jnp.max(first, axis=0, keepdims=True) + hide_a,
                jnp.max(second, axis=0, keepdims=True) + hide_b))
            factor = jnp.exp2(old_top - new_top)
            weights = jnp.concatenate([
                jnp.exp2(first - (new_top - hide_a)).astype(jnp.bfloat16),
                jnp.exp2(second - (new_top - hide_b)).astype(jnp.bfloat16)], axis=0)
            top[head] = new_top
            acc[head] = acc[head] * factor + jnp.dot(
                values, weights, preferred_element_type=jnp.float32)

    for head in range(heads):
        mixed = acc[head, :HEAD_DIM] * (1.0 / acc[head, HEAD_DIM:HEAD_DIM + 1])
        att[:, head * HEAD_DIM:(head + 1) * HEAD_DIM] = mixed.astype(jnp.bfloat16).T
    loads[10].wait()

    def sib_copy(tile, part):
        at = 0 if part == 0 else pl.ds(1, 3)
        return pltpu.make_async_remote_copy(
            src_ref=sib_out.at[tile, at], dst_ref=sib_in.at[tile, at],
            send_sem=sib_send.at[tile, part], recv_sem=sib_recv.at[tile, part],
            device_id=sibling, device_id_type=MESH)

    def project(tile):
        part = jnp.dot(att[...], w[:, tile * TILE:(tile + 1) * TILE],
                       preferred_element_type=jnp.float32).astype(jnp.bfloat16)
        part = part.reshape(4, 2, 32, TILE)
        sib_out[tile] = part[:, 1]
        sib_copy(tile, 0).start()
        sib_copy(tile, 1).start()
        own[tile] = part[:, 0]

    def both(tile, group):
        return own[tile, group].astype(jnp.float32) + sib_in[tile, group].astype(jnp.float32)

    def far_copy(tile):
        return pltpu.make_async_remote_copy(
            src_ref=far_out.at[tile], dst_ref=far_in.at[tile],
            send_sem=far_send.at[tile], recv_sem=far_recv.at[tile],
            device_id=to_next if tile < HALF else to_back, device_id_type=MESH)

    def near_copy(side, tile):
        return pltpu.make_async_remote_copy(
            src_ref=near_out.at[side, tile], dst_ref=near_in.at[side, tile],
            send_sem=near_send.at[side, tile], recv_sem=near_recv.at[side, tile],
            device_id=to_next if side == 0 else to_back, device_id_type=MESH)

    def out_copy(tile):
        at = pl.ds(tile * TILE, TILE)
        return pltpu.make_async_copy(result.at[:, at], out.at[:, at], out_sem.at[tile])

    def send_far(tile):
        sib_copy(tile, 0).wait_recv()
        far_out[tile] = both(tile, 0).astype(jnp.bfloat16)
        far_copy(tile).start()

    def send_near(side, tile):
        second = (tile < HALF) == (side == 0)
        if not second:
            sib_copy(tile, 1).wait_recv()
        total = both(tile, 1 + side)
        if second:
            far_copy(tile).wait_recv()
            total = total + far_in[tile].astype(jnp.float32)
        near_out[side, tile] = total.astype(jnp.bfloat16)
        near_copy(side, tile).start()

    project(ORDER[0])
    for earlier, tile in zip(ORDER, ORDER[1:]):
        project(tile)
        send_far(earlier)
    send_far(ORDER[-1])
    for tile in ORDER:
        send_near(0 if tile >= HALF else 1, tile)
    for tile in ORDER:
        send_near(0 if tile < HALF else 1, tile)
    for tile in ORDER:
        near_copy(0, tile).wait_recv()
        near_copy(1, tile).wait_recv()
        total = both(tile, 3) + (near_in[0, tile].astype(jnp.float32)
                                 + near_in[1, tile].astype(jnp.float32))
        result[:, tile * TILE:(tile + 1) * TILE] = total.astype(out.dtype)
        out_copy(tile).start()

    for copies in COPIES:
        for copy in copies:
            copy_of(*copy).wait_send()
    for tile in range(TILES):
        for part in range(2):
            sib_copy(tile, part).wait_send()
            near_copy(part, tile).wait_send()
        far_copy(tile).wait_send()
        out_copy(tile).wait()


def on_device(queries, keys, values, span_order, out_weight):
    rows, width = queries.shape
    heads = width // HEAD_DIM
    d_out = out_weight.shape[1]
    bf16, f32 = jnp.bfloat16, jnp.float32
    sem = pltpu.SemaphoreType.DMA
    return pl.pallas_call(
        kernel,
        out_shape=jax.ShapeDtypeStruct((rows // 8, d_out), bf16),
        in_specs=[pl.BlockSpec(memory_space=pltpu.SMEM)]
        + [pl.BlockSpec(memory_space=pl.ANY)] * 4,
        out_specs=pl.BlockSpec(memory_space=pl.ANY),
        scratch_shapes=[
            pltpu.VMEM((rows, width), bf16),
            pltpu.VMEM((2, rows, HEAD_DIM), bf16),
            pltpu.VMEM((SPANS, 2, SPAN, HEAD_DIM), bf16),
            pltpu.VMEM((width, d_out), bf16),
            pltpu.VMEM((heads, 2 * HEAD_DIM, rows), bf16),
            pltpu.VMEM((heads, HEAD_DIM + 16, rows), f32),
            pltpu.VMEM((heads, 1, rows), f32),
            pltpu.VMEM((rows, width), bf16),
            pltpu.VMEM((TILES, 4, 32, TILE), bf16),
            pltpu.VMEM((TILES, 4, 32, TILE), bf16),
            pltpu.VMEM((TILES, 4, 32, TILE), bf16),
            pltpu.VMEM((TILES, 32, TILE), bf16),
            pltpu.VMEM((TILES, 32, TILE), bf16),
            pltpu.VMEM((2, TILES, 32, TILE), bf16),
            pltpu.VMEM((2, TILES, 32, TILE), bf16),
            pltpu.VMEM((rows // 8, d_out), bf16),
            pltpu.SMEM((SPANS,), jnp.int32),
            sem((11,)), sem((SPANS - 2,)), sem((SPANS - 2,)),
            sem((TILES, 2)), sem((TILES, 2)), sem((TILES,)), sem((TILES,)),
            sem((2, TILES)), sem((2, TILES)), sem((TILES,)),
        ],
        compiler_params=pltpu.CompilerParams(
            collective_id=0, has_side_effects=True, vmem_limit_bytes=56 * 1024 * 1024),
        cost_estimate=pl.CostEstimate(
            flops=3 * 2 * rows * width * 4096, bytes_accessed=10 * 2**20,
            transcendentals=heads * rows * 4096),
    )(span_order, queries, keys, values, out_weight)


def solution(mesh):
    return jax.shard_map(
        on_device,
        mesh=mesh,
        in_specs=(
            P(("dp", "context"), "tensor"),
            P(("dp", "context"), "tensor"),
            P(("dp", "context"), "tensor"),
            P("dp"),
            P("tensor", None),
        ),
        out_specs=P(("dp", "context", "tensor"), None),
        check_vma=False,
    )
```

```python
import math

import jax
import jax.numpy as jnp
from jax import lax
from jax.experimental import pallas as pl
from jax.experimental.pallas import tpu as pltpu
from jax.sharding import PartitionSpec as P

HEAD_DIM = 128
SPAN = 128
RING = 8
COLUMNS = 2
CHIPS = 4
ROUNDS = 10
TILE = 512
TILES = 8
HALF = TILES // 2
LOWEST = -1e30
MESH = pl.DeviceIdType.MESH

UP = [(0, 1, 0), (0, 1, 1), (0, 2, 0), (0, 2, 1), (0, 3, 0), (0, 3, 1),
      (1, 3, 0), (0, 4, 0), (1, 4, 0), (1, 3, 1)]
DOWN = [(0, -1, 1), (0, -1, 0), (0, -2, 1), (0, -2, 0), (0, -3, 1), (0, -3, 0),
        (0, -4, 1), (1, -3, 1), (1, -3, 0), (1, -4, 1)]
ACROSS = [(1, 0, 0), (1, 0, 1), (1, 1, 0), (1, -1, 1), (1, 2, 0), (1, -2, 1),
          (1, -2, 0), (1, 2, 1), (1, 1, 1), (1, -1, 0)]


def plan():
    slot_of = {(0, 0, 0): 0, (0, 0, 1): 1}
    contents = [(0, 0, 0), (0, 0, 1)]
    up_slot, down_slot, across_slot = {}, {}, {}
    for pair in range(ROUNDS // 2):
        for part in range(2):
            r = 2 * pair + part
            base = 2 * (3 * pair + part + 1)
            up_slot[r], down_slot[r] = base, base + 1
            across_slot[r] = 2 * (3 * pair + 3) + part
    slots = {}
    for r in range(ROUNDS):
        for table, names in ((up_slot, UP), (down_slot, DOWN), (across_slot, ACROSS)):
            slots[table[r]] = names[r]
    for slot in range(2, 2 + 3 * ROUNDS):
        column, offset, half = slots[slot]
        key = (column, offset % RING, half)
        slot_of[key] = slot
        contents.append(key)
    assert len(slot_of) == 2 + 3 * ROUNDS
    copies = []
    for r in range(ROUNDS):
        (uc, uo, uh), (dc, do, dh), (ac, ao, ah) = UP[r], DOWN[r], ACROSS[r]
        copies.append((
            ("minus", slot_of[(uc, (uo - 1) % RING, uh)], up_slot[r]),
            ("plus", slot_of[(dc, (do + 1) % RING, dh)], down_slot[r]),
            ("other", slot_of[(0, ao % RING, ah)], across_slot[r]),
        ))
    return contents, copies


CONTENTS, COPIES = plan()
SPANS = len(CONTENTS)
PAIRS = 3
STEPS = (SPANS - 2) // (2 * PAIRS)
ORDER = tuple(part * HALF + tile for tile in range(HALF) for part in range(2))


def kernel(order, q_hbm, k_hbm, v_hbm, w_hbm, out,
           q_in, kv_in, kv, w, qt, acc, top, att, own, sib_out, sib_in,
           far_out, far_in, near_out, near_in, result, span_of,
           load_sem, kv_send, kv_recv, sib_send, sib_recv,
           far_send, far_recv, near_send, near_recv, out_sem):
    heads = q_in.shape[1] // HEAD_DIM
    rows = q_in.shape[0]
    context = lax.axis_index("context")
    tensor = lax.axis_index("tensor")
    y, z = context // RING, lax.rem(context, RING)
    x, core = tensor // 2, lax.rem(tensor, 2)
    targets = {
        "minus": {"context": y * RING + lax.rem(z + RING - 1, RING)},
        "plus": {"context": y * RING + lax.rem(z + 1, RING)},
        "other": {"context": (1 - y) * RING + z},
    }
    sibling = {"tensor": x * 2 + 1 - core}
    chip_next, chip_back = lax.rem(x + 1, CHIPS), lax.rem(x + CHIPS - 1, CHIPS)
    chip_far = lax.rem(x + 2, CHIPS)
    to_next, to_back = {"tensor": chip_next * 2 + core}, {"tensor": chip_back * 2 + core}

    barrier = pltpu.get_barrier_semaphore()
    for target in (*targets.values(), sibling, to_next, to_back):
        pl.semaphore_signal(barrier, inc=1, device_id=target, device_id_type=MESH)

    loads = [pltpu.make_async_copy(k_hbm, kv_in.at[0], load_sem.at[0]),
             pltpu.make_async_copy(v_hbm, kv_in.at[1], load_sem.at[1])]
    chips = (chip_far, chip_next, chip_back, x)
    for group, chip in enumerate(chips):
        for part, owner in enumerate((core, 1 - core)):
            number = 2 * group + part
            first = pl.multiple_of(chip * 64 + owner * 32, 32)
            loads.append(pltpu.make_async_copy(
                q_hbm.at[pl.ds(first, 32)], q_in.at[pl.ds(32 * number, 32)],
                load_sem.at[2 + number]))
    loads.append(pltpu.make_async_copy(w_hbm, w, load_sem.at[10]))
    for load in loads:
        load.start()

    for slot, (column, offset, half) in enumerate(CONTENTS):
        where = (y if column == 0 else 1 - y) * RING + lax.rem(z + offset, RING)
        span_of[slot] = order[2 * where + half]

    loads[0].wait()
    for half in range(2):
        kv[half, 0] = kv_in[0, half * SPAN:(half + 1) * SPAN]
    loads[1].wait()
    for half in range(2):
        kv[half, 1] = kv_in[1, half * SPAN:(half + 1) * SPAN].T

    pl.semaphore_wait(barrier, 6)

    def copy_of(name, src, dst):
        return pltpu.make_async_remote_copy(
            src_ref=kv.at[src], dst_ref=kv.at[dst],
            send_sem=kv_send.at[dst - 2], recv_sem=kv_recv.at[dst - 2],
            device_id=targets[name], device_id_type=MESH)

    for r in range(2):
        for copy in COPIES[r]:
            copy_of(*copy).start()

    scale = math.log2(math.e) / math.sqrt(HEAD_DIM)
    for load in loads[2:10]:
        load.wait()
    for head in range(heads):
        scaled = q_in[:, head * HEAD_DIM:(head + 1) * HEAD_DIM].astype(jnp.float32).T * scale
        high = scaled.astype(jnp.bfloat16)
        low = (scaled - high.astype(jnp.float32)).astype(jnp.bfloat16)
        qt[head, :HEAD_DIM] = high
        qt[head, HEAD_DIM:] = low

    lane = lax.broadcasted_iota(jnp.int32, (1, rows), 1)
    group_of = lane // 64
    chip_of = jnp.where(group_of == 0, chip_far, jnp.where(
        group_of == 1, chip_next, jnp.where(group_of == 2, chip_back, x)))
    owner_of = jnp.where(lax.rem(lane // 32, 2) == 0, core, 1 - core)
    row_of = chip_of * 64 + owner_of * 32 + lax.rem(lane, 32)
    q_span = jnp.where(row_of < SPAN, span_of[0], span_of[1])
    q_pos = q_span * SPAN + lax.rem(row_of, SPAN)

    def operands(first, pairs):
        keys, values = [], []
        for number in range(pairs):
            pair = kv[pl.ds(first + 2 * number, 2)]
            part = pair[:, 0].reshape(2 * SPAN, HEAD_DIM)
            keys.append(jnp.concatenate([part, part], axis=1))
            values += [pair[0, 1], pair[1, 1]]
        values = jnp.concatenate(values, axis=1)
        ones = jnp.ones((16, 2 * SPAN * pairs), jnp.bfloat16)
        return keys, jnp.concatenate([values, ones], axis=0)

    def scores_of(keys, head):
        return [jnp.dot(part, qt[head], preferred_element_type=jnp.float32) for part in keys]

    def receive(r):
        for copy in COPIES[r]:
            copy_of(*copy).wait_recv()
        if r + 2 < ROUNDS:
            for copy in COPIES[r + 2]:
                copy_of(*copy).start()

    keys, values = operands(0, 1)
    k_row = lax.broadcasted_iota(jnp.int32, (2 * SPAN, 1), 0)
    k_pos = jnp.where(k_row < SPAN, span_of[0], span_of[1]) * SPAN + lax.rem(k_row, SPAN)
    hide = jnp.where(k_pos <= q_pos, 0.0, LOWEST)
    following = scores_of(keys, 0)
    for head in range(heads):
        scores = following[0] + hide
        if head + 1 < heads:
            following = scores_of(keys, head + 1)
        new_top = jnp.max(scores, axis=0, keepdims=True)
        weights = jnp.exp2(scores - new_top).astype(jnp.bfloat16)
        top[head] = new_top
        acc[head] = jnp.dot(values, weights, preferred_element_type=jnp.float32)

    receive(0)

    @pl.loop(0, STEPS)
    def _(step):
        for number in range(STEPS):
            @pl.when(step == number)
            def _():
                receive(2 * number + 1)

        first = 2 + 2 * PAIRS * step
        keys, values = operands(first, PAIRS)
        hide = [jnp.where(span_of[first + number] < q_span, 0.0, LOWEST)
                for number in range(2 * PAIRS)]
        following = scores_of(keys, 0)
        for head in range(heads):
            if head == heads // 2:
                for number in range(STEPS - 1):
                    @pl.when(step == number)
                    def _():
                        receive(2 * number + 2)
            scores = [part[half * SPAN:(half + 1) * SPAN] for part in following for half in range(2)]
            if head + 1 < heads:
                following = scores_of(keys, head + 1)
            old_top = top[head]
            new_top = old_top
            for part, hidden in zip(scores, hide):
                new_top = jnp.maximum(new_top, jnp.max(part, axis=0, keepdims=True) + hidden)
            factor = jnp.exp2(old_top - new_top)
            weights = jnp.concatenate([
                jnp.exp2(part - (new_top - hidden)).astype(jnp.bfloat16)
                for part, hidden in zip(scores, hide)], axis=0)
            top[head] = new_top
            acc[head] = acc[head] * factor + jnp.dot(
                values, weights, preferred_element_type=jnp.float32)

    for head in range(heads):
        mixed = acc[head, :HEAD_DIM] * (1.0 / acc[head, HEAD_DIM:HEAD_DIM + 1])
        att[:, head * HEAD_DIM:(head + 1) * HEAD_DIM] = mixed.astype(jnp.bfloat16).T
    loads[10].wait()

    def sib_copy(tile, part):
        at = 0 if part == 0 else pl.ds(1, 3)
        return pltpu.make_async_remote_copy(
            src_ref=sib_out.at[tile, at], dst_ref=sib_in.at[tile, at],
            send_sem=sib_send.at[tile, part], recv_sem=sib_recv.at[tile, part],
            device_id=sibling, device_id_type=MESH)

    def project(tile):
        part = jnp.dot(att[...], w[:, tile * TILE:(tile + 1) * TILE],
                       preferred_element_type=jnp.float32).astype(jnp.bfloat16)
        part = part.reshape(4, 2, 32, TILE)
        sib_out[tile] = part[:, 1]
        sib_copy(tile, 0).start()
        sib_copy(tile, 1).start()
        own[tile] = part[:, 0]

    def both(tile, group):
        return own[tile, group].astype(jnp.float32) + sib_in[tile, group].astype(jnp.float32)

    def far_copy(tile):
        return pltpu.make_async_remote_copy(
            src_ref=far_out.at[tile], dst_ref=far_in.at[tile],
            send_sem=far_send.at[tile], recv_sem=far_recv.at[tile],
            device_id=to_next if tile < HALF else to_back, device_id_type=MESH)

    def near_copy(side, tile):
        return pltpu.make_async_remote_copy(
            src_ref=near_out.at[side, tile], dst_ref=near_in.at[side, tile],
            send_sem=near_send.at[side, tile], recv_sem=near_recv.at[side, tile],
            device_id=to_next if side == 0 else to_back, device_id_type=MESH)

    def out_copy(tile):
        at = pl.ds(tile * TILE, TILE)
        return pltpu.make_async_copy(result.at[:, at], out.at[:, at], out_sem.at[tile])

    def send_far(tile):
        sib_copy(tile, 0).wait_recv()
        far_out[tile] = both(tile, 0).astype(jnp.bfloat16)
        far_copy(tile).start()

    def send_near(side, tile):
        second = (tile < HALF) == (side == 0)
        if not second:
            sib_copy(tile, 1).wait_recv()
        total = both(tile, 1 + side)
        if second:
            far_copy(tile).wait_recv()
            total = total + far_in[tile].astype(jnp.float32)
        near_out[side, tile] = total.astype(jnp.bfloat16)
        near_copy(side, tile).start()

    project(ORDER[0])
    for earlier, tile in zip(ORDER, ORDER[1:]):
        project(tile)
        send_far(earlier)
    send_far(ORDER[-1])
    for tile in ORDER:
        send_near(0 if tile >= HALF else 1, tile)
    for tile in ORDER:
        send_near(0 if tile < HALF else 1, tile)
    for tile in ORDER:
        near_copy(0, tile).wait_recv()
        near_copy(1, tile).wait_recv()
        total = both(tile, 3) + (near_in[0, tile].astype(jnp.float32)
                                 + near_in[1, tile].astype(jnp.float32))
        result[:, tile * TILE:(tile + 1) * TILE] = total.astype(out.dtype)
        out_copy(tile).start()

    for copies in COPIES:
        for copy in copies:
            copy_of(*copy).wait_send()
    for tile in range(TILES):
        for part in range(2):
            sib_copy(tile, part).wait_send()
            near_copy(part, tile).wait_send()
        far_copy(tile).wait_send()
        out_copy(tile).wait()


def on_device(queries, keys, values, span_order, out_weight):
    rows, width = queries.shape
    heads = width // HEAD_DIM
    d_out = out_weight.shape[1]
    bf16, f32 = jnp.bfloat16, jnp.float32
    sem = pltpu.SemaphoreType.DMA
    return pl.pallas_call(
        kernel,
        out_shape=jax.ShapeDtypeStruct((rows // 8, d_out), bf16),
        in_specs=[pl.BlockSpec(memory_space=pltpu.SMEM)]
        + [pl.BlockSpec(memory_space=pl.ANY)] * 4,
        out_specs=pl.BlockSpec(memory_space=pl.ANY),
        scratch_shapes=[
            pltpu.VMEM((rows, width), bf16),
            pltpu.VMEM((2, rows, HEAD_DIM), bf16),
            pltpu.VMEM((SPANS, 2, SPAN, HEAD_DIM), bf16),
            pltpu.VMEM((width, d_out), bf16),
            pltpu.VMEM((heads, 2 * HEAD_DIM, rows), bf16),
            pltpu.VMEM((heads, HEAD_DIM + 16, rows), f32),
            pltpu.VMEM((heads, 1, rows), f32),
            pltpu.VMEM((rows, width), bf16),
            pltpu.VMEM((TILES, 4, 32, TILE), bf16),
            pltpu.VMEM((TILES, 4, 32, TILE), bf16),
            pltpu.VMEM((TILES, 4, 32, TILE), bf16),
            pltpu.VMEM((TILES, 32, TILE), bf16),
            pltpu.VMEM((TILES, 32, TILE), bf16),
            pltpu.VMEM((2, TILES, 32, TILE), bf16),
            pltpu.VMEM((2, TILES, 32, TILE), bf16),
            pltpu.VMEM((rows // 8, d_out), bf16),
            pltpu.SMEM((SPANS,), jnp.int32),
            sem((11,)), sem((SPANS - 2,)), sem((SPANS - 2,)),
            sem((TILES, 2)), sem((TILES, 2)), sem((TILES,)), sem((TILES,)),
            sem((2, TILES)), sem((2, TILES)), sem((TILES,)),
        ],
        compiler_params=pltpu.CompilerParams(
            collective_id=0, has_side_effects=True, vmem_limit_bytes=56 * 1024 * 1024),
        cost_estimate=pl.CostEstimate(
            flops=3 * 2 * rows * width * 4096, bytes_accessed=10 * 2**20,
            transcendentals=heads * rows * 4096),
    )(span_order, queries, keys, values, out_weight)


def solution(mesh):
    return jax.shard_map(
        on_device,
        mesh=mesh,
        in_specs=(
            P(("dp", "context"), "tensor"),
            P(("dp", "context"), "tensor"),
            P(("dp", "context"), "tensor"),
            P("dp"),
            P("tensor", None),
        ),
        out_specs=P(("dp", "context", "tensor"), None),
        check_vma=False,
    )
```

```python
import math

import jax
import jax.numpy as jnp
from jax import lax
from jax.experimental import pallas as pl
from jax.experimental.pallas import tpu as pltpu
from jax.sharding import PartitionSpec as P

HEAD_DIM = 128
SPAN = 128
RING = 8
COLUMNS = 2
CHIPS = 4
ROUNDS = 10
TILE = 512
TILES = 8
HALF = TILES // 2
LOWEST = -1e30
MESH = pl.DeviceIdType.MESH

UP = [(0, 1, 0), (0, 1, 1), (0, 2, 0), (0, 2, 1), (0, 3, 0), (0, 3, 1),
      (1, 3, 0), (0, 4, 0), (1, 4, 0), (1, 3, 1)]
DOWN = [(0, -1, 1), (0, -1, 0), (0, -2, 1), (0, -2, 0), (0, -3, 1), (0, -3, 0),
        (0, -4, 1), (1, -3, 1), (1, -3, 0), (1, -4, 1)]
ACROSS = [(1, 0, 0), (1, 0, 1), (1, 1, 0), (1, -1, 1), (1, 2, 0), (1, -2, 1),
          (1, -2, 0), (1, 2, 1), (1, 1, 1), (1, -1, 0)]


def plan():
    slot_of = {(0, 0, 0): 0, (0, 0, 1): 1}
    contents = [(0, 0, 0), (0, 0, 1)]
    up_slot = {r: 2 + 3 * r for r in range(ROUNDS)}
    down_slot = {r: 3 + 3 * r for r in range(ROUNDS)}
    across_slot = {r: 4 + 3 * r for r in range(ROUNDS)}
    slots = {}
    for r in range(ROUNDS):
        for table, names in ((up_slot, UP), (down_slot, DOWN), (across_slot, ACROSS)):
            slots[table[r]] = names[r]
    for slot in range(2, 2 + 3 * ROUNDS):
        column, offset, half = slots[slot]
        key = (column, offset % RING, half)
        slot_of[key] = slot
        contents.append(key)
    assert len(slot_of) == 2 + 3 * ROUNDS
    copies = []
    for r in range(ROUNDS):
        (uc, uo, uh), (dc, do, dh), (ac, ao, ah) = UP[r], DOWN[r], ACROSS[r]
        copies.append((
            ("minus", slot_of[(uc, (uo - 1) % RING, uh)], up_slot[r]),
            ("plus", slot_of[(dc, (do + 1) % RING, dh)], down_slot[r]),
            ("other", slot_of[(0, ao % RING, ah)], across_slot[r]),
        ))
    return contents, copies


CONTENTS, COPIES = plan()
SPANS = len(CONTENTS)
ORDER = tuple(part * HALF + tile for tile in range(HALF) for part in range(2))


def kernel(order, q_hbm, k_hbm, v_hbm, w_hbm, out,
           q_in, kv_in, kv, w, qt, acc, top, att, own, sib_out, sib_in,
           far_out, far_in, near_out, near_in, result, span_of,
           load_sem, kv_send, kv_recv, sib_send, sib_recv,
           far_send, far_recv, near_send, near_recv, out_sem):
    heads = q_in.shape[1] // HEAD_DIM
    rows = q_in.shape[0]
    context = lax.axis_index("context")
    tensor = lax.axis_index("tensor")
    y, z = context // RING, lax.rem(context, RING)
    x, core = tensor // 2, lax.rem(tensor, 2)
    targets = {
        "minus": {"context": y * RING + lax.rem(z + RING - 1, RING)},
        "plus": {"context": y * RING + lax.rem(z + 1, RING)},
        "other": {"context": (1 - y) * RING + z},
    }
    sibling = {"tensor": x * 2 + 1 - core}
    chip_next, chip_back = lax.rem(x + 1, CHIPS), lax.rem(x + CHIPS - 1, CHIPS)
    chip_far = lax.rem(x + 2, CHIPS)
    to_next, to_back = {"tensor": chip_next * 2 + core}, {"tensor": chip_back * 2 + core}

    barrier = pltpu.get_barrier_semaphore()
    for target in (*targets.values(), sibling, to_next, to_back):
        pl.semaphore_signal(barrier, inc=1, device_id=target, device_id_type=MESH)

    loads = [pltpu.make_async_copy(k_hbm, kv_in.at[0], load_sem.at[0]),
             pltpu.make_async_copy(v_hbm, kv_in.at[1], load_sem.at[1])]
    chips = (chip_far, chip_next, chip_back, x)
    for group, chip in enumerate(chips):
        for part, owner in enumerate((core, 1 - core)):
            number = 2 * group + part
            first = pl.multiple_of(chip * 64 + owner * 32, 32)
            loads.append(pltpu.make_async_copy(
                q_hbm.at[pl.ds(first, 32)], q_in.at[pl.ds(32 * number, 32)],
                load_sem.at[2 + number]))
    loads.append(pltpu.make_async_copy(w_hbm, w, load_sem.at[10]))
    for load in loads:
        load.start()

    for slot, (column, offset, half) in enumerate(CONTENTS):
        where = (y if column == 0 else 1 - y) * RING + lax.rem(z + offset, RING)
        span_of[slot] = order[2 * where + half]

    loads[0].wait()
    for half in range(2):
        kv[half, 0] = kv_in[0, half * SPAN:(half + 1) * SPAN]
    loads[1].wait()
    for half in range(2):
        kv[half, 1] = kv_in[1, half * SPAN:(half + 1) * SPAN].T

    pl.semaphore_wait(barrier, 6)

    def copy_of(name, src, dst):
        return pltpu.make_async_remote_copy(
            src_ref=kv.at[src], dst_ref=kv.at[dst],
            send_sem=kv_send.at[dst - 2], recv_sem=kv_recv.at[dst - 2],
            device_id=targets[name], device_id_type=MESH)

    for copy in COPIES[0]:
        copy_of(*copy).start()

    scale = math.log2(math.e) / math.sqrt(HEAD_DIM)
    for load in loads[2:10]:
        load.wait()
    for head in range(heads):
        scaled = q_in[:, head * HEAD_DIM:(head + 1) * HEAD_DIM].astype(jnp.float32).T * scale
        high = scaled.astype(jnp.bfloat16)
        low = (scaled - high.astype(jnp.float32)).astype(jnp.bfloat16)
        qt[head, :HEAD_DIM] = high
        qt[head, HEAD_DIM:] = low

    for first, second in zip(COPIES[0], COPIES[1]):
        copy_of(*first).wait_send()
        copy_of(*second).start()

    lane = lax.broadcasted_iota(jnp.int32, (1, rows), 1)
    group_of = lane // 64
    chip_of = jnp.where(group_of == 0, chip_far, jnp.where(
        group_of == 1, chip_next, jnp.where(group_of == 2, chip_back, x)))
    owner_of = jnp.where(lax.rem(lane // 32, 2) == 0, core, 1 - core)
    row_of = chip_of * 64 + owner_of * 32 + lax.rem(lane, 32)
    q_span = jnp.where(row_of < SPAN, span_of[0], span_of[1])
    q_pos = q_span * SPAN + lax.rem(row_of, SPAN)

    def operands(first, count):
        spans = kv[pl.ds(first, count)]
        keys = spans[:, 0].reshape(count * SPAN, HEAD_DIM)
        keys = jnp.concatenate([keys, keys], axis=1)
        values = jnp.concatenate([spans[number, 1] for number in range(count)], axis=1)
        ones = jnp.ones((16, count * SPAN), jnp.bfloat16)
        return keys, jnp.concatenate([values, ones], axis=0)

    def scores_of(keys, head):
        return jnp.dot(keys, qt[head], preferred_element_type=jnp.float32)

    def receive(r):
        following = COPIES[r + 2] if r + 2 < ROUNDS else ()
        here = 2 + 3 * r
        for copy in following:
            if copy[1] < here:
                copy_of(*copy).start()
        for copy in COPIES[r]:
            copy_of(*copy).wait_recv()
            for later in following:
                if later[1] == copy[2]:
                    copy_of(*later).start()

    keys, values = operands(0, 2)
    k_row = lax.broadcasted_iota(jnp.int32, (2 * SPAN, 1), 0)
    k_pos = jnp.where(k_row < SPAN, span_of[0], span_of[1]) * SPAN + lax.rem(k_row, SPAN)
    hide = jnp.where(k_pos <= q_pos, 0.0, LOWEST)
    following = scores_of(keys, 0)
    for head in range(heads):
        scores = following + hide
        if head + 1 < heads:
            following = scores_of(keys, head + 1)
        new_top = jnp.max(scores, axis=0, keepdims=True)
        weights = jnp.exp2(scores - new_top).astype(jnp.bfloat16)
        top[head] = new_top
        acc[head] = jnp.dot(values, weights, preferred_element_type=jnp.float32)

    @pl.loop(0, ROUNDS)
    def _(step):
        for r in range(ROUNDS):
            @pl.when(step == r)
            def _():
                receive(r)

        first = 2 + 3 * step
        keys, values = operands(first, 3)
        hide = [jnp.where(span_of[first + number] < q_span, 0.0, LOWEST) for number in range(3)]
        following = scores_of(keys, 0)
        for head in range(heads):
            scores = [following[number * SPAN:(number + 1) * SPAN] for number in range(3)]
            if head + 1 < heads:
                following = scores_of(keys, head + 1)
            old_top = top[head]
            new_top = old_top
            for part, hidden in zip(scores, hide):
                new_top = jnp.maximum(new_top, jnp.max(part, axis=0, keepdims=True) + hidden)
            factor = jnp.exp2(old_top - new_top)
            weights = jnp.concatenate([
                jnp.exp2(part - (new_top - hidden)).astype(jnp.bfloat16)
                for part, hidden in zip(scores, hide)], axis=0)
            top[head] = new_top
            acc[head] = acc[head] * factor + jnp.dot(
                values, weights, preferred_element_type=jnp.float32)

    for head in range(heads):
        mixed = acc[head, :HEAD_DIM] * (1.0 / acc[head, HEAD_DIM:HEAD_DIM + 1])
        att[:, head * HEAD_DIM:(head + 1) * HEAD_DIM] = mixed.astype(jnp.bfloat16).T
    loads[10].wait()

    def sib_copy(tile, part):
        at = 0 if part == 0 else pl.ds(1, 3)
        return pltpu.make_async_remote_copy(
            src_ref=sib_out.at[tile, at], dst_ref=sib_in.at[tile, at],
            send_sem=sib_send.at[tile, part], recv_sem=sib_recv.at[tile, part],
            device_id=sibling, device_id_type=MESH)

    def project(tile):
        part = jnp.dot(att[...], w[:, tile * TILE:(tile + 1) * TILE],
                       preferred_element_type=jnp.float32).astype(jnp.bfloat16)
        part = part.reshape(4, 2, 32, TILE)
        sib_out[tile] = part[:, 1]
        sib_copy(tile, 0).start()
        sib_copy(tile, 1).start()
        own[tile] = part[:, 0]

    def both(tile, group):
        return own[tile, group].astype(jnp.float32) + sib_in[tile, group].astype(jnp.float32)

    def far_copy(tile):
        return pltpu.make_async_remote_copy(
            src_ref=far_out.at[tile], dst_ref=far_in.at[tile],
            send_sem=far_send.at[tile], recv_sem=far_recv.at[tile],
            device_id=to_next if tile < HALF else to_back, device_id_type=MESH)

    def near_copy(side, tile):
        return pltpu.make_async_remote_copy(
            src_ref=near_out.at[side, tile], dst_ref=near_in.at[side, tile],
            send_sem=near_send.at[side, tile], recv_sem=near_recv.at[side, tile],
            device_id=to_next if side == 0 else to_back, device_id_type=MESH)

    def out_copy(tile):
        at = pl.ds(tile * TILE, TILE)
        return pltpu.make_async_copy(result.at[:, at], out.at[:, at], out_sem.at[tile])

    def send_far(tile):
        sib_copy(tile, 0).wait_recv()
        far_out[tile] = both(tile, 0).astype(jnp.bfloat16)
        far_copy(tile).start()

    def send_near(side, tile):
        second = (tile < HALF) == (side == 0)
        if not second:
            sib_copy(tile, 1).wait_recv()
        total = both(tile, 1 + side)
        if second:
            far_copy(tile).wait_recv()
            total = total + far_in[tile].astype(jnp.float32)
        near_out[side, tile] = total.astype(jnp.bfloat16)
        near_copy(side, tile).start()

    project(ORDER[0])
    for earlier, tile in zip(ORDER, ORDER[1:]):
        project(tile)
        send_far(earlier)
    send_far(ORDER[-1])
    for tile in ORDER:
        send_near(0 if tile >= HALF else 1, tile)
    for tile in ORDER:
        send_near(0 if tile < HALF else 1, tile)
    for tile in ORDER:
        near_copy(0, tile).wait_recv()
        near_copy(1, tile).wait_recv()
        total = both(tile, 3) + (near_in[0, tile].astype(jnp.float32)
                                 + near_in[1, tile].astype(jnp.float32))
        result[:, tile * TILE:(tile + 1) * TILE] = total.astype(out.dtype)
        out_copy(tile).start()

    for copies in COPIES[1:]:
        for copy in copies:
            copy_of(*copy).wait_send()
    for tile in range(TILES):
        for part in range(2):
            sib_copy(tile, part).wait_send()
            near_copy(part, tile).wait_send()
        far_copy(tile).wait_send()
        out_copy(tile).wait()


def on_device(queries, keys, values, span_order, out_weight):
    rows, width = queries.shape
    heads = width // HEAD_DIM
    d_out = out_weight.shape[1]
    bf16, f32 = jnp.bfloat16, jnp.float32
    sem = pltpu.SemaphoreType.DMA
    return pl.pallas_call(
        kernel,
        out_shape=jax.ShapeDtypeStruct((rows // 8, d_out), bf16),
        in_specs=[pl.BlockSpec(memory_space=pltpu.SMEM)]
        + [pl.BlockSpec(memory_space=pl.ANY)] * 4,
        out_specs=pl.BlockSpec(memory_space=pl.ANY),
        scratch_shapes=[
            pltpu.VMEM((rows, width), bf16),
            pltpu.VMEM((2, rows, HEAD_DIM), bf16),
            pltpu.VMEM((SPANS, 2, SPAN, HEAD_DIM), bf16),
            pltpu.VMEM((width, d_out), bf16),
            pltpu.VMEM((heads, 2 * HEAD_DIM, rows), bf16),
            pltpu.VMEM((heads, HEAD_DIM + 16, rows), f32),
            pltpu.VMEM((heads, 1, rows), f32),
            pltpu.VMEM((rows, width), bf16),
            pltpu.VMEM((TILES, 4, 32, TILE), bf16),
            pltpu.VMEM((TILES, 4, 32, TILE), bf16),
            pltpu.VMEM((TILES, 4, 32, TILE), bf16),
            pltpu.VMEM((TILES, 32, TILE), bf16),
            pltpu.VMEM((TILES, 32, TILE), bf16),
            pltpu.VMEM((2, TILES, 32, TILE), bf16),
            pltpu.VMEM((2, TILES, 32, TILE), bf16),
            pltpu.VMEM((rows // 8, d_out), bf16),
            pltpu.SMEM((SPANS,), jnp.int32),
            sem((11,)), sem((SPANS - 2,)), sem((SPANS - 2,)),
            sem((TILES, 2)), sem((TILES, 2)), sem((TILES,)), sem((TILES,)),
            sem((2, TILES)), sem((2, TILES)), sem((TILES,)),
        ],
        compiler_params=pltpu.CompilerParams(
            collective_id=0, has_side_effects=True, vmem_limit_bytes=56 * 1024 * 1024),
        cost_estimate=pl.CostEstimate(
            flops=3 * 2 * rows * width * 4096, bytes_accessed=10 * 2**20,
            transcendentals=heads * rows * 4096),
    )(span_order, queries, keys, values, out_weight)


def solution(mesh):
    return jax.shard_map(
        on_device,
        mesh=mesh,
        in_specs=(
            P(("dp", "context"), "tensor"),
            P(("dp", "context"), "tensor"),
            P(("dp", "context"), "tensor"),
            P("dp"),
            P("tensor", None),
        ),
        out_specs=P(("dp", "context", "tensor"), None),
        check_vma=False,
    )
```

```python
import math

import jax
import jax.numpy as jnp
from jax import lax
from jax.experimental import pallas as pl
from jax.experimental.pallas import tpu as pltpu
from jax.sharding import PartitionSpec as P

HEAD_DIM = 128
SPAN = 128
RING = 8
COLUMNS = 2
CHIPS = 4
ROUNDS = 10
TILE = 512
TILES = 8
HALF = TILES // 2
LOWEST = -1e30
MESH = pl.DeviceIdType.MESH

UP = [(0, 1, 0), (0, 1, 1), (0, 2, 0), (0, 2, 1), (0, 3, 0), (0, 3, 1),
      (1, 3, 0), (0, 4, 0), (1, 4, 0), (1, 3, 1)]
DOWN = [(0, -1, 1), (0, -1, 0), (0, -2, 1), (0, -2, 0), (0, -3, 1), (0, -3, 0),
        (0, -4, 1), (1, -3, 1), (1, -3, 0), (1, -4, 1)]
ACROSS = [(1, 0, 0), (1, 0, 1), (1, 1, 0), (1, -1, 1), (1, 2, 0), (1, -2, 1),
          (1, -2, 0), (1, 2, 1), (1, 1, 1), (1, -1, 0)]


def plan():
    slot_of = {(0, 0, 0): 0, (0, 0, 1): 1}
    contents = [(0, 0, 0), (0, 0, 1)]
    up_slot = {r: 2 + 3 * r for r in range(ROUNDS)}
    down_slot = {r: 3 + 3 * r for r in range(ROUNDS)}
    across_slot = {r: 4 + 3 * r for r in range(ROUNDS)}
    slots = {}
    for r in range(ROUNDS):
        for table, names in ((up_slot, UP), (down_slot, DOWN), (across_slot, ACROSS)):
            slots[table[r]] = names[r]
    for slot in range(2, 2 + 3 * ROUNDS):
        column, offset, half = slots[slot]
        key = (column, offset % RING, half)
        slot_of[key] = slot
        contents.append(key)
    assert len(slot_of) == 2 + 3 * ROUNDS
    copies = []
    for r in range(ROUNDS):
        (uc, uo, uh), (dc, do, dh), (ac, ao, ah) = UP[r], DOWN[r], ACROSS[r]
        copies.append((
            ("minus", slot_of[(uc, (uo - 1) % RING, uh)], up_slot[r]),
            ("plus", slot_of[(dc, (do + 1) % RING, dh)], down_slot[r]),
            ("other", slot_of[(0, ao % RING, ah)], across_slot[r]),
        ))
    return contents, copies


CONTENTS, COPIES = plan()
SPANS = len(CONTENTS)
ORDER = tuple(part * HALF + tile for tile in range(HALF) for part in range(2))


def kernel(order_hbm, q_hbm, k_hbm, v_hbm, w_hbm, out,
           q_in, kv, w, qt, acc, top, att, own, sib_out, sib_in,
           far_out, far_in, near_out, near_in, result, order, span_of,
           load_sem, own_send, own_recv, kv_send, kv_recv, sib_send, sib_recv,
           far_send, far_recv, near_send, near_recv, out_sem):
    heads = q_in.shape[1] // HEAD_DIM
    rows = q_in.shape[0]
    context = lax.axis_index("context")
    tensor = lax.axis_index("tensor")
    y, z = context // RING, lax.rem(context, RING)
    x, core = tensor // 2, lax.rem(tensor, 2)
    targets = {
        "minus": {"context": y * RING + lax.rem(z + RING - 1, RING)},
        "plus": {"context": y * RING + lax.rem(z + 1, RING)},
        "other": {"context": (1 - y) * RING + z},
    }
    sibling = {"tensor": x * 2 + 1 - core}
    chip_next, chip_back = lax.rem(x + 1, CHIPS), lax.rem(x + CHIPS - 1, CHIPS)
    chip_far = lax.rem(x + 2, CHIPS)
    to_next, to_back = {"tensor": chip_next * 2 + core}, {"tensor": chip_back * 2 + core}

    barrier = pltpu.get_barrier_semaphore()
    for target in (*targets.values(), sibling, to_next, to_back):
        pl.semaphore_signal(barrier, inc=1, device_id=target, device_id_type=MESH)

    loads = []
    for half in range(2):
        for part, source in enumerate((k_hbm, v_hbm)):
            loads.append(pltpu.make_async_copy(
                source.at[pl.ds(half * SPAN, SPAN)], kv.at[half, part],
                load_sem.at[2 * half + part]))
    chips = (chip_far, chip_next, chip_back, x)
    for group, chip in enumerate(chips):
        for part, owner in enumerate((core, 1 - core)):
            number = 2 * group + part
            first = pl.multiple_of(chip * 64 + owner * 32, 32)
            loads.append(pltpu.make_async_copy(
                q_hbm.at[pl.ds(first, 32)], q_in.at[pl.ds(32 * number, 32)],
                load_sem.at[4 + number]))
    loads.append(pltpu.make_async_copy(order_hbm, order, load_sem.at[13]))
    loads.append(pltpu.make_async_copy(w_hbm, w, load_sem.at[12]))
    for load in loads[:-1]:
        load.start()

    def own_copies(r):
        for name, src, dst in COPIES[r]:
            for part, source in enumerate((k_hbm, v_hbm)):
                yield pltpu.make_async_remote_copy(
                    src_ref=source.at[pl.ds(src * SPAN, SPAN)], dst_ref=kv.at[dst, part],
                    send_sem=own_send.at[dst - 2, part], recv_sem=own_recv.at[dst - 2, part],
                    device_id=targets[name], device_id_type=MESH)

    def copy_of(name, src, dst):
        return pltpu.make_async_remote_copy(
            src_ref=kv.at[src], dst_ref=kv.at[dst],
            send_sem=kv_send.at[dst - 8], recv_sem=kv_recv.at[dst - 8],
            device_id=targets[name], device_id_type=MESH)

    pl.semaphore_wait(barrier, 6)
    for copy in own_copies(0):
        copy.start()
    loads[-1].start()

    loads[12].wait()
    for slot, (column, offset, half) in enumerate(CONTENTS):
        where = (y if column == 0 else 1 - y) * RING + lax.rem(z + offset, RING)
        span_of[slot] = order[2 * where + half]

    scale = math.log2(math.e) / math.sqrt(HEAD_DIM)
    for load in loads[4:12]:
        load.wait()
    for head in range(heads):
        scaled = q_in[:, head * HEAD_DIM:(head + 1) * HEAD_DIM].astype(jnp.float32).T * scale
        high = scaled.astype(jnp.bfloat16)
        low = (scaled - high.astype(jnp.float32)).astype(jnp.bfloat16)
        qt[head, :HEAD_DIM] = high
        qt[head, HEAD_DIM:] = low

    for first, second in zip(own_copies(0), own_copies(1)):
        first.wait_send()
        second.start()
    for load in loads[:4]:
        load.wait()

    lane = lax.broadcasted_iota(jnp.int32, (1, rows), 1)
    group_of = lane // 64
    chip_of = jnp.where(group_of == 0, chip_far, jnp.where(
        group_of == 1, chip_next, jnp.where(group_of == 2, chip_back, x)))
    owner_of = jnp.where(lax.rem(lane // 32, 2) == 0, core, 1 - core)
    row_of = chip_of * 64 + owner_of * 32 + lax.rem(lane, 32)
    q_span = jnp.where(row_of < SPAN, span_of[0], span_of[1])
    q_pos = q_span * SPAN + lax.rem(row_of, SPAN)

    def operands(first, count):
        spans = kv[pl.ds(first, count)]
        keys = spans[:, 0].reshape(count * SPAN, HEAD_DIM)
        keys = jnp.concatenate([keys, keys], axis=1)
        values = spans[:, 1].reshape(count * SPAN, HEAD_DIM).T
        ones = jnp.ones((16, count * SPAN), jnp.bfloat16)
        return keys, jnp.concatenate([values, ones], axis=0)

    def scores_of(keys, head):
        return jnp.dot(keys, qt[head], preferred_element_type=jnp.float32)

    def receive(r):
        following = COPIES[r + 2] if r + 2 < ROUNDS else ()
        here = 2 + 3 * r
        for copy in following:
            if copy[1] < here:
                copy_of(*copy).start()
        first = list(own_copies(r)) if r < 2 else ()
        for number, copy in enumerate(COPIES[r]):
            if r < 2:
                first[2 * number].wait_recv()
                first[2 * number + 1].wait_recv()
            else:
                copy_of(*copy).wait_recv()
            for later in following:
                if later[1] == copy[2]:
                    copy_of(*later).start()

    keys, values = operands(0, 2)
    k_row = lax.broadcasted_iota(jnp.int32, (2 * SPAN, 1), 0)
    k_pos = jnp.where(k_row < SPAN, span_of[0], span_of[1]) * SPAN + lax.rem(k_row, SPAN)
    hide = jnp.where(k_pos <= q_pos, 0.0, LOWEST)
    following = scores_of(keys, 0)
    for head in range(heads):
        scores = following + hide
        if head + 1 < heads:
            following = scores_of(keys, head + 1)
        new_top = jnp.max(scores, axis=0, keepdims=True)
        weights = jnp.exp2(scores - new_top).astype(jnp.bfloat16)
        top[head] = new_top
        acc[head] = jnp.dot(values, weights, preferred_element_type=jnp.float32)

    @pl.loop(0, ROUNDS)
    def _(step):
        for r in range(ROUNDS):
            @pl.when(step == r)
            def _():
                receive(r)

        first = 2 + 3 * step
        keys, values = operands(first, 3)
        hide = [jnp.where(span_of[first + number] < q_span, 0.0, LOWEST) for number in range(3)]
        following = scores_of(keys, 0)
        for head in range(heads):
            scores = [following[number * SPAN:(number + 1) * SPAN] for number in range(3)]
            if head + 1 < heads:
                following = scores_of(keys, head + 1)
            old_top = top[head]
            new_top = old_top
            for part, hidden in zip(scores, hide):
                new_top = jnp.maximum(new_top, jnp.max(part, axis=0, keepdims=True) + hidden)
            factor = jnp.exp2(old_top - new_top)
            weights = jnp.concatenate([
                jnp.exp2(part - (new_top - hidden)).astype(jnp.bfloat16)
                for part, hidden in zip(scores, hide)], axis=0)
            top[head] = new_top
            acc[head] = acc[head] * factor + jnp.dot(
                values, weights, preferred_element_type=jnp.float32)

    for head in range(heads):
        mixed = acc[head, :HEAD_DIM] * (1.0 / acc[head, HEAD_DIM:HEAD_DIM + 1])
        att[:, head * HEAD_DIM:(head + 1) * HEAD_DIM] = mixed.astype(jnp.bfloat16).T
    loads[13].wait()

    def sib_copy(tile, part):
        at = 0 if part == 0 else pl.ds(1, 3)
        return pltpu.make_async_remote_copy(
            src_ref=sib_out.at[tile, at], dst_ref=sib_in.at[tile, at],
            send_sem=sib_send.at[tile, part], recv_sem=sib_recv.at[tile, part],
            device_id=sibling, device_id_type=MESH)

    def project(tile):
        part = jnp.dot(att[...], w[:, tile * TILE:(tile + 1) * TILE],
                       preferred_element_type=jnp.float32).astype(jnp.bfloat16)
        part = part.reshape(4, 2, 32, TILE)
        sib_out[tile] = part[:, 1]
        sib_copy(tile, 0).start()
        sib_copy(tile, 1).start()
        own[tile] = part[:, 0]

    def both(tile, group):
        return own[tile, group].astype(jnp.float32) + sib_in[tile, group].astype(jnp.float32)

    def far_copy(tile):
        return pltpu.make_async_remote_copy(
            src_ref=far_out.at[tile], dst_ref=far_in.at[tile],
            send_sem=far_send.at[tile], recv_sem=far_recv.at[tile],
            device_id=to_next if tile < HALF else to_back, device_id_type=MESH)

    def near_copy(side, tile):
        return pltpu.make_async_remote_copy(
            src_ref=near_out.at[side, tile], dst_ref=near_in.at[side, tile],
            send_sem=near_send.at[side, tile], recv_sem=near_recv.at[side, tile],
            device_id=to_next if side == 0 else to_back, device_id_type=MESH)

    def out_copy(tile):
        at = pl.ds(tile * TILE, TILE)
        return pltpu.make_async_copy(result.at[:, at], out.at[:, at], out_sem.at[tile])

    def send_far(tile):
        sib_copy(tile, 0).wait_recv()
        far_out[tile] = both(tile, 0).astype(jnp.bfloat16)
        far_copy(tile).start()

    def send_near(side, tile):
        second = (tile < HALF) == (side == 0)
        if not second:
            sib_copy(tile, 1).wait_recv()
        total = both(tile, 1 + side)
        if second:
            far_copy(tile).wait_recv()
            total = total + far_in[tile].astype(jnp.float32)
        near_out[side, tile] = total.astype(jnp.bfloat16)
        near_copy(side, tile).start()

    project(ORDER[0])
    for earlier, tile in zip(ORDER, ORDER[1:]):
        project(tile)
        send_far(earlier)
    send_far(ORDER[-1])
    for tile in ORDER:
        send_near(0 if tile >= HALF else 1, tile)
    for tile in ORDER:
        send_near(0 if tile < HALF else 1, tile)
    for tile in ORDER:
        near_copy(0, tile).wait_recv()
        near_copy(1, tile).wait_recv()
        total = both(tile, 3) + (near_in[0, tile].astype(jnp.float32)
                                 + near_in[1, tile].astype(jnp.float32))
        result[:, tile * TILE:(tile + 1) * TILE] = total.astype(out.dtype)
        out_copy(tile).start()

    for copy in own_copies(1):
        copy.wait_send()
    for copies in COPIES[2:]:
        for copy in copies:
            copy_of(*copy).wait_send()
    for tile in range(TILES):
        for part in range(2):
            sib_copy(tile, part).wait_send()
            near_copy(part, tile).wait_send()
        far_copy(tile).wait_send()
        out_copy(tile).wait()


def copy_kernel(source, out, copy_sem):
    rows = source.shape[0] // 4
    copies = [pltpu.make_async_copy(source.at[pl.ds(rows * part, rows)],
                                    out.at[pl.ds(rows * part, rows)], copy_sem.at[part])
              for part in range(4)]
    for copy in copies:
        copy.start()
    for copy in copies:
        copy.wait()


def on_device(queries, keys, values, span_order, out_weight):
    rows, width = queries.shape
    heads = width // HEAD_DIM
    d_out = out_weight.shape[1]
    bf16, f32 = jnp.bfloat16, jnp.float32
    sem = pltpu.SemaphoreType.DMA
    span_order, queries, keys, values, out_weight = (
        pltpu.with_memory_space_constraint(array, pltpu.HBM)
        for array in (span_order, queries, keys, values, out_weight))
    result = pl.pallas_call(
        kernel,
        out_shape=jax.ShapeDtypeStruct((rows // 8, d_out), bf16),
        in_specs=[pl.BlockSpec(memory_space=pltpu.HBM)] * 5,
        out_specs=pl.BlockSpec(memory_space=pl.ANY),
        scratch_shapes=[
            pltpu.VMEM((rows, width), bf16),
            pltpu.VMEM((SPANS, 2, SPAN, HEAD_DIM), bf16),
            pltpu.VMEM((width, d_out), bf16),
            pltpu.VMEM((heads, 2 * HEAD_DIM, rows), bf16),
            pltpu.VMEM((heads, HEAD_DIM + 16, rows), f32),
            pltpu.VMEM((heads, 1, rows), f32),
            pltpu.VMEM((rows, width), bf16),
            pltpu.VMEM((TILES, 4, 32, TILE), bf16),
            pltpu.VMEM((TILES, 4, 32, TILE), bf16),
            pltpu.VMEM((TILES, 4, 32, TILE), bf16),
            pltpu.VMEM((TILES, 32, TILE), bf16),
            pltpu.VMEM((TILES, 32, TILE), bf16),
            pltpu.VMEM((2, TILES, 32, TILE), bf16),
            pltpu.VMEM((2, TILES, 32, TILE), bf16),
            pltpu.VMEM((rows // 8, d_out), bf16),
            pltpu.SMEM((SPANS,), jnp.int32),
            pltpu.SMEM((SPANS,), jnp.int32),
            sem((14,)), sem((6, 2)), sem((6, 2)), sem((SPANS - 8,)), sem((SPANS - 8,)),
            sem((TILES, 2)), sem((TILES, 2)), sem((TILES,)), sem((TILES,)),
            sem((2, TILES)), sem((2, TILES)), sem((TILES,)),
        ],
        compiler_params=pltpu.CompilerParams(
            collective_id=0, has_side_effects=True, vmem_limit_bytes=32 * 1024 * 1024),
        cost_estimate=pl.CostEstimate(
            flops=3 * 2 * rows * width * 4096, bytes_accessed=10 * 2**20,
            transcendentals=heads * rows * 4096),
    )(span_order, queries, keys, values, out_weight)
    return pl.pallas_call(
        copy_kernel,
        out_shape=jax.ShapeDtypeStruct(result.shape, result.dtype),
        in_specs=[pl.BlockSpec(memory_space=pl.ANY)],
        out_specs=pl.BlockSpec(memory_space=pl.ANY),
        scratch_shapes=[sem((4,))],
    )(result)


def solution(mesh):
    return jax.shard_map(
        on_device,
        mesh=mesh,
        in_specs=(
            P(("dp", "context"), "tensor"),
            P(("dp", "context"), "tensor"),
            P(("dp", "context"), "tensor"),
            P("dp"),
            P("tensor", None),
        ),
        out_specs=P(("dp", "context", "tensor"), None),
        check_vma=False,
    )
```

```python
import math

import jax
import jax.numpy as jnp
from jax import lax
from jax.experimental import pallas as pl
from jax.experimental.pallas import tpu as pltpu
from jax.sharding import PartitionSpec as P

HEAD_DIM = 128
SPAN = 128
RING = 8
COLUMNS = 2
CHIPS = 4
ROUNDS = 10
TILE = 512
TILES = 8
HALF = TILES // 2
LOWEST = -1e30
MESH = pl.DeviceIdType.MESH

UP = [(0, 1, 0), (0, 1, 1), (0, 2, 0), (0, 2, 1), (0, 3, 0), (0, 3, 1),
      (1, 3, 0), (0, 4, 0), (1, 4, 0), (1, 3, 1)]
DOWN = [(0, -1, 1), (0, -1, 0), (0, -2, 1), (0, -2, 0), (0, -3, 1), (0, -3, 0),
        (0, -4, 1), (1, -3, 1), (1, -3, 0), (1, -4, 1)]
ACROSS = [(1, 0, 0), (1, 0, 1), (1, 1, 0), (1, -1, 1), (1, 2, 0), (1, -2, 1),
          (1, -2, 0), (1, 2, 1), (1, 1, 1), (1, -1, 0)]


def plan():
    slot_of = {(0, 0, 0): 0, (0, 0, 1): 1}
    contents = [(0, 0, 0), (0, 0, 1)]
    up_slot = {r: 2 + 3 * r for r in range(ROUNDS)}
    down_slot = {r: 3 + 3 * r for r in range(ROUNDS)}
    across_slot = {r: 4 + 3 * r for r in range(ROUNDS)}
    slots = {}
    for r in range(ROUNDS):
        for table, names in ((up_slot, UP), (down_slot, DOWN), (across_slot, ACROSS)):
            slots[table[r]] = names[r]
    for slot in range(2, 2 + 3 * ROUNDS):
        column, offset, half = slots[slot]
        key = (column, offset % RING, half)
        slot_of[key] = slot
        contents.append(key)
    assert len(slot_of) == 2 + 3 * ROUNDS
    copies = []
    for r in range(ROUNDS):
        (uc, uo, uh), (dc, do, dh), (ac, ao, ah) = UP[r], DOWN[r], ACROSS[r]
        copies.append((
            ("minus", slot_of[(uc, (uo - 1) % RING, uh)], up_slot[r]),
            ("plus", slot_of[(dc, (do + 1) % RING, dh)], down_slot[r]),
            ("other", slot_of[(0, ao % RING, ah)], across_slot[r]),
        ))
    return contents, copies


CONTENTS, COPIES = plan()
SPANS = len(CONTENTS)
ORDER = tuple(part * HALF + tile for tile in range(HALF) for part in range(2))


def kernel(order_hbm, q_hbm, k_hbm, v_hbm, w_hbm, out,
           q_in, kv, w, qt, acc, top, att, own, sib_out, sib_in,
           far_out, far_in, near_out, near_in, result, order, span_of,
           load_sem, own_send, own_recv, kv_send, kv_recv, sib_send, sib_recv,
           far_send, far_recv, near_send, near_recv, out_sem):
    heads = q_in.shape[1] // HEAD_DIM
    rows = q_in.shape[0]
    context = lax.axis_index("context")
    tensor = lax.axis_index("tensor")
    y, z = context // RING, lax.rem(context, RING)
    x, core = tensor // 2, lax.rem(tensor, 2)
    targets = {
        "minus": {"context": y * RING + lax.rem(z + RING - 1, RING)},
        "plus": {"context": y * RING + lax.rem(z + 1, RING)},
        "other": {"context": (1 - y) * RING + z},
    }
    sibling = {"tensor": x * 2 + 1 - core}
    chip_next, chip_back = lax.rem(x + 1, CHIPS), lax.rem(x + CHIPS - 1, CHIPS)
    chip_far = lax.rem(x + 2, CHIPS)
    to_next, to_back = {"tensor": chip_next * 2 + core}, {"tensor": chip_back * 2 + core}

    barrier = pltpu.get_barrier_semaphore()
    for target in (*targets.values(), sibling, to_next, to_back):
        pl.semaphore_signal(barrier, inc=1, device_id=target, device_id_type=MESH)

    loads = []
    for half in range(2):
        for part, source in enumerate((k_hbm, v_hbm)):
            loads.append(pltpu.make_async_copy(
                source.at[pl.ds(half * SPAN, SPAN)], kv.at[half, part],
                load_sem.at[2 * half + part]))
    chips = (chip_far, chip_next, chip_back, x)
    for group, chip in enumerate(chips):
        for part, owner in enumerate((core, 1 - core)):
            number = 2 * group + part
            first = pl.multiple_of(chip * 64 + owner * 32, 32)
            loads.append(pltpu.make_async_copy(
                q_hbm.at[pl.ds(first, 32)], q_in.at[pl.ds(32 * number, 32)],
                load_sem.at[4 + number]))
    loads.append(pltpu.make_async_copy(order_hbm, order, load_sem.at[13]))
    loads.append(pltpu.make_async_copy(w_hbm, w, load_sem.at[12]))
    for load in loads[:-1]:
        load.start()

    def own_copies(r):
        for name, src, dst in COPIES[r]:
            for part, source in enumerate((k_hbm, v_hbm)):
                yield pltpu.make_async_remote_copy(
                    src_ref=source.at[pl.ds(src * SPAN, SPAN)], dst_ref=kv.at[dst, part],
                    send_sem=own_send.at[dst - 2, part], recv_sem=own_recv.at[dst - 2, part],
                    device_id=targets[name], device_id_type=MESH)

    def copy_of(name, src, dst):
        return pltpu.make_async_remote_copy(
            src_ref=kv.at[src], dst_ref=kv.at[dst],
            send_sem=kv_send.at[dst - 8], recv_sem=kv_recv.at[dst - 8],
            device_id=targets[name], device_id_type=MESH)

    pl.semaphore_wait(barrier, 6)
    for copy in own_copies(0):
        copy.start()
    loads[-1].start()

    loads[12].wait()
    for slot, (column, offset, half) in enumerate(CONTENTS):
        where = (y if column == 0 else 1 - y) * RING + lax.rem(z + offset, RING)
        span_of[slot] = order[2 * where + half]

    scale = math.log2(math.e) / math.sqrt(HEAD_DIM)
    for load in loads[4:12]:
        load.wait()
    for head in range(heads):
        scaled = q_in[:, head * HEAD_DIM:(head + 1) * HEAD_DIM].astype(jnp.float32).T * scale
        high = scaled.astype(jnp.bfloat16)
        low = (scaled - high.astype(jnp.float32)).astype(jnp.bfloat16)
        qt[head, :HEAD_DIM] = high
        qt[head, HEAD_DIM:] = low

    for first, second in zip(own_copies(0), own_copies(1)):
        first.wait_send()
        second.start()
    for load in loads[:4]:
        load.wait()

    lane = lax.broadcasted_iota(jnp.int32, (1, rows), 1)
    group_of = lane // 64
    chip_of = jnp.where(group_of == 0, chip_far, jnp.where(
        group_of == 1, chip_next, jnp.where(group_of == 2, chip_back, x)))
    owner_of = jnp.where(lax.rem(lane // 32, 2) == 0, core, 1 - core)
    row_of = chip_of * 64 + owner_of * 32 + lax.rem(lane, 32)
    q_span = jnp.where(row_of < SPAN, span_of[0], span_of[1])
    q_pos = q_span * SPAN + lax.rem(row_of, SPAN)

    def operands(first, count):
        spans = kv[pl.ds(first, count)]
        keys = spans[:, 0].reshape(count * SPAN, HEAD_DIM)
        keys = jnp.concatenate([keys, keys], axis=1)
        values = spans[:, 1].reshape(count * SPAN, HEAD_DIM).T
        ones = jnp.ones((16, count * SPAN), jnp.bfloat16)
        return keys, jnp.concatenate([values, ones], axis=0)

    def scores_of(keys, head):
        return jnp.dot(keys, qt[head], preferred_element_type=jnp.float32)

    def receive(r):
        following = COPIES[r + 2] if r + 2 < ROUNDS else ()
        here = 2 + 3 * r
        for copy in following:
            if copy[1] < here:
                copy_of(*copy).start()
        first = list(own_copies(r)) if r < 2 else ()
        for number, copy in enumerate(COPIES[r]):
            if r < 2:
                first[2 * number].wait_recv()
                first[2 * number + 1].wait_recv()
            else:
                copy_of(*copy).wait_recv()
            for later in following:
                if later[1] == copy[2]:
                    copy_of(*later).start()

    keys, values = operands(0, 2)
    k_row = lax.broadcasted_iota(jnp.int32, (2 * SPAN, 1), 0)
    k_pos = jnp.where(k_row < SPAN, span_of[0], span_of[1]) * SPAN + lax.rem(k_row, SPAN)
    hide = jnp.where(k_pos <= q_pos, 0.0, LOWEST)
    following = scores_of(keys, 0)
    for head in range(heads):
        scores = following + hide
        if head + 1 < heads:
            following = scores_of(keys, head + 1)
        new_top = jnp.max(scores, axis=0, keepdims=True)
        weights = jnp.exp2(scores - new_top).astype(jnp.bfloat16)
        top[head] = new_top
        acc[head] = jnp.dot(values, weights, preferred_element_type=jnp.float32)

    @pl.loop(0, ROUNDS)
    def _(step):
        for r in range(ROUNDS):
            @pl.when(step == r)
            def _():
                receive(r)

        first = 2 + 3 * step
        keys, values = operands(first, 3)
        hide = [jnp.where(span_of[first + number] < q_span, 0.0, LOWEST) for number in range(3)]
        following = scores_of(keys, 0)
        for head in range(heads):
            scores = [following[number * SPAN:(number + 1) * SPAN] for number in range(3)]
            if head + 1 < heads:
                following = scores_of(keys, head + 1)
            old_top = top[head]
            new_top = old_top
            for part, hidden in zip(scores, hide):
                new_top = jnp.maximum(new_top, jnp.max(part, axis=0, keepdims=True) + hidden)
            factor = jnp.exp2(old_top - new_top)
            weights = jnp.concatenate([
                jnp.exp2(part - (new_top - hidden)).astype(jnp.bfloat16)
                for part, hidden in zip(scores, hide)], axis=0)
            top[head] = new_top
            acc[head] = acc[head] * factor + jnp.dot(
                values, weights, preferred_element_type=jnp.float32)

    for head in range(heads):
        mixed = acc[head, :HEAD_DIM] * (1.0 / acc[head, HEAD_DIM:HEAD_DIM + 1])
        att[:, head * HEAD_DIM:(head + 1) * HEAD_DIM] = mixed.astype(jnp.bfloat16).T
    loads[13].wait()

    def sib_copy(tile, part):
        at = 0 if part == 0 else pl.ds(1, 3)
        return pltpu.make_async_remote_copy(
            src_ref=sib_out.at[tile, at], dst_ref=sib_in.at[tile, at],
            send_sem=sib_send.at[tile, part], recv_sem=sib_recv.at[tile, part],
            device_id=sibling, device_id_type=MESH)

    def project(tile):
        part = jnp.dot(att[...], w[:, tile * TILE:(tile + 1) * TILE],
                       preferred_element_type=jnp.float32).astype(jnp.bfloat16)
        part = part.reshape(4, 2, 32, TILE)
        sib_out[tile] = part[:, 1]
        sib_copy(tile, 0).start()
        sib_copy(tile, 1).start()
        own[tile] = part[:, 0]

    def both(tile, group):
        return own[tile, group].astype(jnp.float32) + sib_in[tile, group].astype(jnp.float32)

    def far_copy(tile):
        return pltpu.make_async_remote_copy(
            src_ref=far_out.at[tile], dst_ref=far_in.at[tile],
            send_sem=far_send.at[tile], recv_sem=far_recv.at[tile],
            device_id=to_next if tile < HALF else to_back, device_id_type=MESH)

    def near_copy(side, tile):
        return pltpu.make_async_remote_copy(
            src_ref=near_out.at[side, tile], dst_ref=near_in.at[side, tile],
            send_sem=near_send.at[side, tile], recv_sem=near_recv.at[side, tile],
            device_id=to_next if side == 0 else to_back, device_id_type=MESH)

    def out_copy(tile):
        at = pl.ds(tile * TILE, TILE)
        return pltpu.make_async_copy(result.at[:, at], out.at[:, at], out_sem.at[tile])

    def send_far(tile):
        sib_copy(tile, 0).wait_recv()
        far_out[tile] = both(tile, 0).astype(jnp.bfloat16)
        far_copy(tile).start()

    def send_near(side, tile):
        second = (tile < HALF) == (side == 0)
        if not second:
            sib_copy(tile, 1).wait_recv()
        total = both(tile, 1 + side)
        if second:
            far_copy(tile).wait_recv()
            total = total + far_in[tile].astype(jnp.float32)
        near_out[side, tile] = total.astype(jnp.bfloat16)
        near_copy(side, tile).start()

    project(ORDER[0])
    for earlier, tile in zip(ORDER, ORDER[1:]):
        project(tile)
        send_far(earlier)
    send_far(ORDER[-1])
    for tile in ORDER:
        send_near(0 if tile >= HALF else 1, tile)
    for tile in ORDER:
        send_near(0 if tile < HALF else 1, tile)
    for tile in ORDER:
        near_copy(0, tile).wait_recv()
        near_copy(1, tile).wait_recv()
        total = both(tile, 3) + (near_in[0, tile].astype(jnp.float32)
                                 + near_in[1, tile].astype(jnp.float32))
        result[:, tile * TILE:(tile + 1) * TILE] = total.astype(out.dtype)
        out_copy(tile).start()

    for copy in own_copies(1):
        copy.wait_send()
    for copies in COPIES[2:]:
        for copy in copies:
            copy_of(*copy).wait_send()
    for tile in range(TILES):
        for part in range(2):
            sib_copy(tile, part).wait_send()
            near_copy(part, tile).wait_send()
        far_copy(tile).wait_send()
        out_copy(tile).wait()


def on_device(queries, keys, values, span_order, out_weight):
    rows, width = queries.shape
    heads = width // HEAD_DIM
    d_out = out_weight.shape[1]
    bf16, f32 = jnp.bfloat16, jnp.float32
    sem = pltpu.SemaphoreType.DMA
    span_order, queries, keys, values, out_weight = (
        pltpu.with_memory_space_constraint(array, pltpu.HBM)
        for array in (span_order, queries, keys, values, out_weight))
    return pl.pallas_call(
        kernel,
        out_shape=jax.ShapeDtypeStruct((rows // 8, d_out), bf16),
        in_specs=[pl.BlockSpec(memory_space=pltpu.HBM)] * 5,
        out_specs=pl.BlockSpec(memory_space=pl.ANY),
        scratch_shapes=[
            pltpu.VMEM((rows, width), bf16),
            pltpu.VMEM((SPANS, 2, SPAN, HEAD_DIM), bf16),
            pltpu.VMEM((width, d_out), bf16),
            pltpu.VMEM((heads, 2 * HEAD_DIM, rows), bf16),
            pltpu.VMEM((heads, HEAD_DIM + 16, rows), f32),
            pltpu.VMEM((heads, 1, rows), f32),
            pltpu.VMEM((rows, width), bf16),
            pltpu.VMEM((TILES, 4, 32, TILE), bf16),
            pltpu.VMEM((TILES, 4, 32, TILE), bf16),
            pltpu.VMEM((TILES, 4, 32, TILE), bf16),
            pltpu.VMEM((TILES, 32, TILE), bf16),
            pltpu.VMEM((TILES, 32, TILE), bf16),
            pltpu.VMEM((2, TILES, 32, TILE), bf16),
            pltpu.VMEM((2, TILES, 32, TILE), bf16),
            pltpu.VMEM((rows // 8, d_out), bf16),
            pltpu.SMEM((SPANS,), jnp.int32),
            pltpu.SMEM((SPANS,), jnp.int32),
            sem((14,)), sem((6, 2)), sem((6, 2)), sem((SPANS - 8,)), sem((SPANS - 8,)),
            sem((TILES, 2)), sem((TILES, 2)), sem((TILES,)), sem((TILES,)),
            sem((2, TILES)), sem((2, TILES)), sem((TILES,)),
        ],
        compiler_params=pltpu.CompilerParams(
            collective_id=0, has_side_effects=True, vmem_limit_bytes=32 * 1024 * 1024),
        cost_estimate=pl.CostEstimate(
            flops=3 * 2 * rows * width * 4096, bytes_accessed=10 * 2**20,
            transcendentals=heads * rows * 4096),
    )(span_order, queries, keys, values, out_weight)


def solution(mesh):
    return jax.shard_map(
        on_device,
        mesh=mesh,
        in_specs=(
            P(("dp", "context"), "tensor"),
            P(("dp", "context"), "tensor"),
            P(("dp", "context"), "tensor"),
            P("dp"),
            P("tensor", None),
        ),
        out_specs=P(("dp", "context", "tensor"), None),
        check_vma=False,
    )
```

```python
import math

import jax
import jax.numpy as jnp
from jax import lax
from jax.experimental import pallas as pl
from jax.experimental.pallas import tpu as pltpu
from jax.sharding import PartitionSpec as P

HEAD_DIM = 128
SPAN = 128
RING = 8
COLUMNS = 2
CHIPS = 4
ROUNDS = 10
TILE = 512
TILES = 8
HALF = TILES // 2
LOWEST = -1e30
MESH = pl.DeviceIdType.MESH

UP = [(0, 1, 0), (0, 1, 1), (0, 2, 0), (0, 2, 1), (0, 3, 0), (0, 3, 1),
      (1, 3, 0), (0, 4, 0), (1, 4, 0), (1, 3, 1)]
DOWN = [(0, -1, 1), (0, -1, 0), (0, -2, 1), (0, -2, 0), (0, -3, 1), (0, -3, 0),
        (0, -4, 1), (1, -3, 1), (1, -3, 0), (1, -4, 1)]
ACROSS = [(1, 0, 0), (1, 0, 1), (1, 1, 0), (1, -1, 1), (1, 2, 0), (1, -2, 1),
          (1, -2, 0), (1, 2, 1), (1, 1, 1), (1, -1, 0)]


def plan():
    slot_of = {(0, 0, 0): 0, (0, 0, 1): 1}
    contents = [(0, 0, 0), (0, 0, 1)]
    up_slot = {r: 2 + 3 * r for r in range(ROUNDS)}
    down_slot = {r: 3 + 3 * r for r in range(ROUNDS)}
    across_slot = {r: 4 + 3 * r for r in range(ROUNDS)}
    slots = {}
    for r in range(ROUNDS):
        for table, names in ((up_slot, UP), (down_slot, DOWN), (across_slot, ACROSS)):
            slots[table[r]] = names[r]
    for slot in range(2, 2 + 3 * ROUNDS):
        column, offset, half = slots[slot]
        key = (column, offset % RING, half)
        slot_of[key] = slot
        contents.append(key)
    assert len(slot_of) == 2 + 3 * ROUNDS
    copies = []
    for r in range(ROUNDS):
        (uc, uo, uh), (dc, do, dh), (ac, ao, ah) = UP[r], DOWN[r], ACROSS[r]
        copies.append((
            ("minus", slot_of[(uc, (uo - 1) % RING, uh)], up_slot[r]),
            ("plus", slot_of[(dc, (do + 1) % RING, dh)], down_slot[r]),
            ("other", slot_of[(0, ao % RING, ah)], across_slot[r]),
        ))
    return contents, copies


CONTENTS, COPIES = plan()
SPANS = len(CONTENTS)
ORDER = tuple(part * HALF + tile for tile in range(HALF) for part in range(2))


def kernel(order_hbm, q_hbm, k_hbm, v_hbm, w_hbm, out,
           q_in, kv, w, qt, acc, top, att, own, sib_out, sib_in,
           far_out, far_in, near_out, near_in, result, order, span_of,
           load_sem, own_send, own_recv, kv_send, kv_recv, sib_send, sib_recv,
           far_send, far_recv, near_send, near_recv, out_sem):
    heads = q_in.shape[1] // HEAD_DIM
    rows = q_in.shape[0]
    context = lax.axis_index("context")
    tensor = lax.axis_index("tensor")
    y, z = context // RING, lax.rem(context, RING)
    x, core = tensor // 2, lax.rem(tensor, 2)
    targets = {
        "minus": {"context": y * RING + lax.rem(z + RING - 1, RING)},
        "plus": {"context": y * RING + lax.rem(z + 1, RING)},
        "other": {"context": (1 - y) * RING + z},
    }
    sibling = {"tensor": x * 2 + 1 - core}
    chip_next, chip_back = lax.rem(x + 1, CHIPS), lax.rem(x + CHIPS - 1, CHIPS)
    chip_far = lax.rem(x + 2, CHIPS)
    to_next, to_back = {"tensor": chip_next * 2 + core}, {"tensor": chip_back * 2 + core}

    barrier = pltpu.get_barrier_semaphore()
    for target in (*targets.values(), sibling, to_next, to_back):
        pl.semaphore_signal(barrier, inc=1, device_id=target, device_id_type=MESH)

    loads = []
    for half in range(2):
        for part, source in enumerate((k_hbm, v_hbm)):
            loads.append(pltpu.make_async_copy(
                source.at[pl.ds(half * SPAN, SPAN)], kv.at[half, part],
                load_sem.at[2 * half + part]))
    chips = (chip_far, chip_next, chip_back, x)
    for group, chip in enumerate(chips):
        for part, owner in enumerate((core, 1 - core)):
            number = 2 * group + part
            first = pl.multiple_of(chip * 64 + owner * 32, 32)
            loads.append(pltpu.make_async_copy(
                q_hbm.at[pl.ds(first, 32)], q_in.at[pl.ds(32 * number, 32)],
                load_sem.at[4 + number]))
    loads.append(pltpu.make_async_copy(order_hbm, order, load_sem.at[13]))
    loads.append(pltpu.make_async_copy(w_hbm, w, load_sem.at[12]))
    for load in loads[:-1]:
        load.start()

    def own_copies(r):
        for name, src, dst in COPIES[r]:
            for part, source in enumerate((k_hbm, v_hbm)):
                yield pltpu.make_async_remote_copy(
                    src_ref=source.at[pl.ds(src * SPAN, SPAN)], dst_ref=kv.at[dst, part],
                    send_sem=own_send.at[dst - 2, part], recv_sem=own_recv.at[dst - 2, part],
                    device_id=targets[name], device_id_type=MESH)

    def copy_of(name, src, dst):
        return pltpu.make_async_remote_copy(
            src_ref=kv.at[src], dst_ref=kv.at[dst],
            send_sem=kv_send.at[dst - 8], recv_sem=kv_recv.at[dst - 8],
            device_id=targets[name], device_id_type=MESH)

    pl.semaphore_wait(barrier, 6)
    for copy in own_copies(0):
        copy.start()
    loads[-1].start()

    loads[12].wait()
    for slot, (column, offset, half) in enumerate(CONTENTS):
        where = (y if column == 0 else 1 - y) * RING + lax.rem(z + offset, RING)
        span_of[slot] = order[2 * where + half]

    scale = math.log2(math.e) / math.sqrt(HEAD_DIM)
    for load in loads[4:12]:
        load.wait()
    for head in range(heads):
        scaled = q_in[:, head * HEAD_DIM:(head + 1) * HEAD_DIM].astype(jnp.float32).T * scale
        high = scaled.astype(jnp.bfloat16)
        low = (scaled - high.astype(jnp.float32)).astype(jnp.bfloat16)
        qt[head, :HEAD_DIM] = high
        qt[head, HEAD_DIM:] = low

    for first, second in zip(own_copies(0), own_copies(1)):
        first.wait_send()
        second.start()
    for load in loads[:4]:
        load.wait()

    lane = lax.broadcasted_iota(jnp.int32, (1, rows), 1)
    group_of = lane // 64
    chip_of = jnp.where(group_of == 0, chip_far, jnp.where(
        group_of == 1, chip_next, jnp.where(group_of == 2, chip_back, x)))
    owner_of = jnp.where(lax.rem(lane // 32, 2) == 0, core, 1 - core)
    row_of = chip_of * 64 + owner_of * 32 + lax.rem(lane, 32)
    q_span = jnp.where(row_of < SPAN, span_of[0], span_of[1])
    q_pos = q_span * SPAN + lax.rem(row_of, SPAN)

    def operands(first, count):
        spans = kv[pl.ds(first, count)]
        keys = spans[:, 0].reshape(count * SPAN, HEAD_DIM)
        keys = jnp.concatenate([keys, keys], axis=1)
        values = spans[:, 1].reshape(count * SPAN, HEAD_DIM).T
        ones = jnp.ones((16, count * SPAN), jnp.bfloat16)
        return keys, jnp.concatenate([values, ones], axis=0)

    def scores_of(keys, head):
        return jnp.dot(keys, qt[head], preferred_element_type=jnp.float32)

    def receive(r):
        following = COPIES[r + 2] if r + 2 < ROUNDS else ()
        here = 2 + 3 * r
        for copy in following:
            if copy[1] < here:
                copy_of(*copy).start()
        first = list(own_copies(r)) if r < 2 else ()
        for number, copy in enumerate(COPIES[r]):
            if r < 2:
                first[2 * number].wait_recv()
                first[2 * number + 1].wait_recv()
            else:
                copy_of(*copy).wait_recv()
            for later in following:
                if later[1] == copy[2]:
                    copy_of(*later).start()

    keys, values = operands(0, 2)
    k_row = lax.broadcasted_iota(jnp.int32, (2 * SPAN, 1), 0)
    k_pos = jnp.where(k_row < SPAN, span_of[0], span_of[1]) * SPAN + lax.rem(k_row, SPAN)
    hide = jnp.where(k_pos <= q_pos, 0.0, LOWEST)
    following = scores_of(keys, 0)
    for head in range(heads):
        scores = following + hide
        if head + 1 < heads:
            following = scores_of(keys, head + 1)
        new_top = jnp.max(scores, axis=0, keepdims=True)
        weights = jnp.exp2(scores - new_top).astype(jnp.bfloat16)
        top[head] = new_top
        acc[head] = jnp.dot(values, weights, preferred_element_type=jnp.float32)

    @pl.loop(0, ROUNDS)
    def _(step):
        for r in range(ROUNDS):
            @pl.when(step == r)
            def _():
                receive(r)

        first = 2 + 3 * step
        keys, values = operands(first, 3)
        hide = [jnp.where(span_of[first + number] < q_span, 0.0, LOWEST) for number in range(3)]
        following = scores_of(keys, 0)
        for head in range(heads):
            scores = [following[number * SPAN:(number + 1) * SPAN] for number in range(3)]
            if head + 1 < heads:
                following = scores_of(keys, head + 1)
            old_top = top[head]
            new_top = old_top
            for part, hidden in zip(scores, hide):
                new_top = jnp.maximum(new_top, jnp.max(part, axis=0, keepdims=True) + hidden)
            factor = jnp.exp2(old_top - new_top)
            weights = jnp.concatenate([
                jnp.exp2(part - (new_top - hidden)).astype(jnp.bfloat16)
                for part, hidden in zip(scores, hide)], axis=0)
            top[head] = new_top
            acc[head] = acc[head] * factor + jnp.dot(
                values, weights, preferred_element_type=jnp.float32)

    for head in range(heads):
        mixed = acc[head, :HEAD_DIM] * (1.0 / acc[head, HEAD_DIM:HEAD_DIM + 1])
        att[:, head * HEAD_DIM:(head + 1) * HEAD_DIM] = mixed.astype(jnp.bfloat16).T
    loads[13].wait()

    def sib_copy(tile, part):
        at = 0 if part == 0 else pl.ds(1, 3)
        return pltpu.make_async_remote_copy(
            src_ref=sib_out.at[tile, at], dst_ref=sib_in.at[tile, at],
            send_sem=sib_send.at[tile, part], recv_sem=sib_recv.at[tile, part],
            device_id=sibling, device_id_type=MESH)

    def project(tile):
        part = jnp.dot(att[...], w[:, tile * TILE:(tile + 1) * TILE],
                       preferred_element_type=jnp.float32).astype(jnp.bfloat16)
        part = part.reshape(4, 2, 32, TILE)
        sib_out[tile] = part[:, 1]
        sib_copy(tile, 0).start()
        sib_copy(tile, 1).start()
        own[tile] = part[:, 0]

    def both(tile, group):
        return own[tile, group].astype(jnp.float32) + sib_in[tile, group].astype(jnp.float32)

    def far_copy(tile):
        return pltpu.make_async_remote_copy(
            src_ref=far_out.at[tile], dst_ref=far_in.at[tile],
            send_sem=far_send.at[tile], recv_sem=far_recv.at[tile],
            device_id=to_next if tile < HALF else to_back, device_id_type=MESH)

    def near_copy(side, tile):
        return pltpu.make_async_remote_copy(
            src_ref=near_out.at[side, tile], dst_ref=near_in.at[side, tile],
            send_sem=near_send.at[side, tile], recv_sem=near_recv.at[side, tile],
            device_id=to_next if side == 0 else to_back, device_id_type=MESH)

    def out_copy(tile):
        at = pl.ds(tile * TILE, TILE)
        return pltpu.make_async_copy(result.at[:, at], out.at[:, at], out_sem.at[tile])

    def send_far(tile):
        sib_copy(tile, 0).wait_recv()
        far_out[tile] = both(tile, 0).astype(jnp.bfloat16)
        far_copy(tile).start()

    def send_near(side, tile):
        second = (tile < HALF) == (side == 0)
        if not second:
            sib_copy(tile, 1).wait_recv()
        total = both(tile, 1 + side)
        if second:
            far_copy(tile).wait_recv()
            total = total + far_in[tile].astype(jnp.float32)
        near_out[side, tile] = total.astype(jnp.bfloat16)
        near_copy(side, tile).start()

    def send_first(tile):
        send_far(tile)
        send_near(0 if tile >= HALF else 1, tile)

    project(ORDER[0])
    for earlier, tile in zip(ORDER, ORDER[1:]):
        project(tile)
        send_first(earlier)
    send_first(ORDER[-1])
    for tile in ORDER:
        send_near(0 if tile < HALF else 1, tile)
    for tile in ORDER:
        near_copy(0, tile).wait_recv()
        near_copy(1, tile).wait_recv()
        total = both(tile, 3) + (near_in[0, tile].astype(jnp.float32)
                                 + near_in[1, tile].astype(jnp.float32))
        result[:, tile * TILE:(tile + 1) * TILE] = total.astype(out.dtype)
        out_copy(tile).start()

    for copy in own_copies(1):
        copy.wait_send()
    for copies in COPIES[2:]:
        for copy in copies:
            copy_of(*copy).wait_send()
    for tile in range(TILES):
        for part in range(2):
            sib_copy(tile, part).wait_send()
            near_copy(part, tile).wait_send()
        far_copy(tile).wait_send()
        out_copy(tile).wait()


def on_device(queries, keys, values, span_order, out_weight):
    rows, width = queries.shape
    heads = width // HEAD_DIM
    d_out = out_weight.shape[1]
    bf16, f32 = jnp.bfloat16, jnp.float32
    sem = pltpu.SemaphoreType.DMA
    span_order, queries, keys, values, out_weight = (
        pltpu.with_memory_space_constraint(array, pltpu.HBM)
        for array in (span_order, queries, keys, values, out_weight))
    return pl.pallas_call(
        kernel,
        out_shape=jax.ShapeDtypeStruct((rows // 8, d_out), bf16),
        in_specs=[pl.BlockSpec(memory_space=pltpu.HBM)] * 5,
        out_specs=pl.BlockSpec(memory_space=pl.ANY),
        scratch_shapes=[
            pltpu.VMEM((rows, width), bf16),
            pltpu.VMEM((SPANS, 2, SPAN, HEAD_DIM), bf16),
            pltpu.VMEM((width, d_out), bf16),
            pltpu.VMEM((heads, 2 * HEAD_DIM, rows), bf16),
            pltpu.VMEM((heads, HEAD_DIM + 16, rows), f32),
            pltpu.VMEM((heads, 1, rows), f32),
            pltpu.VMEM((rows, width), bf16),
            pltpu.VMEM((TILES, 4, 32, TILE), bf16),
            pltpu.VMEM((TILES, 4, 32, TILE), bf16),
            pltpu.VMEM((TILES, 4, 32, TILE), bf16),
            pltpu.VMEM((TILES, 32, TILE), bf16),
            pltpu.VMEM((TILES, 32, TILE), bf16),
            pltpu.VMEM((2, TILES, 32, TILE), bf16),
            pltpu.VMEM((2, TILES, 32, TILE), bf16),
            pltpu.VMEM((rows // 8, d_out), bf16),
            pltpu.SMEM((SPANS,), jnp.int32),
            pltpu.SMEM((SPANS,), jnp.int32),
            sem((14,)), sem((6, 2)), sem((6, 2)), sem((SPANS - 8,)), sem((SPANS - 8,)),
            sem((TILES, 2)), sem((TILES, 2)), sem((TILES,)), sem((TILES,)),
            sem((2, TILES)), sem((2, TILES)), sem((TILES,)),
        ],
        compiler_params=pltpu.CompilerParams(
            collective_id=0, has_side_effects=True, vmem_limit_bytes=32 * 1024 * 1024),
        cost_estimate=pl.CostEstimate(
            flops=3 * 2 * rows * width * 4096, bytes_accessed=10 * 2**20,
            transcendentals=heads * rows * 4096),
    )(span_order, queries, keys, values, out_weight)


def solution(mesh):
    return jax.shard_map(
        on_device,
        mesh=mesh,
        in_specs=(
            P(("dp", "context"), "tensor"),
            P(("dp", "context"), "tensor"),
            P(("dp", "context"), "tensor"),
            P("dp"),
            P("tensor", None),
        ),
        out_specs=P(("dp", "context", "tensor"), None),
        check_vma=False,
    )
```

```python
import math

import jax
import jax.numpy as jnp
from jax import lax
from jax.experimental import pallas as pl
from jax.experimental.pallas import tpu as pltpu
from jax.sharding import PartitionSpec as P

HEAD_DIM = 128
SPAN = 128
RING = 8
COLUMNS = 2
CHIPS = 4
ROUNDS = 10
TILE = 512
TILES = 8
HALF = TILES // 2
LAG = 4
LOWEST = -1e30
MESH = pl.DeviceIdType.MESH

UP = [(0, 1, 0), (0, 1, 1), (0, 2, 0), (0, 2, 1), (0, 3, 0), (0, 3, 1),
      (1, 3, 0), (0, 4, 0), (1, 4, 0), (1, 3, 1)]
DOWN = [(0, -1, 1), (0, -1, 0), (0, -2, 1), (0, -2, 0), (0, -3, 1), (0, -3, 0),
        (0, -4, 1), (1, -3, 1), (1, -3, 0), (1, -4, 1)]
ACROSS = [(1, 0, 0), (1, 0, 1), (1, 1, 0), (1, -1, 1), (1, 2, 0), (1, -2, 1),
          (1, -2, 0), (1, 2, 1), (1, 1, 1), (1, -1, 0)]


def plan():
    slot_of = {(0, 0, 0): 0, (0, 0, 1): 1}
    contents = [(0, 0, 0), (0, 0, 1)]
    up_slot = {r: 2 + 3 * r for r in range(ROUNDS)}
    down_slot = {r: 3 + 3 * r for r in range(ROUNDS)}
    across_slot = {r: 4 + 3 * r for r in range(ROUNDS)}
    slots = {}
    for r in range(ROUNDS):
        for table, names in ((up_slot, UP), (down_slot, DOWN), (across_slot, ACROSS)):
            slots[table[r]] = names[r]
    for slot in range(2, 2 + 3 * ROUNDS):
        column, offset, half = slots[slot]
        key = (column, offset % RING, half)
        slot_of[key] = slot
        contents.append(key)
    assert len(slot_of) == 2 + 3 * ROUNDS
    copies = []
    for r in range(ROUNDS):
        (uc, uo, uh), (dc, do, dh), (ac, ao, ah) = UP[r], DOWN[r], ACROSS[r]
        copies.append((
            ("minus", slot_of[(uc, (uo - 1) % RING, uh)], up_slot[r]),
            ("plus", slot_of[(dc, (do + 1) % RING, dh)], down_slot[r]),
            ("other", slot_of[(0, ao % RING, ah)], across_slot[r]),
        ))
    return contents, copies


CONTENTS, COPIES = plan()
SPANS = len(CONTENTS)
ORDER = tuple(part * HALF + tile for tile in range(HALF) for part in range(2))


def kernel(order_hbm, q_hbm, k_hbm, v_hbm, w_hbm, out,
           q_in, kv, w, qt, acc, top, att, own, sib_out, sib_in,
           far_out, far_in, near_out, near_in, result, order, span_of,
           load_sem, own_send, own_recv, kv_send, kv_recv, sib_send, sib_recv,
           far_send, far_recv, near_send, near_recv, out_sem):
    heads = q_in.shape[1] // HEAD_DIM
    rows = q_in.shape[0]
    context = lax.axis_index("context")
    tensor = lax.axis_index("tensor")
    y, z = context // RING, lax.rem(context, RING)
    x, core = tensor // 2, lax.rem(tensor, 2)
    targets = {
        "minus": {"context": y * RING + lax.rem(z + RING - 1, RING)},
        "plus": {"context": y * RING + lax.rem(z + 1, RING)},
        "other": {"context": (1 - y) * RING + z},
    }
    sibling = {"tensor": x * 2 + 1 - core}
    chip_next, chip_back = lax.rem(x + 1, CHIPS), lax.rem(x + CHIPS - 1, CHIPS)
    chip_far = lax.rem(x + 2, CHIPS)
    to_next, to_back = {"tensor": chip_next * 2 + core}, {"tensor": chip_back * 2 + core}

    barrier = pltpu.get_barrier_semaphore()
    for target in (*targets.values(), sibling, to_next, to_back):
        pl.semaphore_signal(barrier, inc=1, device_id=target, device_id_type=MESH)

    loads = []
    for half in range(2):
        for part, source in enumerate((k_hbm, v_hbm)):
            loads.append(pltpu.make_async_copy(
                source.at[pl.ds(half * SPAN, SPAN)], kv.at[half, part],
                load_sem.at[2 * half + part]))
    chips = (chip_far, chip_next, chip_back, x)
    for group, chip in enumerate(chips):
        for part, owner in enumerate((core, 1 - core)):
            number = 2 * group + part
            first = pl.multiple_of(chip * 64 + owner * 32, 32)
            loads.append(pltpu.make_async_copy(
                q_hbm.at[pl.ds(first, 32)], q_in.at[pl.ds(32 * number, 32)],
                load_sem.at[4 + number]))
    loads.append(pltpu.make_async_copy(order_hbm, order, load_sem.at[13]))
    loads.append(pltpu.make_async_copy(w_hbm, w, load_sem.at[12]))
    for load in loads[:-1]:
        load.start()

    def own_copies(r):
        for name, src, dst in COPIES[r]:
            for part, source in enumerate((k_hbm, v_hbm)):
                yield pltpu.make_async_remote_copy(
                    src_ref=source.at[pl.ds(src * SPAN, SPAN)], dst_ref=kv.at[dst, part],
                    send_sem=own_send.at[dst - 2, part], recv_sem=own_recv.at[dst - 2, part],
                    device_id=targets[name], device_id_type=MESH)

    def copy_of(name, src, dst):
        return pltpu.make_async_remote_copy(
            src_ref=kv.at[src], dst_ref=kv.at[dst],
            send_sem=kv_send.at[dst - 8], recv_sem=kv_recv.at[dst - 8],
            device_id=targets[name], device_id_type=MESH)

    pl.semaphore_wait(barrier, 6)
    for copy in own_copies(0):
        copy.start()
    loads[-1].start()

    loads[12].wait()
    for slot, (column, offset, half) in enumerate(CONTENTS):
        where = (y if column == 0 else 1 - y) * RING + lax.rem(z + offset, RING)
        span_of[slot] = order[2 * where + half]

    scale = math.log2(math.e) / math.sqrt(HEAD_DIM)
    for load in loads[4:12]:
        load.wait()
    for head in range(heads):
        scaled = q_in[:, head * HEAD_DIM:(head + 1) * HEAD_DIM].astype(jnp.float32).T * scale
        high = scaled.astype(jnp.bfloat16)
        low = (scaled - high.astype(jnp.float32)).astype(jnp.bfloat16)
        qt[head, :HEAD_DIM] = high
        qt[head, HEAD_DIM:] = low

    for first, second in zip(own_copies(0), own_copies(1)):
        first.wait_send()
        second.start()
    for load in loads[:4]:
        load.wait()

    lane = lax.broadcasted_iota(jnp.int32, (1, rows), 1)
    group_of = lane // 64
    chip_of = jnp.where(group_of == 0, chip_far, jnp.where(
        group_of == 1, chip_next, jnp.where(group_of == 2, chip_back, x)))
    owner_of = jnp.where(lax.rem(lane // 32, 2) == 0, core, 1 - core)
    row_of = chip_of * 64 + owner_of * 32 + lax.rem(lane, 32)
    q_span = jnp.where(row_of < SPAN, span_of[0], span_of[1])
    q_pos = q_span * SPAN + lax.rem(row_of, SPAN)

    def operands(first, count):
        spans = kv[pl.ds(first, count)]
        keys = spans[:, 0].reshape(count * SPAN, HEAD_DIM)
        keys = jnp.concatenate([keys, keys], axis=1)
        values = spans[:, 1].reshape(count * SPAN, HEAD_DIM).T
        ones = jnp.ones((16, count * SPAN), jnp.bfloat16)
        return keys, jnp.concatenate([values, ones], axis=0)

    def scores_of(keys, head):
        return jnp.dot(keys, qt[head], preferred_element_type=jnp.float32)

    def receive(r):
        following = COPIES[r + 2] if r + 2 < ROUNDS else ()
        here = 2 + 3 * r
        for copy in following:
            if copy[1] < here:
                copy_of(*copy).start()
        first = list(own_copies(r)) if r < 2 else ()
        for number, copy in enumerate(COPIES[r]):
            if r < 2:
                first[2 * number].wait_recv()
                first[2 * number + 1].wait_recv()
            else:
                copy_of(*copy).wait_recv()
            for later in following:
                if later[1] == copy[2]:
                    copy_of(*later).start()

    keys, values = operands(0, 2)
    k_row = lax.broadcasted_iota(jnp.int32, (2 * SPAN, 1), 0)
    k_pos = jnp.where(k_row < SPAN, span_of[0], span_of[1]) * SPAN + lax.rem(k_row, SPAN)
    hide = jnp.where(k_pos <= q_pos, 0.0, LOWEST)
    following = scores_of(keys, 0)
    for head in range(heads):
        scores = following + hide
        if head + 1 < heads:
            following = scores_of(keys, head + 1)
        new_top = jnp.max(scores, axis=0, keepdims=True)
        weights = jnp.exp2(scores - new_top).astype(jnp.bfloat16)
        top[head] = new_top
        acc[head] = jnp.dot(values, weights, preferred_element_type=jnp.float32)

    @pl.loop(0, ROUNDS)
    def _(step):
        for r in range(ROUNDS):
            @pl.when(step == r)
            def _():
                receive(r)

        first = 2 + 3 * step
        keys, values = operands(first, 3)
        hide = [jnp.where(span_of[first + number] < q_span, 0.0, LOWEST) for number in range(3)]
        following = scores_of(keys, 0)
        for head in range(heads):
            scores = [following[number * SPAN:(number + 1) * SPAN] for number in range(3)]
            if head + 1 < heads:
                following = scores_of(keys, head + 1)
            old_top = top[head]
            new_top = old_top
            for part, hidden in zip(scores, hide):
                new_top = jnp.maximum(new_top, jnp.max(part, axis=0, keepdims=True) + hidden)
            factor = jnp.exp2(old_top - new_top)
            weights = jnp.concatenate([
                jnp.exp2(part - (new_top - hidden)).astype(jnp.bfloat16)
                for part, hidden in zip(scores, hide)], axis=0)
            top[head] = new_top
            acc[head] = acc[head] * factor + jnp.dot(
                values, weights, preferred_element_type=jnp.float32)

    for head in range(heads):
        mixed = acc[head, :HEAD_DIM] * (1.0 / acc[head, HEAD_DIM:HEAD_DIM + 1])
        att[:, head * HEAD_DIM:(head + 1) * HEAD_DIM] = mixed.astype(jnp.bfloat16).T
    loads[13].wait()

    def sib_copy(tile, part):
        at = 0 if part == 0 else pl.ds(1, 3)
        return pltpu.make_async_remote_copy(
            src_ref=sib_out.at[tile, at], dst_ref=sib_in.at[tile, at],
            send_sem=sib_send.at[tile, part], recv_sem=sib_recv.at[tile, part],
            device_id=sibling, device_id_type=MESH)

    def project(tile):
        part = jnp.dot(att[...], w[:, tile * TILE:(tile + 1) * TILE],
                       preferred_element_type=jnp.float32).astype(jnp.bfloat16)
        part = part.reshape(4, 2, 32, TILE)
        sib_out[tile] = part[:, 1]
        sib_copy(tile, 0).start()
        sib_copy(tile, 1).start()
        own[tile] = part[:, 0]

    def both(tile, group):
        return own[tile, group].astype(jnp.float32) + sib_in[tile, group].astype(jnp.float32)

    def far_copy(tile):
        return pltpu.make_async_remote_copy(
            src_ref=far_out.at[tile], dst_ref=far_in.at[tile],
            send_sem=far_send.at[tile], recv_sem=far_recv.at[tile],
            device_id=to_next if tile < HALF else to_back, device_id_type=MESH)

    def near_copy(side, tile):
        return pltpu.make_async_remote_copy(
            src_ref=near_out.at[side, tile], dst_ref=near_in.at[side, tile],
            send_sem=near_send.at[side, tile], recv_sem=near_recv.at[side, tile],
            device_id=to_next if side == 0 else to_back, device_id_type=MESH)

    def out_copy(tile):
        at = pl.ds(tile * TILE, TILE)
        return pltpu.make_async_copy(result.at[:, at], out.at[:, at], out_sem.at[tile])

    def send_far(tile):
        sib_copy(tile, 0).wait_recv()
        far_out[tile] = both(tile, 0).astype(jnp.bfloat16)
        far_copy(tile).start()

    def send_near(side, tile):
        second = (tile < HALF) == (side == 0)
        if not second:
            sib_copy(tile, 1).wait_recv()
        total = both(tile, 1 + side)
        if second:
            far_copy(tile).wait_recv()
            total = total + far_in[tile].astype(jnp.float32)
        near_out[side, tile] = total.astype(jnp.bfloat16)
        near_copy(side, tile).start()

    def send_first(tile):
        send_far(tile)
        send_near(0 if tile >= HALF else 1, tile)

    def send_second(tile):
        send_near(0 if tile < HALF else 1, tile)

    def finish(tile):
        near_copy(0, tile).wait_recv()
        near_copy(1, tile).wait_recv()
        total = both(tile, 3) + (near_in[0, tile].astype(jnp.float32)
                                 + near_in[1, tile].astype(jnp.float32))
        result[:, tile * TILE:(tile + 1) * TILE] = total.astype(out.dtype)
        out_copy(tile).start()

    for number in range(TILES + LAG + 2):
        if number < TILES:
            project(ORDER[number])
        if 0 <= number - 1 < TILES:
            send_first(ORDER[number - 1])
        if 0 <= number - LAG < TILES:
            send_second(ORDER[number - LAG])
        if 0 <= number - LAG - 2 < TILES and number >= TILES:
            for earlier in ORDER[:number - LAG - 1] if number == TILES else (ORDER[number - LAG - 2],):
                finish(earlier)

    for copy in own_copies(1):
        copy.wait_send()
    for copies in COPIES[2:]:
        for copy in copies:
            copy_of(*copy).wait_send()
    for tile in range(TILES):
        for part in range(2):
            sib_copy(tile, part).wait_send()
            near_copy(part, tile).wait_send()
        far_copy(tile).wait_send()
        out_copy(tile).wait()


def on_device(queries, keys, values, span_order, out_weight):
    rows, width = queries.shape
    heads = width // HEAD_DIM
    d_out = out_weight.shape[1]
    bf16, f32 = jnp.bfloat16, jnp.float32
    sem = pltpu.SemaphoreType.DMA
    span_order, queries, keys, values, out_weight = (
        pltpu.with_memory_space_constraint(array, pltpu.HBM)
        for array in (span_order, queries, keys, values, out_weight))
    return pl.pallas_call(
        kernel,
        out_shape=jax.ShapeDtypeStruct((rows // 8, d_out), bf16),
        in_specs=[pl.BlockSpec(memory_space=pltpu.HBM)] * 5,
        out_specs=pl.BlockSpec(memory_space=pl.ANY),
        scratch_shapes=[
            pltpu.VMEM((rows, width), bf16),
            pltpu.VMEM((SPANS, 2, SPAN, HEAD_DIM), bf16),
            pltpu.VMEM((width, d_out), bf16),
            pltpu.VMEM((heads, 2 * HEAD_DIM, rows), bf16),
            pltpu.VMEM((heads, HEAD_DIM + 16, rows), f32),
            pltpu.VMEM((heads, 1, rows), f32),
            pltpu.VMEM((rows, width), bf16),
            pltpu.VMEM((TILES, 4, 32, TILE), bf16),
            pltpu.VMEM((TILES, 4, 32, TILE), bf16),
            pltpu.VMEM((TILES, 4, 32, TILE), bf16),
            pltpu.VMEM((TILES, 32, TILE), bf16),
            pltpu.VMEM((TILES, 32, TILE), bf16),
            pltpu.VMEM((2, TILES, 32, TILE), bf16),
            pltpu.VMEM((2, TILES, 32, TILE), bf16),
            pltpu.VMEM((rows // 8, d_out), bf16),
            pltpu.SMEM((SPANS,), jnp.int32),
            pltpu.SMEM((SPANS,), jnp.int32),
            sem((14,)), sem((6, 2)), sem((6, 2)), sem((SPANS - 8,)), sem((SPANS - 8,)),
            sem((TILES, 2)), sem((TILES, 2)), sem((TILES,)), sem((TILES,)),
            sem((2, TILES)), sem((2, TILES)), sem((TILES,)),
        ],
        compiler_params=pltpu.CompilerParams(
            collective_id=0, has_side_effects=True, vmem_limit_bytes=32 * 1024 * 1024),
        cost_estimate=pl.CostEstimate(
            flops=3 * 2 * rows * width * 4096, bytes_accessed=10 * 2**20,
            transcendentals=heads * rows * 4096),
    )(span_order, queries, keys, values, out_weight)


def solution(mesh):
    return jax.shard_map(
        on_device,
        mesh=mesh,
        in_specs=(
            P(("dp", "context"), "tensor"),
            P(("dp", "context"), "tensor"),
            P(("dp", "context"), "tensor"),
            P("dp"),
            P("tensor", None),
        ),
        out_specs=P(("dp", "context", "tensor"), None),
        check_vma=False,
    )
```

```python
import math

import jax
import jax.numpy as jnp
from jax import lax
from jax.experimental import pallas as pl
from jax.experimental.pallas import tpu as pltpu
from jax.sharding import PartitionSpec as P

HEAD_DIM = 128
SPAN = 128
RING = 8
COLUMNS = 2
CHIPS = 4
ROUNDS = 10
TILE = 512
TILES = 8
HALF = TILES // 2
LOWEST = -1e30
MESH = pl.DeviceIdType.MESH

UP = [(0, 1, 0), (0, 1, 1), (0, 2, 0), (0, 2, 1), (0, 3, 0), (0, 3, 1),
      (1, 3, 0), (0, 4, 0), (1, 4, 0), (1, 3, 1)]
DOWN = [(0, -1, 1), (0, -1, 0), (0, -2, 1), (0, -2, 0), (0, -3, 1), (0, -3, 0),
        (0, -4, 1), (1, -3, 1), (1, -3, 0), (1, -4, 1)]
ACROSS = [(1, 0, 0), (1, 0, 1), (1, 1, 0), (1, -1, 1), (1, 2, 0), (1, -2, 1),
          (1, -2, 0), (1, 2, 1), (1, 1, 1), (1, -1, 0)]


def plan():
    slot_of = {(0, 0, 0): 0, (0, 0, 1): 1}
    contents = [(0, 0, 0), (0, 0, 1)]
    up_slot = {r: 2 + 3 * r for r in range(ROUNDS)}
    down_slot = {r: 3 + 3 * r for r in range(ROUNDS)}
    across_slot = {r: 4 + 3 * r for r in range(ROUNDS)}
    slots = {}
    for r in range(ROUNDS):
        for table, names in ((up_slot, UP), (down_slot, DOWN), (across_slot, ACROSS)):
            slots[table[r]] = names[r]
    for slot in range(2, 2 + 3 * ROUNDS):
        column, offset, half = slots[slot]
        key = (column, offset % RING, half)
        slot_of[key] = slot
        contents.append(key)
    assert len(slot_of) == 2 + 3 * ROUNDS
    copies = []
    for r in range(ROUNDS):
        (uc, uo, uh), (dc, do, dh), (ac, ao, ah) = UP[r], DOWN[r], ACROSS[r]
        copies.append((
            ("minus", slot_of[(uc, (uo - 1) % RING, uh)], up_slot[r]),
            ("plus", slot_of[(dc, (do + 1) % RING, dh)], down_slot[r]),
            ("other", slot_of[(0, ao % RING, ah)], across_slot[r]),
        ))
    return contents, copies


CONTENTS, COPIES = plan()
SPANS = len(CONTENTS)
ORDER = tuple(part * HALF + tile for tile in range(HALF) for part in range(2))


def kernel(order_hbm, q_hbm, k_hbm, v_hbm, w_hbm, out,
           q_in, kv, w, qt, acc, top, att, own, sib_out, sib_in,
           far_out, far_in, near_out, near_in, result, order, span_of,
           load_sem, own_send, own_recv, kv_send, kv_recv, sib_send, sib_recv,
           far_send, far_recv, near_send, near_recv, out_sem):
    heads = q_in.shape[1] // HEAD_DIM
    rows = q_in.shape[0]
    context = lax.axis_index("context")
    tensor = lax.axis_index("tensor")
    y, z = context // RING, lax.rem(context, RING)
    x, core = tensor // 2, lax.rem(tensor, 2)
    targets = {
        "minus": {"context": y * RING + lax.rem(z + RING - 1, RING)},
        "plus": {"context": y * RING + lax.rem(z + 1, RING)},
        "other": {"context": (1 - y) * RING + z},
    }
    sibling = {"tensor": x * 2 + 1 - core}
    chip_next, chip_back = lax.rem(x + 1, CHIPS), lax.rem(x + CHIPS - 1, CHIPS)
    chip_far = lax.rem(x + 2, CHIPS)
    to_next, to_back = {"tensor": chip_next * 2 + core}, {"tensor": chip_back * 2 + core}

    barrier = pltpu.get_barrier_semaphore()
    for target in (*targets.values(), sibling, to_next, to_back):
        pl.semaphore_signal(barrier, inc=1, device_id=target, device_id_type=MESH)

    loads = []
    for half in range(2):
        for part, source in enumerate((k_hbm, v_hbm)):
            loads.append(pltpu.make_async_copy(
                source.at[pl.ds(half * SPAN, SPAN)], kv.at[half, part],
                load_sem.at[2 * half + part]))
    chips = (chip_far, chip_next, chip_back, x)
    for group, chip in enumerate(chips):
        for part, owner in enumerate((core, 1 - core)):
            number = 2 * group + part
            first = pl.multiple_of(chip * 64 + owner * 32, 32)
            loads.append(pltpu.make_async_copy(
                q_hbm.at[pl.ds(first, 32)], q_in.at[pl.ds(32 * number, 32)],
                load_sem.at[4 + number]))
    loads.append(pltpu.make_async_copy(order_hbm, order, load_sem.at[13]))
    loads.append(pltpu.make_async_copy(w_hbm, w, load_sem.at[12]))
    for load in loads[:-1]:
        load.start()

    def own_copies(r):
        for name, src, dst in COPIES[r]:
            for part, source in enumerate((k_hbm, v_hbm)):
                yield pltpu.make_async_remote_copy(
                    src_ref=source.at[pl.ds(src * SPAN, SPAN)], dst_ref=kv.at[dst, part],
                    send_sem=own_send.at[dst - 2, part], recv_sem=own_recv.at[dst - 2, part],
                    device_id=targets[name], device_id_type=MESH)

    def copy_of(name, src, dst):
        return pltpu.make_async_remote_copy(
            src_ref=kv.at[src], dst_ref=kv.at[dst],
            send_sem=kv_send.at[dst - 8], recv_sem=kv_recv.at[dst - 8],
            device_id=targets[name], device_id_type=MESH)

    pl.semaphore_wait(barrier, 6)
    for copy in own_copies(0):
        copy.start()
    loads[-1].start()

    loads[12].wait()
    for slot, (column, offset, half) in enumerate(CONTENTS):
        where = (y if column == 0 else 1 - y) * RING + lax.rem(z + offset, RING)
        span_of[slot] = order[2 * where + half]

    scale = 1.0 / math.sqrt(HEAD_DIM)
    for load in loads[4:12]:
        load.wait()
    for head in range(heads):
        scaled = q_in[:, head * HEAD_DIM:(head + 1) * HEAD_DIM].astype(jnp.float32).T * scale
        high = scaled.astype(jnp.bfloat16)
        low = (scaled - high.astype(jnp.float32)).astype(jnp.bfloat16)
        qt[head, :HEAD_DIM] = high
        qt[head, HEAD_DIM:] = low

    for first, second in zip(own_copies(0), own_copies(1)):
        first.wait_send()
        second.start()
    for load in loads[:4]:
        load.wait()

    lane = lax.broadcasted_iota(jnp.int32, (1, rows), 1)
    group_of = lane // 64
    chip_of = jnp.where(group_of == 0, chip_far, jnp.where(
        group_of == 1, chip_next, jnp.where(group_of == 2, chip_back, x)))
    owner_of = jnp.where(lax.rem(lane // 32, 2) == 0, core, 1 - core)
    row_of = chip_of * 64 + owner_of * 32 + lax.rem(lane, 32)
    q_span = jnp.where(row_of < SPAN, span_of[0], span_of[1])
    q_pos = q_span * SPAN + lax.rem(row_of, SPAN)

    def operands(first, count):
        spans = kv[pl.ds(first, count)]
        keys = spans[:, 0].reshape(count * SPAN, HEAD_DIM)
        keys = jnp.concatenate([keys, keys], axis=1)
        values = spans[:, 1].reshape(count * SPAN, HEAD_DIM).T
        ones = jnp.ones((16, count * SPAN), jnp.bfloat16)
        return keys, jnp.concatenate([values, ones], axis=0)

    def scores_of(keys, head):
        return jnp.dot(keys, qt[head], preferred_element_type=jnp.float32)

    def receive(r):
        following = COPIES[r + 2] if r + 2 < ROUNDS else ()
        here = 2 + 3 * r
        for copy in following:
            if copy[1] < here:
                copy_of(*copy).start()
        first = list(own_copies(r)) if r < 2 else ()
        for number, copy in enumerate(COPIES[r]):
            if r < 2:
                first[2 * number].wait_recv()
                first[2 * number + 1].wait_recv()
            else:
                copy_of(*copy).wait_recv()
            for later in following:
                if later[1] == copy[2]:
                    copy_of(*later).start()

    keys, values = operands(0, 2)
    k_row = lax.broadcasted_iota(jnp.int32, (2 * SPAN, 1), 0)
    k_pos = jnp.where(k_row < SPAN, span_of[0], span_of[1]) * SPAN + lax.rem(k_row, SPAN)
    hide = jnp.where(k_pos <= q_pos, 0.0, LOWEST)
    following = scores_of(keys, 0)
    for head in range(heads):
        scores = following + hide
        if head + 1 < heads:
            following = scores_of(keys, head + 1)
        new_top = jnp.max(scores, axis=0, keepdims=True)
        weights = jnp.exp(scores - new_top).astype(jnp.bfloat16)
        top[head] = new_top
        acc[head] = jnp.dot(values, weights, preferred_element_type=jnp.float32)

    @pl.loop(0, ROUNDS)
    def _(step):
        for r in range(ROUNDS):
            @pl.when(step == r)
            def _():
                receive(r)

        first = 2 + 3 * step
        keys, values = operands(first, 3)
        hide = [jnp.where(span_of[first + number] < q_span, 0.0, LOWEST) for number in range(3)]
        following = scores_of(keys, 0)
        for head in range(heads):
            scores = [following[number * SPAN:(number + 1) * SPAN] for number in range(3)]
            if head + 1 < heads:
                following = scores_of(keys, head + 1)
            old_top = top[head]
            new_top = old_top
            for part, hidden in zip(scores, hide):
                new_top = jnp.maximum(new_top, jnp.max(part, axis=0, keepdims=True) + hidden)
            factor = jnp.exp(old_top - new_top)
            weights = jnp.concatenate([
                jnp.exp(part - (new_top - hidden)).astype(jnp.bfloat16)
                for part, hidden in zip(scores, hide)], axis=0)
            top[head] = new_top
            acc[head] = acc[head] * factor + jnp.dot(
                values, weights, preferred_element_type=jnp.float32)

    for head in range(heads):
        mixed = acc[head, :HEAD_DIM] * (1.0 / acc[head, HEAD_DIM:HEAD_DIM + 1])
        att[:, head * HEAD_DIM:(head + 1) * HEAD_DIM] = mixed.astype(jnp.bfloat16).T
    loads[13].wait()

    def sib_copy(tile, part):
        at = 0 if part == 0 else pl.ds(1, 3)
        return pltpu.make_async_remote_copy(
            src_ref=sib_out.at[tile, at], dst_ref=sib_in.at[tile, at],
            send_sem=sib_send.at[tile, part], recv_sem=sib_recv.at[tile, part],
            device_id=sibling, device_id_type=MESH)

    def project(tile):
        part = jnp.dot(att[...], w[:, tile * TILE:(tile + 1) * TILE],
                       preferred_element_type=jnp.float32).astype(jnp.bfloat16)
        part = part.reshape(4, 2, 32, TILE)
        sib_out[tile] = part[:, 1]
        sib_copy(tile, 0).start()
        sib_copy(tile, 1).start()
        own[tile] = part[:, 0]

    def both(tile, group):
        return own[tile, group].astype(jnp.float32) + sib_in[tile, group].astype(jnp.float32)

    def far_copy(tile):
        return pltpu.make_async_remote_copy(
            src_ref=far_out.at[tile], dst_ref=far_in.at[tile],
            send_sem=far_send.at[tile], recv_sem=far_recv.at[tile],
            device_id=to_next if tile < HALF else to_back, device_id_type=MESH)

    def near_copy(side, tile):
        return pltpu.make_async_remote_copy(
            src_ref=near_out.at[side, tile], dst_ref=near_in.at[side, tile],
            send_sem=near_send.at[side, tile], recv_sem=near_recv.at[side, tile],
            device_id=to_next if side == 0 else to_back, device_id_type=MESH)

    def out_copy(tile):
        at = pl.ds(tile * TILE, TILE)
        return pltpu.make_async_copy(result.at[:, at], out.at[:, at], out_sem.at[tile])

    def send_far(tile):
        sib_copy(tile, 0).wait_recv()
        far_out[tile] = both(tile, 0).astype(jnp.bfloat16)
        far_copy(tile).start()

    def send_near(side, tile):
        second = (tile < HALF) == (side == 0)
        if not second:
            sib_copy(tile, 1).wait_recv()
        total = both(tile, 1 + side)
        if second:
            far_copy(tile).wait_recv()
            total = total + far_in[tile].astype(jnp.float32)
        near_out[side, tile] = total.astype(jnp.bfloat16)
        near_copy(side, tile).start()

    def send_first(tile):
        send_far(tile)
        send_near(0 if tile >= HALF else 1, tile)

    project(ORDER[0])
    for earlier, tile in zip(ORDER, ORDER[1:]):
        project(tile)
        send_first(earlier)
    send_first(ORDER[-1])
    for tile in ORDER:
        send_near(0 if tile < HALF else 1, tile)
    for tile in ORDER:
        near_copy(0, tile).wait_recv()
        near_copy(1, tile).wait_recv()
        total = both(tile, 3) + (near_in[0, tile].astype(jnp.float32)
                                 + near_in[1, tile].astype(jnp.float32))
        result[:, tile * TILE:(tile + 1) * TILE] = total.astype(out.dtype)
        out_copy(tile).start()

    for copy in own_copies(1):
        copy.wait_send()
    for copies in COPIES[2:]:
        for copy in copies:
            copy_of(*copy).wait_send()
    for tile in range(TILES):
        for part in range(2):
            sib_copy(tile, part).wait_send()
            near_copy(part, tile).wait_send()
        far_copy(tile).wait_send()
        out_copy(tile).wait()


def on_device(queries, keys, values, span_order, out_weight):
    rows, width = queries.shape
    heads = width // HEAD_DIM
    d_out = out_weight.shape[1]
    bf16, f32 = jnp.bfloat16, jnp.float32
    sem = pltpu.SemaphoreType.DMA
    span_order, queries, keys, values, out_weight = (
        pltpu.with_memory_space_constraint(array, pltpu.HBM)
        for array in (span_order, queries, keys, values, out_weight))
    return pl.pallas_call(
        kernel,
        out_shape=jax.ShapeDtypeStruct((rows // 8, d_out), bf16),
        in_specs=[pl.BlockSpec(memory_space=pltpu.HBM)] * 5,
        out_specs=pl.BlockSpec(memory_space=pl.ANY),
        scratch_shapes=[
            pltpu.VMEM((rows, width), bf16),
            pltpu.VMEM((SPANS, 2, SPAN, HEAD_DIM), bf16),
            pltpu.VMEM((width, d_out), bf16),
            pltpu.VMEM((heads, 2 * HEAD_DIM, rows), bf16),
            pltpu.VMEM((heads, HEAD_DIM + 16, rows), f32),
            pltpu.VMEM((heads, 1, rows), f32),
            pltpu.VMEM((rows, width), bf16),
            pltpu.VMEM((TILES, 4, 32, TILE), bf16),
            pltpu.VMEM((TILES, 4, 32, TILE), bf16),
            pltpu.VMEM((TILES, 4, 32, TILE), bf16),
            pltpu.VMEM((TILES, 32, TILE), bf16),
            pltpu.VMEM((TILES, 32, TILE), bf16),
            pltpu.VMEM((2, TILES, 32, TILE), bf16),
            pltpu.VMEM((2, TILES, 32, TILE), bf16),
            pltpu.VMEM((rows // 8, d_out), bf16),
            pltpu.SMEM((SPANS,), jnp.int32),
            pltpu.SMEM((SPANS,), jnp.int32),
            sem((14,)), sem((6, 2)), sem((6, 2)), sem((SPANS - 8,)), sem((SPANS - 8,)),
            sem((TILES, 2)), sem((TILES, 2)), sem((TILES,)), sem((TILES,)),
            sem((2, TILES)), sem((2, TILES)), sem((TILES,)),
        ],
        compiler_params=pltpu.CompilerParams(
            collective_id=0, has_side_effects=True, vmem_limit_bytes=32 * 1024 * 1024),
        cost_estimate=pl.CostEstimate(
            flops=3 * 2 * rows * width * 4096, bytes_accessed=10 * 2**20,
            transcendentals=heads * rows * 4096),
    )(span_order, queries, keys, values, out_weight)


def solution(mesh):
    return jax.shard_map(
        on_device,
        mesh=mesh,
        in_specs=(
            P(("dp", "context"), "tensor"),
            P(("dp", "context"), "tensor"),
            P(("dp", "context"), "tensor"),
            P("dp"),
            P("tensor", None),
        ),
        out_specs=P(("dp", "context", "tensor"), None),
        check_vma=False,
    )
```

```python
import math

import jax
import jax.numpy as jnp
from jax import lax
from jax.experimental import pallas as pl
from jax.experimental.pallas import tpu as pltpu
from jax.sharding import PartitionSpec as P

HEAD_DIM = 128
SPAN = 128
RING = 8
COLUMNS = 2
CHIPS = 4
ROUNDS = 10
TILE = 512
TILES = 8
HALF = TILES // 2
LOWEST = -1e30
MESH = pl.DeviceIdType.MESH

UP = [(0, 1, 0), (0, 1, 1), (0, 2, 0), (0, 2, 1), (0, 3, 0), (0, 3, 1),
      (1, 3, 0), (0, 4, 0), (1, 4, 0), (1, 3, 1)]
DOWN = [(0, -1, 1), (0, -1, 0), (0, -2, 1), (0, -2, 0), (0, -3, 1), (0, -3, 0),
        (0, -4, 1), (1, -3, 1), (1, -3, 0), (1, -4, 1)]
ACROSS = [(1, 0, 0), (1, 0, 1), (1, 1, 0), (1, -1, 1), (1, 2, 0), (1, -2, 1),
          (1, -2, 0), (1, 2, 1), (1, 1, 1), (1, -1, 0)]


def plan():
    slot_of = {(0, 0, 0): 0, (0, 0, 1): 1}
    contents = [(0, 0, 0), (0, 0, 1)]
    up_slot = {r: 2 + 3 * r for r in range(ROUNDS)}
    down_slot = {r: 3 + 3 * r for r in range(ROUNDS)}
    across_slot = {r: 4 + 3 * r for r in range(ROUNDS)}
    slots = {}
    for r in range(ROUNDS):
        for table, names in ((up_slot, UP), (down_slot, DOWN), (across_slot, ACROSS)):
            slots[table[r]] = names[r]
    for slot in range(2, 2 + 3 * ROUNDS):
        column, offset, half = slots[slot]
        key = (column, offset % RING, half)
        slot_of[key] = slot
        contents.append(key)
    assert len(slot_of) == 2 + 3 * ROUNDS
    copies = []
    for r in range(ROUNDS):
        (uc, uo, uh), (dc, do, dh), (ac, ao, ah) = UP[r], DOWN[r], ACROSS[r]
        copies.append((
            ("minus", slot_of[(uc, (uo - 1) % RING, uh)], up_slot[r]),
            ("plus", slot_of[(dc, (do + 1) % RING, dh)], down_slot[r]),
            ("other", slot_of[(0, ao % RING, ah)], across_slot[r]),
        ))
    return contents, copies


CONTENTS, COPIES = plan()
SPANS = len(CONTENTS)
ORDER = tuple(part * HALF + tile for tile in range(HALF) for part in range(2))


def kernel(order_hbm, q_hbm, k_hbm, v_hbm, w_hbm, out,
           q_in, kv, w, qt, acc, top, att, own, sib_out, sib_in,
           far_out, far_in, near_out, near_in, result, order, span_of,
           load_sem, own_send, own_recv, kv_send, kv_recv, sib_send, sib_recv,
           far_send, far_recv, near_send, near_recv, out_sem):
    heads = q_in.shape[1] // HEAD_DIM
    rows = q_in.shape[0]
    context = lax.axis_index("context")
    tensor = lax.axis_index("tensor")
    y, z = context // RING, lax.rem(context, RING)
    x, core = tensor // 2, lax.rem(tensor, 2)
    targets = {
        "minus": {"context": y * RING + lax.rem(z + RING - 1, RING)},
        "plus": {"context": y * RING + lax.rem(z + 1, RING)},
        "other": {"context": (1 - y) * RING + z},
    }
    sibling = {"tensor": x * 2 + 1 - core}
    chip_next, chip_back = lax.rem(x + 1, CHIPS), lax.rem(x + CHIPS - 1, CHIPS)
    chip_far = lax.rem(x + 2, CHIPS)
    to_next, to_back = {"tensor": chip_next * 2 + core}, {"tensor": chip_back * 2 + core}

    barrier = pltpu.get_barrier_semaphore()
    for target in (*targets.values(), sibling, to_next, to_back):
        pl.semaphore_signal(barrier, inc=1, device_id=target, device_id_type=MESH)

    loads = []
    for half in range(2):
        for part, source in enumerate((k_hbm, v_hbm)):
            loads.append(pltpu.make_async_copy(
                source.at[pl.ds(half * SPAN, SPAN)], kv.at[half, part],
                load_sem.at[2 * half + part]))
    chips = (chip_far, chip_next, chip_back, x)
    for group, chip in enumerate(chips):
        for part, owner in enumerate((core, 1 - core)):
            number = 2 * group + part
            first = pl.multiple_of(chip * 64 + owner * 32, 32)
            loads.append(pltpu.make_async_copy(
                q_hbm.at[pl.ds(first, 32)], q_in.at[pl.ds(32 * number, 32)],
                load_sem.at[4 + number]))
    loads.append(pltpu.make_async_copy(order_hbm, order, load_sem.at[13]))
    loads.append(pltpu.make_async_copy(w_hbm, w, load_sem.at[12]))
    for load in loads[:-1]:
        load.start()

    def own_copies(r):
        for name, src, dst in COPIES[r]:
            for part, source in enumerate((k_hbm, v_hbm)):
                yield pltpu.make_async_remote_copy(
                    src_ref=source.at[pl.ds(src * SPAN, SPAN)], dst_ref=kv.at[dst, part],
                    send_sem=own_send.at[dst - 2, part], recv_sem=own_recv.at[dst - 2, part],
                    device_id=targets[name], device_id_type=MESH)

    def copy_of(name, src, dst):
        return pltpu.make_async_remote_copy(
            src_ref=kv.at[src], dst_ref=kv.at[dst],
            send_sem=kv_send.at[dst - 8], recv_sem=kv_recv.at[dst - 8],
            device_id=targets[name], device_id_type=MESH)

    pl.semaphore_wait(barrier, 6)
    for copy in own_copies(0):
        copy.start()
    loads[-1].start()

    loads[12].wait()
    for slot, (column, offset, half) in enumerate(CONTENTS):
        where = (y if column == 0 else 1 - y) * RING + lax.rem(z + offset, RING)
        span_of[slot] = order[2 * where + half]

    for load in loads[4:12]:
        load.wait()
    for head in range(heads):
        qt[head] = q_in[:, head * HEAD_DIM:(head + 1) * HEAD_DIM].T

    for first, second in zip(own_copies(0), own_copies(1)):
        first.wait_send()
        second.start()
    for load in loads[:4]:
        load.wait()

    lane = lax.broadcasted_iota(jnp.int32, (1, rows), 1)
    group_of = lane // 64
    chip_of = jnp.where(group_of == 0, chip_far, jnp.where(
        group_of == 1, chip_next, jnp.where(group_of == 2, chip_back, x)))
    owner_of = jnp.where(lax.rem(lane // 32, 2) == 0, core, 1 - core)
    row_of = chip_of * 64 + owner_of * 32 + lax.rem(lane, 32)
    q_span = jnp.where(row_of < SPAN, span_of[0], span_of[1])
    q_pos = q_span * SPAN + lax.rem(row_of, SPAN)

    def operands(first, count):
        spans = kv[pl.ds(first, count)]
        keys = spans[:, 0].reshape(count * SPAN, HEAD_DIM)
        values = spans[:, 1].reshape(count * SPAN, HEAD_DIM).T
        ones = jnp.ones((16, count * SPAN), jnp.bfloat16)
        return keys, jnp.concatenate([values, ones], axis=0)

    scale = math.log2(math.e) / math.sqrt(HEAD_DIM)

    def scores_of(keys, head):
        return jnp.dot(keys, qt[head], preferred_element_type=jnp.float32)

    def receive(r):
        following = COPIES[r + 2] if r + 2 < ROUNDS else ()
        here = 2 + 3 * r
        for copy in following:
            if copy[1] < here:
                copy_of(*copy).start()
        first = list(own_copies(r)) if r < 2 else ()
        for number, copy in enumerate(COPIES[r]):
            if r < 2:
                first[2 * number].wait_recv()
                first[2 * number + 1].wait_recv()
            else:
                copy_of(*copy).wait_recv()
            for later in following:
                if later[1] == copy[2]:
                    copy_of(*later).start()

    keys, values = operands(0, 2)
    k_row = lax.broadcasted_iota(jnp.int32, (2 * SPAN, 1), 0)
    k_pos = jnp.where(k_row < SPAN, span_of[0], span_of[1]) * SPAN + lax.rem(k_row, SPAN)
    hide = jnp.where(k_pos <= q_pos, 0.0, LOWEST)
    following = scores_of(keys, 0)
    for head in range(heads):
        scores = following * scale + hide
        if head + 1 < heads:
            following = scores_of(keys, head + 1)
        new_top = jnp.max(scores, axis=0, keepdims=True)
        weights = jnp.exp2(scores - new_top).astype(jnp.bfloat16)
        top[head] = new_top
        acc[head] = jnp.dot(values, weights, preferred_element_type=jnp.float32)

    @pl.loop(0, ROUNDS)
    def _(step):
        for r in range(ROUNDS):
            @pl.when(step == r)
            def _():
                receive(r)

        first = 2 + 3 * step
        keys, values = operands(first, 3)
        hide = [jnp.where(span_of[first + number] < q_span, 0.0, LOWEST) for number in range(3)]
        following = scores_of(keys, 0)
        for head in range(heads):
            scores = [following[number * SPAN:(number + 1) * SPAN] for number in range(3)]
            if head + 1 < heads:
                following = scores_of(keys, head + 1)
            old_top = top[head]
            new_top = old_top
            for part, hidden in zip(scores, hide):
                new_top = jnp.maximum(new_top, jnp.max(part, axis=0, keepdims=True) * scale + hidden)
            factor = jnp.exp2(old_top - new_top)
            weights = jnp.concatenate([
                jnp.exp2(part * scale - (new_top - hidden)).astype(jnp.bfloat16)
                for part, hidden in zip(scores, hide)], axis=0)
            top[head] = new_top
            acc[head] = acc[head] * factor + jnp.dot(
                values, weights, preferred_element_type=jnp.float32)

    for head in range(heads):
        mixed = acc[head, :HEAD_DIM] * (1.0 / acc[head, HEAD_DIM:HEAD_DIM + 1])
        att[:, head * HEAD_DIM:(head + 1) * HEAD_DIM] = mixed.astype(jnp.bfloat16).T
    loads[13].wait()

    def sib_copy(tile, part):
        at = 0 if part == 0 else pl.ds(1, 3)
        return pltpu.make_async_remote_copy(
            src_ref=sib_out.at[tile, at], dst_ref=sib_in.at[tile, at],
            send_sem=sib_send.at[tile, part], recv_sem=sib_recv.at[tile, part],
            device_id=sibling, device_id_type=MESH)

    def project(tile):
        part = jnp.dot(att[...], w[:, tile * TILE:(tile + 1) * TILE],
                       preferred_element_type=jnp.float32).astype(jnp.bfloat16)
        part = part.reshape(4, 2, 32, TILE)
        sib_out[tile] = part[:, 1]
        sib_copy(tile, 0).start()
        sib_copy(tile, 1).start()
        own[tile] = part[:, 0]

    def both(tile, group):
        return own[tile, group].astype(jnp.float32) + sib_in[tile, group].astype(jnp.float32)

    def far_copy(tile):
        return pltpu.make_async_remote_copy(
            src_ref=far_out.at[tile], dst_ref=far_in.at[tile],
            send_sem=far_send.at[tile], recv_sem=far_recv.at[tile],
            device_id=to_next if tile < HALF else to_back, device_id_type=MESH)

    def near_copy(side, tile):
        return pltpu.make_async_remote_copy(
            src_ref=near_out.at[side, tile], dst_ref=near_in.at[side, tile],
            send_sem=near_send.at[side, tile], recv_sem=near_recv.at[side, tile],
            device_id=to_next if side == 0 else to_back, device_id_type=MESH)

    def out_copy(tile):
        at = pl.ds(tile * TILE, TILE)
        return pltpu.make_async_copy(result.at[:, at], out.at[:, at], out_sem.at[tile])

    def send_far(tile):
        sib_copy(tile, 0).wait_recv()
        far_out[tile] = both(tile, 0).astype(jnp.bfloat16)
        far_copy(tile).start()

    def send_near(side, tile):
        second = (tile < HALF) == (side == 0)
        if not second:
            sib_copy(tile, 1).wait_recv()
        total = both(tile, 1 + side)
        if second:
            far_copy(tile).wait_recv()
            total = total + far_in[tile].astype(jnp.float32)
        near_out[side, tile] = total.astype(jnp.bfloat16)
        near_copy(side, tile).start()

    def send_first(tile):
        send_far(tile)
        send_near(0 if tile >= HALF else 1, tile)

    project(ORDER[0])
    for earlier, tile in zip(ORDER, ORDER[1:]):
        project(tile)
        send_first(earlier)
    send_first(ORDER[-1])
    for tile in ORDER:
        send_near(0 if tile < HALF else 1, tile)
    for tile in ORDER:
        near_copy(0, tile).wait_recv()
        near_copy(1, tile).wait_recv()
        total = both(tile, 3) + (near_in[0, tile].astype(jnp.float32)
                                 + near_in[1, tile].astype(jnp.float32))
        result[:, tile * TILE:(tile + 1) * TILE] = total.astype(out.dtype)
        out_copy(tile).start()

    for copy in own_copies(1):
        copy.wait_send()
    for copies in COPIES[2:]:
        for copy in copies:
            copy_of(*copy).wait_send()
    for tile in range(TILES):
        for part in range(2):
            sib_copy(tile, part).wait_send()
            near_copy(part, tile).wait_send()
        far_copy(tile).wait_send()
        out_copy(tile).wait()


def on_device(queries, keys, values, span_order, out_weight):
    rows, width = queries.shape
    heads = width // HEAD_DIM
    d_out = out_weight.shape[1]
    bf16, f32 = jnp.bfloat16, jnp.float32
    sem = pltpu.SemaphoreType.DMA
    span_order, queries, keys, values, out_weight = (
        pltpu.with_memory_space_constraint(array, pltpu.HBM)
        for array in (span_order, queries, keys, values, out_weight))
    return pl.pallas_call(
        kernel,
        out_shape=jax.ShapeDtypeStruct((rows // 8, d_out), bf16),
        in_specs=[pl.BlockSpec(memory_space=pltpu.HBM)] * 5,
        out_specs=pl.BlockSpec(memory_space=pl.ANY),
        scratch_shapes=[
            pltpu.VMEM((rows, width), bf16),
            pltpu.VMEM((SPANS, 2, SPAN, HEAD_DIM), bf16),
            pltpu.VMEM((width, d_out), bf16),
            pltpu.VMEM((heads, HEAD_DIM, rows), bf16),
            pltpu.VMEM((heads, HEAD_DIM + 16, rows), f32),
            pltpu.VMEM((heads, 1, rows), f32),
            pltpu.VMEM((rows, width), bf16),
            pltpu.VMEM((TILES, 4, 32, TILE), bf16),
            pltpu.VMEM((TILES, 4, 32, TILE), bf16),
            pltpu.VMEM((TILES, 4, 32, TILE), bf16),
            pltpu.VMEM((TILES, 32, TILE), bf16),
            pltpu.VMEM((TILES, 32, TILE), bf16),
            pltpu.VMEM((2, TILES, 32, TILE), bf16),
            pltpu.VMEM((2, TILES, 32, TILE), bf16),
            pltpu.VMEM((rows // 8, d_out), bf16),
            pltpu.SMEM((SPANS,), jnp.int32),
            pltpu.SMEM((SPANS,), jnp.int32),
            sem((14,)), sem((6, 2)), sem((6, 2)), sem((SPANS - 8,)), sem((SPANS - 8,)),
            sem((TILES, 2)), sem((TILES, 2)), sem((TILES,)), sem((TILES,)),
            sem((2, TILES)), sem((2, TILES)), sem((TILES,)),
        ],
        compiler_params=pltpu.CompilerParams(
            collective_id=0, has_side_effects=True, vmem_limit_bytes=32 * 1024 * 1024),
        cost_estimate=pl.CostEstimate(
            flops=3 * 2 * rows * width * 4096, bytes_accessed=10 * 2**20,
            transcendentals=heads * rows * 4096),
    )(span_order, queries, keys, values, out_weight)


def solution(mesh):
    return jax.shard_map(
        on_device,
        mesh=mesh,
        in_specs=(
            P(("dp", "context"), "tensor"),
            P(("dp", "context"), "tensor"),
            P(("dp", "context"), "tensor"),
            P("dp"),
            P("tensor", None),
        ),
        out_specs=P(("dp", "context", "tensor"), None),
        check_vma=False,
    )
```

```python
import math

import jax
import jax.numpy as jnp
from jax import lax
from jax.experimental import pallas as pl
from jax.experimental.pallas import tpu as pltpu
from jax.sharding import PartitionSpec as P

HEAD_DIM = 128
SPAN = 128
RING = 8
COLUMNS = 2
CHIPS = 4
ROUNDS = 10
TILE = 512
TILES = 8
HALF = TILES // 2
LOWEST = -1e30
MESH = pl.DeviceIdType.MESH

UP = [(0, 1, 0), (0, 1, 1), (0, 2, 0), (0, 2, 1), (0, 3, 0), (0, 3, 1),
      (1, 3, 0), (0, 4, 0), (1, 4, 0), (1, 3, 1)]
DOWN = [(0, -1, 1), (0, -1, 0), (0, -2, 1), (0, -2, 0), (0, -3, 1), (0, -3, 0),
        (0, -4, 1), (1, -3, 1), (1, -3, 0), (1, -4, 1)]
ACROSS = [(1, 0, 0), (1, 0, 1), (1, 1, 0), (1, -1, 1), (1, 2, 0), (1, -2, 1),
          (1, -2, 0), (1, 2, 1), (1, 1, 1), (1, -1, 0)]


def plan():
    slot_of = {(0, 0, 0): 0, (0, 0, 1): 1}
    contents = [(0, 0, 0), (0, 0, 1)]
    up_slot = {r: 2 + 3 * r for r in range(ROUNDS)}
    down_slot = {r: 3 + 3 * r for r in range(ROUNDS)}
    across_slot = {r: 4 + 3 * r for r in range(ROUNDS)}
    slots = {}
    for r in range(ROUNDS):
        for table, names in ((up_slot, UP), (down_slot, DOWN), (across_slot, ACROSS)):
            slots[table[r]] = names[r]
    for slot in range(2, 2 + 3 * ROUNDS):
        column, offset, half = slots[slot]
        key = (column, offset % RING, half)
        slot_of[key] = slot
        contents.append(key)
    assert len(slot_of) == 2 + 3 * ROUNDS
    copies = []
    for r in range(ROUNDS):
        (uc, uo, uh), (dc, do, dh), (ac, ao, ah) = UP[r], DOWN[r], ACROSS[r]
        copies.append((
            ("minus", slot_of[(uc, (uo - 1) % RING, uh)], up_slot[r]),
            ("plus", slot_of[(dc, (do + 1) % RING, dh)], down_slot[r]),
            ("other", slot_of[(0, ao % RING, ah)], across_slot[r]),
        ))
    return contents, copies


CONTENTS, COPIES = plan()
SPANS = len(CONTENTS)
ORDER = tuple(part * HALF + tile for tile in range(HALF) for part in range(2))


def kernel(order_hbm, q_hbm, k_hbm, v_hbm, w_hbm, out,
           q_in, kv, w, qt, acc, top, att, own, sib_out, sib_in,
           far_out, far_in, near_out, near_in, result, order, span_of,
           load_sem, weight_sem, own_send, own_recv, kv_send, kv_recv, sib_send, sib_recv,
           far_send, far_recv, near_send, near_recv, out_sem):
    heads = q_in.shape[1] // HEAD_DIM
    rows = q_in.shape[0]
    context = lax.axis_index("context")
    tensor = lax.axis_index("tensor")
    y, z = context // RING, lax.rem(context, RING)
    x, core = tensor // 2, lax.rem(tensor, 2)
    targets = {
        "minus": {"context": y * RING + lax.rem(z + RING - 1, RING)},
        "plus": {"context": y * RING + lax.rem(z + 1, RING)},
        "other": {"context": (1 - y) * RING + z},
    }
    sibling = {"tensor": x * 2 + 1 - core}
    chip_next, chip_back = lax.rem(x + 1, CHIPS), lax.rem(x + CHIPS - 1, CHIPS)
    chip_far = lax.rem(x + 2, CHIPS)
    to_next, to_back = {"tensor": chip_next * 2 + core}, {"tensor": chip_back * 2 + core}

    barrier = pltpu.get_barrier_semaphore()
    for target in (*targets.values(), sibling, to_next, to_back):
        pl.semaphore_signal(barrier, inc=1, device_id=target, device_id_type=MESH)

    loads = []
    for half in range(2):
        for part, source in enumerate((k_hbm, v_hbm)):
            loads.append(pltpu.make_async_copy(
                source.at[pl.ds(half * SPAN, SPAN)], kv.at[half, part],
                load_sem.at[2 * half + part]))
    chips = (chip_far, chip_next, chip_back, x)
    for group, chip in enumerate(chips):
        for part, owner in enumerate((core, 1 - core)):
            number = 2 * group + part
            first = pl.multiple_of(chip * 64 + owner * 32, 32)
            loads.append(pltpu.make_async_copy(
                q_hbm.at[pl.ds(first, 32)], q_in.at[pl.ds(32 * number, 32)],
                load_sem.at[4 + number]))
    loads.append(pltpu.make_async_copy(order_hbm, order, load_sem.at[12]))
    def weight_load(part):
        at = pl.ds(part * HEAD_DIM, HEAD_DIM)
        return pltpu.make_async_copy(w_hbm.at[at], w.at[at], weight_sem.at[part])

    for load in loads:
        load.start()

    def own_copies(r):
        for name, src, dst in COPIES[r]:
            for part, source in enumerate((k_hbm, v_hbm)):
                yield pltpu.make_async_remote_copy(
                    src_ref=source.at[pl.ds(src * SPAN, SPAN)], dst_ref=kv.at[dst, part],
                    send_sem=own_send.at[dst - 2, part], recv_sem=own_recv.at[dst - 2, part],
                    device_id=targets[name], device_id_type=MESH)

    def copy_of(name, src, dst):
        return pltpu.make_async_remote_copy(
            src_ref=kv.at[src], dst_ref=kv.at[dst],
            send_sem=kv_send.at[dst - 8], recv_sem=kv_recv.at[dst - 8],
            device_id=targets[name], device_id_type=MESH)

    pl.semaphore_wait(barrier, 6)
    for copy in own_copies(0):
        copy.start()

    loads[12].wait()
    for slot, (column, offset, half) in enumerate(CONTENTS):
        where = (y if column == 0 else 1 - y) * RING + lax.rem(z + offset, RING)
        span_of[slot] = order[2 * where + half]

    for load in loads[4:12]:
        load.wait()
    for head in range(heads):
        qt[head] = q_in[:, head * HEAD_DIM:(head + 1) * HEAD_DIM].T

    for copy in own_copies(1):
        copy.start()
    for load in loads[:4]:
        load.wait()

    lane = lax.broadcasted_iota(jnp.int32, (1, rows), 1)
    group_of = lane // 64
    chip_of = jnp.where(group_of == 0, chip_far, jnp.where(
        group_of == 1, chip_next, jnp.where(group_of == 2, chip_back, x)))
    owner_of = jnp.where(lax.rem(lane // 32, 2) == 0, core, 1 - core)
    row_of = chip_of * 64 + owner_of * 32 + lax.rem(lane, 32)
    q_span = jnp.where(row_of < SPAN, span_of[0], span_of[1])
    q_pos = q_span * SPAN + lax.rem(row_of, SPAN)

    def operands(first, count):
        spans = kv[pl.ds(first, count)]
        keys = spans[:, 0].reshape(count * SPAN, HEAD_DIM)
        values = spans[:, 1].reshape(count * SPAN, HEAD_DIM).T
        ones = jnp.ones((16, count * SPAN), jnp.bfloat16)
        return keys, jnp.concatenate([values, ones], axis=0)

    scale = math.log2(math.e) / math.sqrt(HEAD_DIM)

    def scores_of(keys, head):
        return jnp.dot(keys, qt[head], preferred_element_type=jnp.float32)

    def receive(r):
        following = COPIES[r + 2] if r + 2 < ROUNDS else ()
        here = 2 + 3 * r
        for copy in following:
            if copy[1] < here:
                copy_of(*copy).start()
        first = list(own_copies(r)) if r < 2 else ()
        for number, copy in enumerate(COPIES[r]):
            if r < 2:
                first[2 * number].wait_recv()
                first[2 * number + 1].wait_recv()
            else:
                copy_of(*copy).wait_recv()
            for later in following:
                if later[1] == copy[2]:
                    copy_of(*later).start()

    keys, values = operands(0, 2)
    k_row = lax.broadcasted_iota(jnp.int32, (2 * SPAN, 1), 0)
    k_pos = jnp.where(k_row < SPAN, span_of[0], span_of[1]) * SPAN + lax.rem(k_row, SPAN)
    hide = jnp.where(k_pos <= q_pos, 0.0, LOWEST)
    following = scores_of(keys, 0)
    for head in range(heads):
        scores = following * scale + hide
        if head + 1 < heads:
            following = scores_of(keys, head + 1)
        new_top = jnp.max(scores, axis=0, keepdims=True)
        weights = jnp.exp2(scores - new_top).astype(jnp.bfloat16)
        top[head] = new_top
        acc[head] = jnp.dot(values, weights, preferred_element_type=jnp.float32)

    @pl.loop(0, ROUNDS)
    def _(step):
        for r in range(ROUNDS):
            @pl.when(step == r)
            def _():
                receive(r)
                if r < heads:
                    weight_load(r).start()

        first = 2 + 3 * step
        keys, values = operands(first, 3)
        hide = [jnp.where(span_of[first + number] < q_span, 0.0, LOWEST) for number in range(3)]
        following = scores_of(keys, 0)
        for head in range(heads):
            scores = [following[number * SPAN:(number + 1) * SPAN] for number in range(3)]
            if head + 1 < heads:
                following = scores_of(keys, head + 1)
            old_top = top[head]
            new_top = old_top
            for part, hidden in zip(scores, hide):
                new_top = jnp.maximum(new_top, jnp.max(part, axis=0, keepdims=True) * scale + hidden)
            factor = jnp.exp2(old_top - new_top)
            weights = jnp.concatenate([
                jnp.exp2(part * scale - (new_top - hidden)).astype(jnp.bfloat16)
                for part, hidden in zip(scores, hide)], axis=0)
            top[head] = new_top
            acc[head] = acc[head] * factor + jnp.dot(
                values, weights, preferred_element_type=jnp.float32)

    for head in range(heads):
        mixed = acc[head, :HEAD_DIM] * (1.0 / acc[head, HEAD_DIM:HEAD_DIM + 1])
        att[:, head * HEAD_DIM:(head + 1) * HEAD_DIM] = mixed.astype(jnp.bfloat16).T
    for part in range(heads):
        weight_load(part).wait()

    def sib_copy(tile, part):
        at = 0 if part == 0 else pl.ds(1, 3)
        return pltpu.make_async_remote_copy(
            src_ref=sib_out.at[tile, at], dst_ref=sib_in.at[tile, at],
            send_sem=sib_send.at[tile, part], recv_sem=sib_recv.at[tile, part],
            device_id=sibling, device_id_type=MESH)

    def project(tile):
        part = jnp.dot(att[...], w[:, tile * TILE:(tile + 1) * TILE],
                       preferred_element_type=jnp.float32).astype(jnp.bfloat16)
        part = part.reshape(4, 2, 32, TILE)
        sib_out[tile] = part[:, 1]
        sib_copy(tile, 0).start()
        sib_copy(tile, 1).start()
        own[tile] = part[:, 0]

    def both(tile, group):
        return own[tile, group].astype(jnp.float32) + sib_in[tile, group].astype(jnp.float32)

    def far_copy(tile):
        return pltpu.make_async_remote_copy(
            src_ref=far_out.at[tile], dst_ref=far_in.at[tile],
            send_sem=far_send.at[tile], recv_sem=far_recv.at[tile],
            device_id=to_next if tile < HALF else to_back, device_id_type=MESH)

    def near_copy(side, tile):
        return pltpu.make_async_remote_copy(
            src_ref=near_out.at[side, tile], dst_ref=near_in.at[side, tile],
            send_sem=near_send.at[side, tile], recv_sem=near_recv.at[side, tile],
            device_id=to_next if side == 0 else to_back, device_id_type=MESH)

    def out_copy(tile):
        at = pl.ds(tile * TILE, TILE)
        return pltpu.make_async_copy(result.at[:, at], out.at[:, at], out_sem.at[tile])

    def send_far(tile):
        sib_copy(tile, 0).wait_recv()
        far_out[tile] = both(tile, 0).astype(jnp.bfloat16)
        far_copy(tile).start()

    def send_near(side, tile):
        second = (tile < HALF) == (side == 0)
        if not second:
            sib_copy(tile, 1).wait_recv()
        total = both(tile, 1 + side)
        if second:
            far_copy(tile).wait_recv()
            total = total + far_in[tile].astype(jnp.float32)
        near_out[side, tile] = total.astype(jnp.bfloat16)
        near_copy(side, tile).start()

    def send_first(tile):
        send_far(tile)
        send_near(0 if tile >= HALF else 1, tile)

    project(ORDER[0])
    for earlier, tile in zip(ORDER, ORDER[1:]):
        project(tile)
        send_first(earlier)
    send_first(ORDER[-1])
    for tile in ORDER:
        send_near(0 if tile < HALF else 1, tile)
    for tile in ORDER:
        near_copy(0, tile).wait_recv()
        near_copy(1, tile).wait_recv()
        total = both(tile, 3) + (near_in[0, tile].astype(jnp.float32)
                                 + near_in[1, tile].astype(jnp.float32))
        result[:, tile * TILE:(tile + 1) * TILE] = total.astype(out.dtype)
        out_copy(tile).start()

    for r in range(2):
        for copy in own_copies(r):
            copy.wait_send()
    for copies in COPIES[2:]:
        for copy in copies:
            copy_of(*copy).wait_send()
    for tile in range(TILES):
        for part in range(2):
            sib_copy(tile, part).wait_send()
            near_copy(part, tile).wait_send()
        far_copy(tile).wait_send()
        out_copy(tile).wait()


def on_device(queries, keys, values, span_order, out_weight):
    rows, width = queries.shape
    heads = width // HEAD_DIM
    d_out = out_weight.shape[1]
    bf16, f32 = jnp.bfloat16, jnp.float32
    sem = pltpu.SemaphoreType.DMA
    span_order, queries, keys, values, out_weight = (
        pltpu.with_memory_space_constraint(array, pltpu.HBM)
        for array in (span_order, queries, keys, values, out_weight))
    return pl.pallas_call(
        kernel,
        out_shape=jax.ShapeDtypeStruct((rows // 8, d_out), bf16),
        in_specs=[pl.BlockSpec(memory_space=pltpu.HBM)] * 5,
        out_specs=pl.BlockSpec(memory_space=pl.ANY),
        scratch_shapes=[
            pltpu.VMEM((rows, width), bf16),
            pltpu.VMEM((SPANS, 2, SPAN, HEAD_DIM), bf16),
            pltpu.VMEM((width, d_out), bf16),
            pltpu.VMEM((heads, HEAD_DIM, rows), bf16),
            pltpu.VMEM((heads, HEAD_DIM + 16, rows), f32),
            pltpu.VMEM((heads, 1, rows), f32),
            pltpu.VMEM((rows, width), bf16),
            pltpu.VMEM((TILES, 4, 32, TILE), bf16),
            pltpu.VMEM((TILES, 4, 32, TILE), bf16),
            pltpu.VMEM((TILES, 4, 32, TILE), bf16),
            pltpu.VMEM((TILES, 32, TILE), bf16),
            pltpu.VMEM((TILES, 32, TILE), bf16),
            pltpu.VMEM((2, TILES, 32, TILE), bf16),
            pltpu.VMEM((2, TILES, 32, TILE), bf16),
            pltpu.VMEM((rows // 8, d_out), bf16),
            pltpu.SMEM((SPANS,), jnp.int32),
            pltpu.SMEM((SPANS,), jnp.int32),
            sem((13,)), sem((heads,)), sem((6, 2)), sem((6, 2)), sem((SPANS - 8,)), sem((SPANS - 8,)),
            sem((TILES, 2)), sem((TILES, 2)), sem((TILES,)), sem((TILES,)),
            sem((2, TILES)), sem((2, TILES)), sem((TILES,)),
        ],
        compiler_params=pltpu.CompilerParams(
            collective_id=0, has_side_effects=True, vmem_limit_bytes=32 * 1024 * 1024),
        cost_estimate=pl.CostEstimate(
            flops=3 * 2 * rows * width * 4096, bytes_accessed=10 * 2**20,
            transcendentals=heads * rows * 4096),
    )(span_order, queries, keys, values, out_weight)


def solution(mesh):
    return jax.shard_map(
        on_device,
        mesh=mesh,
        in_specs=(
            P(("dp", "context"), "tensor"),
            P(("dp", "context"), "tensor"),
            P(("dp", "context"), "tensor"),
            P("dp"),
            P("tensor", None),
        ),
        out_specs=P(("dp", "context", "tensor"), None),
        check_vma=False,
    )
```

```python
import math

import jax
import jax.numpy as jnp
from jax import lax
from jax.experimental import pallas as pl
from jax.experimental.pallas import tpu as pltpu
from jax.sharding import PartitionSpec as P

HEAD_DIM = 128
SPAN = 128
RING = 8
COLUMNS = 2
CHIPS = 4
ROUNDS = 10
TILE = 512
TILES = 8
HALF = TILES // 2
LOWEST = -1e30
MESH = pl.DeviceIdType.MESH

UP = [(0, 1, 0), (0, 1, 1), (0, 2, 0), (0, 2, 1), (0, 3, 0), (0, 3, 1),
      (1, 3, 0), (0, 4, 0), (1, 4, 0), (1, 3, 1)]
DOWN = [(0, -1, 1), (0, -1, 0), (0, -2, 1), (0, -2, 0), (0, -3, 1), (0, -3, 0),
        (0, -4, 1), (1, -3, 1), (1, -3, 0), (1, -4, 1)]
ACROSS = [(1, 0, 0), (1, 0, 1), (1, 1, 0), (1, -1, 1), (1, 2, 0), (1, -2, 1),
          (1, -2, 0), (1, 2, 1), (1, 1, 1), (1, -1, 0)]


def plan():
    slot_of = {(0, 0, 0): 0, (0, 0, 1): 1}
    contents = [(0, 0, 0), (0, 0, 1)]
    up_slot = {r: 2 + 3 * r for r in range(ROUNDS)}
    down_slot = {r: 3 + 3 * r for r in range(ROUNDS)}
    across_slot = {r: 4 + 3 * r for r in range(ROUNDS)}
    slots = {}
    for r in range(ROUNDS):
        for table, names in ((up_slot, UP), (down_slot, DOWN), (across_slot, ACROSS)):
            slots[table[r]] = names[r]
    for slot in range(2, 2 + 3 * ROUNDS):
        column, offset, half = slots[slot]
        key = (column, offset % RING, half)
        slot_of[key] = slot
        contents.append(key)
    assert len(slot_of) == 2 + 3 * ROUNDS
    copies = []
    for r in range(ROUNDS):
        (uc, uo, uh), (dc, do, dh), (ac, ao, ah) = UP[r], DOWN[r], ACROSS[r]
        copies.append((
            ("minus", slot_of[(uc, (uo - 1) % RING, uh)], up_slot[r]),
            ("plus", slot_of[(dc, (do + 1) % RING, dh)], down_slot[r]),
            ("other", slot_of[(0, ao % RING, ah)], across_slot[r]),
        ))
    return contents, copies


CONTENTS, COPIES = plan()
SPANS = len(CONTENTS)
ORDER = tuple(part * HALF + tile for tile in range(HALF) for part in range(2))


def kernel(order_hbm, q_hbm, k_hbm, v_hbm, w_hbm, out,
           q_in, kv, w, qt, acc, top, att, own, sib_out, sib_in,
           far_out, far_in, near_out, near_in, result, order, span_of,
           load_sem, own_send, own_recv, kv_send, kv_recv, sib_send, sib_recv,
           far_send, far_recv, near_send, near_recv, out_sem):
    heads = q_in.shape[1] // HEAD_DIM
    rows = q_in.shape[0]
    context = lax.axis_index("context")
    tensor = lax.axis_index("tensor")
    y, z = context // RING, lax.rem(context, RING)
    x, core = tensor // 2, lax.rem(tensor, 2)
    targets = {
        "minus": {"context": y * RING + lax.rem(z + RING - 1, RING)},
        "plus": {"context": y * RING + lax.rem(z + 1, RING)},
        "other": {"context": (1 - y) * RING + z},
    }
    sibling = {"tensor": x * 2 + 1 - core}
    chip_next, chip_back = lax.rem(x + 1, CHIPS), lax.rem(x + CHIPS - 1, CHIPS)
    chip_far = lax.rem(x + 2, CHIPS)
    to_next, to_back = {"tensor": chip_next * 2 + core}, {"tensor": chip_back * 2 + core}

    barrier = pltpu.get_barrier_semaphore()
    for target in (*targets.values(), sibling, to_next, to_back):
        pl.semaphore_signal(barrier, inc=1, device_id=target, device_id_type=MESH)

    loads = []
    for half in range(2):
        for part, source in enumerate((k_hbm, v_hbm)):
            loads.append(pltpu.make_async_copy(
                source.at[pl.ds(half * SPAN, SPAN)], kv.at[half, part],
                load_sem.at[2 * half + part]))
    chips = (chip_far, chip_next, chip_back, x)
    for group, chip in enumerate(chips):
        for part, owner in enumerate((core, 1 - core)):
            number = 2 * group + part
            first = pl.multiple_of(chip * 64 + owner * 32, 32)
            loads.append(pltpu.make_async_copy(
                q_hbm.at[pl.ds(first, 32)], q_in.at[pl.ds(32 * number, 32)],
                load_sem.at[4 + number]))
    loads.append(pltpu.make_async_copy(order_hbm, order, load_sem.at[13]))
    loads.append(pltpu.make_async_copy(w_hbm, w, load_sem.at[12]))
    for load in loads[:-1]:
        load.start()

    def own_copies(r):
        for name, src, dst in COPIES[r]:
            for part, source in enumerate((k_hbm, v_hbm)):
                yield pltpu.make_async_remote_copy(
                    src_ref=source.at[pl.ds(src * SPAN, SPAN)], dst_ref=kv.at[dst, part],
                    send_sem=own_send.at[dst - 2, part], recv_sem=own_recv.at[dst - 2, part],
                    device_id=targets[name], device_id_type=MESH)

    def copy_of(name, src, dst):
        return pltpu.make_async_remote_copy(
            src_ref=kv.at[src], dst_ref=kv.at[dst],
            send_sem=kv_send.at[dst - 8], recv_sem=kv_recv.at[dst - 8],
            device_id=targets[name], device_id_type=MESH)

    pl.semaphore_wait(barrier, 6)
    for copy in own_copies(0):
        copy.start()
    loads[-1].start()

    loads[12].wait()
    for slot, (column, offset, half) in enumerate(CONTENTS):
        where = (y if column == 0 else 1 - y) * RING + lax.rem(z + offset, RING)
        span_of[slot] = order[2 * where + half]

    for load in loads[4:12]:
        load.wait()
    for head in range(heads):
        qt[head] = q_in[:, head * HEAD_DIM:(head + 1) * HEAD_DIM].T

    for first, second in zip(own_copies(0), own_copies(1)):
        first.wait_send()
        second.start()
    for load in loads[:4]:
        load.wait()

    lane = lax.broadcasted_iota(jnp.int32, (1, rows), 1)
    group_of = lane // 64
    chip_of = jnp.where(group_of == 0, chip_far, jnp.where(
        group_of == 1, chip_next, jnp.where(group_of == 2, chip_back, x)))
    owner_of = jnp.where(lax.rem(lane // 32, 2) == 0, core, 1 - core)
    row_of = chip_of * 64 + owner_of * 32 + lax.rem(lane, 32)
    q_span = jnp.where(row_of < SPAN, span_of[0], span_of[1])
    q_pos = q_span * SPAN + lax.rem(row_of, SPAN)

    def operands(first, count):
        spans = kv[pl.ds(first, count)]
        keys = spans[:, 0].reshape(count * SPAN, HEAD_DIM)
        values = spans[:, 1].reshape(count * SPAN, HEAD_DIM).T
        ones = jnp.ones((16, count * SPAN), jnp.bfloat16)
        return keys, jnp.concatenate([values, ones], axis=0)

    scale = math.log2(math.e) / math.sqrt(HEAD_DIM)

    def scores_of(keys, head):
        return jnp.dot(keys, qt[head], preferred_element_type=jnp.float32)

    def receive(r):
        following = COPIES[r + 2] if r + 2 < ROUNDS else ()
        here = 2 + 3 * r
        for copy in following:
            if copy[1] < here:
                copy_of(*copy).start()
        first = list(own_copies(r)) if r < 2 else ()
        for number, copy in enumerate(COPIES[r]):
            if r < 2:
                first[2 * number].wait_recv()
                first[2 * number + 1].wait_recv()
            else:
                copy_of(*copy).wait_recv()
            for later in following:
                if later[1] == copy[2]:
                    copy_of(*later).start()

    keys, values = operands(0, 2)
    k_row = lax.broadcasted_iota(jnp.int32, (2 * SPAN, 1), 0)
    k_pos = jnp.where(k_row < SPAN, span_of[0], span_of[1]) * SPAN + lax.rem(k_row, SPAN)
    hide = jnp.where(k_pos <= q_pos, 0.0, LOWEST)
    following = scores_of(keys, 0)
    for head in range(heads):
        scores = following * scale + hide
        if head + 1 < heads:
            following = scores_of(keys, head + 1)
        new_top = jnp.max(scores, axis=0, keepdims=True)
        weights = jnp.exp2((scores - new_top).astype(jnp.bfloat16))
        top[head] = new_top
        acc[head] = jnp.dot(values, weights, preferred_element_type=jnp.float32)

    @pl.loop(0, ROUNDS)
    def _(step):
        for r in range(ROUNDS):
            @pl.when(step == r)
            def _():
                receive(r)

        first = 2 + 3 * step
        keys, values = operands(first, 3)
        hide = [jnp.where(span_of[first + number] < q_span, 0.0, LOWEST) for number in range(3)]
        following = scores_of(keys, 0)
        for head in range(heads):
            scores = [following[number * SPAN:(number + 1) * SPAN] for number in range(3)]
            if head + 1 < heads:
                following = scores_of(keys, head + 1)
            old_top = top[head]
            new_top = old_top
            for part, hidden in zip(scores, hide):
                new_top = jnp.maximum(new_top, jnp.max(part, axis=0, keepdims=True) * scale + hidden)
            factor = jnp.exp2(old_top - new_top)
            weights = jnp.concatenate([
                jnp.exp2((part * scale - (new_top - hidden)).astype(jnp.bfloat16))
                for part, hidden in zip(scores, hide)], axis=0)
            top[head] = new_top
            acc[head] = acc[head] * factor + jnp.dot(
                values, weights, preferred_element_type=jnp.float32)

    for head in range(heads):
        mixed = acc[head, :HEAD_DIM] * (1.0 / acc[head, HEAD_DIM:HEAD_DIM + 1])
        att[:, head * HEAD_DIM:(head + 1) * HEAD_DIM] = mixed.astype(jnp.bfloat16).T
    loads[13].wait()

    def sib_copy(tile, part):
        at = 0 if part == 0 else pl.ds(1, 3)
        return pltpu.make_async_remote_copy(
            src_ref=sib_out.at[tile, at], dst_ref=sib_in.at[tile, at],
            send_sem=sib_send.at[tile, part], recv_sem=sib_recv.at[tile, part],
            device_id=sibling, device_id_type=MESH)

    def project(tile):
        part = jnp.dot(att[...], w[:, tile * TILE:(tile + 1) * TILE],
                       preferred_element_type=jnp.float32).astype(jnp.bfloat16)
        part = part.reshape(4, 2, 32, TILE)
        sib_out[tile] = part[:, 1]
        sib_copy(tile, 0).start()
        sib_copy(tile, 1).start()
        own[tile] = part[:, 0]

    def both(tile, group):
        return own[tile, group].astype(jnp.float32) + sib_in[tile, group].astype(jnp.float32)

    def far_copy(tile):
        return pltpu.make_async_remote_copy(
            src_ref=far_out.at[tile], dst_ref=far_in.at[tile],
            send_sem=far_send.at[tile], recv_sem=far_recv.at[tile],
            device_id=to_next if tile < HALF else to_back, device_id_type=MESH)

    def near_copy(side, tile):
        return pltpu.make_async_remote_copy(
            src_ref=near_out.at[side, tile], dst_ref=near_in.at[side, tile],
            send_sem=near_send.at[side, tile], recv_sem=near_recv.at[side, tile],
            device_id=to_next if side == 0 else to_back, device_id_type=MESH)

    def out_copy(tile):
        at = pl.ds(tile * TILE, TILE)
        return pltpu.make_async_copy(result.at[:, at], out.at[:, at], out_sem.at[tile])

    def send_far(tile):
        sib_copy(tile, 0).wait_recv()
        far_out[tile] = both(tile, 0).astype(jnp.bfloat16)
        far_copy(tile).start()

    def send_near(side, tile):
        second = (tile < HALF) == (side == 0)
        if not second:
            sib_copy(tile, 1).wait_recv()
        total = both(tile, 1 + side)
        if second:
            far_copy(tile).wait_recv()
            total = total + far_in[tile].astype(jnp.float32)
        near_out[side, tile] = total.astype(jnp.bfloat16)
        near_copy(side, tile).start()

    def send_first(tile):
        send_far(tile)
        send_near(0 if tile >= HALF else 1, tile)

    project(ORDER[0])
    for earlier, tile in zip(ORDER, ORDER[1:]):
        project(tile)
        send_first(earlier)
    send_first(ORDER[-1])
    for tile in ORDER:
        send_near(0 if tile < HALF else 1, tile)
    for tile in ORDER:
        near_copy(0, tile).wait_recv()
        near_copy(1, tile).wait_recv()
        total = both(tile, 3) + (near_in[0, tile].astype(jnp.float32)
                                 + near_in[1, tile].astype(jnp.float32))
        result[:, tile * TILE:(tile + 1) * TILE] = total.astype(out.dtype)
        out_copy(tile).start()

    for copy in own_copies(1):
        copy.wait_send()
    for copies in COPIES[2:]:
        for copy in copies:
            copy_of(*copy).wait_send()
    for tile in range(TILES):
        for part in range(2):
            sib_copy(tile, part).wait_send()
            near_copy(part, tile).wait_send()
        far_copy(tile).wait_send()
        out_copy(tile).wait()


def on_device(queries, keys, values, span_order, out_weight):
    rows, width = queries.shape
    heads = width // HEAD_DIM
    d_out = out_weight.shape[1]
    bf16, f32 = jnp.bfloat16, jnp.float32
    sem = pltpu.SemaphoreType.DMA
    span_order, queries, keys, values, out_weight = (
        pltpu.with_memory_space_constraint(array, pltpu.HBM)
        for array in (span_order, queries, keys, values, out_weight))
    return pl.pallas_call(
        kernel,
        out_shape=jax.ShapeDtypeStruct((rows // 8, d_out), bf16),
        in_specs=[pl.BlockSpec(memory_space=pltpu.HBM)] * 5,
        out_specs=pl.BlockSpec(memory_space=pl.ANY),
        scratch_shapes=[
            pltpu.VMEM((rows, width), bf16),
            pltpu.VMEM((SPANS, 2, SPAN, HEAD_DIM), bf16),
            pltpu.VMEM((width, d_out), bf16),
            pltpu.VMEM((heads, HEAD_DIM, rows), bf16),
            pltpu.VMEM((heads, HEAD_DIM + 16, rows), f32),
            pltpu.VMEM((heads, 1, rows), f32),
            pltpu.VMEM((rows, width), bf16),
            pltpu.VMEM((TILES, 4, 32, TILE), bf16),
            pltpu.VMEM((TILES, 4, 32, TILE), bf16),
            pltpu.VMEM((TILES, 4, 32, TILE), bf16),
            pltpu.VMEM((TILES, 32, TILE), bf16),
            pltpu.VMEM((TILES, 32, TILE), bf16),
            pltpu.VMEM((2, TILES, 32, TILE), bf16),
            pltpu.VMEM((2, TILES, 32, TILE), bf16),
            pltpu.VMEM((rows // 8, d_out), bf16),
            pltpu.SMEM((SPANS,), jnp.int32),
            pltpu.SMEM((SPANS,), jnp.int32),
            sem((14,)), sem((6, 2)), sem((6, 2)), sem((SPANS - 8,)), sem((SPANS - 8,)),
            sem((TILES, 2)), sem((TILES, 2)), sem((TILES,)), sem((TILES,)),
            sem((2, TILES)), sem((2, TILES)), sem((TILES,)),
        ],
        compiler_params=pltpu.CompilerParams(
            collective_id=0, has_side_effects=True, vmem_limit_bytes=32 * 1024 * 1024),
        cost_estimate=pl.CostEstimate(
            flops=3 * 2 * rows * width * 4096, bytes_accessed=10 * 2**20,
            transcendentals=heads * rows * 4096),
    )(span_order, queries, keys, values, out_weight)


def solution(mesh):
    return jax.shard_map(
        on_device,
        mesh=mesh,
        in_specs=(
            P(("dp", "context"), "tensor"),
            P(("dp", "context"), "tensor"),
            P(("dp", "context"), "tensor"),
            P("dp"),
            P("tensor", None),
        ),
        out_specs=P(("dp", "context", "tensor"), None),
        check_vma=False,
    )
```

```python
import math

import jax
import jax.numpy as jnp
from jax import lax
from jax.experimental import pallas as pl
from jax.experimental.pallas import tpu as pltpu
from jax.sharding import PartitionSpec as P

HEAD_DIM = 128
SPAN = 128
RING = 8
COLUMNS = 2
CHIPS = 4
ROUNDS = 10
TILE = 512
TILES = 8
HALF = TILES // 2
LOWEST = -1e30
MESH = pl.DeviceIdType.MESH

UP = [(0, 1, 0), (0, 1, 1), (0, 2, 0), (0, 2, 1), (0, 3, 0), (0, 3, 1),
      (1, 3, 0), (0, 4, 0), (1, 4, 0), (1, 3, 1)]
DOWN = [(0, -1, 1), (0, -1, 0), (0, -2, 1), (0, -2, 0), (0, -3, 1), (0, -3, 0),
        (0, -4, 1), (1, -3, 1), (1, -3, 0), (1, -4, 1)]
ACROSS = [(1, 0, 0), (1, 0, 1), (1, 1, 0), (1, -1, 1), (1, 2, 0), (1, -2, 1),
          (1, -2, 0), (1, 2, 1), (1, 1, 1), (1, -1, 0)]


def plan():
    slot_of = {(0, 0, 0): 0, (0, 0, 1): 1}
    contents = [(0, 0, 0), (0, 0, 1)]
    up_slot = {r: 2 + 3 * r for r in range(ROUNDS)}
    down_slot = {r: 3 + 3 * r for r in range(ROUNDS)}
    across_slot = {r: 4 + 3 * r for r in range(ROUNDS)}
    slots = {}
    for r in range(ROUNDS):
        for table, names in ((up_slot, UP), (down_slot, DOWN), (across_slot, ACROSS)):
            slots[table[r]] = names[r]
    for slot in range(2, 2 + 3 * ROUNDS):
        column, offset, half = slots[slot]
        key = (column, offset % RING, half)
        slot_of[key] = slot
        contents.append(key)
    assert len(slot_of) == 2 + 3 * ROUNDS
    copies = []
    for r in range(ROUNDS):
        (uc, uo, uh), (dc, do, dh), (ac, ao, ah) = UP[r], DOWN[r], ACROSS[r]
        copies.append((
            ("minus", slot_of[(uc, (uo - 1) % RING, uh)], up_slot[r]),
            ("plus", slot_of[(dc, (do + 1) % RING, dh)], down_slot[r]),
            ("other", slot_of[(0, ao % RING, ah)], across_slot[r]),
        ))
    return contents, copies


CONTENTS, COPIES = plan()
SPANS = len(CONTENTS)
ORDER = tuple(part * HALF + tile for tile in range(HALF) for part in range(2))


def kernel(order_hbm, q_hbm, k_hbm, v_hbm, w_hbm, out,
           q_in, kv, w, qt, acc, top, att, own, sib_out, sib_in,
           far_out, far_in, near_out, near_in, result, order, span_of,
           load_sem, kv_send, kv_recv, sib_send, sib_recv,
           far_send, far_recv, near_send, near_recv, out_sem):
    heads = q_in.shape[1] // HEAD_DIM
    rows = q_in.shape[0]
    context = lax.axis_index("context")
    tensor = lax.axis_index("tensor")
    y, z = context // RING, lax.rem(context, RING)
    x, core = tensor // 2, lax.rem(tensor, 2)
    targets = {
        "minus": {"context": y * RING + lax.rem(z + RING - 1, RING)},
        "plus": {"context": y * RING + lax.rem(z + 1, RING)},
        "other": {"context": (1 - y) * RING + z},
    }
    sibling = {"tensor": x * 2 + 1 - core}
    chip_next, chip_back = lax.rem(x + 1, CHIPS), lax.rem(x + CHIPS - 1, CHIPS)
    chip_far = lax.rem(x + 2, CHIPS)
    to_next, to_back = {"tensor": chip_next * 2 + core}, {"tensor": chip_back * 2 + core}

    barrier = pltpu.get_barrier_semaphore()
    for target in (*targets.values(), sibling, to_next, to_back):
        pl.semaphore_signal(barrier, inc=1, device_id=target, device_id_type=MESH)

    loads = []
    for half in range(2):
        for part, source in enumerate((k_hbm, v_hbm)):
            loads.append(pltpu.make_async_copy(
                source.at[pl.ds(half * SPAN, SPAN)], kv.at[half, part],
                load_sem.at[2 * half + part]))
    chips = (chip_far, chip_next, chip_back, x)
    for group, chip in enumerate(chips):
        for part, owner in enumerate((core, 1 - core)):
            number = 2 * group + part
            first = pl.multiple_of(chip * 64 + owner * 32, 32)
            loads.append(pltpu.make_async_copy(
                q_hbm.at[pl.ds(first, 32)], q_in.at[pl.ds(32 * number, 32)],
                load_sem.at[4 + number]))
    loads.append(pltpu.make_async_copy(order_hbm, order, load_sem.at[13]))
    loads.append(pltpu.make_async_copy(w_hbm, w, load_sem.at[12]))
    for load in loads[:-1]:
        load.start()

    def copy_of(r, number, part):
        name, src, dst = COPIES[r][number]
        source = kv.at[src, part]
        if r < 2:
            source = (k_hbm, v_hbm)[part].at[pl.ds(src * SPAN, SPAN)]
        return pltpu.make_async_remote_copy(
            src_ref=source, dst_ref=kv.at[dst, part],
            send_sem=kv_send.at[dst - 2, part], recv_sem=kv_recv.at[dst - 2, part],
            device_id=targets[name], device_id_type=MESH)

    def send(r):
        for part in range(2):
            for number in range(3):
                copy_of(r, number, part).start()

    def receive(r, part):
        following = tuple(enumerate(COPIES[r + 2])) if r + 2 < ROUNDS else ()
        for number, copy in following:
            if copy[1] < 2 + 3 * r:
                copy_of(r + 2, number, part).start()
        for here, copy in enumerate(COPIES[r]):
            copy_of(r, here, part).wait_recv()
            for number, later in following:
                if later[1] == copy[2]:
                    copy_of(r + 2, number, part).start()

    pl.semaphore_wait(barrier, 6)
    send(0)
    loads[-1].start()

    loads[12].wait()
    for slot, (column, offset, half) in enumerate(CONTENTS):
        where = (y if column == 0 else 1 - y) * RING + lax.rem(z + offset, RING)
        span_of[slot] = order[2 * where + half]

    for load in loads[4:12]:
        load.wait()
    for head in range(heads):
        qt[head] = q_in[:, head * HEAD_DIM:(head + 1) * HEAD_DIM].T

    send(1)
    for load in loads[:4]:
        load.wait()

    lane = lax.broadcasted_iota(jnp.int32, (1, rows), 1)
    group_of = lane // 64
    chip_of = jnp.where(group_of == 0, chip_far, jnp.where(
        group_of == 1, chip_next, jnp.where(group_of == 2, chip_back, x)))
    owner_of = jnp.where(lax.rem(lane // 32, 2) == 0, core, 1 - core)
    row_of = chip_of * 64 + owner_of * 32 + lax.rem(lane, 32)
    q_span = jnp.where(row_of < SPAN, span_of[0], span_of[1])
    q_pos = q_span * SPAN + lax.rem(row_of, SPAN)

    def operands(first, count):
        spans = kv[pl.ds(first, count)]
        keys = spans[:, 0].reshape(count * SPAN, HEAD_DIM)
        values = spans[:, 1].reshape(count * SPAN, HEAD_DIM).T
        ones = jnp.ones((16, count * SPAN), jnp.bfloat16)
        return keys, jnp.concatenate([values, ones], axis=0)

    scale = math.log2(math.e) / math.sqrt(HEAD_DIM)

    def scores_of(keys, head):
        return jnp.dot(keys, qt[head], preferred_element_type=jnp.float32)

    keys, values = operands(0, 2)
    k_row = lax.broadcasted_iota(jnp.int32, (2 * SPAN, 1), 0)
    k_pos = jnp.where(k_row < SPAN, span_of[0], span_of[1]) * SPAN + lax.rem(k_row, SPAN)
    hide = jnp.where(k_pos <= q_pos, 0.0, LOWEST)
    following = scores_of(keys, 0)
    for head in range(heads):
        if head == heads // 2:
            receive(0, 0)
        scores = following * scale + hide
        if head + 1 < heads:
            following = scores_of(keys, head + 1)
        new_top = jnp.max(scores, axis=0, keepdims=True)
        weights = jnp.exp2(scores - new_top).astype(jnp.bfloat16)
        top[head] = new_top
        acc[head] = jnp.dot(values, weights, preferred_element_type=jnp.float32)

    @pl.loop(0, ROUNDS)
    def _(step):
        for r in range(ROUNDS):
            @pl.when(step == r)
            def _():
                receive(r, 1)

        first = 2 + 3 * step
        keys, values = operands(first, 3)
        hide = [jnp.where(span_of[first + number] < q_span, 0.0, LOWEST) for number in range(3)]
        following = scores_of(keys, 0)
        for head in range(heads):
            if head == heads // 2:
                for r in range(ROUNDS - 1):
                    @pl.when(step == r)
                    def _():
                        receive(r + 1, 0)
            scores = [following[number * SPAN:(number + 1) * SPAN] for number in range(3)]
            if head + 1 < heads:
                following = scores_of(keys, head + 1)
            old_top = top[head]
            new_top = old_top
            for part, hidden in zip(scores, hide):
                new_top = jnp.maximum(new_top, jnp.max(part, axis=0, keepdims=True) * scale + hidden)
            factor = jnp.exp2(old_top - new_top)
            weights = jnp.concatenate([
                jnp.exp2(part * scale - (new_top - hidden)).astype(jnp.bfloat16)
                for part, hidden in zip(scores, hide)], axis=0)
            top[head] = new_top
            acc[head] = acc[head] * factor + jnp.dot(
                values, weights, preferred_element_type=jnp.float32)

    for head in range(heads):
        mixed = acc[head, :HEAD_DIM] * (1.0 / acc[head, HEAD_DIM:HEAD_DIM + 1])
        att[:, head * HEAD_DIM:(head + 1) * HEAD_DIM] = mixed.astype(jnp.bfloat16).T
    loads[13].wait()

    def sib_copy(tile, part):
        at = 0 if part == 0 else pl.ds(1, 3)
        return pltpu.make_async_remote_copy(
            src_ref=sib_out.at[tile, at], dst_ref=sib_in.at[tile, at],
            send_sem=sib_send.at[tile, part], recv_sem=sib_recv.at[tile, part],
            device_id=sibling, device_id_type=MESH)

    def project(tile):
        part = jnp.dot(att[...], w[:, tile * TILE:(tile + 1) * TILE],
                       preferred_element_type=jnp.float32).astype(jnp.bfloat16)
        part = part.reshape(4, 2, 32, TILE)
        sib_out[tile] = part[:, 1]
        sib_copy(tile, 0).start()
        sib_copy(tile, 1).start()
        own[tile] = part[:, 0]

    def both(tile, group):
        return own[tile, group].astype(jnp.float32) + sib_in[tile, group].astype(jnp.float32)

    def far_copy(tile):
        return pltpu.make_async_remote_copy(
            src_ref=far_out.at[tile], dst_ref=far_in.at[tile],
            send_sem=far_send.at[tile], recv_sem=far_recv.at[tile],
            device_id=to_next if tile < HALF else to_back, device_id_type=MESH)

    def near_copy(side, tile):
        return pltpu.make_async_remote_copy(
            src_ref=near_out.at[side, tile], dst_ref=near_in.at[side, tile],
            send_sem=near_send.at[side, tile], recv_sem=near_recv.at[side, tile],
            device_id=to_next if side == 0 else to_back, device_id_type=MESH)

    def out_copy(tile):
        at = pl.ds(tile * TILE, TILE)
        return pltpu.make_async_copy(result.at[:, at], out.at[:, at], out_sem.at[tile])

    def send_far(tile):
        sib_copy(tile, 0).wait_recv()
        far_out[tile] = both(tile, 0).astype(jnp.bfloat16)
        far_copy(tile).start()

    def send_near(side, tile):
        second = (tile < HALF) == (side == 0)
        if not second:
            sib_copy(tile, 1).wait_recv()
        total = both(tile, 1 + side)
        if second:
            far_copy(tile).wait_recv()
            total = total + far_in[tile].astype(jnp.float32)
        near_out[side, tile] = total.astype(jnp.bfloat16)
        near_copy(side, tile).start()

    def send_first(tile):
        send_far(tile)
        send_near(0 if tile >= HALF else 1, tile)

    project(ORDER[0])
    for earlier, tile in zip(ORDER, ORDER[1:]):
        project(tile)
        send_first(earlier)
    send_first(ORDER[-1])
    for tile in ORDER:
        send_near(0 if tile < HALF else 1, tile)
    for tile in ORDER:
        near_copy(0, tile).wait_recv()
        near_copy(1, tile).wait_recv()
        total = both(tile, 3) + (near_in[0, tile].astype(jnp.float32)
                                 + near_in[1, tile].astype(jnp.float32))
        result[:, tile * TILE:(tile + 1) * TILE] = total.astype(out.dtype)
        out_copy(tile).start()

    for r in range(ROUNDS):
        for part in range(2):
            for number in range(3):
                copy_of(r, number, part).wait_send()
    for tile in range(TILES):
        for part in range(2):
            sib_copy(tile, part).wait_send()
            near_copy(part, tile).wait_send()
        far_copy(tile).wait_send()
        out_copy(tile).wait()


def on_device(queries, keys, values, span_order, out_weight):
    rows, width = queries.shape
    heads = width // HEAD_DIM
    d_out = out_weight.shape[1]
    bf16, f32 = jnp.bfloat16, jnp.float32
    sem = pltpu.SemaphoreType.DMA
    span_order, queries, keys, values, out_weight = (
        pltpu.with_memory_space_constraint(array, pltpu.HBM)
        for array in (span_order, queries, keys, values, out_weight))
    return pl.pallas_call(
        kernel,
        out_shape=jax.ShapeDtypeStruct((rows // 8, d_out), bf16),
        in_specs=[pl.BlockSpec(memory_space=pltpu.HBM)] * 5,
        out_specs=pl.BlockSpec(memory_space=pl.ANY),
        scratch_shapes=[
            pltpu.VMEM((rows, width), bf16),
            pltpu.VMEM((SPANS, 2, SPAN, HEAD_DIM), bf16),
            pltpu.VMEM((width, d_out), bf16),
            pltpu.VMEM((heads, HEAD_DIM, rows), bf16),
            pltpu.VMEM((heads, HEAD_DIM + 16, rows), f32),
            pltpu.VMEM((heads, 1, rows), f32),
            pltpu.VMEM((rows, width), bf16),
            pltpu.VMEM((TILES, 4, 32, TILE), bf16),
            pltpu.VMEM((TILES, 4, 32, TILE), bf16),
            pltpu.VMEM((TILES, 4, 32, TILE), bf16),
            pltpu.VMEM((TILES, 32, TILE), bf16),
            pltpu.VMEM((TILES, 32, TILE), bf16),
            pltpu.VMEM((2, TILES, 32, TILE), bf16),
            pltpu.VMEM((2, TILES, 32, TILE), bf16),
            pltpu.VMEM((rows // 8, d_out), bf16),
            pltpu.SMEM((SPANS,), jnp.int32),
            pltpu.SMEM((SPANS,), jnp.int32),
            sem((14,)), sem((SPANS - 2, 2)), sem((SPANS - 2, 2)),
            sem((TILES, 2)), sem((TILES, 2)), sem((TILES,)), sem((TILES,)),
            sem((2, TILES)), sem((2, TILES)), sem((TILES,)),
        ],
        compiler_params=pltpu.CompilerParams(
            collective_id=0, has_side_effects=True, vmem_limit_bytes=32 * 1024 * 1024),
        cost_estimate=pl.CostEstimate(
            flops=3 * 2 * rows * width * 4096, bytes_accessed=10 * 2**20,
            transcendentals=heads * rows * 4096),
    )(span_order, queries, keys, values, out_weight)


def solution(mesh):
    return jax.shard_map(
        on_device,
        mesh=mesh,
        in_specs=(
            P(("dp", "context"), "tensor"),
            P(("dp", "context"), "tensor"),
            P(("dp", "context"), "tensor"),
            P("dp"),
            P("tensor", None),
        ),
        out_specs=P(("dp", "context", "tensor"), None),
        check_vma=False,
    )
```

```python
import math

import jax
import jax.numpy as jnp
from jax import lax
from jax.experimental import pallas as pl
from jax.experimental.pallas import tpu as pltpu
from jax.sharding import PartitionSpec as P

HEAD_DIM = 128
SPAN = 128
RING = 8
COLUMNS = 2
CHIPS = 4
ROUNDS = 10
TILE = 512
TILES = 8
HALF = TILES // 2
LOWEST = -1e30
BLOCK = 512
PAIRS = 4
MESH = pl.DeviceIdType.MESH

UP = [(0, 1, 0), (0, 1, 1), (0, 2, 0), (0, 2, 1), (0, 3, 0), (0, 3, 1),
      (1, 3, 0), (0, 4, 0), (1, 4, 0), (1, 3, 1)]
DOWN = [(0, -1, 1), (0, -1, 0), (0, -2, 1), (0, -2, 0), (0, -3, 1), (0, -3, 0),
        (0, -4, 1), (1, -3, 1), (1, -3, 0), (1, -4, 1)]
ACROSS = [(1, 0, 0), (1, 0, 1), (1, 1, 0), (1, -1, 1), (1, 2, 0), (1, -2, 1),
          (1, -2, 0), (1, 2, 1), (1, 1, 1), (1, -1, 0)]


def plan():
    slot_of = {(0, 0, 0): 0, (0, 0, 1): 1}
    contents = [(0, 0, 0), (0, 0, 1)]
    up_slot = {r: 2 + 3 * r for r in range(ROUNDS)}
    down_slot = {r: 3 + 3 * r for r in range(ROUNDS)}
    across_slot = {r: 4 + 3 * r for r in range(ROUNDS)}
    slots = {}
    for r in range(ROUNDS):
        for table, names in ((up_slot, UP), (down_slot, DOWN), (across_slot, ACROSS)):
            slots[table[r]] = names[r]
    for slot in range(2, 2 + 3 * ROUNDS):
        column, offset, half = slots[slot]
        key = (column, offset % RING, half)
        slot_of[key] = slot
        contents.append(key)
    assert len(slot_of) == 2 + 3 * ROUNDS
    copies = []
    for r in range(ROUNDS):
        (uc, uo, uh), (dc, do, dh), (ac, ao, ah) = UP[r], DOWN[r], ACROSS[r]
        copies.append((
            ("minus", slot_of[(uc, (uo - 1) % RING, uh)], up_slot[r]),
            ("plus", slot_of[(dc, (do + 1) % RING, dh)], down_slot[r]),
            ("other", slot_of[(0, ao % RING, ah)], across_slot[r]),
        ))
    return contents, copies


CONTENTS, COPIES = plan()
SPANS = len(CONTENTS)
ORDER = tuple(part * HALF + tile for tile in range(HALF) for part in range(2))


def kernel(order_hbm, q_hbm, k_hbm, v_hbm, w_hbm, out,
           q_in, kv, w, q_all, acc, top, att, own, sib_out, sib_in,
           far_out, far_in, near_out, near_in, result, order, span_of,
           load_sem, own_send, own_recv, kv_send, kv_recv, sib_send, sib_recv,
           far_send, far_recv, near_send, near_recv, out_sem):
    heads = q_in.shape[1] // HEAD_DIM
    rows = q_in.shape[0]
    context = lax.axis_index("context")
    tensor = lax.axis_index("tensor")
    y, z = context // RING, lax.rem(context, RING)
    x, core = tensor // 2, lax.rem(tensor, 2)
    targets = {
        "minus": {"context": y * RING + lax.rem(z + RING - 1, RING)},
        "plus": {"context": y * RING + lax.rem(z + 1, RING)},
        "other": {"context": (1 - y) * RING + z},
    }
    sibling = {"tensor": x * 2 + 1 - core}
    chip_next, chip_back = lax.rem(x + 1, CHIPS), lax.rem(x + CHIPS - 1, CHIPS)
    chip_far = lax.rem(x + 2, CHIPS)
    to_next, to_back = {"tensor": chip_next * 2 + core}, {"tensor": chip_back * 2 + core}

    barrier = pltpu.get_barrier_semaphore()
    for target in (*targets.values(), sibling, to_next, to_back):
        pl.semaphore_signal(barrier, inc=1, device_id=target, device_id_type=MESH)

    loads = []
    for half in range(2):
        for part, source in enumerate((k_hbm, v_hbm)):
            loads.append(pltpu.make_async_copy(
                source.at[pl.ds(half * SPAN, SPAN)], kv.at[half, part],
                load_sem.at[2 * half + part]))
    chips = (chip_far, chip_next, chip_back, x)
    for group, chip in enumerate(chips):
        for part, owner in enumerate((core, 1 - core)):
            number = 2 * group + part
            first = pl.multiple_of(chip * 64 + owner * 32, 32)
            loads.append(pltpu.make_async_copy(
                q_hbm.at[pl.ds(first, 32)], q_in.at[pl.ds(32 * number, 32)],
                load_sem.at[4 + number]))
    loads.append(pltpu.make_async_copy(order_hbm, order, load_sem.at[13]))
    loads.append(pltpu.make_async_copy(w_hbm, w, load_sem.at[12]))
    for load in loads[:-1]:
        load.start()

    def own_copies(r):
        for name, src, dst in COPIES[r]:
            for part, source in enumerate((k_hbm, v_hbm)):
                yield pltpu.make_async_remote_copy(
                    src_ref=source.at[pl.ds(src * SPAN, SPAN)], dst_ref=kv.at[dst, part],
                    send_sem=own_send.at[dst - 2, part], recv_sem=own_recv.at[dst - 2, part],
                    device_id=targets[name], device_id_type=MESH)

    def copy_of(name, src, dst):
        return pltpu.make_async_remote_copy(
            src_ref=kv.at[src], dst_ref=kv.at[dst],
            send_sem=kv_send.at[dst - 8], recv_sem=kv_recv.at[dst - 8],
            device_id=targets[name], device_id_type=MESH)

    pl.semaphore_wait(barrier, 6)
    for copy in own_copies(0):
        copy.start()
    loads[-1].start()

    loads[12].wait()
    for slot, (column, offset, half) in enumerate(CONTENTS):
        where = (y if column == 0 else 1 - y) * RING + lax.rem(z + offset, RING)
        span_of[slot] = order[2 * where + half]

    for load in loads[4:12]:
        load.wait()
    for head in range(heads):
        q_all[head * rows:(head + 1) * rows] = q_in[:, head * HEAD_DIM:(head + 1) * HEAD_DIM]

    for first, second in zip(own_copies(0), own_copies(1)):
        first.wait_send()
        second.start()
    for load in loads[:4]:
        load.wait()

    number = lax.broadcasted_iota(jnp.int32, (rows, HEAD_DIM), 0)
    group_of = number // 64
    chip_of = jnp.where(group_of == 0, chip_far, jnp.where(
        group_of == 1, chip_next, jnp.where(group_of == 2, chip_back, x)))
    owner_of = jnp.where(lax.rem(number // 32, 2) == 0, core, 1 - core)
    row_of = chip_of * 64 + owner_of * 32 + lax.rem(number, 32)
    q_span = jnp.where(row_of < SPAN, span_of[0], span_of[1])
    q_row = lax.rem(row_of, SPAN)

    scale = math.log2(math.e) / math.sqrt(HEAD_DIM)

    def attend(first, count, hide, halfway=None):
        spans = kv[pl.ds(first, count)]
        keys = spans[:, 0].reshape(count * SPAN, HEAD_DIM).T
        values = spans[:, 1].reshape(count * SPAN, HEAD_DIM)
        values = jnp.concatenate([values, jnp.ones_like(values)], axis=1)
        fresh = halfway is None and count == 2

        def scores_of(block):
            return jnp.dot(q_all[block * BLOCK:(block + 1) * BLOCK], keys,
                           preferred_element_type=jnp.float32)

        blocks = heads * rows // BLOCK
        following = scores_of(0)
        for block in range(blocks):
            if block == blocks // 2 and halfway is not None:
                halfway()
            scores = following
            if block + 1 < blocks:
                following = scores_of(block + 1)
            parts = []
            for span in range(count):
                part = scores[:, span * SPAN:(span + 1) * SPAN].reshape(-1, rows, SPAN)
                parts.append((part * scale + hide[span][None]).reshape(BLOCK, SPAN))
            highest = parts[0]
            for part in parts[1:]:
                highest = jnp.maximum(highest, part)
            highest = jnp.max(highest, axis=1, keepdims=True)
            at = slice(block * BLOCK, (block + 1) * BLOCK)
            new_top = jnp.broadcast_to(highest, (BLOCK, SPAN))
            if not fresh:
                old_top = top[at]
                new_top = jnp.maximum(old_top, new_top)
            weights = jnp.concatenate(
                [jnp.exp2(part - new_top).astype(jnp.bfloat16) for part in parts], axis=1)
            mixed = jnp.dot(weights, values, preferred_element_type=jnp.float32)
            top[at] = new_top
            if not fresh:
                factor = jnp.exp2(old_top - new_top)
                mixed = acc[at] * jnp.concatenate([factor, factor], axis=1) + mixed
            acc[at] = mixed

    def receive(r):
        following = COPIES[r + 2] if r + 2 < ROUNDS else ()
        here = 2 + 3 * r
        for copy in following:
            if copy[1] < here:
                copy_of(*copy).start()
        first = list(own_copies(r)) if r < 2 else ()
        for number, copy in enumerate(COPIES[r]):
            if r < 2:
                first[2 * number].wait_recv()
                first[2 * number + 1].wait_recv()
            else:
                copy_of(*copy).wait_recv()
            for later in following:
                if later[1] == copy[2]:
                    copy_of(*later).start()

    k_row = lax.broadcasted_iota(jnp.int32, (rows, SPAN), 1)
    q_pos = q_span * SPAN + q_row
    attend(0, 2, [jnp.where(span_of[half] * SPAN + k_row <= q_pos, 0.0, LOWEST)
                  for half in range(2)])

    def hidden(first, count):
        return [jnp.where(span_of[first + span] < q_span, 0.0, LOWEST) for span in range(count)]

    receive(0)

    @pl.loop(0, PAIRS)
    def _(step):
        def receive_at(offset):
            for number in range(PAIRS):
                @pl.when(step == number)
                def _():
                    receive(2 * number + offset)

        receive_at(1)
        first = 2 + 6 * step
        attend(first, 6, hidden(first, 6), lambda: receive_at(2))

    for r in range(2 * PAIRS, ROUNDS):
        if r > 2 * PAIRS:
            receive(r)
        attend(2 + 3 * r, 3, hidden(2 + 3 * r, 3))

    for head in range(heads):
        at = slice(head * rows, (head + 1) * rows)
        att[:, head * HEAD_DIM:(head + 1) * HEAD_DIM] = (
            acc[at, :HEAD_DIM] * (1.0 / acc[at, HEAD_DIM:])).astype(jnp.bfloat16)
    loads[13].wait()

    def sib_copy(tile, part):
        at = 0 if part == 0 else pl.ds(1, 3)
        return pltpu.make_async_remote_copy(
            src_ref=sib_out.at[tile, at], dst_ref=sib_in.at[tile, at],
            send_sem=sib_send.at[tile, part], recv_sem=sib_recv.at[tile, part],
            device_id=sibling, device_id_type=MESH)

    def project(tile):
        part = jnp.dot(att[...], w[:, tile * TILE:(tile + 1) * TILE],
                       preferred_element_type=jnp.float32).astype(jnp.bfloat16)
        part = part.reshape(4, 2, 32, TILE)
        sib_out[tile] = part[:, 1]
        sib_copy(tile, 0).start()
        sib_copy(tile, 1).start()
        own[tile] = part[:, 0]

    def both(tile, group):
        return own[tile, group].astype(jnp.float32) + sib_in[tile, group].astype(jnp.float32)

    def far_copy(tile):
        return pltpu.make_async_remote_copy(
            src_ref=far_out.at[tile], dst_ref=far_in.at[tile],
            send_sem=far_send.at[tile], recv_sem=far_recv.at[tile],
            device_id=to_next if tile < HALF else to_back, device_id_type=MESH)

    def near_copy(side, tile):
        return pltpu.make_async_remote_copy(
            src_ref=near_out.at[side, tile], dst_ref=near_in.at[side, tile],
            send_sem=near_send.at[side, tile], recv_sem=near_recv.at[side, tile],
            device_id=to_next if side == 0 else to_back, device_id_type=MESH)

    def out_copy(tile):
        at = pl.ds(tile * TILE, TILE)
        return pltpu.make_async_copy(result.at[:, at], out.at[:, at], out_sem.at[tile])

    def send_far(tile):
        sib_copy(tile, 0).wait_recv()
        far_out[tile] = both(tile, 0).astype(jnp.bfloat16)
        far_copy(tile).start()

    def send_near(side, tile):
        second = (tile < HALF) == (side == 0)
        if not second:
            sib_copy(tile, 1).wait_recv()
        total = both(tile, 1 + side)
        if second:
            far_copy(tile).wait_recv()
            total = total + far_in[tile].astype(jnp.float32)
        near_out[side, tile] = total.astype(jnp.bfloat16)
        near_copy(side, tile).start()

    def send_first(tile):
        send_far(tile)
        send_near(0 if tile >= HALF else 1, tile)

    project(ORDER[0])
    for earlier, tile in zip(ORDER, ORDER[1:]):
        project(tile)
        send_first(earlier)
    send_first(ORDER[-1])
    for tile in ORDER:
        send_near(0 if tile < HALF else 1, tile)
    for tile in ORDER:
        near_copy(0, tile).wait_recv()
        near_copy(1, tile).wait_recv()
        total = both(tile, 3) + (near_in[0, tile].astype(jnp.float32)
                                 + near_in[1, tile].astype(jnp.float32))
        result[:, tile * TILE:(tile + 1) * TILE] = total.astype(out.dtype)
        out_copy(tile).start()

    for copy in own_copies(1):
        copy.wait_send()
    for copies in COPIES[2:]:
        for copy in copies:
            copy_of(*copy).wait_send()
    for tile in range(TILES):
        for part in range(2):
            sib_copy(tile, part).wait_send()
            near_copy(part, tile).wait_send()
        far_copy(tile).wait_send()
        out_copy(tile).wait()


def on_device(queries, keys, values, span_order, out_weight):
    rows, width = queries.shape
    heads = width // HEAD_DIM
    d_out = out_weight.shape[1]
    bf16, f32 = jnp.bfloat16, jnp.float32
    sem = pltpu.SemaphoreType.DMA
    span_order, queries, keys, values, out_weight = (
        pltpu.with_memory_space_constraint(array, pltpu.HBM)
        for array in (span_order, queries, keys, values, out_weight))
    return pl.pallas_call(
        kernel,
        out_shape=jax.ShapeDtypeStruct((rows // 8, d_out), bf16),
        in_specs=[pl.BlockSpec(memory_space=pltpu.HBM)] * 5,
        out_specs=pl.BlockSpec(memory_space=pl.ANY),
        scratch_shapes=[
            pltpu.VMEM((rows, width), bf16),
            pltpu.VMEM((SPANS, 2, SPAN, HEAD_DIM), bf16),
            pltpu.VMEM((width, d_out), bf16),
            pltpu.VMEM((heads * rows, HEAD_DIM), bf16),
            pltpu.VMEM((heads * rows, 2 * HEAD_DIM), f32),
            pltpu.VMEM((heads * rows, HEAD_DIM), f32),
            pltpu.VMEM((rows, width), bf16),
            pltpu.VMEM((TILES, 4, 32, TILE), bf16),
            pltpu.VMEM((TILES, 4, 32, TILE), bf16),
            pltpu.VMEM((TILES, 4, 32, TILE), bf16),
            pltpu.VMEM((TILES, 32, TILE), bf16),
            pltpu.VMEM((TILES, 32, TILE), bf16),
            pltpu.VMEM((2, TILES, 32, TILE), bf16),
            pltpu.VMEM((2, TILES, 32, TILE), bf16),
            pltpu.VMEM((rows // 8, d_out), bf16),
            pltpu.SMEM((SPANS,), jnp.int32),
            pltpu.SMEM((SPANS,), jnp.int32),
            sem((14,)), sem((6, 2)), sem((6, 2)), sem((SPANS - 8,)), sem((SPANS - 8,)),
            sem((TILES, 2)), sem((TILES, 2)), sem((TILES,)), sem((TILES,)),
            sem((2, TILES)), sem((2, TILES)), sem((TILES,)),
        ],
        compiler_params=pltpu.CompilerParams(
            collective_id=0, has_side_effects=True, vmem_limit_bytes=40 * 1024 * 1024),
        cost_estimate=pl.CostEstimate(
            flops=3 * 2 * rows * width * 4096, bytes_accessed=10 * 2**20,
            transcendentals=heads * rows * 4096),
    )(span_order, queries, keys, values, out_weight)


def solution(mesh):
    return jax.shard_map(
        on_device,
        mesh=mesh,
        in_specs=(
            P(("dp", "context"), "tensor"),
            P(("dp", "context"), "tensor"),
            P(("dp", "context"), "tensor"),
            P("dp"),
            P("tensor", None),
        ),
        out_specs=P(("dp", "context", "tensor"), None),
        check_vma=False,
    )
```

```python
import math

import jax
import jax.numpy as jnp
from jax import lax
from jax.experimental import pallas as pl
from jax.experimental.pallas import tpu as pltpu
from jax.sharding import PartitionSpec as P

HEAD_DIM = 128
SPAN = 128
RING = 8
COLUMNS = 2
CHIPS = 4
ROUNDS = 10
TILE = 512
TILES = 8
LOWEST = -1e30
MESH = pl.DeviceIdType.MESH

UP = [(0, 1, 0), (0, 1, 1), (0, 2, 0), (0, 2, 1), (0, 3, 0), (0, 3, 1),
      (1, 3, 0), (0, 4, 0), (1, 4, 0), (1, 3, 1)]
DOWN = [(0, -1, 1), (0, -1, 0), (0, -2, 1), (0, -2, 0), (0, -3, 1), (0, -3, 0),
        (0, -4, 1), (1, -3, 1), (1, -3, 0), (1, -4, 1)]
ACROSS = [(1, 0, 0), (1, 0, 1), (1, 1, 0), (1, -1, 1), (1, 2, 0), (1, -2, 1),
          (1, -2, 0), (1, 2, 1), (1, 1, 1), (1, -1, 0)]


def plan():
    slot_of = {(0, 0, 0): 0, (0, 0, 1): 1}
    contents = [(0, 0, 0), (0, 0, 1)]
    up_slot = {r: 2 + 3 * r for r in range(ROUNDS)}
    down_slot = {r: 3 + 3 * r for r in range(ROUNDS)}
    across_slot = {r: 4 + 3 * r for r in range(ROUNDS)}
    slots = {}
    for r in range(ROUNDS):
        for table, names in ((up_slot, UP), (down_slot, DOWN), (across_slot, ACROSS)):
            slots[table[r]] = names[r]
    for slot in range(2, 2 + 3 * ROUNDS):
        column, offset, half = slots[slot]
        key = (column, offset % RING, half)
        slot_of[key] = slot
        contents.append(key)
    assert len(slot_of) == 2 + 3 * ROUNDS
    copies = []
    for r in range(ROUNDS):
        (uc, uo, uh), (dc, do, dh), (ac, ao, ah) = UP[r], DOWN[r], ACROSS[r]
        copies.append((
            ("minus", slot_of[(uc, (uo - 1) % RING, uh)], up_slot[r]),
            ("plus", slot_of[(dc, (do + 1) % RING, dh)], down_slot[r]),
            ("other", slot_of[(0, ao % RING, ah)], across_slot[r]),
        ))
    return contents, copies


CONTENTS, COPIES = plan()
SPANS = len(CONTENTS)
GROUPS = ((0, 1), (4, 1), (1, 1), (5, 1), (2, 2), (6, 2))


def kernel(order_hbm, q_hbm, k_hbm, v_hbm, w_hbm, out,
           q_in, kv, w, qt, acc, top, att, own, sib_out, sib_in,
           far_out, far_in, near_out, near_in, result, order, span_of,
           load_sem, own_send, own_recv, kv_send, kv_recv, sib_send, sib_recv,
           far_send, far_recv, near_send, near_recv, out_sem):
    heads = q_in.shape[1] // HEAD_DIM
    rows = q_in.shape[0]
    context = lax.axis_index("context")
    tensor = lax.axis_index("tensor")
    y, z = context // RING, lax.rem(context, RING)
    x, core = tensor // 2, lax.rem(tensor, 2)
    targets = {
        "minus": {"context": y * RING + lax.rem(z + RING - 1, RING)},
        "plus": {"context": y * RING + lax.rem(z + 1, RING)},
        "other": {"context": (1 - y) * RING + z},
    }
    sibling = {"tensor": x * 2 + 1 - core}
    chip_next, chip_back = lax.rem(x + 1, CHIPS), lax.rem(x + CHIPS - 1, CHIPS)
    chip_far = lax.rem(x + 2, CHIPS)
    to_next, to_back = {"tensor": chip_next * 2 + core}, {"tensor": chip_back * 2 + core}

    barrier = pltpu.get_barrier_semaphore()
    for target in (*targets.values(), sibling, to_next, to_back):
        pl.semaphore_signal(barrier, inc=1, device_id=target, device_id_type=MESH)

    loads = []
    for half in range(2):
        for part, source in enumerate((k_hbm, v_hbm)):
            loads.append(pltpu.make_async_copy(
                source.at[pl.ds(half * SPAN, SPAN)], kv.at[half, part],
                load_sem.at[2 * half + part]))
    chips = (chip_far, chip_next, chip_back, x)
    for group, chip in enumerate(chips):
        for part, owner in enumerate((core, 1 - core)):
            number = 2 * group + part
            first = pl.multiple_of(chip * 64 + owner * 32, 32)
            loads.append(pltpu.make_async_copy(
                q_hbm.at[pl.ds(first, 32)], q_in.at[pl.ds(32 * number, 32)],
                load_sem.at[4 + number]))
    loads.append(pltpu.make_async_copy(order_hbm, order, load_sem.at[13]))
    loads.append(pltpu.make_async_copy(w_hbm, w, load_sem.at[12]))
    for load in loads[:-1]:
        load.start()

    def own_copies(r):
        for name, src, dst in COPIES[r]:
            for part, source in enumerate((k_hbm, v_hbm)):
                yield pltpu.make_async_remote_copy(
                    src_ref=source.at[pl.ds(src * SPAN, SPAN)], dst_ref=kv.at[dst, part],
                    send_sem=own_send.at[dst - 2, part], recv_sem=own_recv.at[dst - 2, part],
                    device_id=targets[name], device_id_type=MESH)

    def copy_of(name, src, dst):
        return pltpu.make_async_remote_copy(
            src_ref=kv.at[src], dst_ref=kv.at[dst],
            send_sem=kv_send.at[dst - 8], recv_sem=kv_recv.at[dst - 8],
            device_id=targets[name], device_id_type=MESH)

    pl.semaphore_wait(barrier, 6)
    for copy in own_copies(0):
        copy.start()
    loads[-1].start()

    loads[12].wait()
    for slot, (column, offset, half) in enumerate(CONTENTS):
        where = (y if column == 0 else 1 - y) * RING + lax.rem(z + offset, RING)
        span_of[slot] = order[2 * where + half]

    for load in loads[4:12]:
        load.wait()
    for head in range(heads):
        qt[head] = q_in[:, head * HEAD_DIM:(head + 1) * HEAD_DIM].T

    for first, second in zip(own_copies(0), own_copies(1)):
        first.wait_send()
        second.start()
    for load in loads[:4]:
        load.wait()

    lane = lax.broadcasted_iota(jnp.int32, (1, rows), 1)
    group_of = lane // 64
    chip_of = jnp.where(group_of == 0, chip_far, jnp.where(
        group_of == 1, chip_next, jnp.where(group_of == 2, chip_back, x)))
    owner_of = jnp.where(lax.rem(lane // 32, 2) == 0, core, 1 - core)
    row_of = chip_of * 64 + owner_of * 32 + lax.rem(lane, 32)
    q_span = jnp.where(row_of < SPAN, span_of[0], span_of[1])
    q_pos = q_span * SPAN + lax.rem(row_of, SPAN)

    def operands(first, count):
        spans = kv[pl.ds(first, count)]
        keys = spans[:, 0].reshape(count * SPAN, HEAD_DIM)
        values = spans[:, 1].reshape(count * SPAN, HEAD_DIM).T
        ones = jnp.ones((16, count * SPAN), jnp.bfloat16)
        return keys, jnp.concatenate([values, ones], axis=0)

    scale = math.log2(math.e) / math.sqrt(HEAD_DIM)

    def scores_of(keys, head):
        return jnp.dot(keys, qt[head], preferred_element_type=jnp.float32)

    def receive(r):
        following = COPIES[r + 2] if r + 2 < ROUNDS else ()
        here = 2 + 3 * r
        for copy in following:
            if copy[1] < here:
                copy_of(*copy).start()
        first = list(own_copies(r)) if r < 2 else ()
        for number, copy in enumerate(COPIES[r]):
            if r < 2:
                first[2 * number].wait_recv()
                first[2 * number + 1].wait_recv()
            else:
                copy_of(*copy).wait_recv()
            for later in following:
                if later[1] == copy[2]:
                    copy_of(*later).start()

    keys, values = operands(0, 2)
    k_row = lax.broadcasted_iota(jnp.int32, (2 * SPAN, 1), 0)
    k_pos = jnp.where(k_row < SPAN, span_of[0], span_of[1]) * SPAN + lax.rem(k_row, SPAN)
    hide = jnp.where(k_pos <= q_pos, 0.0, LOWEST)
    following = scores_of(keys, 0)
    for head in range(heads):
        scores = following * scale + hide
        if head + 1 < heads:
            following = scores_of(keys, head + 1)
        new_top = jnp.max(scores, axis=0, keepdims=True)
        weights = jnp.exp2(scores - new_top).astype(jnp.bfloat16)
        top[head] = new_top
        acc[head] = jnp.dot(values, weights, preferred_element_type=jnp.float32)

    @pl.loop(0, ROUNDS)
    def _(step):
        for r in range(ROUNDS):
            @pl.when(step == r)
            def _():
                receive(r)

        first = 2 + 3 * step
        keys, values = operands(first, 3)
        hide = [jnp.where(span_of[first + number] < q_span, 0.0, LOWEST) for number in range(3)]
        following = scores_of(keys, 0)
        for head in range(heads):
            scores = [following[number * SPAN:(number + 1) * SPAN] for number in range(3)]
            if head + 1 < heads:
                following = scores_of(keys, head + 1)
            old_top = top[head]
            new_top = old_top
            for part, hidden in zip(scores, hide):
                new_top = jnp.maximum(new_top, jnp.max(part, axis=0, keepdims=True) * scale + hidden)
            factor = jnp.exp2(old_top - new_top)
            weights = jnp.concatenate([
                jnp.exp2(part * scale - (new_top - hidden)).astype(jnp.bfloat16)
                for part, hidden in zip(scores, hide)], axis=0)
            top[head] = new_top
            acc[head] = acc[head] * factor + jnp.dot(
                values, weights, preferred_element_type=jnp.float32)

    for head in range(heads):
        mixed = acc[head, :HEAD_DIM] * (1.0 / acc[head, HEAD_DIM:HEAD_DIM + 1])
        att[:, head * HEAD_DIM:(head + 1) * HEAD_DIM] = mixed.astype(jnp.bfloat16).T
    loads[13].wait()

    def sib_copy(group):
        at = pl.ds(*GROUPS[group])
        return pltpu.make_async_remote_copy(
            src_ref=sib_out.at[at], dst_ref=sib_in.at[at],
            send_sem=sib_send.at[group], recv_sem=sib_recv.at[group],
            device_id=sibling, device_id_type=MESH)

    def tiles_of(group):
        first, count = GROUPS[group]
        return range(first, first + count)

    def project(group):
        for tile in tiles_of(group):
            part = jnp.dot(att[...], w[:, tile * TILE:(tile + 1) * TILE],
                           preferred_element_type=jnp.float32).astype(jnp.bfloat16)
            part = part.reshape(4, 2, 32, TILE)
            sib_out[tile] = part[:, 1]
            own[tile] = part[:, 0]
        sib_copy(group).start()

    def both(tile, owner):
        return own[tile, owner].astype(jnp.float32) + sib_in[tile, owner].astype(jnp.float32)

    def far_copy(group):
        at = pl.ds(*GROUPS[group])
        return pltpu.make_async_remote_copy(
            src_ref=far_out.at[at], dst_ref=far_in.at[at],
            send_sem=far_send.at[group], recv_sem=far_recv.at[group],
            device_id=to_next if group % 2 == 0 else to_back, device_id_type=MESH)

    def near_copy(side, group):
        at = pl.ds(*GROUPS[group])
        return pltpu.make_async_remote_copy(
            src_ref=near_out.at[side, at], dst_ref=near_in.at[side, at],
            send_sem=near_send.at[side, group], recv_sem=near_recv.at[side, group],
            device_id=to_next if side == 0 else to_back, device_id_type=MESH)

    def out_copy(tile):
        at = pl.ds(tile * TILE, TILE)
        return pltpu.make_async_copy(result.at[:, at], out.at[:, at], out_sem.at[tile])

    def send_first(group):
        sib_copy(group).wait_recv()
        side = 1 - group % 2
        for tile in tiles_of(group):
            far_out[tile] = both(tile, 0).astype(jnp.bfloat16)
        far_copy(group).start()
        for tile in tiles_of(group):
            near_out[side, tile] = both(tile, 1 + side).astype(jnp.bfloat16)
        near_copy(side, group).start()

    def send_second(group):
        side = group % 2
        far_copy(group).wait_recv()
        for tile in tiles_of(group):
            total = both(tile, 1 + side) + far_in[tile].astype(jnp.float32)
            near_out[side, tile] = total.astype(jnp.bfloat16)
        near_copy(side, group).start()

    count = len(GROUPS)
    project(0)
    for group in range(1, count):
        project(group)
        send_first(group - 1)
    send_first(count - 1)
    for group in range(count):
        send_second(group)
    for group in range(count):
        near_copy(0, group).wait_recv()
        near_copy(1, group).wait_recv()
        for tile in tiles_of(group):
            total = both(tile, 3) + (near_in[0, tile].astype(jnp.float32)
                                     + near_in[1, tile].astype(jnp.float32))
            result[:, tile * TILE:(tile + 1) * TILE] = total.astype(out.dtype)
            out_copy(tile).start()

    for copy in own_copies(1):
        copy.wait_send()
    for copies in COPIES[2:]:
        for copy in copies:
            copy_of(*copy).wait_send()
    for group in range(count):
        sib_copy(group).wait_send()
        far_copy(group).wait_send()
        for side in range(2):
            near_copy(side, group).wait_send()
    for tile in range(TILES):
        out_copy(tile).wait()


def on_device(queries, keys, values, span_order, out_weight):
    rows, width = queries.shape
    heads = width // HEAD_DIM
    d_out = out_weight.shape[1]
    bf16, f32 = jnp.bfloat16, jnp.float32
    sem = pltpu.SemaphoreType.DMA
    groups = len(GROUPS)
    span_order, queries, keys, values, out_weight = (
        pltpu.with_memory_space_constraint(array, pltpu.HBM)
        for array in (span_order, queries, keys, values, out_weight))
    return pl.pallas_call(
        kernel,
        out_shape=jax.ShapeDtypeStruct((rows // 8, d_out), bf16),
        in_specs=[pl.BlockSpec(memory_space=pltpu.HBM)] * 5,
        out_specs=pl.BlockSpec(memory_space=pl.ANY),
        scratch_shapes=[
            pltpu.VMEM((rows, width), bf16),
            pltpu.VMEM((SPANS, 2, SPAN, HEAD_DIM), bf16),
            pltpu.VMEM((width, d_out), bf16),
            pltpu.VMEM((heads, HEAD_DIM, rows), bf16),
            pltpu.VMEM((heads, HEAD_DIM + 16, rows), f32),
            pltpu.VMEM((heads, 1, rows), f32),
            pltpu.VMEM((rows, width), bf16),
            pltpu.VMEM((TILES, 4, 32, TILE), bf16),
            pltpu.VMEM((TILES, 4, 32, TILE), bf16),
            pltpu.VMEM((TILES, 4, 32, TILE), bf16),
            pltpu.VMEM((TILES, 32, TILE), bf16),
            pltpu.VMEM((TILES, 32, TILE), bf16),
            pltpu.VMEM((2, TILES, 32, TILE), bf16),
            pltpu.VMEM((2, TILES, 32, TILE), bf16),
            pltpu.VMEM((rows // 8, d_out), bf16),
            pltpu.SMEM((SPANS,), jnp.int32),
            pltpu.SMEM((SPANS,), jnp.int32),
            sem((14,)), sem((6, 2)), sem((6, 2)), sem((SPANS - 8,)), sem((SPANS - 8,)),
            sem((groups,)), sem((groups,)), sem((groups,)), sem((groups,)),
            sem((2, groups)), sem((2, groups)), sem((TILES,)),
        ],
        compiler_params=pltpu.CompilerParams(
            collective_id=0, has_side_effects=True, vmem_limit_bytes=32 * 1024 * 1024),
        cost_estimate=pl.CostEstimate(
            flops=3 * 2 * rows * width * 4096, bytes_accessed=10 * 2**20,
            transcendentals=heads * rows * 4096),
    )(span_order, queries, keys, values, out_weight)


def solution(mesh):
    return jax.shard_map(
        on_device,
        mesh=mesh,
        in_specs=(
            P(("dp", "context"), "tensor"),
            P(("dp", "context"), "tensor"),
            P(("dp", "context"), "tensor"),
            P("dp"),
            P("tensor", None),
        ),
        out_specs=P(("dp", "context", "tensor"), None),
        check_vma=False,
    )
```

```python
import math

import jax
import jax.numpy as jnp
from jax import lax
from jax.experimental import pallas as pl
from jax.experimental.pallas import tpu as pltpu
from jax.sharding import PartitionSpec as P

HEAD_DIM = 128
SPAN = 128
RING = 8
COLUMNS = 2
CHIPS = 4
ROUNDS = 10
TILE = 512
TILES = 8
HALF = TILES // 2
LOWEST = -1e30
MESH = pl.DeviceIdType.MESH

UP = [(0, 1, 0), (0, 1, 1), (0, 2, 0), (0, 2, 1), (0, 3, 0), (0, 3, 1),
      (1, 3, 0), (0, 4, 0), (1, 4, 0), (1, 3, 1)]
DOWN = [(0, -1, 1), (0, -1, 0), (0, -2, 1), (0, -2, 0), (0, -3, 1), (0, -3, 0),
        (0, -4, 1), (1, -3, 1), (1, -3, 0), (1, -4, 1)]
ACROSS = [(1, 0, 0), (1, 0, 1), (1, 1, 0), (1, -1, 1), (1, 2, 0), (1, -2, 1),
          (1, -2, 0), (1, 2, 1), (1, 1, 1), (1, -1, 0)]


def plan():
    slot_of = {(0, 0, 0): 0, (0, 0, 1): 1}
    contents = [(0, 0, 0), (0, 0, 1)]
    up_slot = {r: 2 + 3 * r for r in range(ROUNDS)}
    down_slot = {r: 3 + 3 * r for r in range(ROUNDS)}
    across_slot = {r: 4 + 3 * r for r in range(ROUNDS)}
    slots = {}
    for r in range(ROUNDS):
        for table, names in ((up_slot, UP), (down_slot, DOWN), (across_slot, ACROSS)):
            slots[table[r]] = names[r]
    for slot in range(2, 2 + 3 * ROUNDS):
        column, offset, half = slots[slot]
        key = (column, offset % RING, half)
        slot_of[key] = slot
        contents.append(key)
    assert len(slot_of) == 2 + 3 * ROUNDS
    copies = []
    for r in range(ROUNDS):
        (uc, uo, uh), (dc, do, dh), (ac, ao, ah) = UP[r], DOWN[r], ACROSS[r]
        copies.append((
            ("minus", slot_of[(uc, (uo - 1) % RING, uh)], up_slot[r]),
            ("plus", slot_of[(dc, (do + 1) % RING, dh)], down_slot[r]),
            ("other", slot_of[(0, ao % RING, ah)], across_slot[r]),
        ))
    return contents, copies


CONTENTS, COPIES = plan()
SPANS = len(CONTENTS)
ORDER = tuple(part * HALF + tile for tile in range(HALF) for part in range(2))


def kernel(order_hbm, q_hbm, k_hbm, v_hbm, w_hbm, out,
           q_in, kv, w, qt, acc, top, att, own, sib_out, sib_in,
           far_out, far_in, near_out, near_in, result, order, span_of,
           load_sem, own_send, own_recv, kv_send, kv_recv, sib_send, sib_recv,
           far_send, far_recv, near_send, near_recv, out_sem):
    heads = q_in.shape[1] // HEAD_DIM
    rows = q_in.shape[0]
    context = lax.axis_index("context")
    tensor = lax.axis_index("tensor")
    y, z = context // RING, lax.rem(context, RING)
    x, core = tensor // 2, lax.rem(tensor, 2)
    ahead = 1 - 2 * core
    targets = {
        "minus": {"context": y * RING + lax.rem(z + RING - ahead, RING)},
        "plus": {"context": y * RING + lax.rem(z + RING + ahead, RING)},
        "other": {"context": (1 - y) * RING + z},
    }
    sibling = {"tensor": x * 2 + 1 - core}
    chip_next, chip_back = lax.rem(x + CHIPS + ahead, CHIPS), lax.rem(x + CHIPS - ahead, CHIPS)
    chip_far = lax.rem(x + 2, CHIPS)
    to_next, to_back = {"tensor": chip_next * 2 + core}, {"tensor": chip_back * 2 + core}

    barrier = pltpu.get_barrier_semaphore()
    for target in (*targets.values(), sibling, to_next, to_back):
        pl.semaphore_signal(barrier, inc=1, device_id=target, device_id_type=MESH)

    loads = []
    for half in range(2):
        for part, source in enumerate((k_hbm, v_hbm)):
            loads.append(pltpu.make_async_copy(
                source.at[pl.ds(half * SPAN, SPAN)], kv.at[half, part],
                load_sem.at[2 * half + part]))
    chips = ((chip_far, chip_next, chip_back, x), (chip_far, chip_back, chip_next, x))
    for group in range(4):
        for part, owner in enumerate((core, 1 - core)):
            number = 2 * group + part
            chip = chips[part][group]
            first = pl.multiple_of(chip * 64 + owner * 32, 32)
            loads.append(pltpu.make_async_copy(
                q_hbm.at[pl.ds(first, 32)], q_in.at[pl.ds(32 * number, 32)],
                load_sem.at[4 + number]))
    loads.append(pltpu.make_async_copy(order_hbm, order, load_sem.at[13]))
    loads.append(pltpu.make_async_copy(w_hbm, w, load_sem.at[12]))
    for load in loads[:-1]:
        load.start()

    def own_copies(r):
        for name, src, dst in COPIES[r]:
            for part, source in enumerate((k_hbm, v_hbm)):
                yield pltpu.make_async_remote_copy(
                    src_ref=source.at[pl.ds(src * SPAN, SPAN)], dst_ref=kv.at[dst, part],
                    send_sem=own_send.at[dst - 2, part], recv_sem=own_recv.at[dst - 2, part],
                    device_id=targets[name], device_id_type=MESH)

    def copy_of(name, src, dst):
        return pltpu.make_async_remote_copy(
            src_ref=kv.at[src], dst_ref=kv.at[dst],
            send_sem=kv_send.at[dst - 8], recv_sem=kv_recv.at[dst - 8],
            device_id=targets[name], device_id_type=MESH)

    pl.semaphore_wait(barrier, 6)
    for copy in own_copies(0):
        copy.start()
    loads[-1].start()

    loads[12].wait()
    for slot, (column, offset, half) in enumerate(CONTENTS):
        where = (y if column == 0 else 1 - y) * RING + lax.rem(z + RING + ahead * offset, RING)
        span_of[slot] = order[2 * where + half]

    for load in loads[4:12]:
        load.wait()
    for head in range(heads):
        qt[head] = q_in[:, head * HEAD_DIM:(head + 1) * HEAD_DIM].T

    for first, second in zip(own_copies(0), own_copies(1)):
        first.wait_send()
        second.start()
    for load in loads[:4]:
        load.wait()

    lane = lax.broadcasted_iota(jnp.int32, (1, rows), 1)
    group_of = lane // 64
    mine = lax.rem(lane // 32, 2) == 0
    chip_of = jnp.where(group_of == 0, chip_far, jnp.where(group_of == 3, x, jnp.where(
        (group_of == 1) == mine, chip_next, chip_back)))
    owner_of = jnp.where(mine, core, 1 - core)
    row_of = chip_of * 64 + owner_of * 32 + lax.rem(lane, 32)
    q_span = jnp.where(row_of < SPAN, span_of[0], span_of[1])
    q_pos = q_span * SPAN + lax.rem(row_of, SPAN)

    def operands(first, count):
        spans = kv[pl.ds(first, count)]
        keys = spans[:, 0].reshape(count * SPAN, HEAD_DIM)
        values = spans[:, 1].reshape(count * SPAN, HEAD_DIM).T
        ones = jnp.ones((16, count * SPAN), jnp.bfloat16)
        return keys, jnp.concatenate([values, ones], axis=0)

    scale = math.log2(math.e) / math.sqrt(HEAD_DIM)

    def scores_of(keys, head):
        return jnp.dot(keys, qt[head], preferred_element_type=jnp.float32)

    def receive(r):
        following = COPIES[r + 2] if r + 2 < ROUNDS else ()
        here = 2 + 3 * r
        for copy in following:
            if copy[1] < here:
                copy_of(*copy).start()
        first = list(own_copies(r)) if r < 2 else ()
        for number, copy in enumerate(COPIES[r]):
            if r < 2:
                first[2 * number].wait_recv()
                first[2 * number + 1].wait_recv()
            else:
                copy_of(*copy).wait_recv()
            for later in following:
                if later[1] == copy[2]:
                    copy_of(*later).start()

    keys, values = operands(0, 2)
    k_row = lax.broadcasted_iota(jnp.int32, (2 * SPAN, 1), 0)
    k_pos = jnp.where(k_row < SPAN, span_of[0], span_of[1]) * SPAN + lax.rem(k_row, SPAN)
    hide = jnp.where(k_pos <= q_pos, 0.0, LOWEST)
    following = scores_of(keys, 0)
    for head in range(heads):
        scores = following * scale + hide
        if head + 1 < heads:
            following = scores_of(keys, head + 1)
        new_top = jnp.max(scores, axis=0, keepdims=True)
        weights = jnp.exp2(scores - new_top).astype(jnp.bfloat16)
        top[head] = new_top
        acc[head] = jnp.dot(values, weights, preferred_element_type=jnp.float32)

    @pl.loop(0, ROUNDS)
    def _(step):
        for r in range(ROUNDS):
            @pl.when(step == r)
            def _():
                receive(r)

        first = 2 + 3 * step
        keys, values = operands(first, 3)
        hide = [jnp.where(span_of[first + number] < q_span, 0.0, LOWEST) for number in range(3)]
        following = scores_of(keys, 0)
        for head in range(heads):
            scores = [following[number * SPAN:(number + 1) * SPAN] for number in range(3)]
            if head + 1 < heads:
                following = scores_of(keys, head + 1)
            old_top = top[head]
            new_top = old_top
            for part, hidden in zip(scores, hide):
                new_top = jnp.maximum(new_top, jnp.max(part, axis=0, keepdims=True) * scale + hidden)
            factor = jnp.exp2(old_top - new_top)
            weights = jnp.concatenate([
                jnp.exp2(part * scale - (new_top - hidden)).astype(jnp.bfloat16)
                for part, hidden in zip(scores, hide)], axis=0)
            top[head] = new_top
            acc[head] = acc[head] * factor + jnp.dot(
                values, weights, preferred_element_type=jnp.float32)

    for head in range(heads):
        mixed = acc[head, :HEAD_DIM] * (1.0 / acc[head, HEAD_DIM:HEAD_DIM + 1])
        att[:, head * HEAD_DIM:(head + 1) * HEAD_DIM] = mixed.astype(jnp.bfloat16).T
    loads[13].wait()

    def sib_copy(tile, part):
        at = 0 if part == 0 else pl.ds(1, 3)
        return pltpu.make_async_remote_copy(
            src_ref=sib_out.at[tile, at], dst_ref=sib_in.at[tile, at],
            send_sem=sib_send.at[tile, part], recv_sem=sib_recv.at[tile, part],
            device_id=sibling, device_id_type=MESH)

    def project(tile):
        part = jnp.dot(att[...], w[:, tile * TILE:(tile + 1) * TILE],
                       preferred_element_type=jnp.float32).astype(jnp.bfloat16)
        part = part.reshape(4, 2, 32, TILE)
        sib_out[tile] = part[:, 1]
        sib_copy(tile, 0).start()
        sib_copy(tile, 1).start()
        own[tile] = part[:, 0]

    def both(tile, group):
        return own[tile, group].astype(jnp.float32) + sib_in[tile, group].astype(jnp.float32)

    def far_copy(tile):
        return pltpu.make_async_remote_copy(
            src_ref=far_out.at[tile], dst_ref=far_in.at[tile],
            send_sem=far_send.at[tile], recv_sem=far_recv.at[tile],
            device_id=to_next if tile < HALF else to_back, device_id_type=MESH)

    def near_copy(side, tile):
        return pltpu.make_async_remote_copy(
            src_ref=near_out.at[side, tile], dst_ref=near_in.at[side, tile],
            send_sem=near_send.at[side, tile], recv_sem=near_recv.at[side, tile],
            device_id=to_next if side == 0 else to_back, device_id_type=MESH)

    def out_copy(tile):
        at = pl.ds(tile * TILE, TILE)
        return pltpu.make_async_copy(result.at[:, at], out.at[:, at], out_sem.at[tile])

    def send_far(tile):
        sib_copy(tile, 0).wait_recv()
        far_out[tile] = both(tile, 0).astype(jnp.bfloat16)
        far_copy(tile).start()

    def send_near(side, tile):
        second = (tile < HALF) == (side == 0)
        if not second:
            sib_copy(tile, 1).wait_recv()
        total = both(tile, 1 + side)
        if second:
            far_copy(tile).wait_recv()
            total = total + far_in[tile].astype(jnp.float32)
        near_out[side, tile] = total.astype(jnp.bfloat16)
        near_copy(side, tile).start()

    def send_first(tile):
        send_far(tile)
        send_near(0 if tile >= HALF else 1, tile)

    project(ORDER[0])
    for earlier, tile in zip(ORDER, ORDER[1:]):
        project(tile)
        send_first(earlier)
    send_first(ORDER[-1])
    for tile in ORDER:
        send_near(0 if tile < HALF else 1, tile)
    for tile in ORDER:
        near_copy(0, tile).wait_recv()
        near_copy(1, tile).wait_recv()
        total = both(tile, 3) + (near_in[0, tile].astype(jnp.float32)
                                 + near_in[1, tile].astype(jnp.float32))
        result[:, tile * TILE:(tile + 1) * TILE] = total.astype(out.dtype)
        out_copy(tile).start()

    for copy in own_copies(1):
        copy.wait_send()
    for copies in COPIES[2:]:
        for copy in copies:
            copy_of(*copy).wait_send()
    for tile in range(TILES):
        for part in range(2):
            sib_copy(tile, part).wait_send()
            near_copy(part, tile).wait_send()
        far_copy(tile).wait_send()
        out_copy(tile).wait()


def on_device(queries, keys, values, span_order, out_weight):
    rows, width = queries.shape
    heads = width // HEAD_DIM
    d_out = out_weight.shape[1]
    bf16, f32 = jnp.bfloat16, jnp.float32
    sem = pltpu.SemaphoreType.DMA
    span_order, queries, keys, values, out_weight = (
        pltpu.with_memory_space_constraint(array, pltpu.HBM)
        for array in (span_order, queries, keys, values, out_weight))
    return pl.pallas_call(
        kernel,
        out_shape=jax.ShapeDtypeStruct((rows // 8, d_out), bf16),
        in_specs=[pl.BlockSpec(memory_space=pltpu.HBM)] * 5,
        out_specs=pl.BlockSpec(memory_space=pl.ANY),
        scratch_shapes=[
            pltpu.VMEM((rows, width), bf16),
            pltpu.VMEM((SPANS, 2, SPAN, HEAD_DIM), bf16),
            pltpu.VMEM((width, d_out), bf16),
            pltpu.VMEM((heads, HEAD_DIM, rows), bf16),
            pltpu.VMEM((heads, HEAD_DIM + 16, rows), f32),
            pltpu.VMEM((heads, 1, rows), f32),
            pltpu.VMEM((rows, width), bf16),
            pltpu.VMEM((TILES, 4, 32, TILE), bf16),
            pltpu.VMEM((TILES, 4, 32, TILE), bf16),
            pltpu.VMEM((TILES, 4, 32, TILE), bf16),
            pltpu.VMEM((TILES, 32, TILE), bf16),
            pltpu.VMEM((TILES, 32, TILE), bf16),
            pltpu.VMEM((2, TILES, 32, TILE), bf16),
            pltpu.VMEM((2, TILES, 32, TILE), bf16),
            pltpu.VMEM((rows // 8, d_out), bf16),
            pltpu.SMEM((SPANS,), jnp.int32),
            pltpu.SMEM((SPANS,), jnp.int32),
            sem((14,)), sem((6, 2)), sem((6, 2)), sem((SPANS - 8,)), sem((SPANS - 8,)),
            sem((TILES, 2)), sem((TILES, 2)), sem((TILES,)), sem((TILES,)),
            sem((2, TILES)), sem((2, TILES)), sem((TILES,)),
        ],
        compiler_params=pltpu.CompilerParams(
            collective_id=0, has_side_effects=True, vmem_limit_bytes=32 * 1024 * 1024),
        cost_estimate=pl.CostEstimate(
            flops=3 * 2 * rows * width * 4096, bytes_accessed=10 * 2**20,
            transcendentals=heads * rows * 4096),
    )(span_order, queries, keys, values, out_weight)


def solution(mesh):
    return jax.shard_map(
        on_device,
        mesh=mesh,
        in_specs=(
            P(("dp", "context"), "tensor"),
            P(("dp", "context"), "tensor"),
            P(("dp", "context"), "tensor"),
            P("dp"),
            P("tensor", None),
        ),
        out_specs=P(("dp", "context", "tensor"), None),
        check_vma=False,
    )
```

```python
import math

import jax
import jax.numpy as jnp
from jax import lax
from jax.experimental import pallas as pl
from jax.experimental.pallas import tpu as pltpu
from jax.sharding import PartitionSpec as P

HEAD_DIM = 128
SPAN = 128
RING = 8
COLUMNS = 2
CHIPS = 4
ROUNDS = 10
TILE = 512
TILES = 8
HALF = TILES // 2
LOWEST = -1e30
MESH = pl.DeviceIdType.MESH

UP = [(0, 1, 0), (0, 1, 1), (0, 2, 0), (0, 2, 1), (0, 3, 0), (0, 3, 1),
      (1, 3, 0), (0, 4, 0), (1, 4, 0), (1, 3, 1)]
DOWN = [(0, -1, 1), (0, -1, 0), (0, -2, 1), (0, -2, 0), (0, -3, 1), (0, -3, 0),
        (0, -4, 1), (1, -3, 1), (1, -3, 0), (1, -4, 1)]
ACROSS = [(1, 0, 0), (1, 0, 1), (1, 1, 0), (1, -1, 1), (1, 2, 0), (1, -2, 1),
          (1, -2, 0), (1, 2, 1), (1, 1, 1), (1, -1, 0)]


def plan():
    slot_of = {(0, 0, 0): 0, (0, 0, 1): 1}
    contents = [(0, 0, 0), (0, 0, 1)]
    up_slot = {r: 2 + 3 * r for r in range(ROUNDS)}
    down_slot = {r: 3 + 3 * r for r in range(ROUNDS)}
    across_slot = {r: 4 + 3 * r for r in range(ROUNDS)}
    slots = {}
    for r in range(ROUNDS):
        for table, names in ((up_slot, UP), (down_slot, DOWN), (across_slot, ACROSS)):
            slots[table[r]] = names[r]
    for slot in range(2, 2 + 3 * ROUNDS):
        column, offset, half = slots[slot]
        key = (column, offset % RING, half)
        slot_of[key] = slot
        contents.append(key)
    assert len(slot_of) == 2 + 3 * ROUNDS
    copies = []
    for r in range(ROUNDS):
        (uc, uo, uh), (dc, do, dh), (ac, ao, ah) = UP[r], DOWN[r], ACROSS[r]
        copies.append((
            ("minus", slot_of[(uc, (uo - 1) % RING, uh)], up_slot[r]),
            ("plus", slot_of[(dc, (do + 1) % RING, dh)], down_slot[r]),
            ("other", slot_of[(0, ao % RING, ah)], across_slot[r]),
        ))
    return contents, copies


CONTENTS, COPIES = plan()
SPANS = len(CONTENTS)
ORDER = tuple(part * HALF + tile for tile in range(HALF) for part in range(2))


def kernel(order_hbm, q_hbm, k_hbm, v_hbm, w_hbm, out,
           q_in, kv, w, qt, acc, top, att, own, sib_out, sib_in,
           far_out, far_in, near_out, near_in, result, order, span_of,
           load_sem, own_send, own_recv, kv_send, kv_recv, sib_send, sib_recv,
           far_send, far_recv, near_send, near_recv, out_sem):
    heads = q_in.shape[1] // HEAD_DIM
    rows = q_in.shape[0]
    context = lax.axis_index("context")
    tensor = lax.axis_index("tensor")
    y, z = context // RING, lax.rem(context, RING)
    x, core = tensor // 2, lax.rem(tensor, 2)
    ahead = 1 - 2 * core
    targets = {
        "minus": {"context": y * RING + lax.rem(z + RING - ahead, RING)},
        "plus": {"context": y * RING + lax.rem(z + RING + ahead, RING)},
        "other": {"context": (1 - y) * RING + z},
    }
    sibling = {"tensor": x * 2 + 1 - core}
    chip_next, chip_back = lax.rem(x + CHIPS + ahead, CHIPS), lax.rem(x + CHIPS - ahead, CHIPS)
    chip_far = lax.rem(x + 2, CHIPS)
    to_next, to_back = {"tensor": chip_next * 2 + core}, {"tensor": chip_back * 2 + core}

    barrier = pltpu.get_barrier_semaphore()
    for target in (*targets.values(), sibling, to_next, to_back):
        pl.semaphore_signal(barrier, inc=1, device_id=target, device_id_type=MESH)

    loads = []
    for half in range(2):
        for part, source in enumerate((k_hbm, v_hbm)):
            loads.append(pltpu.make_async_copy(
                source.at[pl.ds(half * SPAN, SPAN)], kv.at[half, part],
                load_sem.at[2 * half + part]))
    chips = ((chip_far, chip_next, chip_back, x), (chip_far, chip_back, chip_next, x))
    for group in range(4):
        for part, owner in enumerate((core, 1 - core)):
            number = 2 * group + part
            chip = chips[part][group]
            first = pl.multiple_of(chip * 64 + owner * 32, 32)
            loads.append(pltpu.make_async_copy(
                q_hbm.at[pl.ds(first, 32)], q_in.at[pl.ds(32 * number, 32)],
                load_sem.at[4 + number]))
    loads.append(pltpu.make_async_copy(order_hbm, order, load_sem.at[13]))
    loads.append(pltpu.make_async_copy(w_hbm, w, load_sem.at[12]))
    for load in loads[:-1]:
        load.start()

    def own_copies(r):
        for name, src, dst in COPIES[r]:
            for part, source in enumerate((k_hbm, v_hbm)):
                yield pltpu.make_async_remote_copy(
                    src_ref=source.at[pl.ds(src * SPAN, SPAN)], dst_ref=kv.at[dst, part],
                    send_sem=own_send.at[dst - 2, part], recv_sem=own_recv.at[dst - 2, part],
                    device_id=targets[name], device_id_type=MESH)

    def copy_of(name, src, dst):
        return pltpu.make_async_remote_copy(
            src_ref=kv.at[src], dst_ref=kv.at[dst],
            send_sem=kv_send.at[dst - 8], recv_sem=kv_recv.at[dst - 8],
            device_id=targets[name], device_id_type=MESH)

    pl.semaphore_wait(barrier, 6)
    for copy in own_copies(0):
        copy.start()
    loads[-1].start()

    loads[12].wait()
    for slot, (column, offset, half) in enumerate(CONTENTS):
        where = (y if column == 0 else 1 - y) * RING + lax.rem(z + RING + ahead * offset, RING)
        span_of[slot] = order[2 * where + half]

    for load in loads[4:12]:
        load.wait()
    for head in range(heads):
        qt[head] = q_in[:, head * HEAD_DIM:(head + 1) * HEAD_DIM].T

    for first, second in zip(own_copies(0), own_copies(1)):
        first.wait_send()
        second.start()
    for load in loads[:4]:
        load.wait()

    lane = lax.broadcasted_iota(jnp.int32, (1, rows), 1)
    group_of = lane // 64
    mine = lax.rem(lane // 32, 2) == 0
    chip_of = jnp.where(group_of == 0, chip_far, jnp.where(group_of == 3, x, jnp.where(
        (group_of == 1) == mine, chip_next, chip_back)))
    owner_of = jnp.where(mine, core, 1 - core)
    row_of = chip_of * 64 + owner_of * 32 + lax.rem(lane, 32)
    q_span = jnp.where(row_of < SPAN, span_of[0], span_of[1])
    q_pos = q_span * SPAN + lax.rem(row_of, SPAN)

    def operands(first, count):
        spans = kv[pl.ds(first, count)]
        keys = spans[:, 0].reshape(count * SPAN, HEAD_DIM)
        values = spans[:, 1].reshape(count * SPAN, HEAD_DIM).T
        ones = jnp.ones((16, count * SPAN), jnp.bfloat16)
        return keys, jnp.concatenate([values, ones], axis=0)

    scale = math.log2(math.e) / math.sqrt(HEAD_DIM)

    def scores_of(keys, head):
        return jnp.dot(keys, qt[head], preferred_element_type=jnp.float32)

    def receive(r):
        following = COPIES[r + 2] if r + 2 < ROUNDS else ()
        here = 2 + 3 * r
        for copy in following:
            if copy[1] < here:
                copy_of(*copy).start()
        first = list(own_copies(r)) if r < 2 else ()
        for number, copy in enumerate(COPIES[r]):
            if r < 2:
                first[2 * number].wait_recv()
                first[2 * number + 1].wait_recv()
            else:
                copy_of(*copy).wait_recv()
            for later in following:
                if later[1] == copy[2]:
                    copy_of(*later).start()

    keys, values = operands(0, 2)
    k_row = lax.broadcasted_iota(jnp.int32, (2 * SPAN, 1), 0)
    k_pos = jnp.where(k_row < SPAN, span_of[0], span_of[1]) * SPAN + lax.rem(k_row, SPAN)
    hide = jnp.where(k_pos <= q_pos, 0.0, LOWEST)
    following = scores_of(keys, 0)
    for head in range(heads):
        scores = following * scale + hide
        if head + 1 < heads:
            following = scores_of(keys, head + 1)
        new_top = jnp.max(scores, axis=0, keepdims=True)
        weights = jnp.exp2(scores - new_top).astype(jnp.bfloat16)
        top[head] = new_top
        acc[head] = jnp.dot(values, weights, preferred_element_type=jnp.float32)

    for step in range(ROUNDS):
        receive(step)
        first = 2 + 3 * step
        keys, values = operands(first, 3)
        hide = [jnp.where(span_of[first + number] < q_span, 0.0, LOWEST) for number in range(3)]
        following = scores_of(keys, 0)
        for head in range(heads):
            scores = [following[number * SPAN:(number + 1) * SPAN] for number in range(3)]
            if head + 1 < heads:
                following = scores_of(keys, head + 1)
            old_top = top[head]
            new_top = old_top
            for part, hidden in zip(scores, hide):
                new_top = jnp.maximum(new_top, jnp.max(part, axis=0, keepdims=True) * scale + hidden)
            factor = jnp.exp2(old_top - new_top)
            weights = jnp.concatenate([
                jnp.exp2(part * scale - (new_top - hidden)).astype(jnp.bfloat16)
                for part, hidden in zip(scores, hide)], axis=0)
            top[head] = new_top
            acc[head] = acc[head] * factor + jnp.dot(
                values, weights, preferred_element_type=jnp.float32)

    for head in range(heads):
        mixed = acc[head, :HEAD_DIM] * (1.0 / acc[head, HEAD_DIM:HEAD_DIM + 1])
        att[:, head * HEAD_DIM:(head + 1) * HEAD_DIM] = mixed.astype(jnp.bfloat16).T
    loads[13].wait()

    def sib_copy(tile, part):
        at = 0 if part == 0 else pl.ds(1, 3)
        return pltpu.make_async_remote_copy(
            src_ref=sib_out.at[tile, at], dst_ref=sib_in.at[tile, at],
            send_sem=sib_send.at[tile, part], recv_sem=sib_recv.at[tile, part],
            device_id=sibling, device_id_type=MESH)

    def project(tile):
        part = jnp.dot(att[...], w[:, tile * TILE:(tile + 1) * TILE],
                       preferred_element_type=jnp.float32).astype(jnp.bfloat16)
        part = part.reshape(4, 2, 32, TILE)
        sib_out[tile] = part[:, 1]
        sib_copy(tile, 0).start()
        sib_copy(tile, 1).start()
        own[tile] = part[:, 0]

    def both(tile, group):
        return own[tile, group].astype(jnp.float32) + sib_in[tile, group].astype(jnp.float32)

    def far_copy(tile):
        return pltpu.make_async_remote_copy(
            src_ref=far_out.at[tile], dst_ref=far_in.at[tile],
            send_sem=far_send.at[tile], recv_sem=far_recv.at[tile],
            device_id=to_next if tile < HALF else to_back, device_id_type=MESH)

    def near_copy(side, tile):
        return pltpu.make_async_remote_copy(
            src_ref=near_out.at[side, tile], dst_ref=near_in.at[side, tile],
            send_sem=near_send.at[side, tile], recv_sem=near_recv.at[side, tile],
            device_id=to_next if side == 0 else to_back, device_id_type=MESH)

    def out_copy(tile):
        at = pl.ds(tile * TILE, TILE)
        return pltpu.make_async_copy(result.at[:, at], out.at[:, at], out_sem.at[tile])

    def send_far(tile):
        sib_copy(tile, 0).wait_recv()
        far_out[tile] = both(tile, 0).astype(jnp.bfloat16)
        far_copy(tile).start()

    def send_near(side, tile):
        second = (tile < HALF) == (side == 0)
        if not second:
            sib_copy(tile, 1).wait_recv()
        total = both(tile, 1 + side)
        if second:
            far_copy(tile).wait_recv()
            total = total + far_in[tile].astype(jnp.float32)
        near_out[side, tile] = total.astype(jnp.bfloat16)
        near_copy(side, tile).start()

    def send_first(tile):
        send_far(tile)
        send_near(0 if tile >= HALF else 1, tile)

    project(ORDER[0])
    for earlier, tile in zip(ORDER, ORDER[1:]):
        project(tile)
        send_first(earlier)
    send_first(ORDER[-1])
    for tile in ORDER:
        send_near(0 if tile < HALF else 1, tile)
    for tile in ORDER:
        near_copy(0, tile).wait_recv()
        near_copy(1, tile).wait_recv()
        total = both(tile, 3) + (near_in[0, tile].astype(jnp.float32)
                                 + near_in[1, tile].astype(jnp.float32))
        result[:, tile * TILE:(tile + 1) * TILE] = total.astype(out.dtype)
        out_copy(tile).start()

    for copy in own_copies(1):
        copy.wait_send()
    for copies in COPIES[2:]:
        for copy in copies:
            copy_of(*copy).wait_send()
    for tile in range(TILES):
        for part in range(2):
            sib_copy(tile, part).wait_send()
            near_copy(part, tile).wait_send()
        far_copy(tile).wait_send()
        out_copy(tile).wait()


def on_device(queries, keys, values, span_order, out_weight):
    rows, width = queries.shape
    heads = width // HEAD_DIM
    d_out = out_weight.shape[1]
    bf16, f32 = jnp.bfloat16, jnp.float32
    sem = pltpu.SemaphoreType.DMA
    span_order, queries, keys, values, out_weight = (
        pltpu.with_memory_space_constraint(array, pltpu.HBM)
        for array in (span_order, queries, keys, values, out_weight))
    return pl.pallas_call(
        kernel,
        out_shape=jax.ShapeDtypeStruct((rows // 8, d_out), bf16),
        in_specs=[pl.BlockSpec(memory_space=pltpu.HBM)] * 5,
        out_specs=pl.BlockSpec(memory_space=pl.ANY),
        scratch_shapes=[
            pltpu.VMEM((rows, width), bf16),
            pltpu.VMEM((SPANS, 2, SPAN, HEAD_DIM), bf16),
            pltpu.VMEM((width, d_out), bf16),
            pltpu.VMEM((heads, HEAD_DIM, rows), bf16),
            pltpu.VMEM((heads, HEAD_DIM + 16, rows), f32),
            pltpu.VMEM((heads, 1, rows), f32),
            pltpu.VMEM((rows, width), bf16),
            pltpu.VMEM((TILES, 4, 32, TILE), bf16),
            pltpu.VMEM((TILES, 4, 32, TILE), bf16),
            pltpu.VMEM((TILES, 4, 32, TILE), bf16),
            pltpu.VMEM((TILES, 32, TILE), bf16),
            pltpu.VMEM((TILES, 32, TILE), bf16),
            pltpu.VMEM((2, TILES, 32, TILE), bf16),
            pltpu.VMEM((2, TILES, 32, TILE), bf16),
            pltpu.VMEM((rows // 8, d_out), bf16),
            pltpu.SMEM((SPANS,), jnp.int32),
            pltpu.SMEM((SPANS,), jnp.int32),
            sem((14,)), sem((6, 2)), sem((6, 2)), sem((SPANS - 8,)), sem((SPANS - 8,)),
            sem((TILES, 2)), sem((TILES, 2)), sem((TILES,)), sem((TILES,)),
            sem((2, TILES)), sem((2, TILES)), sem((TILES,)),
        ],
        compiler_params=pltpu.CompilerParams(
            collective_id=0, has_side_effects=True, vmem_limit_bytes=32 * 1024 * 1024),
        cost_estimate=pl.CostEstimate(
            flops=3 * 2 * rows * width * 4096, bytes_accessed=10 * 2**20,
            transcendentals=heads * rows * 4096),
    )(span_order, queries, keys, values, out_weight)


def solution(mesh):
    return jax.shard_map(
        on_device,
        mesh=mesh,
        in_specs=(
            P(("dp", "context"), "tensor"),
            P(("dp", "context"), "tensor"),
            P(("dp", "context"), "tensor"),
            P("dp"),
            P("tensor", None),
        ),
        out_specs=P(("dp", "context", "tensor"), None),
        check_vma=False,
    )
```

```python
import math

import jax
import jax.numpy as jnp
from jax import lax
from jax.experimental import pallas as pl
from jax.experimental.pallas import tpu as pltpu
from jax.sharding import PartitionSpec as P

HEAD_DIM = 128
SPAN = 128
RING = 8
COLUMNS = 2
CHIPS = 4
TILE = 512
TILES = 8
HALF = TILES // 2
LOWEST = -1e30
MESH = pl.DeviceIdType.MESH

BLOCKS = ((0, 0), (0, 1), (0, -1), (1, 0), (0, 2), (0, -2), (1, 1), (0, 3), (0, -3), (1, 2),
          (0, 4), (1, -2), (1, 3), (1, -1), (1, -3), (1, 4))
SENDS = {
    0: (("minus", 0, 1, None), ("plus", 0, 2, None), ("other", 0, 3, None)),
    1: (("minus", 1, 4, None),),
    2: (("plus", 2, 5, None),),
    3: (("other", 1, 6, None),),
    4: (("minus", 4, 7, None),),
    5: (("plus", 5, 8, None),),
    6: (("other", 4, 9, None),),
    7: (("minus", 7, 10, 0),),
    8: (("plus", 8, 10, 1),),
    9: (("other", 5, 11, None), ("minus", 9, 12, None)),
    10: (("other", 2, 13, None),),
    11: (("plus", 11, 14, None),),
    12: (("minus", 12, 15, 0),),
    14: (("plus", 14, 15, 1),),
}
COUNT = len(BLOCKS)
ORDER = tuple(part * HALF + tile for tile in range(HALF) for part in range(2))


def kernel(order_hbm, q_hbm, k_hbm, v_hbm, w_hbm, out,
           q_in, kv, w, qt, acc, top, att, own, sib_out, sib_in,
           far_out, far_in, near_out, near_in, result, order, span_of,
           load_sem, kv_send, kv_recv, sib_send, sib_recv,
           far_send, far_recv, near_send, near_recv, out_sem):
    heads = q_in.shape[1] // HEAD_DIM
    rows = q_in.shape[0]
    context = lax.axis_index("context")
    tensor = lax.axis_index("tensor")
    y, z = context // RING, lax.rem(context, RING)
    x, core = tensor // 2, lax.rem(tensor, 2)
    ahead = 1 - 2 * core
    targets = {
        "minus": {"context": y * RING + lax.rem(z + RING - ahead, RING)},
        "plus": {"context": y * RING + lax.rem(z + RING + ahead, RING)},
        "other": {"context": (1 - y) * RING + z},
    }
    sibling = {"tensor": x * 2 + 1 - core}
    chip_next, chip_back = lax.rem(x + CHIPS + ahead, CHIPS), lax.rem(x + CHIPS - ahead, CHIPS)
    chip_far = lax.rem(x + 2, CHIPS)
    to_next, to_back = {"tensor": chip_next * 2 + core}, {"tensor": chip_back * 2 + core}

    barrier = pltpu.get_barrier_semaphore()
    for target in (*targets.values(), sibling, to_next, to_back):
        pl.semaphore_signal(barrier, inc=1, device_id=target, device_id_type=MESH)

    loads = []
    for part, source in enumerate((k_hbm, v_hbm)):
        loads.append(pltpu.make_async_copy(source, kv.at[0, part], load_sem.at[part]))
    chips = ((chip_far, chip_next, chip_back, x), (chip_far, chip_back, chip_next, x))
    for group in range(4):
        for part, owner in enumerate((core, 1 - core)):
            number = 2 * group + part
            chip = chips[part][group]
            first = pl.multiple_of(chip * 64 + owner * 32, 32)
            loads.append(pltpu.make_async_copy(
                q_hbm.at[pl.ds(first, 32)], q_in.at[pl.ds(32 * number, 32)],
                load_sem.at[2 + number]))
    loads.append(pltpu.make_async_copy(order_hbm, order, load_sem.at[11]))
    loads.append(pltpu.make_async_copy(w_hbm, w, load_sem.at[10]))
    for load in loads[:-1]:
        load.start()

    def copies_of(name, src, dst, half):
        if src == 0:
            pieces = [(k_hbm, kv.at[dst, 0], 0), (v_hbm, kv.at[dst, 1], 1)]
        elif half is None:
            pieces = [(kv.at[src], kv.at[dst], 0)]
        else:
            at = pl.ds(half * SPAN, SPAN)
            pieces = [(kv.at[src, :, at], kv.at[dst, :, at], half)]
        return [pltpu.make_async_remote_copy(
            src_ref=source, dst_ref=target,
            send_sem=kv_send.at[dst - 1, number], recv_sem=kv_recv.at[dst - 1, number],
            device_id=targets[name], device_id_type=MESH) for source, target, number in pieces]

    all_copies = [copy for block in sorted(SENDS) for send in SENDS[block] for copy in copies_of(*send)]

    def start(block):
        for send in SENDS.get(block, ()):
            for copy in copies_of(*send):
                copy.start()

    def receive(block):
        for sends in SENDS.values():
            for send in sends:
                if send[2] == block:
                    for copy in copies_of(*send):
                        copy.wait_recv()
        start(block)

    pl.semaphore_wait(barrier, 6)
    start(0)
    loads[-1].start()

    loads[10].wait()
    for block, (column, offset) in enumerate(BLOCKS):
        where = (y if column == 0 else 1 - y) * RING + lax.rem(z + RING + ahead * offset, RING)
        for half in range(2):
            span_of[2 * block + half] = order[2 * where + half]

    for load in loads[2:10]:
        load.wait()
    for head in range(heads):
        qt[head] = q_in[:, head * HEAD_DIM:(head + 1) * HEAD_DIM].T

    for load in loads[:2]:
        load.wait()

    lane = lax.broadcasted_iota(jnp.int32, (1, rows), 1)
    group_of = lane // 64
    mine = lax.rem(lane // 32, 2) == 0
    chip_of = jnp.where(group_of == 0, chip_far, jnp.where(group_of == 3, x, jnp.where(
        (group_of == 1) == mine, chip_next, chip_back)))
    owner_of = jnp.where(mine, core, 1 - core)
    row_of = chip_of * 64 + owner_of * 32 + lax.rem(lane, 32)
    q_span = jnp.where(row_of < SPAN, span_of[0], span_of[1])
    q_pos = q_span * SPAN + lax.rem(row_of, SPAN)

    def operands(block):
        values = jnp.concatenate([kv[block, 1].T, jnp.ones((16, 2 * SPAN), jnp.bfloat16)], axis=0)
        return kv[block, 0], values

    scale = math.log2(math.e) / math.sqrt(HEAD_DIM)

    def scores_of(keys, head):
        return jnp.dot(keys, qt[head], preferred_element_type=jnp.float32)

    keys, values = operands(0)
    k_row = lax.broadcasted_iota(jnp.int32, (2 * SPAN, 1), 0)
    k_pos = jnp.where(k_row < SPAN, span_of[0], span_of[1]) * SPAN + lax.rem(k_row, SPAN)
    hide = jnp.where(k_pos <= q_pos, 0.0, LOWEST)
    following = scores_of(keys, 0)
    for head in range(heads):
        scores = following * scale + hide
        if head + 1 < heads:
            following = scores_of(keys, head + 1)
        new_top = jnp.max(scores, axis=0, keepdims=True)
        weights = jnp.exp2(scores - new_top).astype(jnp.bfloat16)
        top[head] = new_top
        acc[head] = jnp.dot(values, weights, preferred_element_type=jnp.float32)

    @pl.loop(1, COUNT)
    def _(step):
        for block in range(1, COUNT):
            @pl.when(step == block)
            def _():
                receive(block)

        keys, values = operands(step)
        hide = [jnp.where(span_of[2 * step + half] < q_span, 0.0, LOWEST) for half in range(2)]
        following = scores_of(keys, 0)
        for head in range(heads):
            scores = [following[number * SPAN:(number + 1) * SPAN] for number in range(2)]
            if head + 1 < heads:
                following = scores_of(keys, head + 1)
            old_top = top[head]
            new_top = old_top
            for part, hidden in zip(scores, hide):
                new_top = jnp.maximum(new_top, jnp.max(part, axis=0, keepdims=True) * scale + hidden)
            factor = jnp.exp2(old_top - new_top)
            weights = jnp.concatenate([
                jnp.exp2(part * scale - (new_top - hidden)).astype(jnp.bfloat16)
                for part, hidden in zip(scores, hide)], axis=0)
            top[head] = new_top
            acc[head] = acc[head] * factor + jnp.dot(
                values, weights, preferred_element_type=jnp.float32)

    for head in range(heads):
        mixed = acc[head, :HEAD_DIM] * (1.0 / acc[head, HEAD_DIM:HEAD_DIM + 1])
        att[:, head * HEAD_DIM:(head + 1) * HEAD_DIM] = mixed.astype(jnp.bfloat16).T
    loads[11].wait()

    def sib_copy(tile, part):
        at = 0 if part == 0 else pl.ds(1, 3)
        return pltpu.make_async_remote_copy(
            src_ref=sib_out.at[tile, at], dst_ref=sib_in.at[tile, at],
            send_sem=sib_send.at[tile, part], recv_sem=sib_recv.at[tile, part],
            device_id=sibling, device_id_type=MESH)

    def project(tile):
        part = jnp.dot(att[...], w[:, tile * TILE:(tile + 1) * TILE],
                       preferred_element_type=jnp.float32).astype(jnp.bfloat16)
        part = part.reshape(4, 2, 32, TILE)
        sib_out[tile] = part[:, 1]
        sib_copy(tile, 0).start()
        sib_copy(tile, 1).start()
        own[tile] = part[:, 0]

    def both(tile, group):
        return own[tile, group].astype(jnp.float32) + sib_in[tile, group].astype(jnp.float32)

    def far_copy(tile):
        return pltpu.make_async_remote_copy(
            src_ref=far_out.at[tile], dst_ref=far_in.at[tile],
            send_sem=far_send.at[tile], recv_sem=far_recv.at[tile],
            device_id=to_next if tile < HALF else to_back, device_id_type=MESH)

    def near_copy(side, tile):
        return pltpu.make_async_remote_copy(
            src_ref=near_out.at[side, tile], dst_ref=near_in.at[side, tile],
            send_sem=near_send.at[side, tile], recv_sem=near_recv.at[side, tile],
            device_id=to_next if side == 0 else to_back, device_id_type=MESH)

    def out_copy(tile):
        at = pl.ds(tile * TILE, TILE)
        return pltpu.make_async_copy(result.at[:, at], out.at[:, at], out_sem.at[tile])

    def send_far(tile):
        sib_copy(tile, 0).wait_recv()
        far_out[tile] = both(tile, 0).astype(jnp.bfloat16)
        far_copy(tile).start()

    def send_near(side, tile):
        second = (tile < HALF) == (side == 0)
        if not second:
            sib_copy(tile, 1).wait_recv()
        total = both(tile, 1 + side)
        if second:
            far_copy(tile).wait_recv()
            total = total + far_in[tile].astype(jnp.float32)
        near_out[side, tile] = total.astype(jnp.bfloat16)
        near_copy(side, tile).start()

    def send_first(tile):
        send_far(tile)
        send_near(0 if tile >= HALF else 1, tile)

    project(ORDER[0])
    for earlier, tile in zip(ORDER, ORDER[1:]):
        project(tile)
        send_first(earlier)
    send_first(ORDER[-1])
    for tile in ORDER:
        send_near(0 if tile < HALF else 1, tile)
    for tile in ORDER:
        near_copy(0, tile).wait_recv()
        near_copy(1, tile).wait_recv()
        total = both(tile, 3) + (near_in[0, tile].astype(jnp.float32)
                                 + near_in[1, tile].astype(jnp.float32))
        result[:, tile * TILE:(tile + 1) * TILE] = total.astype(out.dtype)
        out_copy(tile).start()

    for copy in all_copies:
        copy.wait_send()
    for tile in range(TILES):
        for part in range(2):
            sib_copy(tile, part).wait_send()
            near_copy(part, tile).wait_send()
        far_copy(tile).wait_send()
        out_copy(tile).wait()


def on_device(queries, keys, values, span_order, out_weight):
    rows, width = queries.shape
    heads = width // HEAD_DIM
    d_out = out_weight.shape[1]
    bf16, f32 = jnp.bfloat16, jnp.float32
    sem = pltpu.SemaphoreType.DMA
    span_order, queries, keys, values, out_weight = (
        pltpu.with_memory_space_constraint(array, pltpu.HBM)
        for array in (span_order, queries, keys, values, out_weight))
    return pl.pallas_call(
        kernel,
        out_shape=jax.ShapeDtypeStruct((rows // 8, d_out), bf16),
        in_specs=[pl.BlockSpec(memory_space=pltpu.HBM)] * 5,
        out_specs=pl.BlockSpec(memory_space=pl.ANY),
        scratch_shapes=[
            pltpu.VMEM((rows, width), bf16),
            pltpu.VMEM((COUNT, 2, rows, HEAD_DIM), bf16),
            pltpu.VMEM((width, d_out), bf16),
            pltpu.VMEM((heads, HEAD_DIM, rows), bf16),
            pltpu.VMEM((heads, HEAD_DIM + 16, rows), f32),
            pltpu.VMEM((heads, 1, rows), f32),
            pltpu.VMEM((rows, width), bf16),
            pltpu.VMEM((TILES, 4, 32, TILE), bf16),
            pltpu.VMEM((TILES, 4, 32, TILE), bf16),
            pltpu.VMEM((TILES, 4, 32, TILE), bf16),
            pltpu.VMEM((TILES, 32, TILE), bf16),
            pltpu.VMEM((TILES, 32, TILE), bf16),
            pltpu.VMEM((2, TILES, 32, TILE), bf16),
            pltpu.VMEM((2, TILES, 32, TILE), bf16),
            pltpu.VMEM((rows // 8, d_out), bf16),
            pltpu.SMEM((2 * COUNT,), jnp.int32),
            pltpu.SMEM((2 * COUNT,), jnp.int32),
            sem((12,)), sem((COUNT - 1, 2)), sem((COUNT - 1, 2)),
            sem((TILES, 2)), sem((TILES, 2)), sem((TILES,)), sem((TILES,)),
            sem((2, TILES)), sem((2, TILES)), sem((TILES,)),
        ],
        compiler_params=pltpu.CompilerParams(
            collective_id=0, has_side_effects=True, vmem_limit_bytes=32 * 1024 * 1024),
        cost_estimate=pl.CostEstimate(
            flops=3 * 2 * rows * width * 4096, bytes_accessed=10 * 2**20,
            transcendentals=heads * rows * 4096),
    )(span_order, queries, keys, values, out_weight)


def solution(mesh):
    return jax.shard_map(
        on_device,
        mesh=mesh,
        in_specs=(
            P(("dp", "context"), "tensor"),
            P(("dp", "context"), "tensor"),
            P(("dp", "context"), "tensor"),
            P("dp"),
            P("tensor", None),
        ),
        out_specs=P(("dp", "context", "tensor"), None),
        check_vma=False,
    )
```

```python
import math

import jax
import jax.numpy as jnp
from jax import lax
from jax.experimental import pallas as pl
from jax.experimental.pallas import tpu as pltpu
from jax.sharding import PartitionSpec as P

HEAD_DIM = 128
SPAN = 128
RING = 8
COLUMNS = 2
CHIPS = 4
ROUNDS = 10
TILE = 512
TILES = 8
HALF = TILES // 2
LOWEST = -1e30
MESH = pl.DeviceIdType.MESH

UP = [(0, 1, 0), (0, 1, 1), (0, 2, 0), (0, 2, 1), (0, 3, 0), (0, 3, 1),
      (1, 3, 0), (0, 4, 0), (1, 4, 0), (1, 3, 1)]
DOWN = [(0, -1, 1), (0, -1, 0), (0, -2, 1), (0, -2, 0), (0, -3, 1), (0, -3, 0),
        (0, -4, 1), (1, -3, 1), (1, -3, 0), (1, -4, 1)]
ACROSS = [(1, 0, 0), (1, 0, 1), (1, 1, 0), (1, -1, 1), (1, 2, 0), (1, -2, 1),
          (1, -2, 0), (1, 2, 1), (1, 1, 1), (1, -1, 0)]


def plan():
    slot_of = {(0, 0, 0): 0, (0, 0, 1): 1}
    contents = [(0, 0, 0), (0, 0, 1)]
    up_slot = {r: 2 + 3 * r for r in range(ROUNDS)}
    down_slot = {r: 3 + 3 * r for r in range(ROUNDS)}
    across_slot = {r: 4 + 3 * r for r in range(ROUNDS)}
    slots = {}
    for r in range(ROUNDS):
        for table, names in ((up_slot, UP), (down_slot, DOWN), (across_slot, ACROSS)):
            slots[table[r]] = names[r]
    for slot in range(2, 2 + 3 * ROUNDS):
        column, offset, half = slots[slot]
        key = (column, offset % RING, half)
        slot_of[key] = slot
        contents.append(key)
    assert len(slot_of) == 2 + 3 * ROUNDS
    copies = []
    for r in range(ROUNDS):
        (uc, uo, uh), (dc, do, dh), (ac, ao, ah) = UP[r], DOWN[r], ACROSS[r]
        copies.append((
            ("minus", slot_of[(uc, (uo - 1) % RING, uh)], up_slot[r]),
            ("plus", slot_of[(dc, (do + 1) % RING, dh)], down_slot[r]),
            ("other", slot_of[(0, ao % RING, ah)], across_slot[r]),
        ))
    return contents, copies


CONTENTS, COPIES = plan()
SPANS = len(CONTENTS)
ORDER = tuple(part * HALF + tile for tile in range(HALF) for part in range(2))


def kernel(order_hbm, q_hbm, k_hbm, v_hbm, w_hbm, out,
           q_in, kv, w, qt, acc, top, att, own, sib_out, sib_in,
           far_out, far_in, near_out, near_in, result, order, span_of,
           load_sem, own_send, own_recv, kv_send, kv_recv, sib_send, sib_recv,
           far_send, far_recv, near_send, near_recv, out_sem):
    heads = q_in.shape[1] // HEAD_DIM
    rows = q_in.shape[0]
    context = lax.axis_index("context")
    tensor = lax.axis_index("tensor")
    y, z = context // RING, lax.rem(context, RING)
    x, core = tensor // 2, lax.rem(tensor, 2)
    ahead = 1 - 2 * core
    targets = {
        "minus": {"context": y * RING + lax.rem(z + RING - ahead, RING)},
        "plus": {"context": y * RING + lax.rem(z + RING + ahead, RING)},
        "other": {"context": (1 - y) * RING + z},
    }
    sibling = {"tensor": x * 2 + 1 - core}
    chip_next, chip_back = lax.rem(x + CHIPS + ahead, CHIPS), lax.rem(x + CHIPS - ahead, CHIPS)
    chip_far = lax.rem(x + 2, CHIPS)
    to_next, to_back = {"tensor": chip_next * 2 + core}, {"tensor": chip_back * 2 + core}

    barrier = pltpu.get_barrier_semaphore()
    for target in (*targets.values(), sibling, to_next, to_back):
        pl.semaphore_signal(barrier, inc=1, device_id=target, device_id_type=MESH)

    loads = []
    for half in range(2):
        for part, source in enumerate((k_hbm, v_hbm)):
            loads.append(pltpu.make_async_copy(
                source.at[pl.ds(half * SPAN, SPAN)], kv.at[half, part],
                load_sem.at[2 * half + part]))
    chips = ((chip_far, chip_next, chip_back, x), (chip_far, chip_back, chip_next, x))
    for group in range(4):
        for part, owner in enumerate((core, 1 - core)):
            number = 2 * group + part
            chip = chips[part][group]
            first = pl.multiple_of(chip * 64 + owner * 32, 32)
            loads.append(pltpu.make_async_copy(
                q_hbm.at[pl.ds(first, 32)], q_in.at[pl.ds(32 * number, 32)],
                load_sem.at[4 + number]))
    loads.append(pltpu.make_async_copy(order_hbm, order, load_sem.at[13]))
    loads.append(pltpu.make_async_copy(w_hbm, w, load_sem.at[12]))

    def own_copies(r):
        for name, src, dst in COPIES[r]:
            for part, source in enumerate((k_hbm, v_hbm)):
                yield pltpu.make_async_remote_copy(
                    src_ref=source.at[pl.ds(src * SPAN, SPAN)], dst_ref=kv.at[dst, part],
                    send_sem=own_send.at[dst - 2, part], recv_sem=own_recv.at[dst - 2, part],
                    device_id=targets[name], device_id_type=MESH)

    def copy_of(name, src, dst):
        return pltpu.make_async_remote_copy(
            src_ref=kv.at[src], dst_ref=kv.at[dst],
            send_sem=kv_send.at[dst - 8], recv_sem=kv_recv.at[dst - 8],
            device_id=targets[name], device_id_type=MESH)

    pl.semaphore_wait(barrier, 6)
    for copy in own_copies(0):
        copy.start()
    for load in loads:
        load.start()

    loads[12].wait()
    for slot, (column, offset, half) in enumerate(CONTENTS):
        where = (y if column == 0 else 1 - y) * RING + lax.rem(z + RING + ahead * offset, RING)
        span_of[slot] = order[2 * where + half]

    for load in loads[4:12]:
        load.wait()
    for head in range(heads):
        qt[head] = q_in[:, head * HEAD_DIM:(head + 1) * HEAD_DIM].T

    for first, second in zip(own_copies(0), own_copies(1)):
        first.wait_send()
        second.start()
    for load in loads[:4]:
        load.wait()

    lane = lax.broadcasted_iota(jnp.int32, (1, rows), 1)
    group_of = lane // 64
    mine = lax.rem(lane // 32, 2) == 0
    chip_of = jnp.where(group_of == 0, chip_far, jnp.where(group_of == 3, x, jnp.where(
        (group_of == 1) == mine, chip_next, chip_back)))
    owner_of = jnp.where(mine, core, 1 - core)
    row_of = chip_of * 64 + owner_of * 32 + lax.rem(lane, 32)
    q_span = jnp.where(row_of < SPAN, span_of[0], span_of[1])
    q_pos = q_span * SPAN + lax.rem(row_of, SPAN)

    def operands(first, count):
        spans = kv[pl.ds(first, count)]
        keys = spans[:, 0].reshape(count * SPAN, HEAD_DIM)
        values = spans[:, 1].reshape(count * SPAN, HEAD_DIM).T
        ones = jnp.ones((16, count * SPAN), jnp.bfloat16)
        return keys, jnp.concatenate([values, ones], axis=0)

    scale = math.log2(math.e) / math.sqrt(HEAD_DIM)

    def scores_of(keys, head):
        return jnp.dot(keys, qt[head], preferred_element_type=jnp.float32)

    def receive(r):
        following = COPIES[r + 2] if r + 2 < ROUNDS else ()
        here = 2 + 3 * r
        for copy in following:
            if copy[1] < here:
                copy_of(*copy).start()
        first = list(own_copies(r)) if r < 2 else ()
        for number, copy in enumerate(COPIES[r]):
            if r < 2:
                first[2 * number].wait_recv()
                first[2 * number + 1].wait_recv()
            else:
                copy_of(*copy).wait_recv()
            for later in following:
                if later[1] == copy[2]:
                    copy_of(*later).start()

    keys, values = operands(0, 2)
    k_row = lax.broadcasted_iota(jnp.int32, (2 * SPAN, 1), 0)
    k_pos = jnp.where(k_row < SPAN, span_of[0], span_of[1]) * SPAN + lax.rem(k_row, SPAN)
    hide = jnp.where(k_pos <= q_pos, 0.0, LOWEST)
    following = scores_of(keys, 0)
    for head in range(heads):
        scores = following * scale + hide
        if head + 1 < heads:
            following = scores_of(keys, head + 1)
        new_top = jnp.max(scores, axis=0, keepdims=True)
        weights = jnp.exp2(scores - new_top).astype(jnp.bfloat16)
        top[head] = new_top
        acc[head] = jnp.dot(values, weights, preferred_element_type=jnp.float32)

    @pl.loop(0, ROUNDS)
    def _(step):
        for r in range(ROUNDS):
            @pl.when(step == r)
            def _():
                receive(r)

        first = 2 + 3 * step
        keys, values = operands(first, 3)
        hide = [jnp.where(span_of[first + number] < q_span, 0.0, LOWEST) for number in range(3)]
        following = scores_of(keys, 0)
        for head in range(heads):
            scores = [following[number * SPAN:(number + 1) * SPAN] for number in range(3)]
            if head + 1 < heads:
                following = scores_of(keys, head + 1)
            old_top = top[head]
            new_top = old_top
            for part, hidden in zip(scores, hide):
                new_top = jnp.maximum(new_top, jnp.max(part, axis=0, keepdims=True) * scale + hidden)
            factor = jnp.exp2(old_top - new_top)
            weights = jnp.concatenate([
                jnp.exp2(part * scale - (new_top - hidden)).astype(jnp.bfloat16)
                for part, hidden in zip(scores, hide)], axis=0)
            top[head] = new_top
            acc[head] = acc[head] * factor + jnp.dot(
                values, weights, preferred_element_type=jnp.float32)

    for head in range(heads):
        mixed = acc[head, :HEAD_DIM] * (1.0 / acc[head, HEAD_DIM:HEAD_DIM + 1])
        att[:, head * HEAD_DIM:(head + 1) * HEAD_DIM] = mixed.astype(jnp.bfloat16).T
    loads[13].wait()

    def sib_copy(tile, part):
        at = 0 if part == 0 else pl.ds(1, 3)
        return pltpu.make_async_remote_copy(
            src_ref=sib_out.at[tile, at], dst_ref=sib_in.at[tile, at],
            send_sem=sib_send.at[tile, part], recv_sem=sib_recv.at[tile, part],
            device_id=sibling, device_id_type=MESH)

    def project(tile):
        part = jnp.dot(att[...], w[:, tile * TILE:(tile + 1) * TILE],
                       preferred_element_type=jnp.float32).astype(jnp.bfloat16)
        part = part.reshape(4, 2, 32, TILE)
        sib_out[tile] = part[:, 1]
        sib_copy(tile, 0).start()
        sib_copy(tile, 1).start()
        own[tile] = part[:, 0]

    def both(tile, group):
        return own[tile, group].astype(jnp.float32) + sib_in[tile, group].astype(jnp.float32)

    def far_copy(tile):
        return pltpu.make_async_remote_copy(
            src_ref=far_out.at[tile], dst_ref=far_in.at[tile],
            send_sem=far_send.at[tile], recv_sem=far_recv.at[tile],
            device_id=to_next if tile < HALF else to_back, device_id_type=MESH)

    def near_copy(side, tile):
        return pltpu.make_async_remote_copy(
            src_ref=near_out.at[side, tile], dst_ref=near_in.at[side, tile],
            send_sem=near_send.at[side, tile], recv_sem=near_recv.at[side, tile],
            device_id=to_next if side == 0 else to_back, device_id_type=MESH)

    def out_copy(tile):
        at = pl.ds(tile * TILE, TILE)
        return pltpu.make_async_copy(result.at[:, at], out.at[:, at], out_sem.at[tile])

    def send_far(tile):
        sib_copy(tile, 0).wait_recv()
        far_out[tile] = both(tile, 0).astype(jnp.bfloat16)
        far_copy(tile).start()

    def send_near(side, tile):
        second = (tile < HALF) == (side == 0)
        if not second:
            sib_copy(tile, 1).wait_recv()
        total = both(tile, 1 + side)
        if second:
            far_copy(tile).wait_recv()
            total = total + far_in[tile].astype(jnp.float32)
        near_out[side, tile] = total.astype(jnp.bfloat16)
        near_copy(side, tile).start()

    def send_first(tile):
        send_far(tile)
        send_near(0 if tile >= HALF else 1, tile)

    project(ORDER[0])
    for earlier, tile in zip(ORDER, ORDER[1:]):
        project(tile)
        send_first(earlier)
    send_first(ORDER[-1])
    for tile in ORDER:
        send_near(0 if tile < HALF else 1, tile)
    for copy in own_copies(1):
        copy.wait_send()
    for copies in COPIES[2:]:
        for copy in copies:
            copy_of(*copy).wait_send()
    for tile in range(TILES):
        for part in range(2):
            sib_copy(tile, part).wait_send()
        far_copy(tile).wait_send()
        near_copy(0 if tile >= HALF else 1, tile).wait_send()
    for tile in ORDER:
        near_copy(0, tile).wait_recv()
        near_copy(1, tile).wait_recv()
        total = both(tile, 3) + (near_in[0, tile].astype(jnp.float32)
                                 + near_in[1, tile].astype(jnp.float32))
        result[:, tile * TILE:(tile + 1) * TILE] = total.astype(out.dtype)
        out_copy(tile).start()

    for tile in range(TILES):
        near_copy(0 if tile < HALF else 1, tile).wait_send()
        out_copy(tile).wait()


def on_device(queries, keys, values, span_order, out_weight):
    rows, width = queries.shape
    heads = width // HEAD_DIM
    d_out = out_weight.shape[1]
    bf16, f32 = jnp.bfloat16, jnp.float32
    sem = pltpu.SemaphoreType.DMA
    span_order, queries, keys, values, out_weight = (
        pltpu.with_memory_space_constraint(array, pltpu.HBM)
        for array in (span_order, queries, keys, values, out_weight))
    return pl.pallas_call(
        kernel,
        out_shape=jax.ShapeDtypeStruct((rows // 8, d_out), bf16),
        in_specs=[pl.BlockSpec(memory_space=pltpu.HBM)] * 5,
        out_specs=pl.BlockSpec(memory_space=pl.ANY),
        scratch_shapes=[
            pltpu.VMEM((rows, width), bf16),
            pltpu.VMEM((SPANS, 2, SPAN, HEAD_DIM), bf16),
            pltpu.VMEM((width, d_out), bf16),
            pltpu.VMEM((heads, HEAD_DIM, rows), bf16),
            pltpu.VMEM((heads, HEAD_DIM + 16, rows), f32),
            pltpu.VMEM((heads, 1, rows), f32),
            pltpu.VMEM((rows, width), bf16),
            pltpu.VMEM((TILES, 4, 32, TILE), bf16),
            pltpu.VMEM((TILES, 4, 32, TILE), bf16),
            pltpu.VMEM((TILES, 4, 32, TILE), bf16),
            pltpu.VMEM((TILES, 32, TILE), bf16),
            pltpu.VMEM((TILES, 32, TILE), bf16),
            pltpu.VMEM((2, TILES, 32, TILE), bf16),
            pltpu.VMEM((2, TILES, 32, TILE), bf16),
            pltpu.VMEM((rows // 8, d_out), bf16),
            pltpu.SMEM((SPANS,), jnp.int32),
            pltpu.SMEM((SPANS,), jnp.int32),
            sem((14,)), sem((6, 2)), sem((6, 2)), sem((SPANS - 8,)), sem((SPANS - 8,)),
            sem((TILES, 2)), sem((TILES, 2)), sem((TILES,)), sem((TILES,)),
            sem((2, TILES)), sem((2, TILES)), sem((TILES,)),
        ],
        compiler_params=pltpu.CompilerParams(
            collective_id=0, has_side_effects=True, vmem_limit_bytes=32 * 1024 * 1024),
        cost_estimate=pl.CostEstimate(
            flops=3 * 2 * rows * width * 4096, bytes_accessed=10 * 2**20,
            transcendentals=heads * rows * 4096),
    )(span_order, queries, keys, values, out_weight)


def solution(mesh):
    return jax.shard_map(
        on_device,
        mesh=mesh,
        in_specs=(
            P(("dp", "context"), "tensor"),
            P(("dp", "context"), "tensor"),
            P(("dp", "context"), "tensor"),
            P("dp"),
            P("tensor", None),
        ),
        out_specs=P(("dp", "context", "tensor"), None),
        check_vma=False,
    )
```

```python
import math

import jax
import jax.numpy as jnp
from jax import lax
from jax.experimental import pallas as pl
from jax.experimental.pallas import tpu as pltpu
from jax.sharding import PartitionSpec as P

HEAD_DIM = 128
SPAN = 128
RING = 8
COLUMNS = 2
CHIPS = 4
ROUNDS = 10
TILE = 512
TILES = 8
HALF = TILES // 2
LOWEST = -1e30
MESH = pl.DeviceIdType.MESH

UP = [(0, 1, 0), (0, 1, 1), (0, 2, 0), (0, 2, 1), (0, 3, 0), (0, 3, 1),
      (1, 3, 0), (0, 4, 0), (1, 4, 0), (1, 3, 1)]
DOWN = [(0, -1, 1), (0, -1, 0), (0, -2, 1), (0, -2, 0), (0, -3, 1), (0, -3, 0),
        (0, -4, 1), (1, -3, 1), (1, -3, 0), (1, -4, 1)]
ACROSS = [(1, 0, 0), (1, 0, 1), (1, 1, 0), (1, -1, 1), (1, 2, 0), (1, -2, 1),
          (1, -2, 0), (1, 2, 1), (1, 1, 1), (1, -1, 0)]


def plan():
    slot_of = {(0, 0, 0): 0, (0, 0, 1): 1}
    contents = [(0, 0, 0), (0, 0, 1)]
    up_slot = {r: 2 + 3 * r for r in range(ROUNDS)}
    down_slot = {r: 3 + 3 * r for r in range(ROUNDS)}
    across_slot = {r: 4 + 3 * r for r in range(ROUNDS)}
    slots = {}
    for r in range(ROUNDS):
        for table, names in ((up_slot, UP), (down_slot, DOWN), (across_slot, ACROSS)):
            slots[table[r]] = names[r]
    for slot in range(2, 2 + 3 * ROUNDS):
        column, offset, half = slots[slot]
        key = (column, offset % RING, half)
        slot_of[key] = slot
        contents.append(key)
    assert len(slot_of) == 2 + 3 * ROUNDS
    copies = []
    for r in range(ROUNDS):
        (uc, uo, uh), (dc, do, dh), (ac, ao, ah) = UP[r], DOWN[r], ACROSS[r]
        copies.append((
            ("minus", slot_of[(uc, (uo - 1) % RING, uh)], up_slot[r]),
            ("plus", slot_of[(dc, (do + 1) % RING, dh)], down_slot[r]),
            ("other", slot_of[(0, ao % RING, ah)], across_slot[r]),
        ))
    return contents, copies


CONTENTS, COPIES = plan()
SPANS = len(CONTENTS)
ORDER = tuple(part * HALF + tile for tile in range(HALF) for part in range(2))


def kernel(order_hbm, q_hbm, k_hbm, v_hbm, w_hbm, out,
           q_in, kv, w, qt, acc, top, att, own, sib_out, sib_in,
           far_out, far_in, near_out, near_in, result, order, span_of,
           load_sem, own_send, own_recv, kv_send, kv_recv, sib_send, sib_recv,
           far_send, far_recv, near_send, near_recv, out_sem):
    heads = q_in.shape[1] // HEAD_DIM
    rows = q_in.shape[0]
    context = lax.axis_index("context")
    tensor = lax.axis_index("tensor")
    y, z = context // RING, lax.rem(context, RING)
    x, core = tensor // 2, lax.rem(tensor, 2)
    ahead = 1 - 2 * core
    targets = {
        "minus": {"context": y * RING + lax.rem(z + RING - ahead, RING)},
        "plus": {"context": y * RING + lax.rem(z + RING + ahead, RING)},
        "other": {"context": (1 - y) * RING + z},
    }
    sibling = {"tensor": x * 2 + 1 - core}
    chip_next, chip_back = lax.rem(x + CHIPS + ahead, CHIPS), lax.rem(x + CHIPS - ahead, CHIPS)
    chip_far = lax.rem(x + 2, CHIPS)
    to_next, to_back = {"tensor": chip_next * 2 + core}, {"tensor": chip_back * 2 + core}

    barrier = pltpu.get_barrier_semaphore()
    for target in (*targets.values(), sibling, to_next, to_back):
        pl.semaphore_signal(barrier, inc=1, device_id=target, device_id_type=MESH)

    loads = []
    for half in range(2):
        for part, source in enumerate((k_hbm, v_hbm)):
            loads.append(pltpu.make_async_copy(
                source.at[pl.ds(half * SPAN, SPAN)], kv.at[half, part],
                load_sem.at[2 * half + part]))
    chips = ((chip_far, chip_next, chip_back, x), (chip_far, chip_back, chip_next, x))
    for group in range(4):
        for part, owner in enumerate((core, 1 - core)):
            number = 2 * group + part
            chip = chips[part][group]
            first = pl.multiple_of(chip * 64 + owner * 32, 32)
            loads.append(pltpu.make_async_copy(
                q_hbm.at[pl.ds(first, 32)], q_in.at[pl.ds(32 * number, 32)],
                load_sem.at[4 + number]))
    loads.append(pltpu.make_async_copy(order_hbm, order, load_sem.at[13]))
    loads.append(pltpu.make_async_copy(w_hbm, w, load_sem.at[12]))

    def own_copies(r):
        for name, src, dst in COPIES[r]:
            for part, source in enumerate((k_hbm, v_hbm)):
                yield pltpu.make_async_remote_copy(
                    src_ref=source.at[pl.ds(src * SPAN, SPAN)], dst_ref=kv.at[dst, part],
                    send_sem=own_send.at[dst - 2, part], recv_sem=own_recv.at[dst - 2, part],
                    device_id=targets[name], device_id_type=MESH)

    def copy_of(name, src, dst):
        return pltpu.make_async_remote_copy(
            src_ref=kv.at[src], dst_ref=kv.at[dst],
            send_sem=kv_send.at[dst - 8], recv_sem=kv_recv.at[dst - 8],
            device_id=targets[name], device_id_type=MESH)

    pl.semaphore_wait(barrier, 6)
    for copy in own_copies(0):
        copy.start()
    for load in loads:
        load.start()

    loads[12].wait()
    for slot, (column, offset, half) in enumerate(CONTENTS):
        where = (y if column == 0 else 1 - y) * RING + lax.rem(z + RING + ahead * offset, RING)
        span_of[slot] = order[2 * where + half]

    for load in loads[4:12]:
        load.wait()
    for head in range(heads):
        qt[head] = q_in[:, head * HEAD_DIM:(head + 1) * HEAD_DIM].T

    for first, second in zip(own_copies(0), own_copies(1)):
        first.wait_send()
        second.start()
    for load in loads[:4]:
        load.wait()

    lane = lax.broadcasted_iota(jnp.int32, (1, rows), 1)
    group_of = lane // 64
    mine = lax.rem(lane // 32, 2) == 0
    chip_of = jnp.where(group_of == 0, chip_far, jnp.where(group_of == 3, x, jnp.where(
        (group_of == 1) == mine, chip_next, chip_back)))
    owner_of = jnp.where(mine, core, 1 - core)
    row_of = chip_of * 64 + owner_of * 32 + lax.rem(lane, 32)
    q_span = jnp.where(row_of < SPAN, span_of[0], span_of[1])
    q_pos = q_span * SPAN + lax.rem(row_of, SPAN)

    def operands(first, count):
        spans = kv[pl.ds(first, count)]
        keys = spans[:, 0].reshape(count * SPAN, HEAD_DIM)
        values = spans[:, 1].reshape(count * SPAN, HEAD_DIM).T
        ones = jnp.ones((16, count * SPAN), jnp.bfloat16)
        return keys, jnp.concatenate([values, ones], axis=0)

    scale = math.log2(math.e) / math.sqrt(HEAD_DIM)

    def scores_of(keys, head):
        return jnp.dot(keys, qt[head], preferred_element_type=jnp.float32)

    def receive(r):
        following = COPIES[r + 2] if r + 2 < ROUNDS else ()
        here = 2 + 3 * r
        for copy in following:
            if copy[1] < here:
                copy_of(*copy).start()
        first = list(own_copies(r)) if r < 2 else ()
        for number, copy in enumerate(COPIES[r]):
            if r < 2:
                first[2 * number].wait_recv()
                first[2 * number + 1].wait_recv()
            else:
                copy_of(*copy).wait_recv()
            for later in following:
                if later[1] == copy[2]:
                    copy_of(*later).start()

    keys, values = operands(0, 2)
    k_row = lax.broadcasted_iota(jnp.int32, (2 * SPAN, 1), 0)
    k_pos = jnp.where(k_row < SPAN, span_of[0], span_of[1]) * SPAN + lax.rem(k_row, SPAN)
    hide = jnp.where(k_pos <= q_pos, 0.0, LOWEST)
    following = scores_of(keys, 0)
    for head in range(heads):
        scores = following * scale + hide
        if head + 1 < heads:
            following = scores_of(keys, head + 1)
        new_top = jnp.max(scores, axis=0, keepdims=True)
        if head:
            acc[head - 1] = jnp.dot(values, weights, preferred_element_type=jnp.float32)
        weights = jnp.exp2(scores - new_top).astype(jnp.bfloat16)
        top[head] = new_top
    acc[heads - 1] = jnp.dot(values, weights, preferred_element_type=jnp.float32)

    @pl.loop(0, ROUNDS)
    def _(step):
        for r in range(ROUNDS):
            @pl.when(step == r)
            def _():
                receive(r)

        first = 2 + 3 * step
        keys, values = operands(first, 3)
        hide = [jnp.where(span_of[first + number] < q_span, 0.0, LOWEST) for number in range(3)]

        def add(head):
            acc[head] = acc[head] * factor + jnp.dot(
                values, weights, preferred_element_type=jnp.float32)

        following = scores_of(keys, 0)
        for head in range(heads):
            scores = [following[number * SPAN:(number + 1) * SPAN] for number in range(3)]
            if head + 1 < heads:
                following = scores_of(keys, head + 1)
            if head:
                add(head - 1)
            old_top = top[head]
            new_top = old_top
            for part, hidden in zip(scores, hide):
                new_top = jnp.maximum(new_top, jnp.max(part, axis=0, keepdims=True) * scale + hidden)
            factor = jnp.exp2(old_top - new_top)
            weights = jnp.concatenate([
                jnp.exp2(part * scale - (new_top - hidden)).astype(jnp.bfloat16)
                for part, hidden in zip(scores, hide)], axis=0)
            top[head] = new_top
        add(heads - 1)

    for head in range(heads):
        mixed = acc[head, :HEAD_DIM] * (1.0 / acc[head, HEAD_DIM:HEAD_DIM + 1])
        att[:, head * HEAD_DIM:(head + 1) * HEAD_DIM] = mixed.astype(jnp.bfloat16).T
    loads[13].wait()

    def sib_copy(tile, part):
        at = 0 if part == 0 else pl.ds(1, 3)
        return pltpu.make_async_remote_copy(
            src_ref=sib_out.at[tile, at], dst_ref=sib_in.at[tile, at],
            send_sem=sib_send.at[tile, part], recv_sem=sib_recv.at[tile, part],
            device_id=sibling, device_id_type=MESH)

    def project(tile):
        part = jnp.dot(att[...], w[:, tile * TILE:(tile + 1) * TILE],
                       preferred_element_type=jnp.float32).astype(jnp.bfloat16)
        part = part.reshape(4, 2, 32, TILE)
        sib_out[tile] = part[:, 1]
        sib_copy(tile, 0).start()
        sib_copy(tile, 1).start()
        own[tile] = part[:, 0]

    def both(tile, group):
        return own[tile, group].astype(jnp.float32) + sib_in[tile, group].astype(jnp.float32)

    def far_copy(tile):
        return pltpu.make_async_remote_copy(
            src_ref=far_out.at[tile], dst_ref=far_in.at[tile],
            send_sem=far_send.at[tile], recv_sem=far_recv.at[tile],
            device_id=to_next if tile < HALF else to_back, device_id_type=MESH)

    def near_copy(side, tile):
        return pltpu.make_async_remote_copy(
            src_ref=near_out.at[side, tile], dst_ref=near_in.at[side, tile],
            send_sem=near_send.at[side, tile], recv_sem=near_recv.at[side, tile],
            device_id=to_next if side == 0 else to_back, device_id_type=MESH)

    def out_copy(tile):
        at = pl.ds(tile * TILE, TILE)
        return pltpu.make_async_copy(result.at[:, at], out.at[:, at], out_sem.at[tile])

    def send_far(tile):
        sib_copy(tile, 0).wait_recv()
        far_out[tile] = both(tile, 0).astype(jnp.bfloat16)
        far_copy(tile).start()

    def send_near(side, tile):
        second = (tile < HALF) == (side == 0)
        if not second:
            sib_copy(tile, 1).wait_recv()
        total = both(tile, 1 + side)
        if second:
            far_copy(tile).wait_recv()
            total = total + far_in[tile].astype(jnp.float32)
        near_out[side, tile] = total.astype(jnp.bfloat16)
        near_copy(side, tile).start()

    def send_first(tile):
        send_far(tile)
        send_near(0 if tile >= HALF else 1, tile)

    project(ORDER[0])
    for earlier, tile in zip(ORDER, ORDER[1:]):
        project(tile)
        send_first(earlier)
    send_first(ORDER[-1])
    for tile in ORDER:
        send_near(0 if tile < HALF else 1, tile)
    for copy in own_copies(1):
        copy.wait_send()
    for copies in COPIES[2:]:
        for copy in copies:
            copy_of(*copy).wait_send()
    for tile in range(TILES):
        for part in range(2):
            sib_copy(tile, part).wait_send()
        far_copy(tile).wait_send()
        near_copy(0 if tile >= HALF else 1, tile).wait_send()
    for tile in ORDER:
        near_copy(0, tile).wait_recv()
        near_copy(1, tile).wait_recv()
        total = both(tile, 3) + (near_in[0, tile].astype(jnp.float32)
                                 + near_in[1, tile].astype(jnp.float32))
        result[:, tile * TILE:(tile + 1) * TILE] = total.astype(out.dtype)
        out_copy(tile).start()

    for tile in range(TILES):
        near_copy(0 if tile < HALF else 1, tile).wait_send()
        out_copy(tile).wait()


def on_device(queries, keys, values, span_order, out_weight):
    rows, width = queries.shape
    heads = width // HEAD_DIM
    d_out = out_weight.shape[1]
    bf16, f32 = jnp.bfloat16, jnp.float32
    sem = pltpu.SemaphoreType.DMA
    span_order, queries, keys, values, out_weight = (
        pltpu.with_memory_space_constraint(array, pltpu.HBM)
        for array in (span_order, queries, keys, values, out_weight))
    return pl.pallas_call(
        kernel,
        out_shape=jax.ShapeDtypeStruct((rows // 8, d_out), bf16),
        in_specs=[pl.BlockSpec(memory_space=pltpu.HBM)] * 5,
        out_specs=pl.BlockSpec(memory_space=pl.ANY),
        scratch_shapes=[
            pltpu.VMEM((rows, width), bf16),
            pltpu.VMEM((SPANS, 2, SPAN, HEAD_DIM), bf16),
            pltpu.VMEM((width, d_out), bf16),
            pltpu.VMEM((heads, HEAD_DIM, rows), bf16),
            pltpu.VMEM((heads, HEAD_DIM + 16, rows), f32),
            pltpu.VMEM((heads, 1, rows), f32),
            pltpu.VMEM((rows, width), bf16),
            pltpu.VMEM((TILES, 4, 32, TILE), bf16),
            pltpu.VMEM((TILES, 4, 32, TILE), bf16),
            pltpu.VMEM((TILES, 4, 32, TILE), bf16),
            pltpu.VMEM((TILES, 32, TILE), bf16),
            pltpu.VMEM((TILES, 32, TILE), bf16),
            pltpu.VMEM((2, TILES, 32, TILE), bf16),
            pltpu.VMEM((2, TILES, 32, TILE), bf16),
            pltpu.VMEM((rows // 8, d_out), bf16),
            pltpu.SMEM((SPANS,), jnp.int32),
            pltpu.SMEM((SPANS,), jnp.int32),
            sem((14,)), sem((6, 2)), sem((6, 2)), sem((SPANS - 8,)), sem((SPANS - 8,)),
            sem((TILES, 2)), sem((TILES, 2)), sem((TILES,)), sem((TILES,)),
            sem((2, TILES)), sem((2, TILES)), sem((TILES,)),
        ],
        compiler_params=pltpu.CompilerParams(
            collective_id=0, has_side_effects=True, vmem_limit_bytes=32 * 1024 * 1024),
        cost_estimate=pl.CostEstimate(
            flops=3 * 2 * rows * width * 4096, bytes_accessed=10 * 2**20,
            transcendentals=heads * rows * 4096),
    )(span_order, queries, keys, values, out_weight)


def solution(mesh):
    return jax.shard_map(
        on_device,
        mesh=mesh,
        in_specs=(
            P(("dp", "context"), "tensor"),
            P(("dp", "context"), "tensor"),
            P(("dp", "context"), "tensor"),
            P("dp"),
            P("tensor", None),
        ),
        out_specs=P(("dp", "context", "tensor"), None),
        check_vma=False,
    )
```

```python
import math

import jax
import jax.numpy as jnp
from jax import lax
from jax.experimental import pallas as pl
from jax.experimental.pallas import tpu as pltpu
from jax.sharding import PartitionSpec as P

HEAD_DIM = 128
SPAN = 128
RING = 8
COLUMNS = 2
CHIPS = 4
ROUNDS = 10
TILE = 512
TILES = 8
HALF = TILES // 2
LOWEST = -1e30
MESH = pl.DeviceIdType.MESH

UP = [(0, 1, 0), (0, 1, 1), (0, 2, 0), (0, 2, 1), (0, 3, 0), (0, 3, 1),
      (1, 3, 0), (0, 4, 0), (1, 4, 0), (1, 3, 1)]
DOWN = [(0, -1, 1), (0, -1, 0), (0, -2, 1), (0, -2, 0), (0, -3, 1), (0, -3, 0),
        (0, -4, 1), (1, -3, 1), (1, -3, 0), (1, -4, 1)]
ACROSS = [(1, 0, 0), (1, 0, 1), (1, 1, 0), (1, -1, 1), (1, 2, 0), (1, -2, 1),
          (1, -2, 0), (1, 2, 1), (1, 1, 1), (1, -1, 0)]


def plan():
    slot_of = {(0, 0, 0): 0, (0, 0, 1): 1}
    contents = [(0, 0, 0), (0, 0, 1)]
    up_slot = {r: 2 + 3 * r for r in range(ROUNDS)}
    down_slot = {r: 3 + 3 * r for r in range(ROUNDS)}
    across_slot = {r: 4 + 3 * r for r in range(ROUNDS)}
    slots = {}
    for r in range(ROUNDS):
        for table, names in ((up_slot, UP), (down_slot, DOWN), (across_slot, ACROSS)):
            slots[table[r]] = names[r]
    for slot in range(2, 2 + 3 * ROUNDS):
        column, offset, half = slots[slot]
        key = (column, offset % RING, half)
        slot_of[key] = slot
        contents.append(key)
    assert len(slot_of) == 2 + 3 * ROUNDS
    copies = []
    for r in range(ROUNDS):
        (uc, uo, uh), (dc, do, dh), (ac, ao, ah) = UP[r], DOWN[r], ACROSS[r]
        copies.append((
            ("minus", slot_of[(uc, (uo - 1) % RING, uh)], up_slot[r]),
            ("plus", slot_of[(dc, (do + 1) % RING, dh)], down_slot[r]),
            ("other", slot_of[(0, ao % RING, ah)], across_slot[r]),
        ))
    return contents, copies


CONTENTS, COPIES = plan()
SPANS = len(CONTENTS)
ORDER = tuple(part * HALF + tile for tile in range(HALF) for part in range(2))


def kernel(order_hbm, q_hbm, k_hbm, v_hbm, w_hbm, out,
           q_in, kv, w, qt, acc, top, att, own, sib_out, sib_in,
           far_out, far_in, near_out, near_in, result, order, span_of,
           load_sem, own_send, own_recv, kv_send, kv_recv, sib_send, sib_recv,
           far_send, far_recv, near_send, near_recv, out_sem):
    heads = q_in.shape[1] // HEAD_DIM
    rows = q_in.shape[0]
    context = lax.axis_index("context")
    tensor = lax.axis_index("tensor")
    y, z = context // RING, lax.rem(context, RING)
    x, core = tensor // 2, lax.rem(tensor, 2)
    ahead = 1 - 2 * core
    targets = {
        "minus": {"context": y * RING + lax.rem(z + RING - ahead, RING)},
        "plus": {"context": y * RING + lax.rem(z + RING + ahead, RING)},
        "other": {"context": (1 - y) * RING + z},
    }
    sibling = {"tensor": x * 2 + 1 - core}
    chip_next, chip_back = lax.rem(x + CHIPS + ahead, CHIPS), lax.rem(x + CHIPS - ahead, CHIPS)
    chip_far = lax.rem(x + 2, CHIPS)
    to_next, to_back = {"tensor": chip_next * 2 + core}, {"tensor": chip_back * 2 + core}

    barrier = pltpu.get_barrier_semaphore()
    for target in (*targets.values(), sibling, to_next, to_back):
        pl.semaphore_signal(barrier, inc=1, device_id=target, device_id_type=MESH)

    loads = []
    for half in range(2):
        for part, source in enumerate((k_hbm, v_hbm)):
            loads.append(pltpu.make_async_copy(
                source.at[pl.ds(half * SPAN, SPAN)], kv.at[half, part],
                load_sem.at[2 * half + part]))
    chips = ((chip_far, chip_next, chip_back, x), (chip_far, chip_back, chip_next, x))
    for group in range(4):
        for part, owner in enumerate((core, 1 - core)):
            number = 2 * group + part
            chip = chips[part][group]
            first = pl.multiple_of(chip * 64 + owner * 32, 32)
            loads.append(pltpu.make_async_copy(
                q_hbm.at[pl.ds(first, 32)], q_in.at[pl.ds(32 * number, 32)],
                load_sem.at[4 + number]))
    loads.append(pltpu.make_async_copy(order_hbm, order, load_sem.at[13]))
    loads.append(pltpu.make_async_copy(w_hbm, w, load_sem.at[12]))

    def own_copies(r):
        for name, src, dst in COPIES[r]:
            for part, source in enumerate((k_hbm, v_hbm)):
                yield pltpu.make_async_remote_copy(
                    src_ref=source.at[pl.ds(src * SPAN, SPAN)], dst_ref=kv.at[dst, part],
                    send_sem=own_send.at[dst - 2, part], recv_sem=own_recv.at[dst - 2, part],
                    device_id=targets[name], device_id_type=MESH)

    def copy_of(name, src, dst):
        return pltpu.make_async_remote_copy(
            src_ref=kv.at[src], dst_ref=kv.at[dst],
            send_sem=kv_send.at[dst - 8], recv_sem=kv_recv.at[dst - 8],
            device_id=targets[name], device_id_type=MESH)

    pl.semaphore_wait(barrier, 6)
    for copy in own_copies(0):
        copy.start()
    for load in loads:
        load.start()

    loads[12].wait()
    for slot, (column, offset, half) in enumerate(CONTENTS):
        where = (y if column == 0 else 1 - y) * RING + lax.rem(z + RING + ahead * offset, RING)
        span_of[slot] = order[2 * where + half]

    for load in loads[4:12]:
        load.wait()
    for head in range(heads):
        qt[head] = q_in[:, head * HEAD_DIM:(head + 1) * HEAD_DIM].T

    for first, second in zip(own_copies(0), own_copies(1)):
        first.wait_send()
        second.start()
    for load in loads[:4]:
        load.wait()

    lane = lax.broadcasted_iota(jnp.int32, (1, rows), 1)
    group_of = lane // 64
    mine = lax.rem(lane // 32, 2) == 0
    chip_of = jnp.where(group_of == 0, chip_far, jnp.where(group_of == 3, x, jnp.where(
        (group_of == 1) == mine, chip_next, chip_back)))
    owner_of = jnp.where(mine, core, 1 - core)
    row_of = chip_of * 64 + owner_of * 32 + lax.rem(lane, 32)
    q_span = jnp.where(row_of < SPAN, span_of[0], span_of[1])
    q_pos = q_span * SPAN + lax.rem(row_of, SPAN)

    def operands(first, count):
        spans = kv[pl.ds(first, count)]
        keys = spans[:, 0].reshape(count * SPAN, HEAD_DIM)
        values = spans[:, 1].reshape(count * SPAN, HEAD_DIM).T
        ones = jnp.ones((16, count * SPAN), jnp.bfloat16)
        return keys, jnp.concatenate([values, ones], axis=0)

    scale = math.log2(math.e) / math.sqrt(HEAD_DIM)

    def scores_of(keys, head):
        return jnp.dot(keys, qt[head], preferred_element_type=jnp.float32)

    def receive(r):
        following = COPIES[r + 2] if r + 2 < ROUNDS else ()
        here = 2 + 3 * r
        for copy in following:
            if copy[1] < here:
                copy_of(*copy).start()
        first = list(own_copies(r)) if r < 2 else ()
        for number, copy in enumerate(COPIES[r]):
            if r < 2:
                first[2 * number].wait_recv()
                first[2 * number + 1].wait_recv()
            else:
                copy_of(*copy).wait_recv()
            for later in following:
                if later[1] == copy[2]:
                    copy_of(*later).start()

    keys, values = operands(0, 2)
    k_row = lax.broadcasted_iota(jnp.int32, (2 * SPAN, 1), 0)
    k_pos = jnp.where(k_row < SPAN, span_of[0], span_of[1]) * SPAN + lax.rem(k_row, SPAN)
    hide = jnp.where(k_pos <= q_pos, 0.0, LOWEST)
    following = scores_of(keys, 0)
    for head in range(heads):
        scores = following * scale + hide
        if head + 1 < heads:
            following = scores_of(keys, head + 1)
        new_top = jnp.max(scores, axis=0, keepdims=True)
        weights = jnp.exp2(scores - new_top).astype(jnp.bfloat16)
        top[head] = new_top
        acc[head] = jnp.dot(values, weights, preferred_element_type=jnp.float32)

    @pl.loop(0, ROUNDS)
    def _(step):
        for r in range(ROUNDS):
            @pl.when(step == r)
            def _():
                receive(r)

        first = 2 + 3 * step
        keys, values = operands(first, 3)
        hide = [jnp.where(span_of[first + number] < q_span, 0.0, LOWEST) for number in range(3)]
        following = scores_of(keys, 0)
        for head in range(heads):
            scores = [following[number * SPAN:(number + 1) * SPAN] for number in range(3)]
            if head + 1 < heads:
                following = scores_of(keys, head + 1)
            old_top = top[head]
            new_top = old_top
            for part, hidden in zip(scores, hide):
                new_top = jnp.maximum(new_top, jnp.max(part, axis=0, keepdims=True) * scale + hidden)
            factor = jnp.exp2(old_top - new_top)
            weights = jnp.concatenate([
                jnp.exp2(part * scale - (new_top - hidden)).astype(jnp.bfloat16)
                for part, hidden in zip(scores, hide)], axis=0)
            top[head] = new_top
            acc[head] = acc[head] * factor + jnp.dot(
                values, weights, preferred_element_type=jnp.float32)

    for head in range(heads):
        mixed = acc[head, :HEAD_DIM] * (1.0 / acc[head, HEAD_DIM:HEAD_DIM + 1])
        att[:, head * HEAD_DIM:(head + 1) * HEAD_DIM] = mixed.astype(jnp.bfloat16).T
    loads[13].wait()

    def sib_copy(tile, part):
        at = 0 if part == 0 else pl.ds(1, 2)
        return pltpu.make_async_remote_copy(
            src_ref=sib_out.at[tile, at], dst_ref=sib_in.at[tile, at],
            send_sem=sib_send.at[tile, part], recv_sem=sib_recv.at[tile, part],
            device_id=sibling, device_id_type=MESH)

    def home_copy():
        return pltpu.make_async_remote_copy(
            src_ref=sib_out.at[:, 3], dst_ref=sib_in.at[:, 3],
            send_sem=sib_send.at[TILES, 0], recv_sem=sib_recv.at[TILES, 0],
            device_id=sibling, device_id_type=MESH)

    def project(tile):
        part = jnp.dot(att[...], w[:, tile * TILE:(tile + 1) * TILE],
                       preferred_element_type=jnp.float32).astype(jnp.bfloat16)
        part = part.reshape(4, 2, 32, TILE)
        sib_out[tile] = part[:, 1]
        sib_copy(tile, 0).start()
        sib_copy(tile, 1).start()
        own[tile] = part[:, 0]

    def both(tile, group):
        return own[tile, group].astype(jnp.float32) + sib_in[tile, group].astype(jnp.float32)

    def far_copy(tile):
        return pltpu.make_async_remote_copy(
            src_ref=far_out.at[tile], dst_ref=far_in.at[tile],
            send_sem=far_send.at[tile], recv_sem=far_recv.at[tile],
            device_id=to_next if tile < HALF else to_back, device_id_type=MESH)

    def near_copy(side, tile):
        return pltpu.make_async_remote_copy(
            src_ref=near_out.at[side, tile], dst_ref=near_in.at[side, tile],
            send_sem=near_send.at[side, tile], recv_sem=near_recv.at[side, tile],
            device_id=to_next if side == 0 else to_back, device_id_type=MESH)

    def out_copy(tile):
        at = pl.ds(tile * TILE, TILE)
        return pltpu.make_async_copy(result.at[:, at], out.at[:, at], out_sem.at[tile])

    def send_far(tile):
        sib_copy(tile, 0).wait_recv()
        far_out[tile] = both(tile, 0).astype(jnp.bfloat16)
        far_copy(tile).start()

    def send_near(side, tile):
        second = (tile < HALF) == (side == 0)
        if not second:
            sib_copy(tile, 1).wait_recv()
        total = both(tile, 1 + side)
        if second:
            far_copy(tile).wait_recv()
            total = total + far_in[tile].astype(jnp.float32)
        near_out[side, tile] = total.astype(jnp.bfloat16)
        near_copy(side, tile).start()

    def send_first(tile):
        send_far(tile)
        send_near(0 if tile >= HALF else 1, tile)

    project(ORDER[0])
    for earlier, tile in zip(ORDER, ORDER[1:]):
        project(tile)
        send_first(earlier)
    send_first(ORDER[-1])
    home_copy().start()
    for tile in ORDER:
        send_near(0 if tile < HALF else 1, tile)
    for copy in own_copies(1):
        copy.wait_send()
    for copies in COPIES[2:]:
        for copy in copies:
            copy_of(*copy).wait_send()
    for tile in range(TILES):
        for part in range(2):
            sib_copy(tile, part).wait_send()
        far_copy(tile).wait_send()
        near_copy(0 if tile >= HALF else 1, tile).wait_send()
    home_copy().wait()
    for tile in ORDER:
        near_copy(0, tile).wait_recv()
        near_copy(1, tile).wait_recv()
        total = both(tile, 3) + (near_in[0, tile].astype(jnp.float32)
                                 + near_in[1, tile].astype(jnp.float32))
        result[:, tile * TILE:(tile + 1) * TILE] = total.astype(out.dtype)
        out_copy(tile).start()

    for tile in range(TILES):
        near_copy(0 if tile < HALF else 1, tile).wait_send()
        out_copy(tile).wait()


def on_device(queries, keys, values, span_order, out_weight):
    rows, width = queries.shape
    heads = width // HEAD_DIM
    d_out = out_weight.shape[1]
    bf16, f32 = jnp.bfloat16, jnp.float32
    sem = pltpu.SemaphoreType.DMA
    span_order, queries, keys, values, out_weight = (
        pltpu.with_memory_space_constraint(array, pltpu.HBM)
        for array in (span_order, queries, keys, values, out_weight))
    return pl.pallas_call(
        kernel,
        out_shape=jax.ShapeDtypeStruct((rows // 8, d_out), bf16),
        in_specs=[pl.BlockSpec(memory_space=pltpu.HBM)] * 5,
        out_specs=pl.BlockSpec(memory_space=pl.ANY),
        scratch_shapes=[
            pltpu.VMEM((rows, width), bf16),
            pltpu.VMEM((SPANS, 2, SPAN, HEAD_DIM), bf16),
            pltpu.VMEM((width, d_out), bf16),
            pltpu.VMEM((heads, HEAD_DIM, rows), bf16),
            pltpu.VMEM((heads, HEAD_DIM + 16, rows), f32),
            pltpu.VMEM((heads, 1, rows), f32),
            pltpu.VMEM((rows, width), bf16),
            pltpu.VMEM((TILES, 4, 32, TILE), bf16),
            pltpu.VMEM((TILES, 4, 32, TILE), bf16),
            pltpu.VMEM((TILES, 4, 32, TILE), bf16),
            pltpu.VMEM((TILES, 32, TILE), bf16),
            pltpu.VMEM((TILES, 32, TILE), bf16),
            pltpu.VMEM((2, TILES, 32, TILE), bf16),
            pltpu.VMEM((2, TILES, 32, TILE), bf16),
            pltpu.VMEM((rows // 8, d_out), bf16),
            pltpu.SMEM((SPANS,), jnp.int32),
            pltpu.SMEM((SPANS,), jnp.int32),
            sem((14,)), sem((6, 2)), sem((6, 2)), sem((SPANS - 8,)), sem((SPANS - 8,)),
            sem((TILES + 1, 2)), sem((TILES + 1, 2)), sem((TILES,)), sem((TILES,)),
            sem((2, TILES)), sem((2, TILES)), sem((TILES,)),
        ],
        compiler_params=pltpu.CompilerParams(
            collective_id=0, has_side_effects=True, vmem_limit_bytes=32 * 1024 * 1024),
        cost_estimate=pl.CostEstimate(
            flops=3 * 2 * rows * width * 4096, bytes_accessed=10 * 2**20,
            transcendentals=heads * rows * 4096),
    )(span_order, queries, keys, values, out_weight)


def solution(mesh):
    return jax.shard_map(
        on_device,
        mesh=mesh,
        in_specs=(
            P(("dp", "context"), "tensor"),
            P(("dp", "context"), "tensor"),
            P(("dp", "context"), "tensor"),
            P("dp"),
            P("tensor", None),
        ),
        out_specs=P(("dp", "context", "tensor"), None),
        check_vma=False,
    )
```

```python
import math

import jax
import jax.numpy as jnp
from jax import lax
from jax.experimental import pallas as pl
from jax.experimental.pallas import tpu as pltpu
from jax.sharding import PartitionSpec as P

HEAD_DIM = 128
SPAN = 128
RING = 8
COLUMNS = 2
CHIPS = 4
ROUNDS = 10
TILE = 512
TILES = 8
HALF = TILES // 2
LOWEST = -1e30
MESH = pl.DeviceIdType.MESH

UP = [(0, 1, 0), (0, 1, 1), (0, 2, 0), (0, 2, 1), (0, 3, 0), (0, 3, 1),
      (1, 3, 0), (0, 4, 0), (1, 4, 0), (1, 3, 1)]
DOWN = [(0, -1, 1), (0, -1, 0), (0, -2, 1), (0, -2, 0), (0, -3, 1), (0, -3, 0),
        (0, -4, 1), (1, -3, 1), (1, -3, 0), (1, -4, 1)]
ACROSS = [(1, 0, 0), (1, 0, 1), (1, 1, 0), (1, -1, 1), (1, 2, 0), (1, -2, 1),
          (1, -2, 0), (1, 2, 1), (1, 1, 1), (1, -1, 0)]


def plan():
    slot_of = {(0, 0, 0): 0, (0, 0, 1): 1}
    contents = [(0, 0, 0), (0, 0, 1)]
    up_slot = {r: 2 + 3 * r for r in range(ROUNDS)}
    down_slot = {r: 3 + 3 * r for r in range(ROUNDS)}
    across_slot = {r: 4 + 3 * r for r in range(ROUNDS)}
    slots = {}
    for r in range(ROUNDS):
        for table, names in ((up_slot, UP), (down_slot, DOWN), (across_slot, ACROSS)):
            slots[table[r]] = names[r]
    for slot in range(2, 2 + 3 * ROUNDS):
        column, offset, half = slots[slot]
        key = (column, offset % RING, half)
        slot_of[key] = slot
        contents.append(key)
    assert len(slot_of) == 2 + 3 * ROUNDS
    copies = []
    for r in range(ROUNDS):
        (uc, uo, uh), (dc, do, dh), (ac, ao, ah) = UP[r], DOWN[r], ACROSS[r]
        copies.append((
            ("minus", slot_of[(uc, (uo - 1) % RING, uh)], up_slot[r]),
            ("plus", slot_of[(dc, (do + 1) % RING, dh)], down_slot[r]),
            ("other", slot_of[(0, ao % RING, ah)], across_slot[r]),
        ))
    return contents, copies


CONTENTS, COPIES = plan()
SPANS = len(CONTENTS)
ORDER = tuple(part * HALF + tile for tile in range(HALF) for part in range(2))


def kernel(order_hbm, q_hbm, k_hbm, v_hbm, w_hbm, out,
           q_in, kv, w, qt, acc, top, sums, att, own, sib_out, sib_in,
           far_out, far_in, near_out, near_in, result, order, span_of,
           load_sem, own_send, own_recv, kv_send, kv_recv, sib_send, sib_recv,
           far_send, far_recv, near_send, near_recv, out_sem):
    heads = q_in.shape[1] // HEAD_DIM
    rows = q_in.shape[0]
    context = lax.axis_index("context")
    tensor = lax.axis_index("tensor")
    y, z = context // RING, lax.rem(context, RING)
    x, core = tensor // 2, lax.rem(tensor, 2)
    ahead = 1 - 2 * core
    targets = {
        "minus": {"context": y * RING + lax.rem(z + RING - ahead, RING)},
        "plus": {"context": y * RING + lax.rem(z + RING + ahead, RING)},
        "other": {"context": (1 - y) * RING + z},
    }
    sibling = {"tensor": x * 2 + 1 - core}
    chip_next, chip_back = lax.rem(x + CHIPS + ahead, CHIPS), lax.rem(x + CHIPS - ahead, CHIPS)
    chip_far = lax.rem(x + 2, CHIPS)
    to_next, to_back = {"tensor": chip_next * 2 + core}, {"tensor": chip_back * 2 + core}

    barrier = pltpu.get_barrier_semaphore()
    for target in (*targets.values(), sibling, to_next, to_back):
        pl.semaphore_signal(barrier, inc=1, device_id=target, device_id_type=MESH)

    loads = []
    for half in range(2):
        for part, source in enumerate((k_hbm, v_hbm)):
            loads.append(pltpu.make_async_copy(
                source.at[pl.ds(half * SPAN, SPAN)], kv.at[half, part],
                load_sem.at[2 * half + part]))
    chips = ((chip_far, chip_next, chip_back, x), (chip_far, chip_back, chip_next, x))
    for group in range(4):
        for part, owner in enumerate((core, 1 - core)):
            number = 2 * group + part
            chip = chips[part][group]
            first = pl.multiple_of(chip * 64 + owner * 32, 32)
            loads.append(pltpu.make_async_copy(
                q_hbm.at[pl.ds(first, 32)], q_in.at[pl.ds(32 * number, 32)],
                load_sem.at[4 + number]))
    loads.append(pltpu.make_async_copy(order_hbm, order, load_sem.at[13]))
    loads.append(pltpu.make_async_copy(w_hbm, w, load_sem.at[12]))

    def own_copies(r):
        for name, src, dst in COPIES[r]:
            for part, source in enumerate((k_hbm, v_hbm)):
                yield pltpu.make_async_remote_copy(
                    src_ref=source.at[pl.ds(src * SPAN, SPAN)], dst_ref=kv.at[dst, part],
                    send_sem=own_send.at[dst - 2, part], recv_sem=own_recv.at[dst - 2, part],
                    device_id=targets[name], device_id_type=MESH)

    def copy_of(name, src, dst):
        return pltpu.make_async_remote_copy(
            src_ref=kv.at[src], dst_ref=kv.at[dst],
            send_sem=kv_send.at[dst - 8], recv_sem=kv_recv.at[dst - 8],
            device_id=targets[name], device_id_type=MESH)

    pl.semaphore_wait(barrier, 6)
    for copy in own_copies(0):
        copy.start()
    for load in loads:
        load.start()

    loads[12].wait()
    for slot, (column, offset, half) in enumerate(CONTENTS):
        where = (y if column == 0 else 1 - y) * RING + lax.rem(z + RING + ahead * offset, RING)
        span_of[slot] = order[2 * where + half]

    for load in loads[4:12]:
        load.wait()
    for head in range(heads):
        qt[head] = q_in[:, head * HEAD_DIM:(head + 1) * HEAD_DIM].T

    for first, second in zip(own_copies(0), own_copies(1)):
        first.wait_send()
        second.start()
    for load in loads[:4]:
        load.wait()

    lane = lax.broadcasted_iota(jnp.int32, (1, rows), 1)
    group_of = lane // 64
    mine = lax.rem(lane // 32, 2) == 0
    chip_of = jnp.where(group_of == 0, chip_far, jnp.where(group_of == 3, x, jnp.where(
        (group_of == 1) == mine, chip_next, chip_back)))
    owner_of = jnp.where(mine, core, 1 - core)
    row_of = chip_of * 64 + owner_of * 32 + lax.rem(lane, 32)
    q_span = jnp.where(row_of < SPAN, span_of[0], span_of[1])
    q_pos = q_span * SPAN + lax.rem(row_of, SPAN)

    def operands(first, count):
        spans = kv[pl.ds(first, count)]
        keys = spans[:, 0].reshape(count * SPAN, HEAD_DIM)
        return keys, spans[:, 1].reshape(count * SPAN, HEAD_DIM).T

    scale = math.log2(math.e) / math.sqrt(HEAD_DIM)

    def scores_of(keys, head):
        return jnp.dot(keys, qt[head], preferred_element_type=jnp.float32)

    def receive(r):
        following = COPIES[r + 2] if r + 2 < ROUNDS else ()
        here = 2 + 3 * r
        for copy in following:
            if copy[1] < here:
                copy_of(*copy).start()
        first = list(own_copies(r)) if r < 2 else ()
        for number, copy in enumerate(COPIES[r]):
            if r < 2:
                first[2 * number].wait_recv()
                first[2 * number + 1].wait_recv()
            else:
                copy_of(*copy).wait_recv()
            for later in following:
                if later[1] == copy[2]:
                    copy_of(*later).start()

    keys, values = operands(0, 2)
    k_row = lax.broadcasted_iota(jnp.int32, (2 * SPAN, 1), 0)
    k_pos = jnp.where(k_row < SPAN, span_of[0], span_of[1]) * SPAN + lax.rem(k_row, SPAN)
    hide = jnp.where(k_pos <= q_pos, 0.0, LOWEST)
    following = scores_of(keys, 0)
    for head in range(heads):
        scores = following * scale + hide
        if head + 1 < heads:
            following = scores_of(keys, head + 1)
        new_top = jnp.max(scores, axis=0, keepdims=True)
        weights = jnp.exp2(scores - new_top)
        top[head] = new_top
        sums[head] = jnp.sum(weights, axis=0, keepdims=True)
        acc[head] = jnp.dot(values, weights.astype(jnp.bfloat16), preferred_element_type=jnp.float32)

    @pl.loop(0, ROUNDS)
    def _(step):
        for r in range(ROUNDS):
            @pl.when(step == r)
            def _():
                receive(r)

        first = 2 + 3 * step
        keys, values = operands(first, 3)
        hide = [jnp.where(span_of[first + number] < q_span, 0.0, LOWEST) for number in range(3)]
        following = scores_of(keys, 0)
        for head in range(heads):
            scores = [following[number * SPAN:(number + 1) * SPAN] for number in range(3)]
            if head + 1 < heads:
                following = scores_of(keys, head + 1)
            old_top = top[head]
            new_top = old_top
            for part, hidden in zip(scores, hide):
                new_top = jnp.maximum(new_top, jnp.max(part, axis=0, keepdims=True) * scale + hidden)
            factor = jnp.exp2(old_top - new_top)
            weights = [jnp.exp2(part * scale - (new_top - hidden))
                       for part, hidden in zip(scores, hide)]
            top[head] = new_top
            sums[head] = sums[head] * factor + jnp.sum(
                weights[0] + weights[1] + weights[2], axis=0, keepdims=True)
            weights = jnp.concatenate([part.astype(jnp.bfloat16) for part in weights], axis=0)
            acc[head] = acc[head] * factor + jnp.dot(
                values, weights, preferred_element_type=jnp.float32)

    for head in range(heads):
        mixed = acc[head] * (1.0 / sums[head])
        att[:, head * HEAD_DIM:(head + 1) * HEAD_DIM] = mixed.astype(jnp.bfloat16).T
    loads[13].wait()

    def sib_copy(tile, part):
        at = 0 if part == 0 else pl.ds(1, 2)
        return pltpu.make_async_remote_copy(
            src_ref=sib_out.at[tile, at], dst_ref=sib_in.at[tile, at],
            send_sem=sib_send.at[tile, part], recv_sem=sib_recv.at[tile, part],
            device_id=sibling, device_id_type=MESH)

    def home_copy():
        return pltpu.make_async_remote_copy(
            src_ref=sib_out.at[:, 3], dst_ref=sib_in.at[:, 3],
            send_sem=sib_send.at[TILES, 0], recv_sem=sib_recv.at[TILES, 0],
            device_id=sibling, device_id_type=MESH)

    def project(tile):
        part = jnp.dot(att[...], w[:, tile * TILE:(tile + 1) * TILE],
                       preferred_element_type=jnp.float32).astype(jnp.bfloat16)
        part = part.reshape(4, 2, 32, TILE)
        sib_out[tile] = part[:, 1]
        sib_copy(tile, 0).start()
        sib_copy(tile, 1).start()
        own[tile] = part[:, 0]

    def both(tile, group):
        return own[tile, group].astype(jnp.float32) + sib_in[tile, group].astype(jnp.float32)

    def far_copy(tile):
        return pltpu.make_async_remote_copy(
            src_ref=far_out.at[tile], dst_ref=far_in.at[tile],
            send_sem=far_send.at[tile], recv_sem=far_recv.at[tile],
            device_id=to_next if tile < HALF else to_back, device_id_type=MESH)

    def near_copy(side, tile):
        return pltpu.make_async_remote_copy(
            src_ref=near_out.at[side, tile], dst_ref=near_in.at[side, tile],
            send_sem=near_send.at[side, tile], recv_sem=near_recv.at[side, tile],
            device_id=to_next if side == 0 else to_back, device_id_type=MESH)

    def out_copy(tile):
        at = pl.ds(tile * TILE, TILE)
        return pltpu.make_async_copy(result.at[:, at], out.at[:, at], out_sem.at[tile])

    def send_far(tile):
        sib_copy(tile, 0).wait_recv()
        far_out[tile] = both(tile, 0).astype(jnp.bfloat16)
        far_copy(tile).start()

    def send_near(side, tile):
        second = (tile < HALF) == (side == 0)
        if not second:
            sib_copy(tile, 1).wait_recv()
        total = both(tile, 1 + side)
        if second:
            far_copy(tile).wait_recv()
            total = total + far_in[tile].astype(jnp.float32)
        near_out[side, tile] = total.astype(jnp.bfloat16)
        near_copy(side, tile).start()

    def send_first(tile):
        send_far(tile)
        send_near(0 if tile >= HALF else 1, tile)

    project(ORDER[0])
    for earlier, tile in zip(ORDER, ORDER[1:]):
        project(tile)
        send_first(earlier)
    send_first(ORDER[-1])
    home_copy().start()
    for tile in ORDER:
        send_near(0 if tile < HALF else 1, tile)
    for copy in own_copies(1):
        copy.wait_send()
    for copies in COPIES[2:]:
        for copy in copies:
            copy_of(*copy).wait_send()
    for tile in range(TILES):
        for part in range(2):
            sib_copy(tile, part).wait_send()
        far_copy(tile).wait_send()
        near_copy(0 if tile >= HALF else 1, tile).wait_send()
    home_copy().wait()
    for tile in ORDER:
        near_copy(0, tile).wait_recv()
        near_copy(1, tile).wait_recv()
        total = both(tile, 3) + (near_in[0, tile].astype(jnp.float32)
                                 + near_in[1, tile].astype(jnp.float32))
        result[:, tile * TILE:(tile + 1) * TILE] = total.astype(out.dtype)
        out_copy(tile).start()

    for tile in range(TILES):
        near_copy(0 if tile < HALF else 1, tile).wait_send()
        out_copy(tile).wait()


def on_device(queries, keys, values, span_order, out_weight):
    rows, width = queries.shape
    heads = width // HEAD_DIM
    d_out = out_weight.shape[1]
    bf16, f32 = jnp.bfloat16, jnp.float32
    sem = pltpu.SemaphoreType.DMA
    span_order, queries, keys, values, out_weight = (
        pltpu.with_memory_space_constraint(array, pltpu.HBM)
        for array in (span_order, queries, keys, values, out_weight))
    return pl.pallas_call(
        kernel,
        out_shape=jax.ShapeDtypeStruct((rows // 8, d_out), bf16),
        in_specs=[pl.BlockSpec(memory_space=pltpu.HBM)] * 5,
        out_specs=pl.BlockSpec(memory_space=pl.ANY),
        scratch_shapes=[
            pltpu.VMEM((rows, width), bf16),
            pltpu.VMEM((SPANS, 2, SPAN, HEAD_DIM), bf16),
            pltpu.VMEM((width, d_out), bf16),
            pltpu.VMEM((heads, HEAD_DIM, rows), bf16),
            pltpu.VMEM((heads, HEAD_DIM, rows), f32),
            pltpu.VMEM((heads, 1, rows), f32),
            pltpu.VMEM((heads, 1, rows), f32),
            pltpu.VMEM((rows, width), bf16),
            pltpu.VMEM((TILES, 4, 32, TILE), bf16),
            pltpu.VMEM((TILES, 4, 32, TILE), bf16),
            pltpu.VMEM((TILES, 4, 32, TILE), bf16),
            pltpu.VMEM((TILES, 32, TILE), bf16),
            pltpu.VMEM((TILES, 32, TILE), bf16),
            pltpu.VMEM((2, TILES, 32, TILE), bf16),
            pltpu.VMEM((2, TILES, 32, TILE), bf16),
            pltpu.VMEM((rows // 8, d_out), bf16),
            pltpu.SMEM((SPANS,), jnp.int32),
            pltpu.SMEM((SPANS,), jnp.int32),
            sem((14,)), sem((6, 2)), sem((6, 2)), sem((SPANS - 8,)), sem((SPANS - 8,)),
            sem((TILES + 1, 2)), sem((TILES + 1, 2)), sem((TILES,)), sem((TILES,)),
            sem((2, TILES)), sem((2, TILES)), sem((TILES,)),
        ],
        compiler_params=pltpu.CompilerParams(
            collective_id=0, has_side_effects=True, vmem_limit_bytes=32 * 1024 * 1024),
        cost_estimate=pl.CostEstimate(
            flops=3 * 2 * rows * width * 4096, bytes_accessed=10 * 2**20,
            transcendentals=heads * rows * 4096),
    )(span_order, queries, keys, values, out_weight)


def solution(mesh):
    return jax.shard_map(
        on_device,
        mesh=mesh,
        in_specs=(
            P(("dp", "context"), "tensor"),
            P(("dp", "context"), "tensor"),
            P(("dp", "context"), "tensor"),
            P("dp"),
            P("tensor", None),
        ),
        out_specs=P(("dp", "context", "tensor"), None),
        check_vma=False,
    )
```

```python
import math

import jax
import jax.numpy as jnp
from jax import lax
from jax.experimental import pallas as pl
from jax.experimental.pallas import tpu as pltpu
from jax.sharding import PartitionSpec as P

HEAD_DIM = 128
SPAN = 128
RING = 8
COLUMNS = 2
CHIPS = 4
ROUNDS = 10
TILE = 256
TILES = 16
HALF = TILES // 2
LOWEST = -1e30
MESH = pl.DeviceIdType.MESH

UP = [(0, 1, 0), (0, 1, 1), (0, 2, 0), (0, 2, 1), (0, 3, 0), (0, 3, 1),
      (1, 3, 0), (0, 4, 0), (1, 4, 0), (1, 3, 1)]
DOWN = [(0, -1, 1), (0, -1, 0), (0, -2, 1), (0, -2, 0), (0, -3, 1), (0, -3, 0),
        (0, -4, 1), (1, -3, 1), (1, -3, 0), (1, -4, 1)]
ACROSS = [(1, 0, 0), (1, 0, 1), (1, 1, 0), (1, -1, 1), (1, 2, 0), (1, -2, 1),
          (1, -2, 0), (1, 2, 1), (1, 1, 1), (1, -1, 0)]


def plan():
    slot_of = {(0, 0, 0): 0, (0, 0, 1): 1}
    contents = [(0, 0, 0), (0, 0, 1)]
    up_slot = {r: 2 + 3 * r for r in range(ROUNDS)}
    down_slot = {r: 3 + 3 * r for r in range(ROUNDS)}
    across_slot = {r: 4 + 3 * r for r in range(ROUNDS)}
    slots = {}
    for r in range(ROUNDS):
        for table, names in ((up_slot, UP), (down_slot, DOWN), (across_slot, ACROSS)):
            slots[table[r]] = names[r]
    for slot in range(2, 2 + 3 * ROUNDS):
        column, offset, half = slots[slot]
        key = (column, offset % RING, half)
        slot_of[key] = slot
        contents.append(key)
    assert len(slot_of) == 2 + 3 * ROUNDS
    copies = []
    for r in range(ROUNDS):
        (uc, uo, uh), (dc, do, dh), (ac, ao, ah) = UP[r], DOWN[r], ACROSS[r]
        copies.append((
            ("minus", slot_of[(uc, (uo - 1) % RING, uh)], up_slot[r]),
            ("plus", slot_of[(dc, (do + 1) % RING, dh)], down_slot[r]),
            ("other", slot_of[(0, ao % RING, ah)], across_slot[r]),
        ))
    return contents, copies


CONTENTS, COPIES = plan()
SPANS = len(CONTENTS)
ORDER = tuple(part * HALF + tile for tile in range(HALF) for part in range(2))


def kernel(order_hbm, q_hbm, k_hbm, v_hbm, w_hbm, out,
           q_in, kv, w, qt, acc, top, att, own, sib_out, sib_in,
           far_out, far_in, near_out, near_in, result, order, span_of,
           load_sem, own_send, own_recv, kv_send, kv_recv, sib_send, sib_recv,
           far_send, far_recv, near_send, near_recv, out_sem):
    heads = q_in.shape[1] // HEAD_DIM
    rows = q_in.shape[0]
    context = lax.axis_index("context")
    tensor = lax.axis_index("tensor")
    y, z = context // RING, lax.rem(context, RING)
    x, core = tensor // 2, lax.rem(tensor, 2)
    ahead = 1 - 2 * core
    targets = {
        "minus": {"context": y * RING + lax.rem(z + RING - ahead, RING)},
        "plus": {"context": y * RING + lax.rem(z + RING + ahead, RING)},
        "other": {"context": (1 - y) * RING + z},
    }
    sibling = {"tensor": x * 2 + 1 - core}
    chip_next, chip_back = lax.rem(x + CHIPS + ahead, CHIPS), lax.rem(x + CHIPS - ahead, CHIPS)
    chip_far = lax.rem(x + 2, CHIPS)
    to_next, to_back = {"tensor": chip_next * 2 + core}, {"tensor": chip_back * 2 + core}

    barrier = pltpu.get_barrier_semaphore()
    for target in (*targets.values(), sibling, to_next, to_back):
        pl.semaphore_signal(barrier, inc=1, device_id=target, device_id_type=MESH)

    loads = []
    for half in range(2):
        for part, source in enumerate((k_hbm, v_hbm)):
            loads.append(pltpu.make_async_copy(
                source.at[pl.ds(half * SPAN, SPAN)], kv.at[half, part],
                load_sem.at[2 * half + part]))
    chips = ((chip_far, chip_next, chip_back, x), (chip_far, chip_back, chip_next, x))
    for group in range(4):
        for part, owner in enumerate((core, 1 - core)):
            number = 2 * group + part
            chip = chips[part][group]
            first = pl.multiple_of(chip * 64 + owner * 32, 32)
            loads.append(pltpu.make_async_copy(
                q_hbm.at[pl.ds(first, 32)], q_in.at[pl.ds(32 * number, 32)],
                load_sem.at[4 + number]))
    loads.append(pltpu.make_async_copy(order_hbm, order, load_sem.at[13]))
    loads.append(pltpu.make_async_copy(w_hbm, w, load_sem.at[12]))

    def own_copies(r):
        for name, src, dst in COPIES[r]:
            for part, source in enumerate((k_hbm, v_hbm)):
                yield pltpu.make_async_remote_copy(
                    src_ref=source.at[pl.ds(src * SPAN, SPAN)], dst_ref=kv.at[dst, part],
                    send_sem=own_send.at[dst - 2, part], recv_sem=own_recv.at[dst - 2, part],
                    device_id=targets[name], device_id_type=MESH)

    def copy_of(name, src, dst):
        return pltpu.make_async_remote_copy(
            src_ref=kv.at[src], dst_ref=kv.at[dst],
            send_sem=kv_send.at[dst - 8], recv_sem=kv_recv.at[dst - 8],
            device_id=targets[name], device_id_type=MESH)

    pl.semaphore_wait(barrier, 6)
    for copy in own_copies(0):
        copy.start()
    for load in loads:
        load.start()

    loads[12].wait()
    for slot, (column, offset, half) in enumerate(CONTENTS):
        where = (y if column == 0 else 1 - y) * RING + lax.rem(z + RING + ahead * offset, RING)
        span_of[slot] = order[2 * where + half]

    for load in loads[4:12]:
        load.wait()
    for head in range(heads):
        qt[head] = q_in[:, head * HEAD_DIM:(head + 1) * HEAD_DIM].T

    for first, second in zip(own_copies(0), own_copies(1)):
        first.wait_send()
        second.start()
    for load in loads[:4]:
        load.wait()

    lane = lax.broadcasted_iota(jnp.int32, (1, rows), 1)
    group_of = lane // 64
    mine = lax.rem(lane // 32, 2) == 0
    chip_of = jnp.where(group_of == 0, chip_far, jnp.where(group_of == 3, x, jnp.where(
        (group_of == 1) == mine, chip_next, chip_back)))
    owner_of = jnp.where(mine, core, 1 - core)
    row_of = chip_of * 64 + owner_of * 32 + lax.rem(lane, 32)
    q_span = jnp.where(row_of < SPAN, span_of[0], span_of[1])
    q_pos = q_span * SPAN + lax.rem(row_of, SPAN)

    def operands(first, count):
        spans = kv[pl.ds(first, count)]
        keys = spans[:, 0].reshape(count * SPAN, HEAD_DIM)
        values = spans[:, 1].reshape(count * SPAN, HEAD_DIM).T
        ones = jnp.ones((16, count * SPAN), jnp.bfloat16)
        return keys, jnp.concatenate([values, ones], axis=0)

    scale = math.log2(math.e) / math.sqrt(HEAD_DIM)

    def scores_of(keys, head):
        return jnp.dot(keys, qt[head], preferred_element_type=jnp.float32)

    def receive(r):
        following = COPIES[r + 2] if r + 2 < ROUNDS else ()
        here = 2 + 3 * r
        for copy in following:
            if copy[1] < here:
                copy_of(*copy).start()
        first = list(own_copies(r)) if r < 2 else ()
        for number, copy in enumerate(COPIES[r]):
            if r < 2:
                first[2 * number].wait_recv()
                first[2 * number + 1].wait_recv()
            else:
                copy_of(*copy).wait_recv()
            for later in following:
                if later[1] == copy[2]:
                    copy_of(*later).start()

    keys, values = operands(0, 2)
    k_row = lax.broadcasted_iota(jnp.int32, (2 * SPAN, 1), 0)
    k_pos = jnp.where(k_row < SPAN, span_of[0], span_of[1]) * SPAN + lax.rem(k_row, SPAN)
    hide = jnp.where(k_pos <= q_pos, 0.0, LOWEST)
    following = scores_of(keys, 0)
    for head in range(heads):
        scores = following * scale + hide
        if head + 1 < heads:
            following = scores_of(keys, head + 1)
        new_top = jnp.max(scores, axis=0, keepdims=True)
        weights = jnp.exp2(scores - new_top).astype(jnp.bfloat16)
        top[head] = new_top
        acc[head] = jnp.dot(values, weights, preferred_element_type=jnp.float32)

    @pl.loop(0, ROUNDS)
    def _(step):
        for r in range(ROUNDS):
            @pl.when(step == r)
            def _():
                receive(r)

        first = 2 + 3 * step
        keys, values = operands(first, 3)
        hide = [jnp.where(span_of[first + number] < q_span, 0.0, LOWEST) for number in range(3)]
        following = scores_of(keys, 0)
        for head in range(heads):
            scores = [following[number * SPAN:(number + 1) * SPAN] for number in range(3)]
            if head + 1 < heads:
                following = scores_of(keys, head + 1)
            old_top = top[head]
            new_top = old_top
            for part, hidden in zip(scores, hide):
                new_top = jnp.maximum(new_top, jnp.max(part, axis=0, keepdims=True) * scale + hidden)
            factor = jnp.exp2(old_top - new_top)
            weights = jnp.concatenate([
                jnp.exp2(part * scale - (new_top - hidden)).astype(jnp.bfloat16)
                for part, hidden in zip(scores, hide)], axis=0)
            top[head] = new_top
            acc[head] = acc[head] * factor + jnp.dot(
                values, weights, preferred_element_type=jnp.float32)

    for head in range(heads):
        mixed = acc[head, :HEAD_DIM] * (1.0 / acc[head, HEAD_DIM:HEAD_DIM + 1])
        att[:, head * HEAD_DIM:(head + 1) * HEAD_DIM] = mixed.astype(jnp.bfloat16).T
    loads[13].wait()

    def sib_copy(tile, part):
        at = 0 if part == 0 else pl.ds(1, 2)
        return pltpu.make_async_remote_copy(
            src_ref=sib_out.at[tile, at], dst_ref=sib_in.at[tile, at],
            send_sem=sib_send.at[tile, part], recv_sem=sib_recv.at[tile, part],
            device_id=sibling, device_id_type=MESH)

    def home_copy():
        return pltpu.make_async_remote_copy(
            src_ref=sib_out.at[:, 3], dst_ref=sib_in.at[:, 3],
            send_sem=sib_send.at[TILES, 0], recv_sem=sib_recv.at[TILES, 0],
            device_id=sibling, device_id_type=MESH)

    def project(tile):
        part = jnp.dot(att[...], w[:, tile * TILE:(tile + 1) * TILE],
                       preferred_element_type=jnp.float32).astype(jnp.bfloat16)
        part = part.reshape(4, 2, 32, TILE)
        sib_out[tile] = part[:, 1]
        sib_copy(tile, 0).start()
        sib_copy(tile, 1).start()
        own[tile] = part[:, 0]

    def both(tile, group):
        return own[tile, group].astype(jnp.float32) + sib_in[tile, group].astype(jnp.float32)

    def far_copy(tile):
        return pltpu.make_async_remote_copy(
            src_ref=far_out.at[tile], dst_ref=far_in.at[tile],
            send_sem=far_send.at[tile], recv_sem=far_recv.at[tile],
            device_id=to_next if tile < HALF else to_back, device_id_type=MESH)

    def near_copy(side, tile):
        return pltpu.make_async_remote_copy(
            src_ref=near_out.at[side, tile], dst_ref=near_in.at[side, tile],
            send_sem=near_send.at[side, tile], recv_sem=near_recv.at[side, tile],
            device_id=to_next if side == 0 else to_back, device_id_type=MESH)

    def out_copy(tile):
        at = pl.ds(tile * TILE, TILE)
        return pltpu.make_async_copy(result.at[:, at], out.at[:, at], out_sem.at[tile])

    def send_far(tile):
        sib_copy(tile, 0).wait_recv()
        far_out[tile] = both(tile, 0).astype(jnp.bfloat16)
        far_copy(tile).start()

    def send_near(side, tile):
        second = (tile < HALF) == (side == 0)
        if not second:
            sib_copy(tile, 1).wait_recv()
        total = both(tile, 1 + side)
        if second:
            far_copy(tile).wait_recv()
            total = total + far_in[tile].astype(jnp.float32)
        near_out[side, tile] = total.astype(jnp.bfloat16)
        near_copy(side, tile).start()

    def send_first(tile):
        send_far(tile)
        send_near(0 if tile >= HALF else 1, tile)

    project(ORDER[0])
    for earlier, tile in zip(ORDER, ORDER[1:]):
        project(tile)
        send_first(earlier)
    send_first(ORDER[-1])
    home_copy().start()
    for tile in ORDER:
        send_near(0 if tile < HALF else 1, tile)
    for copy in own_copies(1):
        copy.wait_send()
    for copies in COPIES[2:]:
        for copy in copies:
            copy_of(*copy).wait_send()
    for tile in range(TILES):
        for part in range(2):
            sib_copy(tile, part).wait_send()
        far_copy(tile).wait_send()
        near_copy(0 if tile >= HALF else 1, tile).wait_send()
    home_copy().wait()
    for tile in ORDER:
        near_copy(0, tile).wait_recv()
        near_copy(1, tile).wait_recv()
        total = both(tile, 3) + (near_in[0, tile].astype(jnp.float32)
                                 + near_in[1, tile].astype(jnp.float32))
        result[:, tile * TILE:(tile + 1) * TILE] = total.astype(out.dtype)
        out_copy(tile).start()

    for tile in range(TILES):
        near_copy(0 if tile < HALF else 1, tile).wait_send()
        out_copy(tile).wait()


def on_device(queries, keys, values, span_order, out_weight):
    rows, width = queries.shape
    heads = width // HEAD_DIM
    d_out = out_weight.shape[1]
    bf16, f32 = jnp.bfloat16, jnp.float32
    sem = pltpu.SemaphoreType.DMA
    span_order, queries, keys, values, out_weight = (
        pltpu.with_memory_space_constraint(array, pltpu.HBM)
        for array in (span_order, queries, keys, values, out_weight))
    return pl.pallas_call(
        kernel,
        out_shape=jax.ShapeDtypeStruct((rows // 8, d_out), bf16),
        in_specs=[pl.BlockSpec(memory_space=pltpu.HBM)] * 5,
        out_specs=pl.BlockSpec(memory_space=pl.ANY),
        scratch_shapes=[
            pltpu.VMEM((rows, width), bf16),
            pltpu.VMEM((SPANS, 2, SPAN, HEAD_DIM), bf16),
            pltpu.VMEM((width, d_out), bf16),
            pltpu.VMEM((heads, HEAD_DIM, rows), bf16),
            pltpu.VMEM((heads, HEAD_DIM + 16, rows), f32),
            pltpu.VMEM((heads, 1, rows), f32),
            pltpu.VMEM((rows, width), bf16),
            pltpu.VMEM((TILES, 4, 32, TILE), bf16),
            pltpu.VMEM((TILES, 4, 32, TILE), bf16),
            pltpu.VMEM((TILES, 4, 32, TILE), bf16),
            pltpu.VMEM((TILES, 32, TILE), bf16),
            pltpu.VMEM((TILES, 32, TILE), bf16),
            pltpu.VMEM((2, TILES, 32, TILE), bf16),
            pltpu.VMEM((2, TILES, 32, TILE), bf16),
            pltpu.VMEM((rows // 8, d_out), bf16),
            pltpu.SMEM((SPANS,), jnp.int32),
            pltpu.SMEM((SPANS,), jnp.int32),
            sem((14,)), sem((6, 2)), sem((6, 2)), sem((SPANS - 8,)), sem((SPANS - 8,)),
            sem((TILES + 1, 2)), sem((TILES + 1, 2)), sem((TILES,)), sem((TILES,)),
            sem((2, TILES)), sem((2, TILES)), sem((TILES,)),
        ],
        compiler_params=pltpu.CompilerParams(
            collective_id=0, has_side_effects=True, vmem_limit_bytes=32 * 1024 * 1024),
        cost_estimate=pl.CostEstimate(
            flops=3 * 2 * rows * width * 4096, bytes_accessed=10 * 2**20,
            transcendentals=heads * rows * 4096),
    )(span_order, queries, keys, values, out_weight)


def solution(mesh):
    return jax.shard_map(
        on_device,
        mesh=mesh,
        in_specs=(
            P(("dp", "context"), "tensor"),
            P(("dp", "context"), "tensor"),
            P(("dp", "context"), "tensor"),
            P("dp"),
            P("tensor", None),
        ),
        out_specs=P(("dp", "context", "tensor"), None),
        check_vma=False,
    )
```

```python
import math

import jax
import jax.numpy as jnp
from jax import lax
from jax.experimental import pallas as pl
from jax.experimental.pallas import tpu as pltpu
from jax.sharding import PartitionSpec as P

HEAD_DIM = 128
SPAN = 128
RING = 8
COLUMNS = 2
CHIPS = 4
ROUNDS = 10
TILE = 512
TILES = 8
HALF = TILES // 2
LOWEST = -1e30
MESH = pl.DeviceIdType.MESH

UP = [(0, 1, 0), (0, 1, 1), (0, 2, 0), (0, 2, 1), (0, 3, 0), (0, 3, 1),
      (1, 3, 0), (0, 4, 0), (1, 4, 0), (1, 3, 1)]
DOWN = [(0, -1, 1), (0, -1, 0), (0, -2, 1), (0, -2, 0), (0, -3, 1), (0, -3, 0),
        (0, -4, 1), (1, -3, 1), (1, -3, 0), (1, -4, 1)]
ACROSS = [(1, 0, 0), (1, 0, 1), (1, 1, 0), (1, -1, 1), (1, 2, 0), (1, -2, 1),
          (1, -2, 0), (1, 2, 1), (1, 1, 1), (1, -1, 0)]


def plan():
    slot_of = {(0, 0, 0): 0, (0, 0, 1): 1}
    contents = [(0, 0, 0), (0, 0, 1)]
    up_slot = {r: 2 + 3 * r for r in range(ROUNDS)}
    down_slot = {r: 3 + 3 * r for r in range(ROUNDS)}
    across_slot = {r: 4 + 3 * r for r in range(ROUNDS)}
    slots = {}
    for r in range(ROUNDS):
        for table, names in ((up_slot, UP), (down_slot, DOWN), (across_slot, ACROSS)):
            slots[table[r]] = names[r]
    for slot in range(2, 2 + 3 * ROUNDS):
        column, offset, half = slots[slot]
        key = (column, offset % RING, half)
        slot_of[key] = slot
        contents.append(key)
    assert len(slot_of) == 2 + 3 * ROUNDS
    copies = []
    for r in range(ROUNDS):
        (uc, uo, uh), (dc, do, dh), (ac, ao, ah) = UP[r], DOWN[r], ACROSS[r]
        copies.append((
            ("minus", slot_of[(uc, (uo - 1) % RING, uh)], up_slot[r]),
            ("plus", slot_of[(dc, (do + 1) % RING, dh)], down_slot[r]),
            ("other", slot_of[(0, ao % RING, ah)], across_slot[r]),
        ))
    return contents, copies


CONTENTS, COPIES = plan()
SPANS = len(CONTENTS)
PAIRED = (0, 4, 2, 6)
ORDER = tuple(part * HALF + tile for tile in range(HALF) for part in range(2))


def kernel(order_hbm, q_hbm, k_hbm, v_hbm, w_hbm, out,
           q_in, kv, w, qt, acc, top, att, own, sib_out, sib_in,
           far_out, far_in, near_out, near_in, result, order, span_of,
           load_sem, kv_send, kv_recv, sib_send, sib_recv,
           far_send, far_recv, near_send, near_recv, out_sem):
    heads = q_in.shape[1] // HEAD_DIM
    rows = q_in.shape[0]
    context = lax.axis_index("context")
    tensor = lax.axis_index("tensor")
    y, z = context // RING, lax.rem(context, RING)
    x, core = tensor // 2, lax.rem(tensor, 2)
    ahead = 1 - 2 * core
    targets = {
        "minus": {"context": y * RING + lax.rem(z + RING - ahead, RING)},
        "plus": {"context": y * RING + lax.rem(z + RING + ahead, RING)},
        "other": {"context": (1 - y) * RING + z},
    }
    sibling = {"tensor": x * 2 + 1 - core}
    chip_next, chip_back = lax.rem(x + CHIPS + ahead, CHIPS), lax.rem(x + CHIPS - ahead, CHIPS)
    chip_far = lax.rem(x + 2, CHIPS)
    to_next, to_back = {"tensor": chip_next * 2 + core}, {"tensor": chip_back * 2 + core}

    barrier = pltpu.get_barrier_semaphore()
    for target in (*targets.values(), sibling, to_next, to_back):
        pl.semaphore_signal(barrier, inc=1, device_id=target, device_id_type=MESH)

    loads = []
    for half in range(2):
        for part, source in enumerate((k_hbm, v_hbm)):
            loads.append(pltpu.make_async_copy(
                source.at[pl.ds(half * SPAN, SPAN)], kv.at[half, part],
                load_sem.at[2 * half + part]))
    chips = ((chip_far, chip_next, chip_back, x), (chip_far, chip_back, chip_next, x))
    for group in range(4):
        for part, owner in enumerate((core, 1 - core)):
            number = 2 * group + part
            chip = chips[part][group]
            first = pl.multiple_of(chip * 64 + owner * 32, 32)
            loads.append(pltpu.make_async_copy(
                q_hbm.at[pl.ds(first, 32)], q_in.at[pl.ds(32 * number, 32)],
                load_sem.at[4 + number]))
    loads.append(pltpu.make_async_copy(order_hbm, order, load_sem.at[13]))
    loads.append(pltpu.make_async_copy(w_hbm, w, load_sem.at[12]))

    def own_copies(r):
        for name, src, dst in COPIES[r]:
            for part, source in enumerate((k_hbm, v_hbm)):
                yield pltpu.make_async_remote_copy(
                    src_ref=source.at[pl.ds(src * SPAN, SPAN)], dst_ref=kv.at[dst, part],
                    send_sem=kv_send.at[r], recv_sem=kv_recv.at[r],
                    device_id=targets[name], device_id_type=MESH)

    def copy_of(r, name, src, dst):
        return pltpu.make_async_remote_copy(
            src_ref=kv.at[src], dst_ref=kv.at[dst],
            send_sem=kv_send.at[r], recv_sem=kv_recv.at[r],
            device_id=targets[name], device_id_type=MESH)

    def whole(r):
        spans = kv.at[pl.ds(2 + 3 * r, 3)]
        return pltpu.make_async_remote_copy(
            src_ref=spans, dst_ref=spans, send_sem=kv_send.at[r], recv_sem=kv_recv.at[r],
            device_id=targets["other"], device_id_type=MESH)

    pl.semaphore_wait(barrier, 6)
    for copy in own_copies(0):
        copy.start()
    for load in loads:
        load.start()

    loads[12].wait()
    for slot, (column, offset, half) in enumerate(CONTENTS):
        where = (y if column == 0 else 1 - y) * RING + lax.rem(z + RING + ahead * offset, RING)
        span_of[slot] = order[2 * where + half]

    for load in loads[4:12]:
        load.wait()
    for head in range(heads):
        qt[head] = q_in[:, head * HEAD_DIM:(head + 1) * HEAD_DIM].T

    whole(0).wait_send()
    for copy in own_copies(1):
        copy.start()
    for load in loads[:4]:
        load.wait()

    lane = lax.broadcasted_iota(jnp.int32, (1, rows), 1)
    group_of = lane // 64
    mine = lax.rem(lane // 32, 2) == 0
    chip_of = jnp.where(group_of == 0, chip_far, jnp.where(group_of == 3, x, jnp.where(
        (group_of == 1) == mine, chip_next, chip_back)))
    owner_of = jnp.where(mine, core, 1 - core)
    row_of = chip_of * 64 + owner_of * 32 + lax.rem(lane, 32)
    q_span = jnp.where(row_of < SPAN, span_of[0], span_of[1])
    q_pos = q_span * SPAN + lax.rem(row_of, SPAN)

    def operands(first, count):
        spans = kv[pl.ds(first, count)]
        keys = spans[:, 0].reshape(count * SPAN, HEAD_DIM)
        values = spans[:, 1].reshape(count * SPAN, HEAD_DIM).T
        ones = jnp.ones((16, count * SPAN), jnp.bfloat16)
        return keys, jnp.concatenate([values, ones], axis=0)

    scale = math.log2(math.e) / math.sqrt(HEAD_DIM)

    def scores_of(keys, head):
        return jnp.dot(keys, qt[head], preferred_element_type=jnp.float32)

    def receive(r):
        following = COPIES[r + 2] if r + 2 < ROUNDS else ()
        here = 2 + 3 * r
        for copy in following:
            if copy[1] < here:
                copy_of(r + 2, *copy).start()
        whole(r).wait_recv()
        for copy in following:
            if copy[1] >= here:
                copy_of(r + 2, *copy).start()

    keys, values = operands(0, 2)
    k_row = lax.broadcasted_iota(jnp.int32, (2 * SPAN, 1), 0)
    k_pos = jnp.where(k_row < SPAN, span_of[0], span_of[1]) * SPAN + lax.rem(k_row, SPAN)
    hide = jnp.where(k_pos <= q_pos, 0.0, LOWEST)
    following = scores_of(keys, 0)
    for head in range(heads):
        scores = following * scale + hide
        if head + 1 < heads:
            following = scores_of(keys, head + 1)
        new_top = jnp.max(scores, axis=0, keepdims=True)
        weights = jnp.exp2(scores - new_top).astype(jnp.bfloat16)
        top[head] = new_top
        acc[head] = jnp.dot(values, weights, preferred_element_type=jnp.float32)

    @pl.loop(0, ROUNDS)
    def _(step):
        for r in range(ROUNDS):
            @pl.when(step == r)
            def _():
                receive(r)

        first = 2 + 3 * step
        keys, values = operands(first, 3)
        hide = [jnp.where(span_of[first + number] < q_span, 0.0, LOWEST) for number in range(3)]
        following = scores_of(keys, 0)
        for head in range(heads):
            scores = [following[number * SPAN:(number + 1) * SPAN] for number in range(3)]
            if head + 1 < heads:
                following = scores_of(keys, head + 1)
            old_top = top[head]
            new_top = old_top
            for part, hidden in zip(scores, hide):
                new_top = jnp.maximum(new_top, jnp.max(part, axis=0, keepdims=True) * scale + hidden)
            factor = jnp.exp2(old_top - new_top)
            weights = jnp.concatenate([
                jnp.exp2(part * scale - (new_top - hidden)).astype(jnp.bfloat16)
                for part, hidden in zip(scores, hide)], axis=0)
            top[head] = new_top
            acc[head] = acc[head] * factor + jnp.dot(
                values, weights, preferred_element_type=jnp.float32)

    for head in range(heads):
        mixed = acc[head, :HEAD_DIM] * (1.0 / acc[head, HEAD_DIM:HEAD_DIM + 1])
        att[:, head * HEAD_DIM:(head + 1) * HEAD_DIM] = mixed.astype(jnp.bfloat16).T
    loads[13].wait()

    def sib_copy(tile):
        at = pl.ds(0, 3)
        return pltpu.make_async_remote_copy(
            src_ref=sib_out.at[tile, at], dst_ref=sib_in.at[tile, at],
            send_sem=sib_send.at[tile], recv_sem=sib_recv.at[tile],
            device_id=sibling, device_id_type=MESH)

    def home_copy():
        return pltpu.make_async_remote_copy(
            src_ref=sib_out.at[:, 3], dst_ref=sib_in.at[:, 3],
            send_sem=sib_send.at[TILES], recv_sem=sib_recv.at[TILES],
            device_id=sibling, device_id_type=MESH)

    def project(tile):
        part = jnp.dot(att[...], w[:, tile * TILE:(tile + 1) * TILE],
                       preferred_element_type=jnp.float32).astype(jnp.bfloat16)
        part = part.reshape(4, 2, 32, TILE)
        sib_out[tile] = part[:, 1]
        sib_copy(tile).start()
        own[tile] = part[:, 0]

    def both(tile, group):
        return own[tile, group].astype(jnp.float32) + sib_in[tile, group].astype(jnp.float32)

    def far_copy(tile):
        return pltpu.make_async_remote_copy(
            src_ref=far_out.at[tile], dst_ref=far_in.at[tile],
            send_sem=far_send.at[tile], recv_sem=far_recv.at[tile],
            device_id=to_next if tile < HALF else to_back, device_id_type=MESH)

    def near_copy(side, tile, count):
        at = pl.ds(tile, count)
        return pltpu.make_async_remote_copy(
            src_ref=near_out.at[side, at], dst_ref=near_in.at[side, at],
            send_sem=near_send.at[side, tile], recv_sem=near_recv.at[side, tile],
            device_id=to_next if side == 0 else to_back, device_id_type=MESH)

    def out_copy(tile):
        at = pl.ds(tile * TILE, TILE)
        return pltpu.make_async_copy(result.at[:, at], out.at[:, at], out_sem.at[tile])

    def first_side(tile):
        return 0 if tile >= HALF else 1

    def send_first(tile):
        sib_copy(tile).wait_recv()
        far_out[tile] = both(tile, 0).astype(jnp.bfloat16)
        far_copy(tile).start()
        side = first_side(tile)
        near_out[side, tile] = both(tile, 1 + side).astype(jnp.bfloat16)
        near_copy(side, tile, 1).start()

    def send_second(tile):
        side = 1 - first_side(tile)
        for one in (tile, tile + 1):
            far_copy(one).wait_recv()
            total = both(one, 1 + side) + far_in[one].astype(jnp.float32)
            near_out[side, one] = total.astype(jnp.bfloat16)
        near_copy(side, tile, 2).start()

    project(ORDER[0])
    for earlier, tile in zip(ORDER, ORDER[1:]):
        project(tile)
        send_first(earlier)
    send_first(ORDER[-1])
    home_copy().start()
    for tile in PAIRED:
        send_second(tile)
    for r in range(1, ROUNDS):
        whole(r).wait_send()
    for tile in range(TILES):
        sib_copy(tile).wait_send()
        far_copy(tile).wait_send()
        near_copy(first_side(tile), tile, 1).wait_send()
    home_copy().wait()
    for pair in PAIRED:
        near_copy(1 - first_side(pair), pair, 2).wait_recv()
        for tile in (pair, pair + 1):
            near_copy(first_side(tile), tile, 1).wait_recv()
            total = both(tile, 3) + (near_in[0, tile].astype(jnp.float32)
                                     + near_in[1, tile].astype(jnp.float32))
            result[:, tile * TILE:(tile + 1) * TILE] = total.astype(out.dtype)
            out_copy(tile).start()

    for pair in PAIRED:
        near_copy(1 - first_side(pair), pair, 2).wait_send()
        for tile in (pair, pair + 1):
            out_copy(tile).wait()


def on_device(queries, keys, values, span_order, out_weight):
    rows, width = queries.shape
    heads = width // HEAD_DIM
    d_out = out_weight.shape[1]
    bf16, f32 = jnp.bfloat16, jnp.float32
    sem = pltpu.SemaphoreType.DMA
    span_order, queries, keys, values, out_weight = (
        pltpu.with_memory_space_constraint(array, pltpu.HBM)
        for array in (span_order, queries, keys, values, out_weight))
    return pl.pallas_call(
        kernel,
        out_shape=jax.ShapeDtypeStruct((rows // 8, d_out), bf16),
        in_specs=[pl.BlockSpec(memory_space=pltpu.HBM)] * 5,
        out_specs=pl.BlockSpec(memory_space=pl.ANY),
        scratch_shapes=[
            pltpu.VMEM((rows, width), bf16),
            pltpu.VMEM((SPANS, 2, SPAN, HEAD_DIM), bf16),
            pltpu.VMEM((width, d_out), bf16),
            pltpu.VMEM((heads, HEAD_DIM, rows), bf16),
            pltpu.VMEM((heads, HEAD_DIM + 16, rows), f32),
            pltpu.VMEM((heads, 1, rows), f32),
            pltpu.VMEM((rows, width), bf16),
            pltpu.VMEM((TILES, 4, 32, TILE), bf16),
            pltpu.VMEM((TILES, 4, 32, TILE), bf16),
            pltpu.VMEM((TILES, 4, 32, TILE), bf16),
            pltpu.VMEM((TILES, 32, TILE), bf16),
            pltpu.VMEM((TILES, 32, TILE), bf16),
            pltpu.VMEM((2, TILES, 32, TILE), bf16),
            pltpu.VMEM((2, TILES, 32, TILE), bf16),
            pltpu.VMEM((rows // 8, d_out), bf16),
            pltpu.SMEM((SPANS,), jnp.int32),
            pltpu.SMEM((SPANS,), jnp.int32),
            sem((14,)), sem((ROUNDS,)), sem((ROUNDS,)),
            sem((TILES + 1,)), sem((TILES + 1,)), sem((TILES,)), sem((TILES,)),
            sem((2, TILES)), sem((2, TILES)), sem((TILES,)),
        ],
        compiler_params=pltpu.CompilerParams(
            collective_id=0, has_side_effects=True, vmem_limit_bytes=32 * 1024 * 1024),
        cost_estimate=pl.CostEstimate(
            flops=3 * 2 * rows * width * 4096, bytes_accessed=10 * 2**20,
            transcendentals=heads * rows * 4096),
    )(span_order, queries, keys, values, out_weight)


def solution(mesh):
    return jax.shard_map(
        on_device,
        mesh=mesh,
        in_specs=(
            P(("dp", "context"), "tensor"),
            P(("dp", "context"), "tensor"),
            P(("dp", "context"), "tensor"),
            P("dp"),
            P("tensor", None),
        ),
        out_specs=P(("dp", "context", "tensor"), None),
        check_vma=False,
    )
```

```python
import math

import jax
import jax.numpy as jnp
from jax import lax
from jax.experimental import pallas as pl
from jax.experimental.pallas import tpu as pltpu
from jax.sharding import PartitionSpec as P

HEAD_DIM = 128
SPAN = 128
RING = 8
COLUMNS = 2
CHIPS = 4
ROUNDS = 10
TILE = 512
TILES = 8
HALF = TILES // 2
LOWEST = -1e30
MESH = pl.DeviceIdType.MESH

UP = [(0, 1, 0), (0, 1, 1), (0, 2, 0), (0, 2, 1), (0, 3, 0), (0, 3, 1),
      (1, 3, 0), (0, 4, 0), (1, 4, 0), (1, 3, 1)]
DOWN = [(0, -1, 1), (0, -1, 0), (0, -2, 1), (0, -2, 0), (0, -3, 1), (0, -3, 0),
        (0, -4, 1), (1, -3, 1), (1, -3, 0), (1, -4, 1)]
ACROSS = [(1, 0, 0), (1, 0, 1), (1, 1, 0), (1, -1, 1), (1, 2, 0), (1, -2, 1),
          (1, -2, 0), (1, 2, 1), (1, 1, 1), (1, -1, 0)]


def plan():
    slot_of = {(0, 0, 0): 0, (0, 0, 1): 1}
    contents = [(0, 0, 0), (0, 0, 1)]
    up_slot = {r: 2 + 3 * r for r in range(ROUNDS)}
    down_slot = {r: 3 + 3 * r for r in range(ROUNDS)}
    across_slot = {r: 4 + 3 * r for r in range(ROUNDS)}
    slots = {}
    for r in range(ROUNDS):
        for table, names in ((up_slot, UP), (down_slot, DOWN), (across_slot, ACROSS)):
            slots[table[r]] = names[r]
    for slot in range(2, 2 + 3 * ROUNDS):
        column, offset, half = slots[slot]
        key = (column, offset % RING, half)
        slot_of[key] = slot
        contents.append(key)
    assert len(slot_of) == 2 + 3 * ROUNDS
    copies = []
    for r in range(ROUNDS):
        (uc, uo, uh), (dc, do, dh), (ac, ao, ah) = UP[r], DOWN[r], ACROSS[r]
        copies.append((
            ("minus", slot_of[(uc, (uo - 1) % RING, uh)], up_slot[r]),
            ("plus", slot_of[(dc, (do + 1) % RING, dh)], down_slot[r]),
            ("other", slot_of[(0, ao % RING, ah)], across_slot[r]),
        ))
    return contents, copies


CONTENTS, COPIES = plan()
SPANS = len(CONTENTS)
PAIRED = (0, 4, 2, 6)
ORDER = tuple(part * HALF + tile for tile in range(HALF) for part in range(2))


def kernel(order_hbm, q_hbm, k_hbm, v_hbm, w_hbm, out,
           q_in, kv, w, qt, acc, top, att, own, sib_out, sib_in,
           far_out, far_in, near_out, near_in, result, order, span_of,
           load_sem, kv_send, kv_recv, sib_send, sib_recv,
           far_send, far_recv, near_send, near_recv, out_sem):
    heads = q_in.shape[1] // HEAD_DIM
    rows = q_in.shape[0]
    context = lax.axis_index("context")
    tensor = lax.axis_index("tensor")
    y, z = context // RING, lax.rem(context, RING)
    x, core = tensor // 2, lax.rem(tensor, 2)
    ahead = 1 - 2 * core
    targets = {
        "minus": {"context": y * RING + lax.rem(z + RING - ahead, RING)},
        "plus": {"context": y * RING + lax.rem(z + RING + ahead, RING)},
        "other": {"context": (1 - y) * RING + z},
    }
    sibling = {"tensor": x * 2 + 1 - core}
    chip_next, chip_back = lax.rem(x + CHIPS + ahead, CHIPS), lax.rem(x + CHIPS - ahead, CHIPS)
    chip_far = lax.rem(x + 2, CHIPS)
    to_next, to_back = {"tensor": chip_next * 2 + core}, {"tensor": chip_back * 2 + core}

    barrier = pltpu.get_barrier_semaphore()
    for target in (*targets.values(), sibling, to_next, to_back):
        pl.semaphore_signal(barrier, inc=1, device_id=target, device_id_type=MESH)

    loads = []
    for half in range(2):
        for part, source in enumerate((k_hbm, v_hbm)):
            loads.append(pltpu.make_async_copy(
                source.at[pl.ds(half * SPAN, SPAN)], kv.at[half, part],
                load_sem.at[2 * half + part]))
    chips = ((chip_far, chip_next, chip_back, x), (chip_far, chip_back, chip_next, x))
    for group in range(4):
        for part, owner in enumerate((core, 1 - core)):
            number = 2 * group + part
            chip = chips[part][group]
            first = pl.multiple_of(chip * 64 + owner * 32, 32)
            loads.append(pltpu.make_async_copy(
                q_hbm.at[pl.ds(first, 32)], q_in.at[pl.ds(32 * number, 32)],
                load_sem.at[4 + number]))
    loads.append(pltpu.make_async_copy(order_hbm, order, load_sem.at[13]))
    loads.append(pltpu.make_async_copy(w_hbm, w, load_sem.at[12]))

    def own_copies(r):
        for name, src, dst in COPIES[r]:
            for part, source in enumerate((k_hbm, v_hbm)):
                yield pltpu.make_async_remote_copy(
                    src_ref=source.at[pl.ds(src * SPAN, SPAN)], dst_ref=kv.at[dst, part],
                    send_sem=kv_send.at[r], recv_sem=kv_recv.at[r],
                    device_id=targets[name], device_id_type=MESH)

    def copy_of(r, name, src, dst):
        return pltpu.make_async_remote_copy(
            src_ref=kv.at[src], dst_ref=kv.at[dst],
            send_sem=kv_send.at[r], recv_sem=kv_recv.at[r],
            device_id=targets[name], device_id_type=MESH)

    def whole(r):
        spans = kv.at[pl.ds(2 + 3 * r, 3)]
        return pltpu.make_async_remote_copy(
            src_ref=spans, dst_ref=spans, send_sem=kv_send.at[r], recv_sem=kv_recv.at[r],
            device_id=targets["other"], device_id_type=MESH)

    pl.semaphore_wait(barrier, 6)
    for copy in own_copies(0):
        copy.start()
    for load in loads:
        load.start()

    loads[12].wait()
    for slot, (column, offset, half) in enumerate(CONTENTS):
        where = (y if column == 0 else 1 - y) * RING + lax.rem(z + RING + ahead * offset, RING)
        span_of[slot] = order[2 * where + half]

    for load in loads[4:12]:
        load.wait()
    for head in range(heads):
        qt[head] = q_in[:, head * HEAD_DIM:(head + 1) * HEAD_DIM].T

    whole(0).wait_send()
    for copy in own_copies(1):
        copy.start()
    for load in loads[:4]:
        load.wait()

    lane = lax.broadcasted_iota(jnp.int32, (1, rows), 1)
    group_of = lane // 64
    mine = lax.rem(lane // 32, 2) == 0
    chip_of = jnp.where(group_of == 0, chip_far, jnp.where(group_of == 3, x, jnp.where(
        (group_of == 1) == mine, chip_next, chip_back)))
    owner_of = jnp.where(mine, core, 1 - core)
    row_of = chip_of * 64 + owner_of * 32 + lax.rem(lane, 32)
    q_span = jnp.where(row_of < SPAN, span_of[0], span_of[1])
    q_pos = q_span * SPAN + lax.rem(row_of, SPAN)

    def operands(first, count):
        spans = kv[pl.ds(first, count)]
        keys = spans[:, 0].reshape(count * SPAN, HEAD_DIM)
        values = spans[:, 1].reshape(count * SPAN, HEAD_DIM).T
        ones = jnp.ones((16, count * SPAN), jnp.bfloat16)
        return keys, jnp.concatenate([values, ones], axis=0)

    scale = math.log2(math.e) / math.sqrt(HEAD_DIM)

    def scores_of(keys, head):
        return jnp.dot(keys, qt[head], preferred_element_type=jnp.float32)

    def receive(r):
        following = COPIES[r + 2] if r + 2 < ROUNDS else ()
        here = 2 + 3 * r
        for copy in following:
            if copy[1] < here:
                copy_of(r + 2, *copy).start()
        whole(r).wait_recv()
        for copy in following:
            if copy[1] >= here:
                copy_of(r + 2, *copy).start()

    keys, values = operands(0, 2)
    k_row = lax.broadcasted_iota(jnp.int32, (2 * SPAN, 1), 0)
    k_pos = jnp.where(k_row < SPAN, span_of[0], span_of[1]) * SPAN + lax.rem(k_row, SPAN)
    hide = jnp.where(k_pos <= q_pos, 0.0, LOWEST)
    following = scores_of(keys, 0)
    for head in range(heads):
        scores = following * scale + hide
        if head + 1 < heads:
            following = scores_of(keys, head + 1)
        new_top = jnp.max(scores, axis=0, keepdims=True)
        weights = jnp.exp2(scores - new_top).astype(jnp.bfloat16)
        top[head] = new_top
        acc[head] = jnp.dot(values, weights, preferred_element_type=jnp.float32)

    @pl.loop(0, ROUNDS)
    def _(step):
        for r in range(ROUNDS):
            @pl.when(step == r)
            def _():
                receive(r)

        first = 2 + 3 * step
        keys, values = operands(first, 3)
        hide = [jnp.where(span_of[first + number] < q_span, 0.0, LOWEST) for number in range(3)]
        following = scores_of(keys, 0)
        for head in range(heads):
            scores = [following[number * SPAN:(number + 1) * SPAN] for number in range(3)]
            if head + 1 < heads:
                following = scores_of(keys, head + 1)
            old_top = top[head]
            new_top = old_top
            for part, hidden in zip(scores, hide):
                new_top = jnp.maximum(new_top, jnp.max(part, axis=0, keepdims=True) * scale + hidden)
            factor = jnp.exp2(old_top - new_top)
            weights = jnp.concatenate([
                jnp.exp2(part * scale - (new_top - hidden)).astype(jnp.bfloat16)
                for part, hidden in zip(scores, hide)], axis=0)
            top[head] = new_top
            acc[head] = acc[head] * factor + jnp.dot(
                values, weights, preferred_element_type=jnp.float32)

    for head in range(heads):
        mixed = acc[head, :HEAD_DIM] * (1.0 / acc[head, HEAD_DIM:HEAD_DIM + 1])
        att[:, head * HEAD_DIM:(head + 1) * HEAD_DIM] = mixed.astype(jnp.bfloat16).T
    loads[13].wait()

    def sib_copy(tile):
        at = pl.ds(0, 3)
        return pltpu.make_async_remote_copy(
            src_ref=sib_out.at[tile, at], dst_ref=sib_in.at[tile, at],
            send_sem=sib_send.at[tile], recv_sem=sib_recv.at[tile],
            device_id=sibling, device_id_type=MESH)

    def home_copy():
        return pltpu.make_async_remote_copy(
            src_ref=sib_out.at[:, 3], dst_ref=sib_in.at[:, 3],
            send_sem=sib_send.at[TILES], recv_sem=sib_recv.at[TILES],
            device_id=sibling, device_id_type=MESH)

    def product(rows_from, rows_to, tile):
        part = jnp.dot(att[rows_from:rows_to], w[:, tile * TILE:(tile + 1) * TILE],
                       preferred_element_type=jnp.float32).astype(jnp.bfloat16)
        return part.reshape(-1, 2, 32, TILE)

    def project(tile):
        part = product(0, 192, tile)
        sib_out[tile, :3] = part[:, 1]
        sib_copy(tile).start()
        own[tile, :3] = part[:, 0]

    def project_home(tile):
        part = product(192, 256, tile)
        sib_out[tile, 3] = part[0, 1]
        own[tile, 3] = part[0, 0]

    def both(tile, group):
        return own[tile, group].astype(jnp.float32) + sib_in[tile, group].astype(jnp.float32)

    def far_copy(tile):
        return pltpu.make_async_remote_copy(
            src_ref=far_out.at[tile], dst_ref=far_in.at[tile],
            send_sem=far_send.at[tile], recv_sem=far_recv.at[tile],
            device_id=to_next if tile < HALF else to_back, device_id_type=MESH)

    def near_copy(side, tile, count):
        at = pl.ds(tile, count)
        return pltpu.make_async_remote_copy(
            src_ref=near_out.at[side, at], dst_ref=near_in.at[side, at],
            send_sem=near_send.at[side, tile], recv_sem=near_recv.at[side, tile],
            device_id=to_next if side == 0 else to_back, device_id_type=MESH)

    def out_copy(tile):
        at = pl.ds(tile * TILE, TILE)
        return pltpu.make_async_copy(result.at[:, at], out.at[:, at], out_sem.at[tile])

    def first_side(tile):
        return 0 if tile >= HALF else 1

    def send_first(tile):
        sib_copy(tile).wait_recv()
        far_out[tile] = both(tile, 0).astype(jnp.bfloat16)
        far_copy(tile).start()
        side = first_side(tile)
        near_out[side, tile] = both(tile, 1 + side).astype(jnp.bfloat16)
        near_copy(side, tile, 1).start()

    def send_second(tile):
        side = 1 - first_side(tile)
        for one in (tile, tile + 1):
            far_copy(one).wait_recv()
            total = both(one, 1 + side) + far_in[one].astype(jnp.float32)
            near_out[side, one] = total.astype(jnp.bfloat16)
        near_copy(side, tile, 2).start()

    project(ORDER[0])
    for earlier, tile in zip(ORDER, ORDER[1:]):
        project(tile)
        send_first(earlier)
    send_first(ORDER[-1])
    for tile in PAIRED[:2]:
        send_second(tile)
    for tile in ORDER:
        project_home(tile)
    home_copy().start()
    for tile in PAIRED[2:]:
        send_second(tile)
    for r in range(1, ROUNDS):
        whole(r).wait_send()
    for tile in range(TILES):
        sib_copy(tile).wait_send()
        far_copy(tile).wait_send()
        near_copy(first_side(tile), tile, 1).wait_send()
    home_copy().wait()
    for pair in PAIRED:
        near_copy(1 - first_side(pair), pair, 2).wait_recv()
        for tile in (pair, pair + 1):
            near_copy(first_side(tile), tile, 1).wait_recv()
            total = both(tile, 3) + (near_in[0, tile].astype(jnp.float32)
                                     + near_in[1, tile].astype(jnp.float32))
            result[:, tile * TILE:(tile + 1) * TILE] = total.astype(out.dtype)
            out_copy(tile).start()

    for pair in PAIRED:
        near_copy(1 - first_side(pair), pair, 2).wait_send()
        for tile in (pair, pair + 1):
            out_copy(tile).wait()


def on_device(queries, keys, values, span_order, out_weight):
    rows, width = queries.shape
    heads = width // HEAD_DIM
    d_out = out_weight.shape[1]
    bf16, f32 = jnp.bfloat16, jnp.float32
    sem = pltpu.SemaphoreType.DMA
    span_order, queries, keys, values, out_weight = (
        pltpu.with_memory_space_constraint(array, pltpu.HBM)
        for array in (span_order, queries, keys, values, out_weight))
    return pl.pallas_call(
        kernel,
        out_shape=jax.ShapeDtypeStruct((rows // 8, d_out), bf16),
        in_specs=[pl.BlockSpec(memory_space=pltpu.HBM)] * 5,
        out_specs=pl.BlockSpec(memory_space=pl.ANY),
        scratch_shapes=[
            pltpu.VMEM((rows, width), bf16),
            pltpu.VMEM((SPANS, 2, SPAN, HEAD_DIM), bf16),
            pltpu.VMEM((width, d_out), bf16),
            pltpu.VMEM((heads, HEAD_DIM, rows), bf16),
            pltpu.VMEM((heads, HEAD_DIM + 16, rows), f32),
            pltpu.VMEM((heads, 1, rows), f32),
            pltpu.VMEM((rows, width), bf16),
            pltpu.VMEM((TILES, 4, 32, TILE), bf16),
            pltpu.VMEM((TILES, 4, 32, TILE), bf16),
            pltpu.VMEM((TILES, 4, 32, TILE), bf16),
            pltpu.VMEM((TILES, 32, TILE), bf16),
            pltpu.VMEM((TILES, 32, TILE), bf16),
            pltpu.VMEM((2, TILES, 32, TILE), bf16),
            pltpu.VMEM((2, TILES, 32, TILE), bf16),
            pltpu.VMEM((rows // 8, d_out), bf16),
            pltpu.SMEM((SPANS,), jnp.int32),
            pltpu.SMEM((SPANS,), jnp.int32),
            sem((14,)), sem((ROUNDS,)), sem((ROUNDS,)),
            sem((TILES + 1,)), sem((TILES + 1,)), sem((TILES,)), sem((TILES,)),
            sem((2, TILES)), sem((2, TILES)), sem((TILES,)),
        ],
        compiler_params=pltpu.CompilerParams(
            collective_id=0, has_side_effects=True, vmem_limit_bytes=32 * 1024 * 1024),
        cost_estimate=pl.CostEstimate(
            flops=3 * 2 * rows * width * 4096, bytes_accessed=10 * 2**20,
            transcendentals=heads * rows * 4096),
    )(span_order, queries, keys, values, out_weight)


def solution(mesh):
    return jax.shard_map(
        on_device,
        mesh=mesh,
        in_specs=(
            P(("dp", "context"), "tensor"),
            P(("dp", "context"), "tensor"),
            P(("dp", "context"), "tensor"),
            P("dp"),
            P("tensor", None),
        ),
        out_specs=P(("dp", "context", "tensor"), None),
        check_vma=False,
    )
```

```python
import math

import jax
import jax.numpy as jnp
from jax import lax
from jax.experimental import pallas as pl
from jax.experimental.pallas import tpu as pltpu
from jax.sharding import PartitionSpec as P

HEAD_DIM = 128
SPAN = 128
RING = 8
COLUMNS = 2
CHIPS = 4
ROUNDS = 10
TILE = 512
TILES = 8
HALF = TILES // 2
LOWEST = -1e30
MESH = pl.DeviceIdType.MESH

UP = [(0, 1, 0), (0, 1, 1), (0, 2, 0), (0, 2, 1), (0, 3, 0), (0, 3, 1),
      (1, 3, 0), (0, 4, 0), (1, 4, 0), (1, 3, 1)]
DOWN = [(0, -1, 1), (0, -1, 0), (0, -2, 1), (0, -2, 0), (0, -3, 1), (0, -3, 0),
        (0, -4, 1), (1, -3, 1), (1, -3, 0), (1, -4, 1)]
ACROSS = [(1, 0, 0), (1, 0, 1), (1, 1, 0), (1, -1, 1), (1, 2, 0), (1, -2, 1),
          (1, -2, 0), (1, 2, 1), (1, 1, 1), (1, -1, 0)]


def plan():
    slot_of = {(0, 0, 0): 0, (0, 0, 1): 1}
    contents = [(0, 0, 0), (0, 0, 1)]
    up_slot = {r: 2 + 3 * r for r in range(ROUNDS)}
    down_slot = {r: 3 + 3 * r for r in range(ROUNDS)}
    across_slot = {r: 4 + 3 * r for r in range(ROUNDS)}
    slots = {}
    for r in range(ROUNDS):
        for table, names in ((up_slot, UP), (down_slot, DOWN), (across_slot, ACROSS)):
            slots[table[r]] = names[r]
    for slot in range(2, 2 + 3 * ROUNDS):
        column, offset, half = slots[slot]
        key = (column, offset % RING, half)
        slot_of[key] = slot
        contents.append(key)
    assert len(slot_of) == 2 + 3 * ROUNDS
    copies = []
    for r in range(ROUNDS):
        (uc, uo, uh), (dc, do, dh), (ac, ao, ah) = UP[r], DOWN[r], ACROSS[r]
        copies.append((
            ("minus", slot_of[(uc, (uo - 1) % RING, uh)], up_slot[r]),
            ("plus", slot_of[(dc, (do + 1) % RING, dh)], down_slot[r]),
            ("other", slot_of[(0, ao % RING, ah)], across_slot[r]),
        ))
    return contents, copies


CONTENTS, COPIES = plan()
SPANS = len(CONTENTS)
PAIRED = (0, 4, 2, 6)
ORDER = tuple(part * HALF + tile for tile in range(HALF) for part in range(2))


def kernel(order_hbm, q_hbm, k_hbm, v_hbm, w_hbm, out,
           q_in, kv, w, qt, acc, top, att, own, sib_out, sib_in,
           far_out, far_in, near_out, near_in, result, order, span_of,
           load_sem, kv_send, kv_recv, sib_send, sib_recv,
           far_send, far_recv, near_send, near_recv, out_sem):
    heads = q_in.shape[1] // HEAD_DIM
    rows = q_in.shape[0]
    context = lax.axis_index("context")
    tensor = lax.axis_index("tensor")
    y, z = context // RING, lax.rem(context, RING)
    x, core = tensor // 2, lax.rem(tensor, 2)
    ahead = 1 - 2 * core
    targets = {
        "minus": {"context": y * RING + lax.rem(z + RING - ahead, RING)},
        "plus": {"context": y * RING + lax.rem(z + RING + ahead, RING)},
        "other": {"context": (1 - y) * RING + z},
    }
    sibling = {"tensor": x * 2 + 1 - core}
    chip_next, chip_back = lax.rem(x + CHIPS + ahead, CHIPS), lax.rem(x + CHIPS - ahead, CHIPS)
    chip_far = lax.rem(x + 2, CHIPS)
    to_next, to_back = {"tensor": chip_next * 2 + core}, {"tensor": chip_back * 2 + core}

    barrier = pltpu.get_barrier_semaphore()
    for target in (*targets.values(), sibling, to_next, to_back):
        pl.semaphore_signal(barrier, inc=1, device_id=target, device_id_type=MESH)

    loads = []
    for half in range(2):
        for part, source in enumerate((k_hbm, v_hbm)):
            loads.append(pltpu.make_async_copy(
                source.at[pl.ds(half * SPAN, SPAN)], kv.at[half, part],
                load_sem.at[2 * half + part]))
    chips = ((chip_far, chip_next, chip_back, x), (chip_far, chip_back, chip_next, x))
    for group in range(4):
        for part, owner in enumerate((core, 1 - core)):
            number = 2 * group + part
            chip = chips[part][group]
            first = pl.multiple_of(chip * 64 + owner * 32, 32)
            loads.append(pltpu.make_async_copy(
                q_hbm.at[pl.ds(first, 32)], q_in.at[pl.ds(32 * number, 32)],
                load_sem.at[4 + number]))
    loads.append(pltpu.make_async_copy(order_hbm, order, load_sem.at[13]))
    loads.append(pltpu.make_async_copy(w_hbm, w, load_sem.at[12]))

    def own_copies(r):
        for name, src, dst in COPIES[r]:
            for part, source in enumerate((k_hbm, v_hbm)):
                yield pltpu.make_async_remote_copy(
                    src_ref=source.at[pl.ds(src * SPAN, SPAN)], dst_ref=kv.at[dst, part],
                    send_sem=kv_send.at[r], recv_sem=kv_recv.at[r],
                    device_id=targets[name], device_id_type=MESH)

    def copy_of(r, name, src, dst):
        return pltpu.make_async_remote_copy(
            src_ref=kv.at[src], dst_ref=kv.at[dst],
            send_sem=kv_send.at[r], recv_sem=kv_recv.at[r],
            device_id=targets[name], device_id_type=MESH)

    def whole(r):
        spans = kv.at[pl.ds(2 + 3 * r, 3)]
        return pltpu.make_async_remote_copy(
            src_ref=spans, dst_ref=spans, send_sem=kv_send.at[r], recv_sem=kv_recv.at[r],
            device_id=targets["other"], device_id_type=MESH)

    pl.semaphore_wait(barrier, 6)
    for copy in own_copies(0):
        copy.start()
    for load in loads:
        load.start()

    loads[12].wait()
    for slot, (column, offset, half) in enumerate(CONTENTS):
        where = (y if column == 0 else 1 - y) * RING + lax.rem(z + RING + ahead * offset, RING)
        span_of[slot] = order[2 * where + half]

    for load in loads[4:12]:
        load.wait()
    for head in range(heads):
        qt[head] = q_in[:, head * HEAD_DIM:(head + 1) * HEAD_DIM].T

    for copy in own_copies(1):
        copy.start()
    for load in loads[:4]:
        load.wait()

    lane = lax.broadcasted_iota(jnp.int32, (1, rows), 1)
    group_of = lane // 64
    mine = lax.rem(lane // 32, 2) == 0
    chip_of = jnp.where(group_of == 0, chip_far, jnp.where(group_of == 3, x, jnp.where(
        (group_of == 1) == mine, chip_next, chip_back)))
    owner_of = jnp.where(mine, core, 1 - core)
    row_of = chip_of * 64 + owner_of * 32 + lax.rem(lane, 32)
    q_span = jnp.where(row_of < SPAN, span_of[0], span_of[1])
    q_pos = q_span * SPAN + lax.rem(row_of, SPAN)

    def operands(first, count):
        spans = kv[pl.ds(first, count)]
        keys = spans[:, 0].reshape(count * SPAN, HEAD_DIM)
        values = spans[:, 1].reshape(count * SPAN, HEAD_DIM).T
        ones = jnp.ones((16, count * SPAN), jnp.bfloat16)
        return keys, jnp.concatenate([values, ones], axis=0)

    scale = math.log2(math.e) / math.sqrt(HEAD_DIM)

    def scores_of(keys, head):
        return jnp.dot(keys, qt[head], preferred_element_type=jnp.float32)

    def receive(r):
        following = COPIES[r + 2] if r + 2 < ROUNDS else ()
        here = 2 + 3 * r
        for copy in following:
            if copy[1] < here:
                copy_of(r + 2, *copy).start()
        whole(r).wait_recv()
        for copy in following:
            if copy[1] >= here:
                copy_of(r + 2, *copy).start()

    keys, values = operands(0, 2)
    k_row = lax.broadcasted_iota(jnp.int32, (2 * SPAN, 1), 0)
    k_pos = jnp.where(k_row < SPAN, span_of[0], span_of[1]) * SPAN + lax.rem(k_row, SPAN)
    hide = jnp.where(k_pos <= q_pos, 0.0, LOWEST)
    following = scores_of(keys, 0)
    for head in range(heads):
        scores = following * scale + hide
        if head + 1 < heads:
            following = scores_of(keys, head + 1)
        new_top = jnp.max(scores, axis=0, keepdims=True)
        weights = jnp.exp2(scores - new_top).astype(jnp.bfloat16)
        top[head] = new_top
        acc[head] = jnp.dot(values, weights, preferred_element_type=jnp.float32)

    @pl.loop(0, ROUNDS)
    def _(step):
        for r in range(ROUNDS):
            @pl.when(step == r)
            def _():
                receive(r)

        first = 2 + 3 * step
        keys, values = operands(first, 3)
        hide = [jnp.where(span_of[first + number] < q_span, 0.0, LOWEST) for number in range(3)]
        following = scores_of(keys, 0)
        for head in range(heads):
            scores = [following[number * SPAN:(number + 1) * SPAN] for number in range(3)]
            if head + 1 < heads:
                following = scores_of(keys, head + 1)
            old_top = top[head]
            new_top = old_top
            for part, hidden in zip(scores, hide):
                new_top = jnp.maximum(new_top, jnp.max(part, axis=0, keepdims=True) * scale + hidden)
            factor = jnp.exp2(old_top - new_top)
            weights = jnp.concatenate([
                jnp.exp2(part * scale - (new_top - hidden)).astype(jnp.bfloat16)
                for part, hidden in zip(scores, hide)], axis=0)
            top[head] = new_top
            acc[head] = acc[head] * factor + jnp.dot(
                values, weights, preferred_element_type=jnp.float32)

    for head in range(heads):
        mixed = acc[head, :HEAD_DIM] * (1.0 / acc[head, HEAD_DIM:HEAD_DIM + 1])
        att[:, head * HEAD_DIM:(head + 1) * HEAD_DIM] = mixed.astype(jnp.bfloat16).T
    loads[13].wait()

    def sib_copy(tile):
        at = pl.ds(0, 3)
        return pltpu.make_async_remote_copy(
            src_ref=sib_out.at[tile, at], dst_ref=sib_in.at[tile, at],
            send_sem=sib_send.at[tile], recv_sem=sib_recv.at[tile],
            device_id=sibling, device_id_type=MESH)

    def home_copy():
        return pltpu.make_async_remote_copy(
            src_ref=sib_out.at[:, 3], dst_ref=sib_in.at[:, 3],
            send_sem=sib_send.at[TILES], recv_sem=sib_recv.at[TILES],
            device_id=sibling, device_id_type=MESH)

    def product(rows_from, rows_to, tile):
        part = jnp.dot(att[rows_from:rows_to], w[:, tile * TILE:(tile + 1) * TILE],
                       preferred_element_type=jnp.float32).astype(jnp.bfloat16)
        return part.reshape(-1, 2, 32, TILE)

    def project(tile):
        part = product(0, 192, tile)
        sib_out[tile, :3] = part[:, 1]
        sib_copy(tile).start()
        own[tile, :3] = part[:, 0]

    def project_home(tile):
        part = product(192, 256, tile)
        sib_out[tile, 3] = part[0, 1]
        own[tile, 3] = part[0, 0]

    def both(tile, group):
        return own[tile, group].astype(jnp.float32) + sib_in[tile, group].astype(jnp.float32)

    def far_copy(tile):
        return pltpu.make_async_remote_copy(
            src_ref=far_out.at[tile], dst_ref=far_in.at[tile],
            send_sem=far_send.at[tile], recv_sem=far_recv.at[tile],
            device_id=to_next if tile < HALF else to_back, device_id_type=MESH)

    def near_copy(side, tile, count):
        at = pl.ds(tile, count)
        return pltpu.make_async_remote_copy(
            src_ref=near_out.at[side, at], dst_ref=near_in.at[side, at],
            send_sem=near_send.at[side, tile], recv_sem=near_recv.at[side, tile],
            device_id=to_next if side == 0 else to_back, device_id_type=MESH)

    def out_copy(tile):
        at = pl.ds(tile * TILE, TILE)
        return pltpu.make_async_copy(result.at[:, at], out.at[:, at], out_sem.at[tile])

    def first_side(tile):
        return 0 if tile >= HALF else 1

    def send_first(tile):
        sib_copy(tile).wait_recv()
        far_out[tile] = both(tile, 0).astype(jnp.bfloat16)
        far_copy(tile).start()
        side = first_side(tile)
        near_out[side, tile] = both(tile, 1 + side).astype(jnp.bfloat16)
        near_copy(side, tile, 1).start()

    def send_second(tile):
        side = 1 - first_side(tile)
        for one in (tile, tile + 1):
            far_copy(one).wait_recv()
            total = both(one, 1 + side) + far_in[one].astype(jnp.float32)
            near_out[side, one] = total.astype(jnp.bfloat16)
        near_copy(side, tile, 2).start()

    project(ORDER[0])
    for earlier, tile in zip(ORDER, ORDER[1:]):
        project(tile)
        send_first(earlier)
    send_first(ORDER[-1])
    for tile in PAIRED[:2]:
        send_second(tile)
    for tile in ORDER:
        project_home(tile)
    home_copy().start()
    for tile in PAIRED[2:]:
        send_second(tile)
    for r in range(ROUNDS):
        whole(r).wait_send()
    for tile in range(TILES):
        sib_copy(tile).wait_send()
        far_copy(tile).wait_send()
        near_copy(first_side(tile), tile, 1).wait_send()
    home_copy().wait()
    for pair in PAIRED:
        near_copy(1 - first_side(pair), pair, 2).wait_recv()
        for tile in (pair, pair + 1):
            near_copy(first_side(tile), tile, 1).wait_recv()
            total = both(tile, 3) + (near_in[0, tile].astype(jnp.float32)
                                     + near_in[1, tile].astype(jnp.float32))
            result[:, tile * TILE:(tile + 1) * TILE] = total.astype(out.dtype)
            out_copy(tile).start()

    for pair in PAIRED:
        near_copy(1 - first_side(pair), pair, 2).wait_send()
        for tile in (pair, pair + 1):
            out_copy(tile).wait()


def on_device(queries, keys, values, span_order, out_weight):
    rows, width = queries.shape
    heads = width // HEAD_DIM
    d_out = out_weight.shape[1]
    bf16, f32 = jnp.bfloat16, jnp.float32
    sem = pltpu.SemaphoreType.DMA
    span_order, queries, keys, values, out_weight = (
        pltpu.with_memory_space_constraint(array, pltpu.HBM)
        for array in (span_order, queries, keys, values, out_weight))
    return pl.pallas_call(
        kernel,
        out_shape=jax.ShapeDtypeStruct((rows // 8, d_out), bf16),
        in_specs=[pl.BlockSpec(memory_space=pltpu.HBM)] * 5,
        out_specs=pl.BlockSpec(memory_space=pl.ANY),
        scratch_shapes=[
            pltpu.VMEM((rows, width), bf16),
            pltpu.VMEM((SPANS, 2, SPAN, HEAD_DIM), bf16),
            pltpu.VMEM((width, d_out), bf16),
            pltpu.VMEM((heads, HEAD_DIM, rows), bf16),
            pltpu.VMEM((heads, HEAD_DIM + 16, rows), f32),
            pltpu.VMEM((heads, 1, rows), f32),
            pltpu.VMEM((rows, width), bf16),
            pltpu.VMEM((TILES, 4, 32, TILE), bf16),
            pltpu.VMEM((TILES, 4, 32, TILE), bf16),
            pltpu.VMEM((TILES, 4, 32, TILE), bf16),
            pltpu.VMEM((TILES, 32, TILE), bf16),
            pltpu.VMEM((TILES, 32, TILE), bf16),
            pltpu.VMEM((2, TILES, 32, TILE), bf16),
            pltpu.VMEM((2, TILES, 32, TILE), bf16),
            pltpu.VMEM((rows // 8, d_out), bf16),
            pltpu.SMEM((SPANS,), jnp.int32),
            pltpu.SMEM((SPANS,), jnp.int32),
            sem((14,)), sem((ROUNDS,)), sem((ROUNDS,)),
            sem((TILES + 1,)), sem((TILES + 1,)), sem((TILES,)), sem((TILES,)),
            sem((2, TILES)), sem((2, TILES)), sem((TILES,)),
        ],
        compiler_params=pltpu.CompilerParams(
            collective_id=0, has_side_effects=True, vmem_limit_bytes=32 * 1024 * 1024),
        cost_estimate=pl.CostEstimate(
            flops=3 * 2 * rows * width * 4096, bytes_accessed=10 * 2**20,
            transcendentals=heads * rows * 4096),
    )(span_order, queries, keys, values, out_weight)


def solution(mesh):
    return jax.shard_map(
        on_device,
        mesh=mesh,
        in_specs=(
            P(("dp", "context"), "tensor"),
            P(("dp", "context"), "tensor"),
            P(("dp", "context"), "tensor"),
            P("dp"),
            P("tensor", None),
        ),
        out_specs=P(("dp", "context", "tensor"), None),
        check_vma=False,
    )
```
